32 devices in a mesh: dp: 4 (over z), fsdp: 8 (over y, x, core).
Axes of the slice: x: 2, y: 2, z: 4, core: 2. Of those that a mesh axis runs over, the one named last changes fastest.
Arguments:
- tokens: bfloat16 [12288, 2048], P(('dp', 'fsdp')), may hold values from -6 to 6
- lengths: int32 [32], P(('dp', 'fsdp')), may hold values from 1 to 384, 6144 in all
- cotangent: bfloat16 [12288, 2048], P(('dp', 'fsdp')), may hold values from -6 to 6
- attention_gain: bfloat16 [2048], P(('dp', 'fsdp')), may hold values from 0.099609375 to 1.8984375
- query_weight: bfloat16 [2048, 2048], P(('dp', 'fsdp')), may hold values from -0.125 to 0.125
- key_matrix: bfloat16 [2048, 1024], P(('dp', 'fsdp')), may hold values from -0.125 to 0.125
- value_matrix: bfloat16 [2048, 1024], P(('dp', 'fsdp')), may hold values from -0.125 to 0.125
- head_gate_weight: bfloat16 [2048, 16], P(('dp', 'fsdp')), may hold values from -0.125 to 0.125
- output_weight: bfloat16 [2048, 2048], P(('dp', 'fsdp')), may hold values from -2 to 2
- query_key_gain: bfloat16 [2, 128], P(None, ('dp', 'fsdp')), may hold values from 0.099609375 to 1.8984375
- feedforward_gain: bfloat16 [2048], P(('dp', 'fsdp')), may hold values from 0.099609375 to 1.8984375
- gate_weight: bfloat16 [2048, 6144], P(('dp', 'fsdp')), may hold values from -0.125 to 0.125
- up_weight: bfloat16 [2048, 6144], P(('dp', 'fsdp')), may hold values from -0.125 to 0.125
- down_weight: bfloat16 [6144, 2048], P(('dp', 'fsdp')), may hold values from -0.078125 to 0.078125
Outputs:
- layer_output: bfloat16 [12288, 2048], P(('dp', 'fsdp'))
- tokens_grad: bfloat16 [12288, 2048], P(('dp', 'fsdp'))
- attention_gain_grad: float32 [2048], P(('dp', 'fsdp'))
- query_grad: float32 [2048, 2048], P(('dp', 'fsdp'))
- key_grad: float32 [2048, 1024], P(('dp', 'fsdp'))
- value_grad: float32 [2048, 1024], P(('dp', 'fsdp'))
- head_gate_grad: float32 [2048, 16], P(('dp', 'fsdp'))
- output_grad: float32 [2048, 2048], P(('dp', 'fsdp'))
- query_key_gain_grad: float32 [2, 128], P(None, ('dp', 'fsdp'))
- feedforward_gain_grad: float32 [2048], P(('dp', 'fsdp'))
- gate_grad: float32 [2048, 6144], P(('dp', 'fsdp'))
- up_grad: float32 [2048, 6144], P(('dp', 'fsdp'))
- down_grad: float32 [6144, 2048], P(('dp', 'fsdp'))
The draws below stay inside these ranges and needn't reach their ends.
Inputs may be any that keep to these rules, and one draw needn't show every extreme that they name: `lengths`: one length a sequence; they sum to 6144 and the longest is exactly 384.
All inputs are finite; a program needn't handle non-finite values. No bound on the sum of `lengths` on one device may be relied on, other than what follows from the above.
Results may differ from the reference program's by a relative error of at most 0.015.
Values may be sent and summed in bfloat16 or wider, within the bound.
A program may use at most 448 MiB of HBM per device.

```python
import math
import jax
import jax.numpy as jnp
import numpy as np
from jax import lax

MODEL_WIDTH = 2048
FF = 6144
HQ = 16
KEY_VALUE_HEADS = 8
HEAD_WIDTH = 128
PADDED_LENGTH = 384
SEQUENCE_COUNT = 32
TOKENS = 12288


def block_scale(rng, extent, split, least, top_value):
    def one(dim, blocks):
        heights = jax.random.uniform(jax.random.fold_in(jax.random.fold_in(rng, 6), dim), (blocks,), jnp.float32, least / len(split), top_value / len(split))
        return jnp.repeat(jnp.exp(heights), extent[dim] // blocks).reshape((-1,) + (1,) * (len(extent) - dim - 1))

    level = one(*split[0])
    for cut in split[1:]:
        level = level * one(*cut)
    return level


def profile(count, total, limit, slope):
    weights = [(1 << 20) // math.isqrt(standing ** slope) + 1 for standing in range(2, count + 1)]
    spare, holding = total - limit - (count - 1), [1] * (count - 1)
    while spare > 0:
        movable = [i for i in range(count - 1) if holding[i] < limit]
        mass, remaining = sum([weights[i] for i in movable]), spare
        for i in movable:
            addition = min(limit - holding[i], max(1, remaining * weights[i] // mass), spare)
            holding[i] = holding[i] + addition
            spare = spare - addition
    return np.array([limit] + holding)


def uneven(rng, count, total, most, slope):
    if count == 2:
        one = jax.random.randint(rng, (), max(1, total - most), min(most, total - 1) + 1)
        return jnp.stack([one, total - one])
    sizes = jnp.asarray(profile(count, total, most, slope), jnp.int32)
    couples = (count - 1) // 2
    giver, receiver = sizes[1:1 + 2 * couples:2], sizes[2:2 + 2 * couples:2]
    margin = jnp.minimum(giver - 1, most - receiver)
    passed = jax.random.randint(jax.random.fold_in(rng, 1), (couples,), 0, 1 << 20) % (margin + 1)
    sizes = sizes.at[1:1 + 2 * couples:2].set(giver - passed).at[2:2 + 2 * couples:2].set(receiver + passed)
    return sizes[jax.random.permutation(jax.random.fold_in(rng, 2), count)]


def normal_values(key, extent, width, most, cuts=(), held_as=jnp.bfloat16):
    level = block_scale(key, extent, cuts, -0.22, 0.18) if cuts else 1.0
    values = jax.random.normal(key, extent, jnp.float32) * width * level
    return jnp.minimum(jnp.maximum(values, -most), most).astype(held_as)


def setup_inputs(seed: int = 0) -> dict:
    arg_keys = jax.random.split(jax.random.key(seed), 15)
    return {
        "tokens": normal_values(arg_keys[0], (TOKENS, MODEL_WIDTH), 1.0, 6.0, ((0, 32),)),
        "lengths": uneven(arg_keys[1], SEQUENCE_COUNT, SEQUENCE_COUNT * PADDED_LENGTH // 2, PADDED_LENGTH, 2).astype(jnp.int32),
        "cotangent": normal_values(arg_keys[2], (TOKENS, MODEL_WIDTH), 1.0, 6.0, ((0, 32),)),
        "attention_gain": jnp.clip(1.0 + 0.18 * jax.random.normal(arg_keys[3], (MODEL_WIDTH,), jnp.float32), 0.099609375, 1.8984375).astype(jnp.bfloat16),
        "query_weight": normal_values(arg_keys[4], (MODEL_WIDTH, HQ * HEAD_WIDTH), MODEL_WIDTH ** -0.5, 0.125, ((0, 32),)),
        "key_matrix": normal_values(arg_keys[5], (MODEL_WIDTH, KEY_VALUE_HEADS * HEAD_WIDTH), MODEL_WIDTH ** -0.5, 0.125, ((0, 32),)),
        "value_matrix": normal_values(arg_keys[6], (MODEL_WIDTH, KEY_VALUE_HEADS * HEAD_WIDTH), MODEL_WIDTH ** -0.5, 0.125, ((0, 32),)),
        "head_gate_weight": normal_values(arg_keys[7], (MODEL_WIDTH, HQ), MODEL_WIDTH ** -0.5, 0.125, ((0, 32),)),
        "output_weight": normal_values(arg_keys[8], (HQ * HEAD_WIDTH, MODEL_WIDTH), (max(1, HQ * HEAD_WIDTH * 2 // PADDED_LENGTH)) ** -0.5, 2.0, ((0, 32),)),
        "query_key_gain": jnp.clip(1.0 + 0.18 * jax.random.normal(arg_keys[9], (2, HEAD_WIDTH), jnp.float32), 0.099609375, 1.8984375).astype(jnp.bfloat16),
        "feedforward_gain": jnp.clip(1.0 + 0.18 * jax.random.normal(arg_keys[10], (MODEL_WIDTH,), jnp.float32), 0.099609375, 1.8984375).astype(jnp.bfloat16),
        "gate_weight": normal_values(arg_keys[11], (MODEL_WIDTH, FF), MODEL_WIDTH ** -0.5, 0.125, ((0, 32),)),
        "up_weight": normal_values(arg_keys[12], (MODEL_WIDTH, FF), MODEL_WIDTH ** -0.5, 0.125, ((0, 32),)),
        "down_weight": normal_values(arg_keys[13], (FF, MODEL_WIDTH), FF ** -0.5, 0.078125, ((0, 32),)),
    }


EPSILON = 1e-06
ROPE_BASE = 1000000.0
HIGHEST = lax.Precision.HIGHEST

@jax.custom_vjp
def reduced_precision(v):
    return lax.optimization_barrier(v.astype(jnp.bfloat16)).astype(jnp.float32)

@jax.custom_vjp
def reduced_precision_backward(v):
    return v

def low_keep(v):
    return (reduced_precision(v), None)

def low_pass(kept, grad):
    return (grad,)

def back_keep(v):
    return (v, None)

def back_low(kept, grad):
    return (reduced_precision(grad),)
reduced_precision.defvjp(low_keep, low_pass)
reduced_precision_backward.defvjp(back_keep, back_low)

def matrix_product(left, right):
    return jnp.dot(left, right, precision=HIGHEST)

def norm_scale(tensor, gain_vector):
    return tensor * lax.rsqrt(lax.optimization_barrier(jnp.mean(tensor * tensor, axis=-1, keepdims=True)) + EPSILON) * gain_vector

def rotary(tensor):
    length = tensor.shape[-3]
    half_size = tensor.shape[-1] // 2
    exponent = jnp.arange(half_size, dtype=jnp.float32) * (-2.0 / tensor.shape[-1])
    frequency = jnp.power(ROPE_BASE, exponent)
    angles = jnp.arange(length, dtype=jnp.float32)[:, None] * frequency[None, :]
    cosine = jnp.cos(angles)[:, None, :]
    sine_part = jnp.sin(angles)[:, None, :]
    first = tensor[..., :half_size]
    second = tensor[..., half_size:]
    return jnp.concatenate([first * cosine - second * sine_part, second * cosine + first * sine_part], axis=-1)

def attend_one(operands):
    query_rot, key_rot, value_rows = operands
    length, head_count, head_size = query_rot.shape
    kv_count = key_rot.shape[1]
    grouped = query_rot.reshape(length, kv_count, head_count // kv_count, head_size)
    scores = reduced_precision_backward(jnp.einsum('qkgd,skd->kgqs', grouped, key_rot, precision=HIGHEST) * head_size ** (-0.5))
    causal = jnp.arange(length)[None, :] <= jnp.arange(length)[:, None]
    attention = jax.nn.softmax(jnp.where(causal, scores, -jnp.inf), axis=-1)
    mixture = jnp.einsum('kgqs,skd->qkgd', reduced_precision(attention), value_rows, precision=HIGHEST)
    return mixture.reshape(length, head_count, head_size)

def forward(params, live_rows):
    inputs, attention_gain, query_weight, key_matrix, value_matrix, head_gate_weight, output_weight, query_key_gain, feedforward_gain, gate_weight, up_weight, down_weight = params
    token_count = inputs.shape[0]
    normalized_input = reduced_precision(norm_scale(inputs, attention_gain))
    query_raw = reduced_precision_backward(matrix_product(normalized_input, query_weight)).reshape(SEQUENCE_COUNT, PADDED_LENGTH, HQ, HEAD_WIDTH)
    key_unrotated = reduced_precision_backward(matrix_product(normalized_input, key_matrix)).reshape(SEQUENCE_COUNT, PADDED_LENGTH, KEY_VALUE_HEADS, HEAD_WIDTH)
    value_rows = reduced_precision(reduced_precision_backward(matrix_product(normalized_input, value_matrix))).reshape(SEQUENCE_COUNT, PADDED_LENGTH, KEY_VALUE_HEADS, HEAD_WIDTH)
    gate_logit = reduced_precision_backward(matrix_product(normalized_input, head_gate_weight))
    query_rot = reduced_precision(rotary(norm_scale(query_raw, query_key_gain[0])))
    key_rot = reduced_precision(rotary(norm_scale(key_unrotated, query_key_gain[1])))
    mixture = lax.map(jax.checkpoint(attend_one), (query_rot, key_rot, value_rows))
    mixture = reduced_precision_backward(mixture.reshape(token_count, HQ, HEAD_WIDTH))
    gated = reduced_precision(mixture * jax.nn.sigmoid(gate_logit)[:, :, None]).reshape(token_count, HQ * HEAD_WIDTH)
    hidden_state = inputs + reduced_precision_backward(matrix_product(gated, output_weight))
    normed_two = reduced_precision(norm_scale(hidden_state, feedforward_gain))
    gate_part = reduced_precision_backward(matrix_product(normed_two, gate_weight))
    up_part = reduced_precision_backward(matrix_product(normed_two, up_weight))
    inner = reduced_precision(jax.nn.silu(gate_part) * up_part)
    return (hidden_state + reduced_precision_backward(matrix_product(inner, down_weight))) * live_rows

def reference(tokens, lengths, cotangent, attention_gain, query_weight, key_matrix, value_matrix, head_gate_weight, output_weight, query_key_gain, feedforward_gain, gate_weight, up_weight, down_weight):
    positions = jnp.arange(PADDED_LENGTH, dtype=jnp.int32)
    live_rows = (positions[None, :] < lengths[:, None]).astype(jnp.float32).reshape(SEQUENCE_COUNT * PADDED_LENGTH, 1)
    primal = tuple((array.astype(jnp.float32) for array in (tokens, attention_gain, query_weight, key_matrix, value_matrix, head_gate_weight, output_weight, query_key_gain, feedforward_gain, gate_weight, up_weight, down_weight)))

    def layer(params):
        return forward(params, live_rows)
    result, pullback = jax.vjp(layer, primal)
    grads = pullback(cotangent.astype(jnp.float32))[0]
    return (result.astype(jnp.bfloat16), grads[0].astype(jnp.bfloat16), grads[1], grads[2], grads[3], grads[4], grads[5], grads[6], grads[7], grads[8], grads[9], grads[10], grads[11])
```

```python
import jax
import jax.numpy as jnp
from jax import lax
from jax.sharding import PartitionSpec as P

EPSILON = 1e-06
ROPE_BASE = 1000000.0
TEAM = 8
ALL = ("dp", "fsdp")
F32 = jnp.float32
BF16 = jnp.bfloat16


def product(left, right):
    return jnp.dot(left, right, preferred_element_type=F32)


def product_nt(left, right):
    return lax.dot_general(left, right, (((1,), (1,)), ((), ())), preferred_element_type=F32)


def product_tn(left, right):
    return lax.dot_general(left, right, (((0,), (0,)), ((), ())), preferred_element_type=F32)


def world():
    return lax.axis_size(ALL)


def member():
    return lax.axis_index(ALL) % TEAM


def teams():
    return [[first + t for t in range(TEAM)] for first in range(0, world(), TEAM)]


def lines():
    return [list(range(t, world(), TEAM)) for t in range(TEAM)]


def permute(array, pairs):
    return lax.ppermute(
        array, ALL, [(team[a], team[b]) for team in teams() for a, b in pairs]
    )


def swap(array, bits):
    return permute(array, [(i, i ^ bits) for i in range(TEAM)])


def exchange(blocks):
    if lax.axis_size("fsdp") == TEAM:
        return lax.all_to_all(blocks, "fsdp", 0, 0, tiled=True)
    return lax.all_to_all(blocks, ALL, 0, 0, tiled=True, axis_index_groups=teams())


def line_gather(shard):
    if lax.axis_size("fsdp") == TEAM:
        return lax.all_gather(shard, "dp", axis=0, tiled=True)
    return lax.all_gather(shard, ALL, axis=0, tiled=True, axis_index_groups=lines())


def line_sum(array):
    if lax.axis_size("fsdp") == TEAM:
        return lax.psum_scatter(array, "dp", scatter_dimension=0, tiled=True)
    return lax.psum_scatter(array, ALL, scatter_dimension=0, tiled=True, axis_index_groups=lines())


def team_gather(own):
    half = own.shape[0] // 2
    a1 = swap(own, 1)
    a2 = swap(own, 2)
    a4 = swap(own, 4)
    a6 = jnp.concatenate([swap(a4[:half], 2), swap(a2[half:], 4)], axis=0)
    a3 = swap(a2, 1)
    a5 = swap(a4, 1)
    a7 = swap(a6, 1)
    return [own, a1, a2, a3, a4, a5, a6, a7]


def team_sum(parts):
    half = parts[0].shape[0] // 2

    def pair(r):
        return parts[r].astype(F32) + swap(parts[r + 1].astype(BF16), 1).astype(F32)

    s6 = pair(6).astype(BF16)
    u4 = swap(s6[:half], 2).astype(F32)
    u2 = swap(s6[half:], 4).astype(F32)
    s2 = pair(2)
    s4 = pair(4)
    x_top = swap(s2[:half].astype(BF16), 2).astype(F32)
    y_low = swap(s4[half:].astype(BF16), 4).astype(F32)
    x_low = swap((s2[half:] + u2).astype(BF16), 2).astype(F32)
    y_top = swap((s4[:half] + u4).astype(BF16), 4).astype(F32)
    s0 = pair(0)
    return s0 + jnp.concatenate([x_top + y_top, x_low + y_low], axis=0)


def out_weight_in(shard, groups):
    t = member()
    if groups < TEAM:
        gathered = line_gather(shard[None])
        per = TEAM // groups
        b, z = t % groups, t // per
        result = jnp.zeros_like(gathered)
        for j in range(groups):
            perm = [(i, per * ((i % groups + j) % groups) + i // groups) for i in range(TEAM)]
            piece = lax.dynamic_index_in_dim(gathered, (b + j) % groups, 0, keepdims=True)
            piece = permute(piece, perm)
            result = lax.dynamic_update_slice_in_dim(result, piece, (z - j + groups) % groups, 0)
        return result.reshape(-1, shard.shape[1])
    full = lax.all_gather(shard, ALL, axis=0, tiled=True)
    rows = full.shape[0] // TEAM
    return lax.dynamic_slice_in_dim(full, t * rows, rows, 0)


def out_weight_back(grad, groups):
    t = member()
    if groups < TEAM:
        per = TEAM // groups
        b, z = t % groups, t // per
        grad = grad.reshape(groups, -1, grad.shape[1])
        placed = jnp.zeros_like(grad)
        for j in range(groups):
            perm = [(per * ((i % groups + j) % groups) + i // groups, i) for i in range(TEAM)]
            piece = lax.dynamic_index_in_dim(grad, (z - j + groups) % groups, 0, keepdims=True)
            piece = permute(piece, perm)
            placed = lax.dynamic_update_slice_in_dim(placed, piece, (b + j) % groups, 0)
        return line_sum(placed)[0]
    whole = jnp.zeros((grad.shape[0] * TEAM, grad.shape[1]), grad.dtype)
    whole = lax.dynamic_update_slice_in_dim(whole, grad, t * grad.shape[0], 0)
    return lax.psum_scatter(whole, ALL, scatter_dimension=0, tiled=True)


def rms_pull(value, gain, grad):
    scale = lax.rsqrt(jnp.mean(value * value, axis=-1, keepdims=True) + EPSILON)
    weighted = grad * gain
    mean = jnp.mean(weighted * value, axis=-1, keepdims=True)
    back = scale * weighted - scale * scale * scale * value * mean
    return back, jnp.sum((grad * value * scale).reshape(-1, value.shape[-1]), axis=0)


def rms(value, gain):
    return value * lax.rsqrt(jnp.mean(value * value, axis=-1, keepdims=True) + EPSILON) * gain


def rotate(u, cosine, sine):
    c = u.shape[-1] // 2
    a, b = u[..., :c], u[..., c:]
    return jnp.concatenate([a * cosine - b * sine, b * cosine + a * sine], axis=-1)


def local(
    groups,
    tokens,
    lengths,
    cotangent,
    attention_gain,
    query_weight,
    key_matrix,
    value_matrix,
    head_gate_weight,
    output_weight,
    query_key_gain,
    feedforward_gain,
    gate_weight,
    up_weight,
    down_weight,
):
    t = member()
    everyone = groups * TEAM
    rows, width = tokens.shape
    rho = query_weight.shape[0]
    phi = down_weight.shape[0]
    ff = gate_weight.shape[1]
    pair_cols = query_key_gain.shape[1]
    size = pair_cols * everyone
    heads = query_weight.shape[1] // size
    mine = heads // TEAM
    q_cols = query_weight.shape[1] // TEAM
    k_cols = key_matrix.shape[1] // TEAM
    ff_cols = ff // TEAM

    small = jnp.zeros((rho, 128), BF16)
    small = small.at[:, :heads].set(head_gate_weight)
    small = small.at[:, heads].set(attention_gain)
    small = small.at[:, heads + 1].set(feedforward_gain)
    small = small.at[0, heads + 2 : heads + 2 + 2 * pair_cols].set(query_key_gain.reshape(-1))
    small = lax.all_gather(small, ALL, axis=0)
    gain_one = small[:, :, heads].reshape(-1).astype(F32)
    gain_two = small[:, :, heads + 1].reshape(-1).astype(F32)
    gain_pair = (
        small[:, 0, heads + 2 : heads + 2 + 2 * pair_cols]
        .reshape(everyone, 2, pair_cols)
        .transpose(1, 0, 2)
        .reshape(2, size)
        .astype(F32)
    )
    weight_head = lax.dynamic_slice_in_dim(
        small[:, :, :heads].reshape(-1, heads), t * mine, mine, 1
    )

    attn = jnp.concatenate(
        [
            query_weight.reshape(rho, TEAM, q_cols),
            key_matrix.reshape(rho, TEAM, k_cols),
            value_matrix.reshape(rho, TEAM, k_cols),
        ],
        axis=2,
    ).transpose(1, 0, 2)
    attn = exchange(attn).reshape(TEAM * rho, -1)
    weight_attn = line_gather(attn)
    weight_out = out_weight_in(output_weight, groups)
    weight_down = line_gather(down_weight)

    def ff_split(w):
        return w.reshape(rho, groups, TEAM, phi).transpose(2, 0, 1, 3).reshape(TEAM, rho, ff_cols)

    feed = jnp.concatenate([ff_split(gate_weight), ff_split(up_weight)], axis=2)
    feed = exchange(feed).reshape(TEAM * rho, -1)
    weight_feed = line_gather(feed)

    team_tokens = jnp.concatenate(team_gather(tokens), axis=0)
    normed = rms(team_tokens.astype(F32), gain_one).astype(BF16)
    qkv = product(normed, weight_attn)
    gate_logit = product(normed, weight_head)
    query_raw = qkv[:, :q_cols].reshape(TEAM, rows, mine, size)
    key_raw = qkv[:, q_cols : q_cols + k_cols].reshape(TEAM, rows, 1, size)
    values = qkv[:, q_cols + k_cols :].astype(BF16).reshape(TEAM, rows, size)
    exponent = jnp.arange(size // 2, dtype=F32) * (-2.0 / size)
    frequency = jnp.power(ROPE_BASE, exponent)
    angles = jnp.arange(rows, dtype=F32)[:, None] * frequency[None, :]
    cosine = jnp.cos(angles)[:, None, :]
    sine = jnp.sin(angles)[:, None, :]
    query_rot = rotate(rms(query_raw, gain_pair[0]), cosine, sine).astype(BF16)
    key_rot = rotate(rms(key_raw, gain_pair[1]), cosine, sine).astype(BF16)[:, :, 0]
    score_scale = size ** (-0.5)
    scores = jnp.einsum("bqgd,bsd->bgqs", query_rot, key_rot, preferred_element_type=F32) * score_scale
    causal = lax.broadcasted_iota(jnp.int32, (rows, rows), 1) <= lax.broadcasted_iota(
        jnp.int32, (rows, rows), 0
    )
    masked = jnp.where(causal, scores, -jnp.inf)
    terms = jnp.exp(masked - jnp.max(masked, axis=-1, keepdims=True))
    attention = terms / jnp.sum(terms, axis=-1, keepdims=True)
    mixture = jnp.einsum(
        "bgqs,bsd->bqgd", attention.astype(BF16), values, preferred_element_type=F32
    )
    gate_value = jax.nn.sigmoid(gate_logit).reshape(TEAM, rows, mine, 1)
    gated = (mixture * gate_value).astype(BF16).reshape(TEAM * rows, q_cols)

    def blocks(array):
        return [array[r * rows : (r + 1) * rows] for r in range(TEAM)]

    inputs = tokens.astype(F32)
    hidden_state = inputs + team_sum(blocks(product(gated, weight_out).astype(BF16)))

    live_rows = (lax.broadcasted_iota(jnp.int32, (rows, 1), 0) < lengths[0]).astype(F32)
    upstream = cotangent.astype(F32) * live_rows
    team_upstream = jnp.concatenate(team_gather(upstream.astype(BF16)), axis=0)
    normed_two = rms(hidden_state, gain_two).astype(BF16)
    team_two = jnp.concatenate(team_gather(normed_two), axis=0)
    both = product(team_two, weight_feed)
    gate_part, up_part = both[:, :ff_cols], both[:, ff_cols:]
    sig = jax.nn.sigmoid(gate_part)
    silu = gate_part * sig
    inner = (silu * up_part).astype(BF16)
    feed_out = team_sum(blocks(product(inner, weight_down).astype(BF16)))
    layer_output = ((hidden_state + feed_out) * live_rows).astype(BF16)

    inner_grad = product_nt(team_upstream, weight_down)
    gate_back = (inner_grad * up_part * (sig + gate_part * sig * (1.0 - sig))).astype(BF16)
    up_back = (inner_grad * silu).astype(BF16)
    feed_back = jnp.concatenate([gate_back, up_back], axis=1)
    two_grad = team_sum(blocks(product_nt(feed_back, weight_feed).astype(BF16)))
    down_part = product_tn(inner, team_upstream).astype(BF16)
    down_grad = line_sum(down_part)
    feed_part = product_tn(team_two, feed_back).astype(BF16)
    feed_grad = line_sum(feed_part)
    feed_grad = exchange(feed_grad.reshape(TEAM, rho, 2 * ff_cols))

    def ff_join(w):
        return w.reshape(TEAM, rho, groups, phi).transpose(1, 2, 0, 3).reshape(rho, ff)

    gate_grad = ff_join(feed_grad[:, :, :ff_cols])
    up_grad = ff_join(feed_grad[:, :, ff_cols:])

    hidden_part, gain_two_grad = rms_pull(hidden_state, gain_two, two_grad)
    hidden_grad = upstream + hidden_part

    team_hidden = jnp.concatenate(team_gather(hidden_grad.astype(BF16)), axis=0)
    out_part = product_tn(gated, team_hidden).astype(BF16)
    output_grad = out_weight_back(out_part, groups)
    gated_grad = product_nt(team_hidden, weight_out).reshape(TEAM, rows, mine, size)
    mixture_back = (gated_grad * gate_value).astype(BF16)
    logit_back = (
        (jnp.sum(gated_grad * mixture, axis=-1, keepdims=True) * gate_value * (1.0 - gate_value))
        .astype(BF16)
        .reshape(TEAM * rows, mine)
    )
    values_back = jnp.einsum(
        "bgqs,bqgd->bsd", attention.astype(BF16), mixture_back, preferred_element_type=F32
    )
    attention_grad = jnp.einsum("bqgd,bsd->bgqs", mixture_back, values, preferred_element_type=F32)
    scores_back = (
        attention
        * (attention_grad - jnp.sum(attention_grad * attention, axis=-1, keepdims=True))
    ).astype(BF16)
    query_rot_grad = (
        jnp.einsum("bgqs,bsd->bqgd", scores_back, key_rot, preferred_element_type=F32) * score_scale
    )
    key_rot_grad = (
        jnp.einsum("bgqs,bqgd->bsd", scores_back, query_rot, preferred_element_type=F32)
        * score_scale
    )[:, :, None]
    query_chain, query_gain_back = rms_pull(
        query_raw, gain_pair[0], rotate(query_rot_grad, cosine, -sine)
    )
    key_chain, key_gain_back = rms_pull(key_raw, gain_pair[1], rotate(key_rot_grad, cosine, -sine))
    attn_back = jnp.concatenate(
        [
            query_chain.reshape(TEAM * rows, q_cols).astype(BF16),
            key_chain.reshape(TEAM * rows, k_cols).astype(BF16),
            values_back.reshape(TEAM * rows, k_cols).astype(BF16),
        ],
        axis=1,
    )
    normed_part = product_nt(attn_back, weight_attn) + product_nt(logit_back, weight_head)
    normed_grad = team_sum(blocks(normed_part.astype(BF16)))
    input_part, gain_one_grad = rms_pull(inputs, gain_one, normed_grad)
    tokens_grad = (hidden_grad + input_part).astype(BF16)
    attn_part = product_tn(normed, attn_back).astype(BF16)
    attn_grad = line_sum(attn_part)
    attn_grad = exchange(attn_grad.reshape(TEAM, rho, -1)).transpose(1, 0, 2)
    head_part = product_tn(normed, logit_back)

    head_full = lax.dynamic_update_slice_in_dim(
        jnp.zeros((width, heads), F32), head_part, t * mine, 1
    )
    pair_grad = jnp.stack([query_gain_back, key_gain_back], axis=0)
    packed = jnp.concatenate(
        [
            head_full.reshape(everyone, rho * heads),
            gain_one_grad.reshape(everyone, rho),
            gain_two_grad.reshape(everyone, rho),
            pair_grad.reshape(2, everyone, pair_cols).transpose(1, 0, 2).reshape(everyone, -1),
        ],
        axis=1,
    )
    packed = lax.psum_scatter(packed, ALL, scatter_dimension=0, tiled=True)[0]
    head_gate_grad = packed[: rho * heads].reshape(rho, heads)
    rest = packed[rho * heads :]
    return (
        layer_output,
        tokens_grad,
        rest[:rho],
        attn_grad[:, :, :q_cols].reshape(rho, -1).astype(F32),
        attn_grad[:, :, q_cols : q_cols + k_cols].reshape(rho, -1).astype(F32),
        attn_grad[:, :, q_cols + k_cols :].reshape(rho, -1).astype(F32),
        head_gate_grad,
        output_grad.astype(F32),
        rest[2 * rho :].reshape(2, pair_cols),
        rest[rho : 2 * rho],
        gate_grad.astype(F32),
        up_grad.astype(F32),
        down_grad.astype(F32),
    )


def solution(mesh):
    groups = mesh.size // TEAM
    rows, vector, columns = P(ALL, None), P(ALL), P(None, ALL)

    def step(*args):
        return local(groups, *args)

    return jax.shard_map(
        step,
        mesh=mesh,
        in_specs=(
            rows, vector, rows, vector, rows, rows, rows, rows, rows, columns, vector, rows, rows, rows,
        ),
        out_specs=(
            rows, rows, vector, rows, rows, rows, rows, rows, columns, vector, rows, rows, rows,
        ),
        check_vma=False,
    )
```

```python
import jax
import jax.numpy as jnp
from jax import lax
from jax.experimental import pallas as pl
from jax.experimental.pallas import tpu as pltpu
from jax.sharding import PartitionSpec as P

EPSILON = 1e-06
ROPE_BASE = 1000000.0
TEAM = 8
ALL = ("dp", "fsdp")
F32 = jnp.float32
BF16 = jnp.bfloat16
TILE = 128
ORDER_BACK = (3, 1, 2, 0)
ORDER_LATE = (0, 1, 3, 2)
ANY = pl.BlockSpec(memory_space=pl.ANY)
VMEM = pl.BlockSpec(memory_space=pltpu.VMEM)
SMEM = pl.BlockSpec(memory_space=pltpu.SMEM)


def product(left, right):
    return jnp.dot(left, right, preferred_element_type=F32)


def product_nt(left, right):
    return lax.dot_general(left, right, (((1,), (1,)), ((), ())), preferred_element_type=F32)


def product_tn(left, right):
    return lax.dot_general(left, right, (((0,), (0,)), ((), ())), preferred_element_type=F32)


def world():
    return lax.axis_size(ALL)


def member():
    return lax.axis_index(ALL) % TEAM


def teams():
    return [[first + t for t in range(TEAM)] for first in range(0, world(), TEAM)]


def lines():
    return [list(range(t, world(), TEAM)) for t in range(TEAM)]


def permute(array, pairs):
    return lax.ppermute(
        array, ALL, [(team[a], team[b]) for team in teams() for a, b in pairs]
    )


def swap(array, bits):
    return permute(array, [(i, i ^ bits) for i in range(TEAM)])


def exchange(blocks):
    if lax.axis_size("fsdp") == TEAM:
        return lax.all_to_all(blocks, "fsdp", 0, 0, tiled=True)
    return lax.all_to_all(blocks, ALL, 0, 0, tiled=True, axis_index_groups=teams())


def exchange_by_swaps(blocks):
    t = member()
    result = blocks
    pieces = [lax.dynamic_index_in_dim(blocks, t ^ r, 0, keepdims=True) for r in range(1, TEAM)]
    for r in range(1, TEAM):
        result = lax.dynamic_update_slice_in_dim(result, swap(pieces[r - 1], r), t ^ r, 0)
    return result


def line_gather(shard):
    if lax.axis_size("fsdp") == TEAM:
        return lax.all_gather(shard, "dp", axis=0, tiled=True)
    return lax.all_gather(shard, ALL, axis=0, tiled=True, axis_index_groups=lines())


def line_sum(array):
    if lax.axis_size("fsdp") == TEAM:
        return lax.psum_scatter(array, "dp", scatter_dimension=0, tiled=True)
    return lax.psum_scatter(array, ALL, scatter_dimension=0, tiled=True, axis_index_groups=lines())


def team_gather(own):
    half = own.shape[0] // 2
    a1 = swap(own, 1)
    a2 = swap(own, 2)
    a4 = swap(own, 4)
    a6 = jnp.concatenate([swap(a4[:half], 2), swap(a2[half:], 4)], axis=0)
    a3 = swap(a2, 1)
    a5 = swap(a4, 1)
    a7 = swap(a6, 1)
    return [own, a1, a2, a3, a4, a5, a6, a7]


class TeamSum:
    def add(self, pair, even, odd):
        half = even.shape[0] // 2
        total = even.astype(F32) + swap(odd, 1).astype(F32)
        if pair == 3:
            self.low6 = total.astype(BF16)
            self.u4 = swap(self.low6[:half], 2)
            self.u2 = swap(self.low6[half:], 4)
        elif pair == 1:
            self.s2_low = total[half:]
            self.x_top = swap(total[:half].astype(BF16), 2)
        elif pair == 2:
            self.s4_top = total[:half]
            self.y_low = swap(total[half:].astype(BF16), 4)
        else:
            self.s0 = total

    def total(self):
        x_low = swap((self.s2_low + self.u2.astype(F32)).astype(BF16), 2).astype(F32)
        y_top = swap((self.s4_top + self.u4.astype(F32)).astype(BF16), 4).astype(F32)
        top = self.x_top.astype(F32) + y_top
        low = x_low + self.y_low.astype(F32)
        return self.s0 + jnp.concatenate([top, low], axis=0)


def team_sum(parts):
    total = TeamSum()
    for pair in ORDER_BACK:
        total.add(pair, parts[2 * pair], parts[2 * pair + 1])
    return total.total()


def out_weight_in(shard, groups):
    t = member()
    if groups < TEAM:
        gathered = line_gather(shard[None])
        per = TEAM // groups
        b, z = t % groups, t // per
        result = jnp.zeros_like(gathered)
        for j in range(groups):
            perm = [(i, per * ((i % groups + j) % groups) + i // groups) for i in range(TEAM)]
            piece = lax.dynamic_index_in_dim(gathered, (b + j) % groups, 0, keepdims=True)
            piece = permute(piece, perm)
            result = lax.dynamic_update_slice_in_dim(result, piece, (z - j + groups) % groups, 0)
        return result.reshape(-1, shard.shape[1])
    full = lax.all_gather(shard, ALL, axis=0, tiled=True)
    rows = full.shape[0] // TEAM
    return lax.dynamic_slice_in_dim(full, t * rows, rows, 0)


def out_weight_back(grad, groups, done):
    t = member()
    if groups < TEAM:
        per = TEAM // groups
        b, z = t % groups, t // per
        grad = grad.reshape(groups, -1, grad.shape[1])
        placed = jnp.zeros_like(grad)
        for j in range(groups):
            perm = [(per * ((i % groups + j) % groups) + i // groups, i) for i in range(TEAM)]
            piece = lax.dynamic_index_in_dim(grad, (z - j + groups) % groups, 0, keepdims=True)
            piece = permute(piece, perm)
            placed = lax.dynamic_update_slice_in_dim(placed, piece, (b + j) % groups, 0)
        return line_sum(hold([placed], done)[0])[0]
    whole = jnp.zeros((grad.shape[0] * TEAM, grad.shape[1]), grad.dtype)
    whole = lax.dynamic_update_slice_in_dim(whole, grad, t * grad.shape[0], 0)
    return lax.psum_scatter(whole, ALL, scatter_dimension=0, tiled=True)


def rms_pull(value, gain, grad):
    scale = lax.rsqrt(jnp.mean(value * value, axis=-1, keepdims=True) + EPSILON)
    weighted = grad * gain
    mean = jnp.mean(weighted * value, axis=-1, keepdims=True)
    return scale * weighted - scale * scale * scale * value * mean


def rms(value, gain):
    return value * lax.rsqrt(jnp.mean(value * value, axis=-1, keepdims=True) + EPSILON) * gain


def struct(shape, dtype):
    return jax.ShapeDtypeStruct(shape, dtype)


def hold(arrays, tick):
    def kernel(*refs):
        del refs

    count = len(arrays)
    return pl.pallas_call(
        kernel,
        out_shape=[struct(a.shape, a.dtype) for a in arrays],
        in_specs=[ANY] * count + [ANY],
        out_specs=[ANY] * count,
        input_output_aliases={i: i for i in range(count)},
    )(*arrays, tick)


def mark(arrays):
    def kernel(*refs):
        refs[-1][...] = jnp.zeros_like(refs[-1])

    return pl.pallas_call(
        kernel,
        out_shape=struct((8, 128), jnp.int32),
        in_specs=[ANY] * len(arrays),
        out_specs=VMEM,
    )(*arrays)


def for_tiles(tiles, most, body):
    for m in range(1, most + 1):

        @pl.when(tiles == m)
        def _(m=m):
            body(m * TILE)


def turned(u, cosine, sine):
    return u * cosine + pltpu.roll(u, u.shape[-1] // 2, 1) * sine


def head_norm(u):
    return lax.rsqrt(jnp.mean(u * u, axis=-1, keepdims=True) + EPSILON)


def head_back(grad, raw, gain, cosine, sine):
    e = turned(grad, cosine, -sine)
    scale = head_norm(raw)
    weighted = e * gain
    mean = jnp.mean(weighted * raw, axis=-1, keepdims=True)
    back = scale * weighted - scale * scale * scale * raw * mean
    return back, jnp.sum(e * raw * scale, axis=0, keepdims=True)


def weights_of(query, key, factor):
    scores = product_nt(query, key) * factor
    n = scores.shape[0]
    causal = lax.broadcasted_iota(jnp.int32, (n, n), 1) <= lax.broadcasted_iota(jnp.int32, (n, n), 0)
    scores = jnp.where(causal, scores, -jnp.inf)
    terms = jnp.exp(scores - jnp.max(scores, axis=-1, keepdims=True))
    return terms * (1.0 / jnp.sum(terms, axis=-1, keepdims=True))


def attend(pair, tiles, tokens, consts, kept, mine, after):
    weight_attn, weight_head, weight_out, gain, gains, cosine, sine = consts
    rows, width = tokens[0].shape
    size = gains.shape[1]
    q_cols = mine * size
    cols = weight_attn.shape[1]
    factor = size ** (-0.5)
    first = kept is None
    count = 0 if first else 4

    def kernel(*refs):
        tiles_ref, tok_a, tok_b, wa, wh, wo, gain_ref, gains_ref, cos_ref, sin_ref, _ = refs[:11]
        outs = refs[11 + count : 18 + count]
        part_a, part_b, normed_all, qkv_all, logit_all, gated_all, tick = outs
        tok_v, wa_v, wh_v, wo_v, part_v, normed_v, qkv_v, logit_v, gated_v, in_sem, out_sem = refs[
            18 + count :
        ]
        tick[...] = jnp.zeros_like(tick)
        loads = [
            pltpu.make_async_copy(src, dst, in_sem.at[j])
            for j, (src, dst) in enumerate(
                ((tok_a, tok_v.at[0]), (wa, wa_v), (wh, wh_v), (wo, wo_v), (tok_b, tok_v.at[1]))
            )
        ]
        for load in loads:
            load.start()
        stores = []
        for i in range(2):
            for load in loads[:4] if i == 0 else loads[4:]:
                load.wait()
            block = 2 * pair + i

            def body(n, i=i):
                value = tok_v[i, :n].astype(F32)
                normed = rms(value, gain_ref[...]).astype(BF16)
                normed_v[i, :n] = normed
                qkv = product(normed, wa_v[...])
                qkv_v[i, :n] = qkv
                logit = product_nt(normed, wh_v[...])
                logit_v[i, :n] = logit
                cos, sin = cos_ref[:n], sin_ref[:n]
                key = qkv[:, q_cols : q_cols + size]
                key = turned(key * head_norm(key) * gains_ref[1:2], cos, sin).astype(BF16)
                values = qkv[:, q_cols + size :].astype(BF16)
                for h in range(mine):
                    query = qkv[:, h * size : (h + 1) * size]
                    query = turned(query * head_norm(query) * gains_ref[0:1], cos, sin).astype(BF16)
                    attention = weights_of(query, key, factor)
                    mixture = product(attention.astype(BF16), values)
                    gate = jax.nn.sigmoid(logit[:, h : h + 1])
                    gated_v[i, :n, h * size : (h + 1) * size] = (mixture * gate).astype(BF16)
                part_v[i, :n] = product(gated_v[i, :n], wo_v[...]).astype(BF16)
                if n < rows:
                    part_v[i, n:] = jnp.zeros((rows - n, width), BF16)
                    normed_v[i, n:] = jnp.zeros((rows - n, width), BF16)
                    gated_v[i, n:] = jnp.zeros((rows - n, q_cols), BF16)

            for_tiles(tiles_ref[block], rows // TILE, body)
            span = pl.ds(block * rows, rows)
            for j, (src, dst) in enumerate(
                (
                    (part_v, (part_a, part_b)[i]),
                    (normed_v, normed_all.at[span]),
                    (qkv_v, qkv_all.at[span]),
                    (logit_v, logit_all.at[span]),
                    (gated_v, gated_all.at[span]),
                )
            ):
                store = pltpu.make_async_copy(src.at[i], dst, out_sem.at[5 * i + j])
                store.start()
                stores.append(store)
        for store in stores:
            store.wait()

    whole = TEAM * rows
    result = pl.pallas_call(
        kernel,
        out_shape=[
            struct((rows, width), BF16),
            struct((rows, width), BF16),
            struct((whole, width), BF16),
            struct((whole, cols), F32),
            struct((whole, TILE), F32),
            struct((whole, q_cols), BF16),
            struct((8, 128), jnp.int32),
        ],
        in_specs=[SMEM] + [ANY] * 5 + [VMEM] * 4 + [ANY] + [ANY] * count,
        out_specs=[ANY] * 6 + [VMEM],
        scratch_shapes=[
            pltpu.VMEM((2, rows, width), BF16),
            pltpu.VMEM(weight_attn.shape, BF16),
            pltpu.VMEM(weight_head.shape, BF16),
            pltpu.VMEM(weight_out.shape, BF16),
            pltpu.VMEM((2, rows, width), BF16),
            pltpu.VMEM((2, rows, width), BF16),
            pltpu.VMEM((2, rows, cols), F32),
            pltpu.VMEM((2, rows, TILE), F32),
            pltpu.VMEM((2, rows, q_cols), BF16),
            pltpu.SemaphoreType.DMA((5,)),
            pltpu.SemaphoreType.DMA((10,)),
        ],
        input_output_aliases={11 + j: 2 + j for j in range(count)},
        compiler_params=pltpu.CompilerParams(vmem_limit_bytes=48 << 20),
        cost_estimate=pl.CostEstimate(flops=8 << 30, bytes_accessed=16 << 20, transcendentals=1 << 20),
    )(tiles, *tokens, weight_attn, weight_head, weight_out, gain, gains, cosine, sine, after, *(kept or ()))
    return result[0], result[1], result[2:6], result[6]


def attend_back(pair, tiles, hidden, consts, saved, kept, mine, after):
    weight_attn, weight_head, weight_out, gain, gains, cosine, sine = consts
    rows, width = hidden[0].shape
    size = gains.shape[1]
    q_cols = mine * size
    cols = weight_attn.shape[1]
    factor = size ** (-0.5)
    first = kept is None
    count = 0 if first else 3

    def kernel(*refs):
        (
            tiles_ref, hid_a, hid_b, wa, wh, wo, normed_all, qkv_all, logit_all,
            gains_ref, cos_ref, sin_ref, _,
        ) = refs[:13]
        part_a, part_b, back_all, logit_back_all, hidden_all, gain_sum, gains_sum, tick = refs[
            13 + count : 21 + count
        ]
        (
            hid_v, wa_v, wh_v, wo_v, normed_v, qkv_v, logit_v, part_v, back_v, logit_back_v,
            in_sem, out_sem,
        ) = refs[21 + count :]
        tick[...] = jnp.zeros_like(tick)
        gain_sum[...] = jnp.zeros_like(gain_sum)
        gains_sum[...] = jnp.zeros_like(gains_sum)
        spans = [pl.ds((2 * pair + i) * rows, rows) for i in range(2)]
        moves = [(hid_a, hid_v.at[0]), (wo, wo_v)]
        for i in range(2):
            if i:
                moves.append((hid_b, hid_v.at[1]))
            moves.append((qkv_all.at[spans[i]], qkv_v.at[i]))
            moves.append((logit_all.at[spans[i]], logit_v.at[i]))
            moves.append((normed_all.at[spans[i]], normed_v.at[i]))
            if not i:
                moves.append((wa, wa_v))
                moves.append((wh, wh_v))
        loads = [pltpu.make_async_copy(src, dst, in_sem.at[j]) for j, (src, dst) in enumerate(moves)]
        for load in loads:
            load.start()
        stores = []
        for i in range(2):
            for load in loads[:7] if i == 0 else loads[7:]:
                load.wait()
            store = pltpu.make_async_copy(hid_v.at[i], hidden_all.at[spans[i]], out_sem.at[4 * i + 3])
            store.start()
            stores.append(store)

            def body(n, i=i):
                gated_grad = product_nt(hid_v[i, :n], wo_v[...])
                cos, sin = cos_ref[:n], sin_ref[:n]
                key_raw = qkv_v[i, :n, q_cols : q_cols + size]
                key = turned(key_raw * head_norm(key_raw) * gains_ref[1:2], cos, sin).astype(BF16)
                values = qkv_v[i, :n, q_cols + size :].astype(BF16)
                lane = lax.broadcasted_iota(jnp.int32, (n, TILE), 1)
                logit_back = jnp.zeros((n, TILE), F32)
                values_back = jnp.zeros((n, size), F32)
                key_grad = jnp.zeros((n, size), F32)
                query_sum = jnp.zeros((1, size), F32)
                for h in range(mine):
                    span = slice(h * size, (h + 1) * size)
                    query_raw = qkv_v[i, :n, span]
                    query = turned(query_raw * head_norm(query_raw) * gains_ref[0:1], cos, sin).astype(BF16)
                    attention = weights_of(query, key, factor)
                    attention_low = attention.astype(BF16)
                    mixture = product(attention_low, values)
                    gate = jax.nn.sigmoid(logit_v[i, :n, h : h + 1])
                    head_grad = gated_grad[:, span]
                    mixture_back = (head_grad * gate).astype(BF16)
                    one = jnp.sum(head_grad * mixture, axis=-1, keepdims=True) * gate * (1.0 - gate)
                    logit_back = jnp.where(lane == h, one, logit_back)
                    values_back += product_tn(attention_low, mixture_back)
                    attention_grad = product_nt(mixture_back, values)
                    scores_back = (
                        attention
                        * (attention_grad - jnp.sum(attention_grad * attention, axis=-1, keepdims=True))
                    ).astype(BF16)
                    query_grad = product(scores_back, key) * factor
                    key_grad += product_tn(scores_back, query)
                    back, total = head_back(query_grad, query_raw, gains_ref[0:1], cos, sin)
                    back_v[i, :n, span] = back.astype(BF16)
                    query_sum += total
                back, key_sum = head_back(key_grad * factor, key_raw, gains_ref[1:2], cos, sin)
                back_v[i, :n, q_cols : q_cols + size] = back.astype(BF16)
                back_v[i, :n, q_cols + size :] = values_back.astype(BF16)
                logit_back = logit_back.astype(BF16)
                logit_back_v[i, :n] = logit_back
                gains_sum[0:1] += query_sum
                gains_sum[1:2] += key_sum
                part = product_nt(back_v[i, :n], wa_v[...]) + product(logit_back, wh_v[...])
                part_v[i, :n] = part.astype(BF16)
                gain_sum[0:1] += jnp.sum(part * normed_v[i, :n].astype(F32), axis=0, keepdims=True)
                if n < rows:
                    part_v[i, n:] = jnp.zeros((rows - n, width), BF16)
                    back_v[i, n:] = jnp.zeros((rows - n, cols), BF16)
                    logit_back_v[i, n:] = jnp.zeros((rows - n, TILE), BF16)

            for_tiles(tiles_ref[2 * pair + i], rows // TILE, body)
            for j, (src, dst) in enumerate(
                (
                    (part_v, (part_a, part_b)[i]),
                    (back_v, back_all.at[spans[i]]),
                    (logit_back_v, logit_back_all.at[spans[i]]),
                )
            ):
                store = pltpu.make_async_copy(src.at[i], dst, out_sem.at[4 * i + j])
                store.start()
                stores.append(store)
        for store in stores:
            store.wait()

    whole = TEAM * rows
    result = pl.pallas_call(
        kernel,
        out_shape=[
            struct((rows, width), BF16),
            struct((rows, width), BF16),
            struct((whole, cols), BF16),
            struct((whole, TILE), BF16),
            struct((whole, width), BF16),
            struct((8, width), F32),
            struct((8, size), F32),
            struct((8, 128), jnp.int32),
        ],
        in_specs=[SMEM] + [ANY] * 8 + [VMEM] * 3 + [ANY] + [ANY] * count,
        out_specs=[ANY] * 5 + [VMEM] * 3,
        scratch_shapes=[
            pltpu.VMEM((2, rows, width), BF16),
            pltpu.VMEM(weight_attn.shape, BF16),
            pltpu.VMEM(weight_head.shape, BF16),
            pltpu.VMEM(weight_out.shape, BF16),
            pltpu.VMEM((2, rows, width), BF16),
            pltpu.VMEM((2, rows, cols), F32),
            pltpu.VMEM((2, rows, TILE), F32),
            pltpu.VMEM((2, rows, width), BF16),
            pltpu.VMEM((2, rows, cols), BF16),
            pltpu.VMEM((2, rows, TILE), BF16),
            pltpu.SemaphoreType.DMA((11,)),
            pltpu.SemaphoreType.DMA((8,)),
        ],
        input_output_aliases={13 + j: 2 + j for j in range(count)},
        compiler_params=pltpu.CompilerParams(vmem_limit_bytes=48 << 20),
        cost_estimate=pl.CostEstimate(flops=12 << 30, bytes_accessed=20 << 20, transcendentals=1 << 20),
    )(
        tiles, *hidden, weight_attn, weight_head, weight_out, *saved, gains, cosine, sine, after,
        *(kept or ()),
    )
    return result[0], result[1], result[2:5], result[5], result[6], result[7]


def tile_places(tiles_ref, rows):
    places, total = [], 0
    for r in range(TEAM):
        count = tiles_ref[r]
        for j in range(rows // TILE):
            places.append((r, j, j < count, total + j))
        total = total + count
    return places, total


def rows_of(tile, size=TILE):
    return pl.ds(pl.multiple_of(tile * size, size), size)


def feed_up(tiles, twos, upstreams, weight_gate, weight_up, after):
    rows, width = twos[0].shape
    ff_cols = weight_gate.shape[1]
    whole = TEAM * rows
    chunk = 2 * TILE
    chunks = whole // chunk

    def kernel(*refs):
        tiles_ref, twos_ref, ups_ref = refs[0], refs[1 : 1 + TEAM], refs[1 + TEAM : 1 + 2 * TEAM]
        weights_ref = refs[1 + 2 * TEAM : 3 + 2 * TEAM]
        inner_all, both_all, two_all, ups_all = refs[4 + 2 * TEAM : 8 + 2 * TEAM]
        two_v, wg_v, wu_v, inner_v, both_v, zero_v, w_sem, load_sem, ups_sem, out_sem = refs[8 + 2 * TEAM :]
        places, total = tile_places(tiles_ref, rows)
        used = (total + 1) // 2

        def loads():
            for k, (r, j, live, place) in enumerate(places):
                yield live, pltpu.make_async_copy(
                    twos_ref[r].at[rows_of(j)], two_v.at[rows_of(place)], load_sem.at[k]
                )

        for live, copy in loads():
            pl.when(live)(copy.start)
        weights = [
            pltpu.make_async_copy(weights_ref[0], wg_v, w_sem.at[0]),
            pltpu.make_async_copy(weights_ref[1], wu_v, w_sem.at[1]),
        ]
        for load in weights:
            load.start()
        zero_v[...] = jnp.zeros_like(zero_v)
        for k, (r, j, live, place) in enumerate(places):
            copy = pltpu.make_async_copy(
                ups_ref[r].at[rows_of(j)], ups_all.at[rows_of(place)], ups_sem.at[k]
            )
            pl.when(live)(copy.start)
        for k in range(TEAM, len(places)):
            copy = pltpu.make_async_copy(
                zero_v.at[:TILE], ups_all.at[rows_of(k)], ups_sem.at[len(places) + k]
            )
            pl.when(k >= total)(copy.start)

        @pl.when(total % 2 == 1)
        def _():
            two_v[rows_of(total)] = jnp.zeros((TILE, width), BF16)

        for live, copy in loads():
            pl.when(live)(copy.wait)
        for load in weights:
            load.wait()

        def stores(c, sources):
            for j, (src, dst) in enumerate(zip(sources, (two_all, inner_all, both_all))):
                yield pltpu.make_async_copy(src, dst.at[rows_of(c, chunk)], out_sem.at[j, c])

        zeros = (zero_v, zero_v.at[:, :ff_cols], zero_v.at[:, : 2 * ff_cols])
        for c in range(TEAM // 2, chunks):

            @pl.when(c >= used)
            def _(c=c):
                for store in stores(c, zeros):
                    store.start()

        def body(c, carry):
            span = rows_of(c, chunk)
            gate_part = product(two_v[span], wg_v[...])
            up_part = product(two_v[span], wu_v[...])
            inner_v[span] = (gate_part * jax.nn.sigmoid(gate_part) * up_part).astype(BF16)
            both_v[span, :ff_cols] = gate_part.astype(BF16)
            both_v[span, ff_cols:] = up_part.astype(BF16)
            for store in stores(c, (two_v.at[span], inner_v.at[span], both_v.at[span])):
                store.start()
            return carry

        lax.fori_loop(0, used, body, 0)
        for k, (r, j, live, place) in enumerate(places):
            copy = pltpu.make_async_copy(
                ups_ref[r].at[rows_of(j)], ups_all.at[rows_of(place)], ups_sem.at[k]
            )
            pl.when(live)(copy.wait)
        for k in range(TEAM, len(places)):
            copy = pltpu.make_async_copy(
                zero_v.at[:TILE], ups_all.at[rows_of(k)], ups_sem.at[len(places) + k]
            )
            pl.when(k >= total)(copy.wait)
        for c in range(chunks):
            for store in stores(c, zeros):
                store.wait()

    count = whole // TILE
    return pl.pallas_call(
        kernel,
        out_shape=[
            struct((whole, ff_cols), BF16),
            struct((whole, 2 * ff_cols), BF16),
            struct((whole, width), BF16),
            struct((whole, width), BF16),
        ],
        in_specs=[SMEM] + [ANY] * (3 + 2 * TEAM),
        out_specs=[ANY] * 4,
        scratch_shapes=[
            pltpu.VMEM((whole, width), BF16),
            pltpu.VMEM(weight_gate.shape, BF16),
            pltpu.VMEM(weight_up.shape, BF16),
            pltpu.VMEM((whole, ff_cols), BF16),
            pltpu.VMEM((whole, 2 * ff_cols), BF16),
            pltpu.VMEM((chunk, width), BF16),
            pltpu.SemaphoreType.DMA((2,)),
            pltpu.SemaphoreType.DMA((count,)),
            pltpu.SemaphoreType.DMA((2 * count,)),
            pltpu.SemaphoreType.DMA((3, chunks)),
        ],
        compiler_params=pltpu.CompilerParams(vmem_limit_bytes=50 << 20),
        cost_estimate=pl.CostEstimate(flops=20 << 30, bytes_accessed=60 << 20, transcendentals=1 << 20),
    )(tiles, *twos, *upstreams, weight_gate, weight_up, after)


def feed_down(second, tiles, saved, weight_gate, weight_up, weight_down, kept, after):
    count = 2 * TEAM + 1 if second else 0
    ff_cols, width = weight_down.shape
    whole = saved[0].shape[0]
    rows = whole // TEAM
    chunk = 2 * TILE
    chunks = whole // chunk

    def kernel(*refs):
        tiles_ref, inner_all, both_all, ups_all, wg, wu, wd = refs[:7]
        outs_ref = refs[8 + count : 8 + count + TEAM]
        grads_ref = refs[8 + count + TEAM : 8 + count + 2 * TEAM]
        back_all = refs[8 + count + 2 * TEAM]
        (
            ups_v, both_v, inner_v, back_v, wg_v, wu_v, wd_v, out_v, grad_v, zero_v,
            in_sem, w_sem, out_sem, grad_sem, back_sem, zero_sem,
        ) = refs[9 + count + 2 * TEAM :]
        places, total = tile_places(tiles_ref, rows)
        used = (total + 1) // 2
        first_chunk = used // 2 if second else 0
        end_chunk = used if second else used // 2

        def loads(c):
            slot = c % 2
            for j, (src, dst) in enumerate(((ups_all, ups_v), (both_all, both_v), (inner_all, inner_v))):
                yield pltpu.make_async_copy(src.at[rows_of(c, chunk)], dst.at[slot], in_sem.at[j, slot])

        for load in loads(first_chunk):
            load.start()
        weights = [
            pltpu.make_async_copy(src, dst, w_sem.at[j])
            for j, (src, dst) in enumerate(((wd, wd_v), (wg, wg_v), (wu, wu_v)))
        ]
        for load in weights:
            load.start()
        if not second:
            zero_v[...] = jnp.zeros_like(zero_v)

        def tile_stores(k, r, j, sources):
            yield pltpu.make_async_copy(sources[0], grads_ref[r].at[rows_of(j)], grad_sem.at[k])
            yield pltpu.make_async_copy(sources[1], outs_ref[r].at[rows_of(j)], out_sem.at[k])

        zeros = (zero_v.at[:TILE], zero_v.at[:TILE])
        def now(live, place):
            in_span = jnp.logical_and(place // 2 >= first_chunk, place // 2 < end_chunk)
            if second:
                return jnp.logical_and(live, in_span)
            return jnp.logical_or(jnp.logical_not(live), in_span)

        for k, (r, j, live, place) in enumerate(places) if not second else ():

            @pl.when(jnp.logical_not(live))
            def _(k=k, r=r, j=j):
                for store in tile_stores(k, r, j, zeros):
                    store.start()

        def back_zero(c):
            return pltpu.make_async_copy(
                zero_v.at[:, : 2 * ff_cols], back_all.at[rows_of(c, chunk)], zero_sem.at[c]
            )

        for c in range(TEAM // 2, chunks) if not second else ():
            pl.when(c >= used)(back_zero(c).start)

        def back_store(c):
            return pltpu.make_async_copy(
                back_v.at[c % 2], back_all.at[rows_of(c, chunk)], back_sem.at[c % 2]
            )

        for load in weights:
            load.wait()

        def body(c, carry):
            slot = c % 2

            @pl.when(c + 1 < end_chunk)
            def _():
                for load in loads(c + 1):
                    load.start()

            for load in loads(c):
                load.wait()

            @pl.when(c >= first_chunk + 2)
            def _():
                back_store(c - 2).wait()

            span = rows_of(c, chunk)
            inner_grad = product_nt(ups_v[slot], wd_v[...])
            gate_part = both_v[slot, :, :ff_cols].astype(F32)
            up_part = both_v[slot, :, ff_cols:].astype(F32)
            sig = jax.nn.sigmoid(gate_part)
            silu = gate_part * sig
            back_v[slot, :, :ff_cols] = (inner_grad * up_part * (sig + silu * (1.0 - sig))).astype(BF16)
            back_v[slot, :, ff_cols:] = (inner_grad * silu).astype(BF16)
            back_store(c).start()
            grad = product_nt(back_v[slot, :, :ff_cols], wg_v[...]) + product_nt(back_v[slot, :, ff_cols:], wu_v[...])
            grad_v[span] = grad.astype(BF16)
            out_v[span] = product(inner_v[slot], wd_v[...]).astype(BF16)
            for k, (r, j, live, place) in enumerate(places):

                @pl.when(jnp.logical_and(live, place // 2 == c))
                def _(k=k, r=r, j=j, place=place):
                    here = rows_of(place)
                    for store in tile_stores(k, r, j, (grad_v.at[here], out_v.at[here])):
                        store.start()

            return carry

        lax.fori_loop(first_chunk, end_chunk, body, 0)
        back_store(end_chunk - 2).wait()
        back_store(end_chunk - 1).wait()
        for c in range(TEAM // 2, chunks) if not second else ():
            pl.when(c >= used)(back_zero(c).wait)
        for k, (r, j, live, place) in enumerate(places):

            @pl.when(now(live, place))
            def _(k=k, r=r, j=j):
                for store in tile_stores(k, r, j, zeros):
                    store.wait()

    tile_count = whole // TILE
    result = pl.pallas_call(
        kernel,
        out_shape=[struct((rows, width), BF16)] * (2 * TEAM) + [struct((whole, 2 * ff_cols), BF16)],
        in_specs=[SMEM] + [ANY] * (7 + count),
        out_specs=[ANY] * (2 * TEAM + 1),
        input_output_aliases={8 + j: j for j in range(count)},
        scratch_shapes=[
            pltpu.VMEM((2, chunk, width), BF16),
            pltpu.VMEM((2, chunk, 2 * ff_cols), BF16),
            pltpu.VMEM((2, chunk, ff_cols), BF16),
            pltpu.VMEM((2, chunk, 2 * ff_cols), BF16),
            pltpu.VMEM(weight_gate.shape, BF16),
            pltpu.VMEM(weight_up.shape, BF16),
            pltpu.VMEM(weight_down.shape, BF16),
            pltpu.VMEM((whole, width), BF16),
            pltpu.VMEM((whole, width), BF16),
            pltpu.VMEM((chunk, width), BF16),
            pltpu.SemaphoreType.DMA((3, 2)),
            pltpu.SemaphoreType.DMA((3,)),
            pltpu.SemaphoreType.DMA((tile_count,)),
            pltpu.SemaphoreType.DMA((tile_count,)),
            pltpu.SemaphoreType.DMA((2,)),
            pltpu.SemaphoreType.DMA((chunks,)),
        ],
        compiler_params=pltpu.CompilerParams(vmem_limit_bytes=56 << 20),
        cost_estimate=pl.CostEstimate(flops=40 << 30, bytes_accessed=80 << 20, transcendentals=1 << 20),
    )(tiles, *saved, weight_gate, weight_up, weight_down, after, *(kept or ()))
    return result


def local(
    groups,
    tokens,
    lengths,
    cotangent,
    attention_gain,
    query_weight,
    key_matrix,
    value_matrix,
    head_gate_weight,
    output_weight,
    query_key_gain,
    feedforward_gain,
    gate_weight,
    up_weight,
    down_weight,
):
    t = member()
    everyone = groups * TEAM
    rows, width = tokens.shape
    rho = query_weight.shape[0]
    phi = down_weight.shape[0]
    ff = gate_weight.shape[1]
    pair_cols = query_key_gain.shape[1]
    size = pair_cols * everyone
    heads = query_weight.shape[1] // size
    mine = heads // TEAM
    q_cols = query_weight.shape[1] // TEAM
    k_cols = key_matrix.shape[1] // TEAM
    ff_cols = ff // TEAM

    def everyone_in_team(vector):
        return jnp.broadcast_to(vector.reshape(1, -1), (TEAM, vector.size))

    live_tiles = (lengths + (TILE - 1)) // TILE
    row = jnp.concatenate(
        [
            head_gate_weight.reshape(rho, TEAM, mine).transpose(1, 2, 0).reshape(TEAM, -1),
            everyone_in_team(attention_gain),
            everyone_in_team(feedforward_gain),
            everyone_in_team(query_key_gain),
            everyone_in_team(live_tiles.astype(BF16)),
        ],
        axis=1,
    )
    cols = q_cols + 2 * k_cols
    row = jnp.pad(row, ((0, 0), (0, cols - row.shape[1])))[:, None, :]
    attn = jnp.concatenate(
        [
            query_weight.reshape(rho, TEAM, q_cols),
            key_matrix.reshape(rho, TEAM, k_cols),
            value_matrix.reshape(rho, TEAM, k_cols),
        ],
        axis=2,
    ).transpose(1, 0, 2)
    attn = jnp.concatenate([attn, jnp.pad(row, ((0, 0), (0, 7), (0, 0)))], axis=1)
    attn = exchange(attn)
    head_lanes = mine * rho
    at_one, at_two, at_pair = head_lanes, head_lanes + rho, head_lanes + 2 * rho
    at_tiles = at_pair + 2 * pair_cols
    team_tiles = attn[:, rho, at_tiles].astype(jnp.int32)
    order = jnp.arange(TEAM, dtype=jnp.int32)
    tiles = jnp.sum(jnp.where((order[:, None] ^ t) == order[None, :], team_tiles[None, :], 0), axis=1)
    attn = line_gather(attn.reshape(TEAM * (rho + 8), cols)).reshape(everyone, rho + 8, cols)
    weight_attn = attn[:, :rho].reshape(width, cols)
    rows_small = attn[:, rho]
    weight_head = jnp.pad(
        rows_small[:, :head_lanes].reshape(everyone, mine, rho).transpose(1, 0, 2).reshape(mine, width),
        ((0, TILE - mine), (0, 0)),
    )
    gain_one = rows_small[:, at_one:at_two].reshape(1, width).astype(F32)
    gain_two = rows_small[:, at_two:at_pair].reshape(1, width).astype(F32)
    gain_pair = (
        rows_small[:, at_pair:at_tiles]
        .reshape(everyone, 2, pair_cols)
        .transpose(1, 0, 2)
        .reshape(2, size)
        .astype(F32)
    )
    weight_out = out_weight_in(output_weight, groups)

    def ff_split(w):
        return w.reshape(rho, groups, TEAM, phi).transpose(2, 0, 1, 3).reshape(TEAM, rho, ff_cols)

    feed_shard = jnp.concatenate([ff_split(gate_weight), ff_split(up_weight)], axis=2)
    feed_shard = exchange_by_swaps(feed_shard).reshape(TEAM * rho, -1)
    weight_gate = line_gather(feed_shard[:, :ff_cols])

    exponent = jnp.arange(size // 2, dtype=F32) * (-2.0 / size)
    frequency = jnp.power(ROPE_BASE, exponent)
    angles = jnp.arange(rows, dtype=F32)[:, None] * frequency[None, :]
    cosine = jnp.concatenate([jnp.cos(angles), jnp.cos(angles)], axis=1)
    sine = jnp.concatenate([-jnp.sin(angles), jnp.sin(angles)], axis=1)
    consts = (weight_attn, weight_head, weight_out, gain_one, gain_pair, cosine, sine)
    team_tokens = team_gather(tokens)
    kept, arrived = None, TeamSum()
    live = lax.broadcasted_iota(jnp.int32, (rows, 1), 0) < lengths[0]
    live_rows = live.astype(F32)
    upstream = cotangent.astype(F32) * live_rows
    tick = mark([team_tokens[6]])
    later = lax.broadcasted_iota(jnp.int32, (rows, 1), 0) < lengths[0] + tick[0, 0]
    team_upstream = team_gather(jnp.where(later, cotangent, jnp.zeros_like(cotangent)))
    ticks = []
    for step, pair in enumerate(ORDER_BACK):
        if step == 0:
            after = mark([feed_shard])
        if step == 1:
            after = mark([team_upstream[1], team_upstream[2], team_upstream[4]])
        if step == 2:
            after = arrived.low6
        if step == 3:
            after = weight_gate
        a, b, kept, tick = attend(
            pair, tiles, team_tokens[2 * pair : 2 * pair + 2], consts, kept, mine, after
        )
        arrived.add(pair, a, b)
        if step == 0:
            weight_up = line_gather(hold([feed_shard[:, ff_cols:]], tick)[0])
        if step == 1:
            weight_down = line_gather(hold([down_weight], tick)[0])
    normed, qkv, logit, gated = kept
    inputs = tokens.astype(F32)
    hidden_state = inputs + arrived.total()

    normed_two = rms(hidden_state, gain_two).astype(BF16)
    normed_two = hold([normed_two], mark(team_upstream + [weight_up]))[0]
    team_two = team_gather(normed_two)
    saved = feed_up(tiles, team_two, team_upstream, weight_gate, weight_up, weight_down)
    inner, both, two_all, ups_all = saved
    down_part = product_tn(inner, ups_all).astype(BF16)
    half_width = width // 2
    down_grads = [line_sum(down_part[:, :half_width])]
    kept = feed_down(
        False, tiles, (inner, both, ups_all), weight_gate, weight_up, weight_down, None, mark([down_part])
    )
    kept = feed_down(
        True, tiles, (inner, both, ups_all), weight_gate, weight_up, weight_down, kept, down_grads[0]
    )
    down_grads.append(line_sum(hold([down_part[:, half_width:]], down_grads[0])[0]))
    down_grad = jnp.concatenate(down_grads, axis=1)
    outs, grads, feed_back = kept[:TEAM], kept[TEAM : 2 * TEAM], kept[2 * TEAM]
    two_grad = team_sum(grads)
    gate_part = product_tn(two_all, feed_back[:, :ff_cols]).astype(BF16)
    up_part = product_tn(two_all, feed_back[:, ff_cols:]).astype(BF16)
    gate_part = hold([gate_part], down_grads[1])[0]
    after = mark([gate_part, up_part])
    gate_grad = line_sum(gate_part)
    up_grad = line_sum(hold([up_part], gate_grad)[0])

    hidden_grad = upstream + rms_pull(hidden_state, gain_two, two_grad)

    team_hidden = team_gather(hold([hidden_grad.astype(BF16)], after)[0])
    two_scale = lax.rsqrt(jnp.mean(hidden_state * hidden_state, axis=-1, keepdims=True) + EPSILON)
    two_sum = jnp.sum(two_grad * hidden_state * two_scale, axis=0)
    kept, one_sum, pair_sum, ticks, arrived = None, 0.0, 0.0, [], TeamSum()
    for step, pair in enumerate(ORDER_LATE):
        if step == 1:
            after = gate_grad
        if step == 2:
            after = up_grad
        if step == 3:
            after = arrived.low6
        a, b, kept, total, pair_total, tick = attend_back(
            pair, tiles, team_hidden[2 * pair : 2 * pair + 2], consts, (normed, qkv, logit), kept, mine, after
        )
        arrived.add(pair, a, b)
        one_sum = one_sum + total[0]
        pair_sum = pair_sum + pair_total[:2]
        ticks.append(tick)
    attn_back, logit_back, hidden_all = kept
    outs = hold(outs, ticks[2])
    feed_grad = jnp.concatenate([gate_grad, hold([up_grad], ticks[3])[0]], axis=1)
    feed_grad = exchange(feed_grad.reshape(TEAM, rho, 2 * ff_cols))
    feed_done = up_grad

    def ff_join(w):
        return w.reshape(TEAM, rho, groups, phi).transpose(1, 2, 0, 3).reshape(rho, ff)

    gate_grad = ff_join(feed_grad[:, :, :ff_cols])
    up_grad = ff_join(feed_grad[:, :, ff_cols:])
    layer_output = ((hidden_state + team_sum(outs)) * live_rows).astype(BF16)
    normed_grad = arrived.total()
    tokens_grad = (hidden_grad + rms_pull(inputs, gain_one, normed_grad)).astype(BF16)
    out_part = product_tn(gated, hidden_all).astype(BF16)
    attn_part = product_tn(normed, attn_back).astype(BF16)
    head_part = product_tn(logit_back, normed)[:mine]
    row = jnp.concatenate(
        [
            head_part.reshape(mine, everyone, rho).transpose(1, 0, 2).reshape(everyone, -1),
            (one_sum / gain_one[0]).reshape(everyone, rho),
            two_sum.reshape(everyone, rho),
            pair_sum.reshape(2, everyone, pair_cols).transpose(1, 0, 2).reshape(everyone, -1),
        ],
        axis=1,
    ).astype(BF16)
    row = jnp.pad(row, ((0, 0), (0, cols - row.shape[1])))[:, None, :]
    packed = jnp.concatenate(
        [attn_part.reshape(everyone, rho, cols), jnp.pad(row, ((0, 0), (0, 7), (0, 0)))], axis=1
    )
    packed = packed.reshape(everyone * (rho + 8), cols)
    packed = line_sum(hold([packed], feed_done)[0])
    output_grad = out_weight_back(out_part, groups, packed)
    packed = exchange(packed.reshape(TEAM, rho + 8, cols))
    attn_grad = packed[:, :rho].transpose(1, 0, 2)
    rows_small = packed[:, rho].astype(F32)
    sums = jnp.sum(rows_small[:, head_lanes:], axis=0)
    head_gate_grad = rows_small[:, :head_lanes].reshape(heads, rho).T
    return (
        layer_output,
        tokens_grad,
        sums[:rho],
        attn_grad[:, :, :q_cols].reshape(rho, -1).astype(F32),
        attn_grad[:, :, q_cols : q_cols + k_cols].reshape(rho, -1).astype(F32),
        attn_grad[:, :, q_cols + k_cols :].reshape(rho, -1).astype(F32),
        head_gate_grad,
        output_grad.astype(F32),
        sums[2 * rho : 2 * rho + 2 * pair_cols].reshape(2, pair_cols),
        sums[rho : 2 * rho],
        gate_grad.astype(F32),
        up_grad.astype(F32),
        down_grad.astype(F32),
    )


def solution(mesh):
    groups = mesh.size // TEAM
    rows, vector, columns = P(ALL, None), P(ALL), P(None, ALL)

    def step(*args):
        return local(groups, *args)

    return jax.shard_map(
        step,
        mesh=mesh,
        in_specs=(
            rows, vector, rows, vector, rows, rows, rows, rows, rows, columns, vector, rows, rows, rows,
        ),
        out_specs=(
            rows, rows, vector, rows, rows, rows, rows, rows, columns, vector, rows, rows, rows,
        ),
        check_vma=False,
    )
```

```python
import jax
import jax.numpy as jnp
from jax import lax
from jax.experimental import pallas as pl
from jax.experimental.pallas import tpu as pltpu
from jax.sharding import PartitionSpec as P

EPSILON = 1e-06
ROPE_BASE = 1000000.0
TEAM = 8
ALL = ("dp", "fsdp")
F32 = jnp.float32
BF16 = jnp.bfloat16
TILE = 128
ORDER_BACK = (3, 1, 2, 0)
ORDER_LATE = (0, 1, 3, 2)
ANY = pl.BlockSpec(memory_space=pl.ANY)
VMEM = pl.BlockSpec(memory_space=pltpu.VMEM)
SMEM = pl.BlockSpec(memory_space=pltpu.SMEM)


def product(left, right):
    return jnp.dot(left, right, preferred_element_type=F32)


def product_nt(left, right):
    return lax.dot_general(left, right, (((1,), (1,)), ((), ())), preferred_element_type=F32)


def product_tn(left, right):
    return lax.dot_general(left, right, (((0,), (0,)), ((), ())), preferred_element_type=F32)


def world():
    return lax.axis_size(ALL)


def member():
    return lax.axis_index(ALL) % TEAM


def teams():
    return [[first + t for t in range(TEAM)] for first in range(0, world(), TEAM)]


def lines():
    return [list(range(t, world(), TEAM)) for t in range(TEAM)]


def permute(array, pairs):
    return lax.ppermute(
        array, ALL, [(team[a], team[b]) for team in teams() for a, b in pairs]
    )


def swap(array, bits):
    return permute(array, [(i, i ^ bits) for i in range(TEAM)])


def exchange(blocks):
    if lax.axis_size("fsdp") == TEAM:
        return lax.all_to_all(blocks, "fsdp", 0, 0, tiled=True)
    return lax.all_to_all(blocks, ALL, 0, 0, tiled=True, axis_index_groups=teams())


def line_gather(shard):
    if lax.axis_size("fsdp") == TEAM:
        return lax.all_gather(shard, "dp", axis=0, tiled=True)
    return lax.all_gather(shard, ALL, axis=0, tiled=True, axis_index_groups=lines())


def line_sum(array):
    if lax.axis_size("fsdp") == TEAM:
        return lax.psum_scatter(array, "dp", scatter_dimension=0, tiled=True)
    return lax.psum_scatter(array, ALL, scatter_dimension=0, tiled=True, axis_index_groups=lines())


class TeamGather:
    def __init__(self, own):
        self.own = own
        self.a1 = swap(own, 1)
        self.a2 = swap(own, 2)
        self.a4 = swap(own, 4)

    def blocks(self, tick=None):
        a2, a4 = self.a2, self.a4
        if tick is not None:
            a2, a4 = hold([a2, a4], tick)
        half = self.own.shape[0] // 2
        a6 = jnp.concatenate([swap(a4[:half], 2), swap(a2[half:], 4)], axis=0)
        return [self.own, self.a1, a2, swap(a2, 1), a4, swap(a4, 1), a6, swap(a6, 1)]


def team_gather(own):
    return TeamGather(own).blocks()


class TeamSum:
    def add(self, pair, even, odd):
        half = even.shape[0] // 2
        total = even.astype(F32) + swap(odd, 1).astype(F32)
        if pair == 3:
            self.low6 = total.astype(BF16)
            self.u4 = swap(self.low6[:half], 2)
            self.u2 = swap(self.low6[half:], 4)
        elif pair == 1:
            self.s2_low = total[half:]
            self.x_top = swap(total[:half].astype(BF16), 2)
        elif pair == 2:
            self.s4_top = total[:half]
            self.y_low = swap(total[half:].astype(BF16), 4)
        else:
            self.s0 = total

    def total(self):
        x_low = swap((self.s2_low + self.u2.astype(F32)).astype(BF16), 2).astype(F32)
        y_top = swap((self.s4_top + self.u4.astype(F32)).astype(BF16), 4).astype(F32)
        top = self.x_top.astype(F32) + y_top
        low = x_low + self.y_low.astype(F32)
        return self.s0 + jnp.concatenate([top, low], axis=0)


def team_sum(parts):
    total = TeamSum()
    for pair in ORDER_BACK:
        total.add(pair, parts[2 * pair], parts[2 * pair + 1])
    return total.total()


def out_weight_in(shard, groups):
    t = member()
    if groups < TEAM:
        gathered = line_gather(shard[None])
        per = TEAM // groups
        b, z = t % groups, t // per
        result = jnp.zeros_like(gathered)
        for j in range(groups):
            perm = [(i, per * ((i % groups + j) % groups) + i // groups) for i in range(TEAM)]
            piece = lax.dynamic_index_in_dim(gathered, (b + j) % groups, 0, keepdims=True)
            piece = permute(piece, perm)
            result = lax.dynamic_update_slice_in_dim(result, piece, (z - j + groups) % groups, 0)
        return result.reshape(-1, shard.shape[1])
    full = lax.all_gather(shard, ALL, axis=0, tiled=True)
    rows = full.shape[0] // TEAM
    return lax.dynamic_slice_in_dim(full, t * rows, rows, 0)


def out_weight_back(grad, groups, done):
    t = member()
    if groups < TEAM:
        per = TEAM // groups
        b, z = t % groups, t // per
        grad = grad.reshape(groups, -1, grad.shape[1])
        placed = jnp.zeros_like(grad)
        for j in range(groups):
            perm = [(per * ((i % groups + j) % groups) + i // groups, i) for i in range(TEAM)]
            piece = lax.dynamic_index_in_dim(grad, (z - j + groups) % groups, 0, keepdims=True)
            piece = permute(piece, perm)
            placed = lax.dynamic_update_slice_in_dim(placed, piece, (b + j) % groups, 0)
        placed = hold([placed], done)[0]
        return line_sum(placed)[0], hold([done], placed)[0]
    whole = jnp.zeros((grad.shape[0] * TEAM, grad.shape[1]), grad.dtype)
    whole = lax.dynamic_update_slice_in_dim(whole, grad, t * grad.shape[0], 0)
    return lax.psum_scatter(whole, ALL, scatter_dimension=0, tiled=True), done


def rms_pull(value, gain, grad):
    scale = lax.rsqrt(jnp.mean(value * value, axis=-1, keepdims=True) + EPSILON)
    weighted = grad * gain
    mean = jnp.mean(weighted * value, axis=-1, keepdims=True)
    return scale * weighted - scale * scale * scale * value * mean


def rms(value, gain):
    return value * lax.rsqrt(jnp.mean(value * value, axis=-1, keepdims=True) + EPSILON) * gain


def struct(shape, dtype):
    return jax.ShapeDtypeStruct(shape, dtype)


def hold(arrays, tick):
    def kernel(*refs):
        del refs

    count = len(arrays)
    return pl.pallas_call(
        kernel,
        out_shape=[struct(a.shape, a.dtype) for a in arrays],
        in_specs=[ANY] * count + [ANY],
        out_specs=[ANY] * count,
        input_output_aliases={i: i for i in range(count)},
    )(*arrays, tick)


def mark(arrays):
    def kernel(*refs):
        refs[-1][...] = jnp.zeros_like(refs[-1])

    return pl.pallas_call(
        kernel,
        out_shape=struct((8, 128), jnp.int32),
        in_specs=[ANY] * len(arrays),
        out_specs=VMEM,
    )(*arrays)


def for_tiles(tiles, most, body):
    for m in range(1, most + 1):

        @pl.when(tiles == m)
        def _(m=m):
            body(m * TILE)


def turned(u, cosine, sine):
    return u * cosine + pltpu.roll(u, u.shape[-1] // 2, 1) * sine


def head_norm(u):
    return lax.rsqrt(jnp.mean(u * u, axis=-1, keepdims=True) + EPSILON)


def head_back(grad, raw, gain, cosine, sine):
    e = turned(grad, cosine, -sine)
    scale = head_norm(raw)
    weighted = e * gain
    mean = jnp.mean(weighted * raw, axis=-1, keepdims=True)
    back = scale * weighted - scale * scale * scale * raw * mean
    return back, jnp.sum(e * raw * scale, axis=0, keepdims=True)


def weights_of(query, key, factor):
    scores = product_nt(query, key) * factor
    n = scores.shape[0]
    causal = lax.broadcasted_iota(jnp.int32, (n, n), 1) <= lax.broadcasted_iota(jnp.int32, (n, n), 0)
    scores = jnp.where(causal, scores, -jnp.inf)
    terms = jnp.exp(scores - jnp.max(scores, axis=-1, keepdims=True))
    return terms * (1.0 / jnp.sum(terms, axis=-1, keepdims=True))


def attend(pair, tiles, tokens, consts, kept, mine, after):
    weight_attn, weight_head, weight_out, gain, gains, cosine, sine = consts
    rows, width = tokens[0].shape
    size = gains.shape[1]
    q_cols = mine * size
    cols = weight_attn.shape[1]
    factor = size ** (-0.5)
    first = kept is None
    count = 0 if first else 4

    def kernel(*refs):
        tiles_ref, tok_a, tok_b, wa, wh, wo, gain_ref, gains_ref, cos_ref, sin_ref, _ = refs[:11]
        outs = refs[11 + count : 18 + count]
        part_a, part_b, normed_all, qkv_all, logit_all, gated_all, tick = outs
        tok_v, wa_v, wh_v, wo_v, part_v, normed_v, qkv_v, logit_v, gated_v, in_sem, out_sem = refs[
            18 + count :
        ]
        tick[...] = jnp.zeros_like(tick)
        loads = [
            pltpu.make_async_copy(src, dst, in_sem.at[j])
            for j, (src, dst) in enumerate(
                ((tok_a, tok_v.at[0]), (wa, wa_v), (wh, wh_v), (wo, wo_v), (tok_b, tok_v.at[1]))
            )
        ]
        for load in loads:
            load.start()
        stores = []
        for i in range(2):
            for load in loads[:4] if i == 0 else loads[4:]:
                load.wait()
            block = 2 * pair + i

            def body(n, i=i):
                value = tok_v[i, :n].astype(F32)
                normed = rms(value, gain_ref[...]).astype(BF16)
                normed_v[i, :n] = normed
                qkv = product(normed, wa_v[...])
                qkv_v[i, :n] = qkv
                logit = product_nt(normed, wh_v[...])
                logit_v[i, :n] = logit
                cos, sin = cos_ref[:n], sin_ref[:n]
                key = qkv[:, q_cols : q_cols + size]
                key = turned(key * head_norm(key) * gains_ref[1:2], cos, sin).astype(BF16)
                values = qkv[:, q_cols + size :].astype(BF16)
                for h in range(mine):
                    query = qkv[:, h * size : (h + 1) * size]
                    query = turned(query * head_norm(query) * gains_ref[0:1], cos, sin).astype(BF16)
                    attention = weights_of(query, key, factor)
                    mixture = product(attention.astype(BF16), values)
                    gate = jax.nn.sigmoid(logit[:, h : h + 1])
                    gated_v[i, :n, h * size : (h + 1) * size] = (mixture * gate).astype(BF16)
                part_v[i, :n] = product(gated_v[i, :n], wo_v[...]).astype(BF16)
                if n < rows:
                    part_v[i, n:] = jnp.zeros((rows - n, width), BF16)
                    normed_v[i, n:] = jnp.zeros((rows - n, width), BF16)
                    gated_v[i, n:] = jnp.zeros((rows - n, q_cols), BF16)

            for_tiles(tiles_ref[block], rows // TILE, body)
            span = pl.ds(block * rows, rows)
            for j, (src, dst) in enumerate(
                (
                    (part_v, (part_a, part_b)[i]),
                    (normed_v, normed_all.at[span]),
                    (qkv_v, qkv_all.at[span]),
                    (logit_v, logit_all.at[span]),
                    (gated_v, gated_all.at[span]),
                )
            ):
                store = pltpu.make_async_copy(src.at[i], dst, out_sem.at[5 * i + j])
                store.start()
                stores.append(store)
        for store in stores:
            store.wait()

    whole = TEAM * rows
    result = pl.pallas_call(
        kernel,
        out_shape=[
            struct((rows, width), BF16),
            struct((rows, width), BF16),
            struct((whole, width), BF16),
            struct((whole, cols), F32),
            struct((whole, TILE), F32),
            struct((whole, q_cols), BF16),
            struct((8, 128), jnp.int32),
        ],
        in_specs=[SMEM] + [ANY] * 5 + [VMEM] * 4 + [ANY] + [ANY] * count,
        out_specs=[ANY] * 6 + [VMEM],
        scratch_shapes=[
            pltpu.VMEM((2, rows, width), BF16),
            pltpu.VMEM(weight_attn.shape, BF16),
            pltpu.VMEM(weight_head.shape, BF16),
            pltpu.VMEM(weight_out.shape, BF16),
            pltpu.VMEM((2, rows, width), BF16),
            pltpu.VMEM((2, rows, width), BF16),
            pltpu.VMEM((2, rows, cols), F32),
            pltpu.VMEM((2, rows, TILE), F32),
            pltpu.VMEM((2, rows, q_cols), BF16),
            pltpu.SemaphoreType.DMA((5,)),
            pltpu.SemaphoreType.DMA((10,)),
        ],
        input_output_aliases={11 + j: 2 + j for j in range(count)},
        compiler_params=pltpu.CompilerParams(vmem_limit_bytes=48 << 20),
        cost_estimate=pl.CostEstimate(flops=8 << 30, bytes_accessed=16 << 20, transcendentals=1 << 20),
    )(tiles, *tokens, weight_attn, weight_head, weight_out, gain, gains, cosine, sine, after, *(kept or ()))
    return result[0], result[1], result[2:6], result[6]


def attend_back(pair, tiles, hidden, consts, saved, kept, mine, after):
    weight_attn, weight_head, weight_out, gain, gains, cosine, sine = consts
    rows, width = hidden[0].shape
    size = gains.shape[1]
    q_cols = mine * size
    cols = weight_attn.shape[1]
    factor = size ** (-0.5)
    first = kept is None
    count = 0 if first else 3

    def kernel(*refs):
        (
            tiles_ref, hid_a, hid_b, wa, wh, wo, normed_all, qkv_all, logit_all,
            gains_ref, cos_ref, sin_ref, _,
        ) = refs[:13]
        part_a, part_b, back_all, logit_back_all, hidden_all, gain_sum, gains_sum, tick = refs[
            13 + count : 21 + count
        ]
        (
            hid_v, wa_v, wh_v, wo_v, normed_v, qkv_v, logit_v, part_v, back_v, logit_back_v,
            in_sem, out_sem,
        ) = refs[21 + count :]
        tick[...] = jnp.zeros_like(tick)
        gain_sum[...] = jnp.zeros_like(gain_sum)
        gains_sum[...] = jnp.zeros_like(gains_sum)
        spans = [pl.ds((2 * pair + i) * rows, rows) for i in range(2)]
        moves = [(hid_a, hid_v.at[0]), (wo, wo_v)]
        for i in range(2):
            if i:
                moves.append((hid_b, hid_v.at[1]))
            moves.append((qkv_all.at[spans[i]], qkv_v.at[i]))
            moves.append((logit_all.at[spans[i]], logit_v.at[i]))
            moves.append((normed_all.at[spans[i]], normed_v.at[i]))
            if not i:
                moves.append((wa, wa_v))
                moves.append((wh, wh_v))
        loads = [pltpu.make_async_copy(src, dst, in_sem.at[j]) for j, (src, dst) in enumerate(moves)]
        for load in loads:
            load.start()
        stores = []
        for i in range(2):
            for load in loads[:7] if i == 0 else loads[7:]:
                load.wait()
            store = pltpu.make_async_copy(hid_v.at[i], hidden_all.at[spans[i]], out_sem.at[4 * i + 3])
            store.start()
            stores.append(store)

            def body(n, i=i):
                gated_grad = product_nt(hid_v[i, :n], wo_v[...])
                cos, sin = cos_ref[:n], sin_ref[:n]
                key_raw = qkv_v[i, :n, q_cols : q_cols + size]
                key = turned(key_raw * head_norm(key_raw) * gains_ref[1:2], cos, sin).astype(BF16)
                values = qkv_v[i, :n, q_cols + size :].astype(BF16)
                lane = lax.broadcasted_iota(jnp.int32, (n, TILE), 1)
                logit_back = jnp.zeros((n, TILE), F32)
                values_back = jnp.zeros((n, size), F32)
                key_grad = jnp.zeros((n, size), F32)
                query_sum = jnp.zeros((1, size), F32)
                for h in range(mine):
                    span = slice(h * size, (h + 1) * size)
                    query_raw = qkv_v[i, :n, span]
                    query = turned(query_raw * head_norm(query_raw) * gains_ref[0:1], cos, sin).astype(BF16)
                    attention = weights_of(query, key, factor)
                    attention_low = attention.astype(BF16)
                    mixture = product(attention_low, values)
                    gate = jax.nn.sigmoid(logit_v[i, :n, h : h + 1])
                    head_grad = gated_grad[:, span]
                    mixture_back = (head_grad * gate).astype(BF16)
                    one = jnp.sum(head_grad * mixture, axis=-1, keepdims=True) * gate * (1.0 - gate)
                    logit_back = jnp.where(lane == h, one, logit_back)
                    values_back += product_tn(attention_low, mixture_back)
                    attention_grad = product_nt(mixture_back, values)
                    scores_back = (
                        attention
                        * (attention_grad - jnp.sum(attention_grad * attention, axis=-1, keepdims=True))
                    ).astype(BF16)
                    query_grad = product(scores_back, key) * factor
                    key_grad += product_tn(scores_back, query)
                    back, total = head_back(query_grad, query_raw, gains_ref[0:1], cos, sin)
                    back_v[i, :n, span] = back.astype(BF16)
                    query_sum += total
                back, key_sum = head_back(key_grad * factor, key_raw, gains_ref[1:2], cos, sin)
                back_v[i, :n, q_cols : q_cols + size] = back.astype(BF16)
                back_v[i, :n, q_cols + size :] = values_back.astype(BF16)
                logit_back = logit_back.astype(BF16)
                logit_back_v[i, :n] = logit_back
                gains_sum[0:1] += query_sum
                gains_sum[1:2] += key_sum
                part = product_nt(back_v[i, :n], wa_v[...]) + product(logit_back, wh_v[...])
                part_v[i, :n] = part.astype(BF16)
                gain_sum[0:1] += jnp.sum(part * normed_v[i, :n].astype(F32), axis=0, keepdims=True)
                if n < rows:
                    part_v[i, n:] = jnp.zeros((rows - n, width), BF16)
                    back_v[i, n:] = jnp.zeros((rows - n, cols), BF16)
                    logit_back_v[i, n:] = jnp.zeros((rows - n, TILE), BF16)

            for_tiles(tiles_ref[2 * pair + i], rows // TILE, body)
            for j, (src, dst) in enumerate(
                (
                    (part_v, (part_a, part_b)[i]),
                    (back_v, back_all.at[spans[i]]),
                    (logit_back_v, logit_back_all.at[spans[i]]),
                )
            ):
                store = pltpu.make_async_copy(src.at[i], dst, out_sem.at[4 * i + j])
                store.start()
                stores.append(store)
        for store in stores:
            store.wait()

    whole = TEAM * rows
    result = pl.pallas_call(
        kernel,
        out_shape=[
            struct((rows, width), BF16),
            struct((rows, width), BF16),
            struct((whole, cols), BF16),
            struct((whole, TILE), BF16),
            struct((whole, width), BF16),
            struct((8, width), F32),
            struct((8, size), F32),
            struct((8, 128), jnp.int32),
        ],
        in_specs=[SMEM] + [ANY] * 8 + [VMEM] * 3 + [ANY] + [ANY] * count,
        out_specs=[ANY] * 5 + [VMEM] * 3,
        scratch_shapes=[
            pltpu.VMEM((2, rows, width), BF16),
            pltpu.VMEM(weight_attn.shape, BF16),
            pltpu.VMEM(weight_head.shape, BF16),
            pltpu.VMEM(weight_out.shape, BF16),
            pltpu.VMEM((2, rows, width), BF16),
            pltpu.VMEM((2, rows, cols), F32),
            pltpu.VMEM((2, rows, TILE), F32),
            pltpu.VMEM((2, rows, width), BF16),
            pltpu.VMEM((2, rows, cols), BF16),
            pltpu.VMEM((2, rows, TILE), BF16),
            pltpu.SemaphoreType.DMA((11,)),
            pltpu.SemaphoreType.DMA((8,)),
        ],
        input_output_aliases={13 + j: 2 + j for j in range(count)},
        compiler_params=pltpu.CompilerParams(vmem_limit_bytes=48 << 20),
        cost_estimate=pl.CostEstimate(flops=12 << 30, bytes_accessed=20 << 20, transcendentals=1 << 20),
    )(
        tiles, *hidden, weight_attn, weight_head, weight_out, *saved, gains, cosine, sine, after,
        *(kept or ()),
    )
    return result[0], result[1], result[2:5], result[5], result[6], result[7]


def tile_places(tiles_ref, rows):
    places, total = [], 0
    for r in range(TEAM):
        count = tiles_ref[r]
        for j in range(rows // TILE):
            places.append((r, j, j < count, total + j))
        total = total + count
    return places, total


def rows_of(tile, size=TILE):
    return pl.ds(pl.multiple_of(tile * size, size), size)


def feed_up(tiles, twos, upstreams, weight_gate, weight_up, after):
    rows, width = twos[0].shape
    ff_cols = weight_gate.shape[1]
    whole = TEAM * rows
    chunk = 2 * TILE
    chunks = whole // chunk

    def kernel(*refs):
        tiles_ref, twos_ref, ups_ref = refs[0], refs[1 : 1 + TEAM], refs[1 + TEAM : 1 + 2 * TEAM]
        weights_ref = refs[1 + 2 * TEAM : 3 + 2 * TEAM]
        inner_all, both_all, two_all, ups_all = refs[4 + 2 * TEAM : 8 + 2 * TEAM]
        two_v, ups_v, wg_v, wu_v, inner_v, both_v, zero_v, w_sem, load_sem, out_sem = refs[8 + 2 * TEAM :]
        places, total = tile_places(tiles_ref, rows)
        used = (total + 1) // 2

        def loads(sources, packed, which):
            for k, (r, j, live, place) in enumerate(places):
                yield live, pltpu.make_async_copy(
                    sources[r].at[rows_of(j)], packed.at[rows_of(place)], load_sem.at[which, k]
                )

        for live, copy in loads(twos_ref, two_v, 0):
            pl.when(live)(copy.start)
        weights = [
            pltpu.make_async_copy(weights_ref[0], wg_v, w_sem.at[0]),
            pltpu.make_async_copy(weights_ref[1], wu_v, w_sem.at[1]),
        ]
        for load in weights:
            load.start()
        for live, copy in loads(ups_ref, ups_v, 1):
            pl.when(live)(copy.start)
        zero_v[...] = jnp.zeros_like(zero_v)

        @pl.when(total % 2 == 1)
        def _():
            two_v[rows_of(total)] = jnp.zeros((TILE, width), BF16)
            ups_v[rows_of(total)] = jnp.zeros((TILE, width), BF16)

        for live, copy in loads(twos_ref, two_v, 0):
            pl.when(live)(copy.wait)
        for load in weights:
            load.wait()

        def stores(c, sources):
            for j, (src, dst) in enumerate(zip(sources, (two_all, ups_all, inner_all, both_all))):
                yield pltpu.make_async_copy(src, dst.at[rows_of(c, chunk)], out_sem.at[j, c])

        zeros = (zero_v, zero_v, zero_v.at[:, :ff_cols], zero_v.at[:, : 2 * ff_cols])
        for c in range(TEAM // 2, chunks):

            @pl.when(c >= used)
            def _(c=c):
                for store in stores(c, zeros):
                    store.start()

        for live, copy in loads(ups_ref, ups_v, 1):
            pl.when(live)(copy.wait)

        def body(c, carry):
            span = rows_of(c, chunk)
            gate_part = product(two_v[span], wg_v[...])
            up_part = product(two_v[span], wu_v[...])
            inner_v[span] = (gate_part * jax.nn.sigmoid(gate_part) * up_part).astype(BF16)
            both_v[span, :ff_cols] = gate_part.astype(BF16)
            both_v[span, ff_cols:] = up_part.astype(BF16)
            for store in stores(c, (two_v.at[span], ups_v.at[span], inner_v.at[span], both_v.at[span])):
                store.start()
            return carry

        lax.fori_loop(0, used, body, 0)
        for c in range(chunks):
            for store in stores(c, zeros):
                store.wait()

    count = whole // TILE
    return pl.pallas_call(
        kernel,
        out_shape=[
            struct((whole, ff_cols), BF16),
            struct((whole, 2 * ff_cols), BF16),
            struct((whole, width), BF16),
            struct((whole, width), BF16),
        ],
        in_specs=[SMEM] + [ANY] * (3 + 2 * TEAM),
        out_specs=[ANY] * 4,
        scratch_shapes=[
            pltpu.VMEM((whole, width), BF16),
            pltpu.VMEM((whole, width), BF16),
            pltpu.VMEM(weight_gate.shape, BF16),
            pltpu.VMEM(weight_up.shape, BF16),
            pltpu.VMEM((whole, ff_cols), BF16),
            pltpu.VMEM((whole, 2 * ff_cols), BF16),
            pltpu.VMEM((chunk, width), BF16),
            pltpu.SemaphoreType.DMA((2,)),
            pltpu.SemaphoreType.DMA((2, count)),
            pltpu.SemaphoreType.DMA((4, chunks)),
        ],
        compiler_params=pltpu.CompilerParams(vmem_limit_bytes=58 << 20),
        cost_estimate=pl.CostEstimate(flops=20 << 30, bytes_accessed=60 << 20, transcendentals=1 << 20),
    )(tiles, *twos, *upstreams, weight_gate, weight_up, after)


def feed_down(second, tiles, saved, weight_gate, weight_up, weight_down, kept, after):
    count = 2 * TEAM + 1 if second else 0
    ff_cols, width = weight_down.shape
    whole = saved[0].shape[0]
    rows = whole // TEAM
    chunk = 2 * TILE
    chunks = whole // chunk

    def kernel(*refs):
        tiles_ref, inner_all, both_all, ups_all, wg, wu, wd = refs[:7]
        outs_ref = refs[8 + count : 8 + count + TEAM]
        grads_ref = refs[8 + count + TEAM : 8 + count + 2 * TEAM]
        back_all = refs[8 + count + 2 * TEAM]
        (
            ups_v, both_v, inner_v, back_v, wg_v, wu_v, wd_v, out_v, grad_v, zero_v,
            in_sem, w_sem, out_sem, grad_sem, back_sem, zero_sem,
        ) = refs[9 + count + 2 * TEAM :]
        places, total = tile_places(tiles_ref, rows)
        used = (total + 1) // 2
        first_chunk = used // 2 if second else 0
        end_chunk = used if second else used // 2

        def loads(c):
            slot = c % 2
            for j, (src, dst) in enumerate(((ups_all, ups_v), (both_all, both_v), (inner_all, inner_v))):
                yield pltpu.make_async_copy(src.at[rows_of(c, chunk)], dst.at[slot], in_sem.at[j, slot])

        for load in loads(first_chunk):
            load.start()
        weights = [
            pltpu.make_async_copy(src, dst, w_sem.at[j])
            for j, (src, dst) in enumerate(((wd, wd_v), (wg, wg_v), (wu, wu_v)))
        ]
        for load in weights:
            load.start()
        if not second:
            zero_v[...] = jnp.zeros_like(zero_v)

        def tile_stores(k, r, j, sources):
            yield pltpu.make_async_copy(sources[0], grads_ref[r].at[rows_of(j)], grad_sem.at[k])
            yield pltpu.make_async_copy(sources[1], outs_ref[r].at[rows_of(j)], out_sem.at[k])

        zeros = (zero_v.at[:TILE], zero_v.at[:TILE])
        def now(live, place):
            in_span = jnp.logical_and(place // 2 >= first_chunk, place // 2 < end_chunk)
            if second:
                return jnp.logical_and(live, in_span)
            return jnp.logical_or(jnp.logical_not(live), in_span)

        for k, (r, j, live, place) in enumerate(places) if not second else ():

            @pl.when(jnp.logical_not(live))
            def _(k=k, r=r, j=j):
                for store in tile_stores(k, r, j, zeros):
                    store.start()

        def back_zero(c):
            return pltpu.make_async_copy(
                zero_v.at[:, : 2 * ff_cols], back_all.at[rows_of(c, chunk)], zero_sem.at[c]
            )

        for c in range(TEAM // 2, chunks) if not second else ():
            pl.when(c >= used)(back_zero(c).start)

        def back_store(c):
            return pltpu.make_async_copy(
                back_v.at[c % 2], back_all.at[rows_of(c, chunk)], back_sem.at[c % 2]
            )

        for load in weights:
            load.wait()

        def body(c, carry):
            slot = c % 2

            @pl.when(c + 1 < end_chunk)
            def _():
                for load in loads(c + 1):
                    load.start()

            for load in loads(c):
                load.wait()

            @pl.when(c >= first_chunk + 2)
            def _():
                back_store(c - 2).wait()

            span = rows_of(c, chunk)
            inner_grad = product_nt(ups_v[slot], wd_v[...])
            gate_part = both_v[slot, :, :ff_cols].astype(F32)
            up_part = both_v[slot, :, ff_cols:].astype(F32)
            sig = jax.nn.sigmoid(gate_part)
            silu = gate_part * sig
            back_v[slot, :, :ff_cols] = (inner_grad * up_part * (sig + silu * (1.0 - sig))).astype(BF16)
            back_v[slot, :, ff_cols:] = (inner_grad * silu).astype(BF16)
            back_store(c).start()
            grad = product_nt(back_v[slot, :, :ff_cols], wg_v[...]) + product_nt(back_v[slot, :, ff_cols:], wu_v[...])
            grad_v[span] = grad.astype(BF16)
            out_v[span] = product(inner_v[slot], wd_v[...]).astype(BF16)
            for k, (r, j, live, place) in enumerate(places):

                @pl.when(jnp.logical_and(live, place // 2 == c))
                def _(k=k, r=r, j=j, place=place):
                    here = rows_of(place)
                    for store in tile_stores(k, r, j, (grad_v.at[here], out_v.at[here])):
                        store.start()

            return carry

        lax.fori_loop(first_chunk, end_chunk, body, 0)
        back_store(end_chunk - 2).wait()
        back_store(end_chunk - 1).wait()
        for c in range(TEAM // 2, chunks) if not second else ():
            pl.when(c >= used)(back_zero(c).wait)
        for k, (r, j, live, place) in enumerate(places):

            @pl.when(now(live, place))
            def _(k=k, r=r, j=j):
                for store in tile_stores(k, r, j, zeros):
                    store.wait()

    tile_count = whole // TILE
    result = pl.pallas_call(
        kernel,
        out_shape=[struct((rows, width), BF16)] * (2 * TEAM) + [struct((whole, 2 * ff_cols), BF16)],
        in_specs=[SMEM] + [ANY] * (7 + count),
        out_specs=[ANY] * (2 * TEAM + 1),
        input_output_aliases={8 + j: j for j in range(count)},
        scratch_shapes=[
            pltpu.VMEM((2, chunk, width), BF16),
            pltpu.VMEM((2, chunk, 2 * ff_cols), BF16),
            pltpu.VMEM((2, chunk, ff_cols), BF16),
            pltpu.VMEM((2, chunk, 2 * ff_cols), BF16),
            pltpu.VMEM(weight_gate.shape, BF16),
            pltpu.VMEM(weight_up.shape, BF16),
            pltpu.VMEM(weight_down.shape, BF16),
            pltpu.VMEM((whole, width), BF16),
            pltpu.VMEM((whole, width), BF16),
            pltpu.VMEM((chunk, width), BF16),
            pltpu.SemaphoreType.DMA((3, 2)),
            pltpu.SemaphoreType.DMA((3,)),
            pltpu.SemaphoreType.DMA((tile_count,)),
            pltpu.SemaphoreType.DMA((tile_count,)),
            pltpu.SemaphoreType.DMA((2,)),
            pltpu.SemaphoreType.DMA((chunks,)),
        ],
        compiler_params=pltpu.CompilerParams(vmem_limit_bytes=56 << 20),
        cost_estimate=pl.CostEstimate(flops=40 << 30, bytes_accessed=80 << 20, transcendentals=1 << 20),
    )(tiles, *saved, weight_gate, weight_up, weight_down, after, *(kept or ()))
    return result


def local(
    groups,
    tokens,
    lengths,
    cotangent,
    attention_gain,
    query_weight,
    key_matrix,
    value_matrix,
    head_gate_weight,
    output_weight,
    query_key_gain,
    feedforward_gain,
    gate_weight,
    up_weight,
    down_weight,
):
    t = member()
    everyone = groups * TEAM
    rows, width = tokens.shape
    rho = query_weight.shape[0]
    phi = down_weight.shape[0]
    ff = gate_weight.shape[1]
    pair_cols = query_key_gain.shape[1]
    size = pair_cols * everyone
    heads = query_weight.shape[1] // size
    mine = heads // TEAM
    q_cols = query_weight.shape[1] // TEAM
    k_cols = key_matrix.shape[1] // TEAM
    ff_cols = ff // TEAM

    def everyone_in_team(vector):
        return jnp.broadcast_to(vector.reshape(1, -1), (TEAM, vector.size))

    live_tiles = (lengths + (TILE - 1)) // TILE
    row = jnp.concatenate(
        [
            head_gate_weight.reshape(rho, TEAM, mine).transpose(1, 2, 0).reshape(TEAM, -1),
            everyone_in_team(attention_gain),
            everyone_in_team(feedforward_gain),
            everyone_in_team(query_key_gain),
            everyone_in_team(live_tiles.astype(BF16)),
        ],
        axis=1,
    )
    cols = q_cols + 2 * k_cols
    row = jnp.pad(row, ((0, 0), (0, cols - row.shape[1])))[:, None, :]
    attn = jnp.concatenate(
        [
            query_weight.reshape(rho, TEAM, q_cols),
            key_matrix.reshape(rho, TEAM, k_cols),
            value_matrix.reshape(rho, TEAM, k_cols),
        ],
        axis=2,
    ).transpose(1, 0, 2)
    attn = jnp.concatenate([attn, jnp.pad(row, ((0, 0), (0, 7), (0, 0)))], axis=1)
    attn = exchange(attn)
    head_lanes = mine * rho
    at_one, at_two, at_pair = head_lanes, head_lanes + rho, head_lanes + 2 * rho
    at_tiles = at_pair + 2 * pair_cols
    team_tiles = attn[:, rho, at_tiles].astype(jnp.int32)
    order = jnp.arange(TEAM, dtype=jnp.int32)
    tiles = jnp.sum(jnp.where((order[:, None] ^ t) == order[None, :], team_tiles[None, :], 0), axis=1)
    attn = line_gather(attn.reshape(TEAM * (rho + 8), cols)).reshape(everyone, rho + 8, cols)
    weight_attn = attn[:, :rho].reshape(width, cols)
    rows_small = attn[:, rho]
    weight_head = jnp.pad(
        rows_small[:, :head_lanes].reshape(everyone, mine, rho).transpose(1, 0, 2).reshape(mine, width),
        ((0, TILE - mine), (0, 0)),
    )
    gain_one = rows_small[:, at_one:at_two].reshape(1, width).astype(F32)
    gain_two = rows_small[:, at_two:at_pair].reshape(1, width).astype(F32)
    gain_pair = (
        rows_small[:, at_pair:at_tiles]
        .reshape(everyone, 2, pair_cols)
        .transpose(1, 0, 2)
        .reshape(2, size)
        .astype(F32)
    )
    weight_out = out_weight_in(output_weight, groups)

    def ff_split(w):
        return w.reshape(rho, groups, TEAM, phi).transpose(2, 0, 1, 3).reshape(TEAM, rho, ff_cols)

    feed_shard = jnp.concatenate([ff_split(gate_weight), ff_split(up_weight)], axis=2)
    feed_shard = exchange(feed_shard).reshape(TEAM * rho, -1)
    weight_gate = line_gather(feed_shard[:, :ff_cols])

    exponent = jnp.arange(size // 2, dtype=F32) * (-2.0 / size)
    frequency = jnp.power(ROPE_BASE, exponent)
    angles = jnp.arange(rows, dtype=F32)[:, None] * frequency[None, :]
    cosine = jnp.concatenate([jnp.cos(angles), jnp.cos(angles)], axis=1)
    sine = jnp.concatenate([-jnp.sin(angles), jnp.sin(angles)], axis=1)
    consts = (weight_attn, weight_head, weight_out, gain_one, gain_pair, cosine, sine)
    team_tokens = team_gather(tokens)
    kept, arrived = None, TeamSum()
    live = lax.broadcasted_iota(jnp.int32, (rows, 1), 0) < lengths[0]
    live_rows = live.astype(F32)
    upstream = cotangent.astype(F32) * live_rows
    ticks = []
    for step, pair in enumerate(ORDER_BACK):
        if step == 0:
            after = mark([feed_shard])
        if step == 2:
            after = arrived.low6
        if step == 3:
            after = mark([team_upstream[1], team_upstream[2], team_upstream[4], weight_gate])
        a, b, kept, tick = attend(
            pair, tiles, team_tokens[2 * pair : 2 * pair + 2], consts, kept, mine, after
        )
        arrived.add(pair, a, b)
        if step == 0:
            weight_up = line_gather(hold([feed_shard[:, ff_cols:]], tick)[0])
            later = lax.broadcasted_iota(jnp.int32, (rows, 1), 0) < lengths[0] + tick[0, 0]
            team_upstream = team_gather(jnp.where(later, cotangent, jnp.zeros_like(cotangent)))
        if step == 1:
            weight_down = line_gather(hold([down_weight], tick)[0])
    normed, qkv, logit, gated = kept
    inputs = tokens.astype(F32)
    hidden_state = inputs + arrived.total()

    normed_two = rms(hidden_state, gain_two).astype(BF16)
    normed_two = hold([normed_two], mark(team_upstream + [weight_up]))[0]
    team_two = team_gather(normed_two)
    saved = feed_up(tiles, team_two, team_upstream, weight_gate, weight_up, weight_down)
    inner, both, two_all, ups_all = saved
    down_part = product_tn(inner, ups_all).astype(BF16)
    half_width = width // 2
    down_grads = [line_sum(down_part[:, :half_width])]
    kept = feed_down(
        False, tiles, (inner, both, ups_all), weight_gate, weight_up, weight_down, None, mark([down_part])
    )
    kept = feed_down(
        True, tiles, (inner, both, ups_all), weight_gate, weight_up, weight_down, kept, down_grads[0]
    )
    down_grads.append(line_sum(hold([down_part[:, half_width:]], down_grads[0])[0]))
    down_grad = jnp.concatenate(down_grads, axis=1)
    outs, grads, feed_back = kept[:TEAM], kept[TEAM : 2 * TEAM], kept[2 * TEAM]
    arrived = TeamSum()
    for pair in ORDER_BACK:
        arrived.add(pair, grads[2 * pair], grads[2 * pair + 1])
    two_grad = arrived.total()
    feed_back = hold([feed_back], arrived.low6)[0]
    gate_part = product_tn(two_all, feed_back[:, :ff_cols]).astype(BF16)
    up_part = product_tn(two_all, feed_back[:, ff_cols:]).astype(BF16)
    gate_part = hold([gate_part], down_grads[1])[0]
    after = mark([gate_part, up_part])
    gate_grad = line_sum(gate_part)
    up_grad = line_sum(hold([up_part], gate_grad)[0])

    hidden_grad = upstream + rms_pull(hidden_state, gain_two, two_grad)

    hidden_levels = TeamGather(hold([hidden_grad.astype(BF16)], after)[0])
    team_hidden = [hidden_levels.own, hidden_levels.a1]
    two_scale = lax.rsqrt(jnp.mean(hidden_state * hidden_state, axis=-1, keepdims=True) + EPSILON)
    two_sum = jnp.sum(two_grad * hidden_state * two_scale, axis=0)
    kept, one_sum, pair_sum, ticks, arrived = None, 0.0, 0.0, [], TeamSum()
    for step, pair in enumerate(ORDER_LATE):
        if step == 1:
            after = gate_grad
        if step == 2:
            after = up_grad
        if step == 3:
            after = mark([arrived.low6, fed.u2, fed.u4, fed.x_top, fed.y_low])
        a, b, kept, total, pair_total, tick = attend_back(
            pair, tiles, team_hidden[2 * pair : 2 * pair + 2], consts, (normed, qkv, logit), kept, mine, after
        )
        arrived.add(pair, a, b)
        one_sum = one_sum + total[0]
        pair_sum = pair_sum + pair_total[:2]
        if step == 0:
            team_hidden = hidden_levels.blocks(tick)
            outs = hold(outs, tick)
            fed = TeamSum()
            for other in ORDER_BACK:
                fed.add(other, outs[2 * other], outs[2 * other + 1])
    attn_back, logit_back, hidden_all = kept
    feed_done = up_grad
    layer_output = ((hidden_state + fed.total()) * live_rows).astype(BF16)
    normed_grad = arrived.total()
    feed_grad = jnp.concatenate([gate_grad, hold([up_grad], normed_grad)[0]], axis=1)
    feed_grad = exchange(feed_grad.reshape(TEAM, rho, 2 * ff_cols))
    def ff_join(w):
        return w.reshape(TEAM, rho, groups, phi).transpose(1, 2, 0, 3).reshape(rho, ff)

    gate_grad = ff_join(feed_grad[:, :, :ff_cols])
    up_grad = ff_join(feed_grad[:, :, ff_cols:])
    tokens_grad = (hidden_grad + rms_pull(inputs, gain_one, normed_grad)).astype(BF16)
    out_part = product_tn(gated, hidden_all).astype(BF16)
    attn_part = product_tn(normed, attn_back).astype(BF16)
    head_part = product_tn(logit_back, normed)[:mine]
    row = jnp.concatenate(
        [
            head_part.reshape(mine, everyone, rho).transpose(1, 0, 2).reshape(everyone, -1),
            (one_sum / gain_one[0]).reshape(everyone, rho),
            two_sum.reshape(everyone, rho),
            pair_sum.reshape(2, everyone, pair_cols).transpose(1, 0, 2).reshape(everyone, -1),
        ],
        axis=1,
    ).astype(BF16)
    row = jnp.pad(row, ((0, 0), (0, cols - row.shape[1])))[:, None, :]
    packed = jnp.concatenate(
        [attn_part.reshape(everyone, rho, cols), jnp.pad(row, ((0, 0), (0, 7), (0, 0)))], axis=1
    )
    packed = packed.reshape(everyone * (rho + 8), cols)
    packed = line_sum(hold([packed], feed_done)[0])
    output_grad, packed = out_weight_back(out_part, groups, packed)
    packed = exchange(packed.reshape(TEAM, rho + 8, cols))
    attn_grad = packed[:, :rho].transpose(1, 0, 2)
    rows_small = packed[:, rho].astype(F32)
    sums = jnp.sum(rows_small[:, head_lanes:], axis=0)
    head_gate_grad = rows_small[:, :head_lanes].reshape(heads, rho).T
    return (
        layer_output,
        tokens_grad,
        sums[:rho],
        attn_grad[:, :, :q_cols].reshape(rho, -1).astype(F32),
        attn_grad[:, :, q_cols : q_cols + k_cols].reshape(rho, -1).astype(F32),
        attn_grad[:, :, q_cols + k_cols :].reshape(rho, -1).astype(F32),
        head_gate_grad,
        output_grad.astype(F32),
        sums[2 * rho : 2 * rho + 2 * pair_cols].reshape(2, pair_cols),
        sums[rho : 2 * rho],
        gate_grad.astype(F32),
        up_grad.astype(F32),
        down_grad.astype(F32),
    )


def solution(mesh):
    groups = mesh.size // TEAM
    rows, vector, columns = P(ALL, None), P(ALL), P(None, ALL)

    def step(*args):
        return local(groups, *args)

    return jax.shard_map(
        step,
        mesh=mesh,
        in_specs=(
            rows, vector, rows, vector, rows, rows, rows, rows, rows, columns, vector, rows, rows, rows,
        ),
        out_specs=(
            rows, rows, vector, rows, rows, rows, rows, rows, columns, vector, rows, rows, rows,
        ),
        check_vma=False,
    )
```

```python
import jax
import jax.numpy as jnp
from jax import lax
from jax.experimental import pallas as pl
from jax.experimental.pallas import tpu as pltpu
from jax.sharding import PartitionSpec as P

EPSILON = 1e-06
ROPE_BASE = 1000000.0
TEAM = 8
ALL = ("dp", "fsdp")
F32 = jnp.float32
BF16 = jnp.bfloat16
TILE = 128
ANY = pl.BlockSpec(memory_space=pl.ANY)
VMEM = pl.BlockSpec(memory_space=pltpu.VMEM)
SMEM = pl.BlockSpec(memory_space=pltpu.SMEM)


def product(left, right):
    return jnp.dot(left, right, preferred_element_type=F32)


def product_nt(left, right):
    return lax.dot_general(left, right, (((1,), (1,)), ((), ())), preferred_element_type=F32)


def product_tn(left, right):
    return lax.dot_general(left, right, (((0,), (0,)), ((), ())), preferred_element_type=F32)


def world():
    return lax.axis_size(ALL)


def member():
    return lax.axis_index(ALL) % TEAM


def teams():
    return [[first + t for t in range(TEAM)] for first in range(0, world(), TEAM)]


def lines():
    return [list(range(t, world(), TEAM)) for t in range(TEAM)]


def permute(array, pairs):
    return lax.ppermute(
        array, ALL, [(team[a], team[b]) for team in teams() for a, b in pairs]
    )


def swap(array, bits):
    return permute(array, [(i, i ^ bits) for i in range(TEAM)])


def exchange(blocks):
    if lax.axis_size("fsdp") == TEAM:
        return lax.all_to_all(blocks, "fsdp", 0, 0, tiled=True)
    return lax.all_to_all(blocks, ALL, 0, 0, tiled=True, axis_index_groups=teams())


def line_gather(shard):
    if lax.axis_size("fsdp") == TEAM:
        return lax.all_gather(shard, "dp", axis=0, tiled=True)
    return lax.all_gather(shard, ALL, axis=0, tiled=True, axis_index_groups=lines())


def line_sum(array):
    if lax.axis_size("fsdp") == TEAM:
        return lax.psum_scatter(array, "dp", scatter_dimension=0, tiled=True)
    return lax.psum_scatter(array, ALL, scatter_dimension=0, tiled=True, axis_index_groups=lines())


class TeamGather:
    def __init__(self, own):
        self.own = own
        self.a1 = swap(own, 1)
        self.a2 = swap(own, 2)
        self.a4 = swap(own, 4)

    def blocks(self, tick=None):
        a2, a4 = self.a2, self.a4
        if tick is not None:
            a2, a4 = hold([a2, a4], tick)
        half = self.own.shape[0] // 2
        a6 = jnp.concatenate([swap(a4[:half], 2), swap(a2[half:], 4)], axis=0)
        return [self.own, self.a1, a2, swap(a2, 1), a4, swap(a4, 1), a6, swap(a6, 1)]


def team_gather(own):
    return TeamGather(own).blocks()


class TeamSum:
    def __init__(self, parts):
        half = parts[0].shape[0] // 2
        odd = {r: swap(parts[r + 1], 1) for r in (6, 2, 4, 0)}
        self.total6, self.total2, self.total4, self.total0 = (
            parts[r].astype(F32) + odd[r].astype(F32) for r in (6, 2, 4, 0)
        )
        self.half = half
        self.low6 = self.total6.astype(BF16)
        self.ready = [self.low6, self.total2[:half].astype(BF16), self.total4[half:].astype(BF16)]

    def first(self, tick=None):
        half = self.half
        low6, x_top, y_low = self.ready if tick is None else hold(self.ready, tick)
        self.u4 = swap(low6[:half], 2)
        self.u2 = swap(low6[half:], 4)
        self.x_top = swap(x_top, 2)
        self.y_low = swap(y_low, 4)
        self.sent = [low6, x_top, y_low]
        return [self.u4, self.u2, self.x_top, self.y_low]

    def total(self):
        half = self.half
        x_low = swap((self.total2[half:] + self.u2.astype(F32)).astype(BF16), 2).astype(F32)
        y_top = swap((self.total4[:half] + self.u4.astype(F32)).astype(BF16), 4).astype(F32)
        top = self.x_top.astype(F32) + y_top
        low = x_low + self.y_low.astype(F32)
        return self.total0 + jnp.concatenate([top, low], axis=0)


def out_weight_in(shard, groups):
    t = member()
    if groups < TEAM:
        gathered = line_gather(shard[None])
        per = TEAM // groups
        b, z = t % groups, t // per
        result = jnp.zeros_like(gathered)
        for j in range(groups):
            perm = [(i, per * ((i % groups + j) % groups) + i // groups) for i in range(TEAM)]
            piece = lax.dynamic_index_in_dim(gathered, (b + j) % groups, 0, keepdims=True)
            piece = permute(piece, perm)
            result = lax.dynamic_update_slice_in_dim(result, piece, (z - j + groups) % groups, 0)
        return result.reshape(-1, shard.shape[1])
    full = lax.all_gather(shard, ALL, axis=0, tiled=True)
    rows = full.shape[0] // TEAM
    return lax.dynamic_slice_in_dim(full, t * rows, rows, 0)


def out_weight_back(grad, groups, done):
    t = member()
    if groups < TEAM:
        per = TEAM // groups
        b, z = t % groups, t // per
        grad = grad.reshape(groups, -1, grad.shape[1])
        placed = jnp.zeros_like(grad)
        for j in range(groups):
            perm = [(per * ((i % groups + j) % groups) + i // groups, i) for i in range(TEAM)]
            piece = lax.dynamic_index_in_dim(grad, (z - j + groups) % groups, 0, keepdims=True)
            piece = permute(piece, perm)
            placed = lax.dynamic_update_slice_in_dim(placed, piece, (b + j) % groups, 0)
        placed = hold([placed], done)[0]
        return line_sum(placed)[0], hold([done], placed)[0]
    whole = jnp.zeros((grad.shape[0] * TEAM, grad.shape[1]), grad.dtype)
    whole = lax.dynamic_update_slice_in_dim(whole, grad, t * grad.shape[0], 0)
    return lax.psum_scatter(whole, ALL, scatter_dimension=0, tiled=True), done


def rms_pull(value, gain, grad):
    scale = lax.rsqrt(jnp.mean(value * value, axis=-1, keepdims=True) + EPSILON)
    weighted = grad * gain
    mean = jnp.mean(weighted * value, axis=-1, keepdims=True)
    return scale * weighted - scale * scale * scale * value * mean


def rms(value, gain):
    return value * lax.rsqrt(jnp.mean(value * value, axis=-1, keepdims=True) + EPSILON) * gain


def struct(shape, dtype):
    return jax.ShapeDtypeStruct(shape, dtype)


def hold(arrays, tick):
    def kernel(*refs):
        del refs

    count = len(arrays)
    return pl.pallas_call(
        kernel,
        out_shape=[struct(a.shape, a.dtype) for a in arrays],
        in_specs=[ANY] * count + [ANY],
        out_specs=[ANY] * count,
        input_output_aliases={i: i for i in range(count)},
    )(*arrays, tick)


def mark(arrays):
    def kernel(*refs):
        refs[-1][...] = jnp.zeros_like(refs[-1])

    return pl.pallas_call(
        kernel,
        out_shape=struct((8, 128), jnp.int32),
        in_specs=[ANY] * len(arrays),
        out_specs=VMEM,
    )(*arrays)


def for_tiles(tiles, most, body):
    for m in range(1, most + 1):

        @pl.when(tiles == m)
        def _(m=m):
            body(m * TILE)


def turned(u, cosine, sine):
    return u * cosine + pltpu.roll(u, u.shape[-1] // 2, 1) * sine


def head_norm(u):
    return lax.rsqrt(jnp.mean(u * u, axis=-1, keepdims=True) + EPSILON)


def head_back(grad, raw, gain, cosine, sine):
    e = turned(grad, cosine, -sine)
    scale = head_norm(raw)
    weighted = e * gain
    mean = jnp.mean(weighted * raw, axis=-1, keepdims=True)
    back = scale * weighted - scale * scale * scale * raw * mean
    return back, jnp.sum(e * raw * scale, axis=0, keepdims=True)


def weights_of(query, key, factor):
    scores = product_nt(query, key) * factor
    n = scores.shape[0]
    causal = lax.broadcasted_iota(jnp.int32, (n, n), 1) <= lax.broadcasted_iota(jnp.int32, (n, n), 0)
    scores = jnp.where(causal, scores, -jnp.inf)
    terms = jnp.exp(scores - jnp.max(scores, axis=-1, keepdims=True))
    return terms * (1.0 / jnp.sum(terms, axis=-1, keepdims=True))


def rows_of(tile, size=TILE):
    return pl.ds(pl.multiple_of(tile * size, size), size)


def each_block(r, body):
    for k in range(TEAM):
        pl.when(r == k)(lambda k=k: body(k))


def attend(tiles, tokens, consts, mine, after):
    weight_attn, weight_head, weight_out, gain, gains, cosine, sine = consts
    rows, width = tokens[0].shape
    size = gains.shape[1]
    q_cols = mine * size
    cols = weight_attn.shape[1]
    factor = size ** (-0.5)

    def kernel(*refs):
        tiles_ref, toks = refs[0], refs[1 : 1 + TEAM]
        wa, wh, wo, gain_ref, gains_ref, cos_ref, sin_ref, _ = refs[1 + TEAM : 9 + TEAM]
        parts = refs[9 + TEAM : 9 + 2 * TEAM]
        normed_all, qkv_all, logit_all, gated_all, tick = refs[9 + 2 * TEAM : 14 + 2 * TEAM]
        (
            tok_v, wa_v, wh_v, wo_v, part_v, normed_v, qkv_v, logit_v, gated_v, w_sem, in_sem, out_sem,
        ) = refs[14 + 2 * TEAM :]
        tick[...] = jnp.zeros_like(tick)

        def load(k, slot):
            return pltpu.make_async_copy(toks[k], tok_v.at[slot], in_sem.at[slot])

        def store(r, slot, j, k=0):
            src = (part_v, normed_v, qkv_v, logit_v, gated_v)[j].at[slot]
            dst = parts[k] if j == 0 else (normed_all, qkv_all, logit_all, gated_all)[j - 1].at[rows_of(r, rows)]
            return pltpu.make_async_copy(src, dst, out_sem.at[j, slot])

        load(0, 0).start()
        weights = [
            pltpu.make_async_copy(src, dst, w_sem.at[j])
            for j, (src, dst) in enumerate(((wa, wa_v), (wh, wh_v), (wo, wo_v)))
        ]
        for copy in weights:
            copy.start()
        for copy in weights:
            copy.wait()

        def step(r, carry):
            slot = r % 2

            @pl.when(r + 1 < TEAM)
            def _():
                each_block(r + 1, lambda k: load(k, 1 - slot).start())

            load(0, slot).wait()

            @pl.when(r >= 2)
            def _():
                for j in range(5):
                    store(r - 2, slot, j).wait()

            def body(n):
                value = tok_v[slot, :n].astype(F32)
                normed = rms(value, gain_ref[...]).astype(BF16)
                normed_v[slot, :n] = normed
                qkv = product(normed, wa_v[...])
                qkv_v[slot, :n] = qkv
                logit = product_nt(normed, wh_v[...])
                logit_v[slot, :n] = logit
                cos, sin = cos_ref[:n], sin_ref[:n]
                key = qkv[:, q_cols : q_cols + size]
                key = turned(key * head_norm(key) * gains_ref[1:2], cos, sin).astype(BF16)
                values = qkv[:, q_cols + size :].astype(BF16)
                for h in range(mine):
                    query = qkv[:, h * size : (h + 1) * size]
                    query = turned(query * head_norm(query) * gains_ref[0:1], cos, sin).astype(BF16)
                    attention = weights_of(query, key, factor)
                    mixture = product(attention.astype(BF16), values)
                    gate = jax.nn.sigmoid(logit[:, h : h + 1])
                    gated_v[slot, :n, h * size : (h + 1) * size] = (mixture * gate).astype(BF16)
                part_v[slot, :n] = product(gated_v[slot, :n], wo_v[...]).astype(BF16)
                if n < rows:
                    part_v[slot, n:] = jnp.zeros((rows - n, width), BF16)
                    normed_v[slot, n:] = jnp.zeros((rows - n, width), BF16)
                    gated_v[slot, n:] = jnp.zeros((rows - n, q_cols), BF16)

            for_tiles(tiles_ref[r], rows // TILE, body)
            each_block(r, lambda k: store(r, slot, 0, k).start())
            for j in range(1, 5):
                store(r, slot, j).start()
            return carry

        lax.fori_loop(0, TEAM, step, 0)
        for r in (TEAM - 2, TEAM - 1):
            for j in range(5):
                store(r, r % 2, j).wait()

    whole = TEAM * rows
    result = pl.pallas_call(
        kernel,
        out_shape=[struct((rows, width), BF16)] * TEAM
        + [
            struct((whole, width), BF16),
            struct((whole, cols), F32),
            struct((whole, TILE), F32),
            struct((whole, q_cols), BF16),
            struct((8, 128), jnp.int32),
        ],
        in_specs=[SMEM] + [ANY] * (TEAM + 3) + [VMEM] * 4 + [ANY],
        out_specs=[ANY] * (TEAM + 4) + [VMEM],
        scratch_shapes=[
            pltpu.VMEM((2, rows, width), BF16),
            pltpu.VMEM(weight_attn.shape, BF16),
            pltpu.VMEM(weight_head.shape, BF16),
            pltpu.VMEM(weight_out.shape, BF16),
            pltpu.VMEM((2, rows, width), BF16),
            pltpu.VMEM((2, rows, width), BF16),
            pltpu.VMEM((2, rows, cols), F32),
            pltpu.VMEM((2, rows, TILE), F32),
            pltpu.VMEM((2, rows, q_cols), BF16),
            pltpu.SemaphoreType.DMA((3,)),
            pltpu.SemaphoreType.DMA((2,)),
            pltpu.SemaphoreType.DMA((5, 2)),
        ],
        compiler_params=pltpu.CompilerParams(vmem_limit_bytes=48 << 20),
        cost_estimate=pl.CostEstimate(flops=30 << 30, bytes_accessed=60 << 20, transcendentals=1 << 20),
    )(tiles, *tokens, weight_attn, weight_head, weight_out, gain, gains, cosine, sine, after)
    return result[:TEAM], result[TEAM : TEAM + 4], result[TEAM + 4]


def attend_back(tiles, hidden, consts, saved, mine, after):
    weight_attn, weight_head, weight_out, gain, gains, cosine, sine = consts
    rows, width = hidden[0].shape
    size = gains.shape[1]
    q_cols = mine * size
    cols = weight_attn.shape[1]
    factor = size ** (-0.5)

    def kernel(*refs):
        tiles_ref, hids = refs[0], refs[1 : 1 + TEAM]
        wa, wh, wo, normed_all, qkv_all, logit_all, gated_all = refs[1 + TEAM : 8 + TEAM]
        gains_ref, cos_ref, sin_ref, _ = refs[8 + TEAM : 12 + TEAM]
        parts = refs[12 + TEAM : 12 + 2 * TEAM]
        attn_sum, out_sum, gain_sum, gains_sum = refs[12 + 2 * TEAM : 16 + 2 * TEAM]
        (
            hid_v, wa_v, wh_v, wo_v, normed_v, qkv_v, logit_v, gated_v, part_v, back_v,
            w_sem, in_sem, out_sem,
        ) = refs[16 + 2 * TEAM :]

        def loads(r, slot, k):
            yield pltpu.make_async_copy(hids[k], hid_v.at[slot], in_sem.at[0, slot])
            here = rows_of(r, rows)
            for j, (src, dst) in enumerate(
                ((qkv_all, qkv_v), (logit_all, logit_v), (normed_all, normed_v), (gated_all, gated_v))
            ):
                yield pltpu.make_async_copy(src.at[here], dst.at[slot], in_sem.at[1 + j, slot])

        def start_loads(r, slot):
            def body(k):
                for copy in loads(r, slot, k):
                    copy.start()

            each_block(r, body)

        def store(slot, k=0):
            return pltpu.make_async_copy(part_v.at[slot], parts[k], out_sem.at[slot])

        for copy in loads(0, 0, 0):
            copy.start()
        weights = [
            pltpu.make_async_copy(src, dst, w_sem.at[j])
            for j, (src, dst) in enumerate(((wo, wo_v), (wa, wa_v), (wh, wh_v)))
        ]
        for copy in weights:
            copy.start()
        for ref in (attn_sum, out_sum, gain_sum, gains_sum):
            ref[...] = jnp.zeros_like(ref)
        for copy in weights:
            copy.wait()

        def step(r, carry):
            slot = r % 2

            @pl.when(r + 1 < TEAM)
            def _():
                start_loads(r + 1, 1 - slot)

            for copy in loads(r, slot, 0):
                copy.wait()

            @pl.when(r >= 2)
            def _():
                store(slot).wait()

            def body(n):
                hidden_low = hid_v[slot, :n]
                normed = normed_v[slot, :n]
                out_sum[...] += product_tn(gated_v[slot, :n], hidden_low)
                gated_grad = product_nt(hidden_low, wo_v[...])
                cos, sin = cos_ref[:n], sin_ref[:n]
                key_raw = qkv_v[slot, :n, q_cols : q_cols + size]
                key = turned(key_raw * head_norm(key_raw) * gains_ref[1:2], cos, sin).astype(BF16)
                values = qkv_v[slot, :n, q_cols + size :].astype(BF16)
                lane = lax.broadcasted_iota(jnp.int32, (n, TILE), 1)
                logit_back = jnp.zeros((n, TILE), F32)
                values_back = jnp.zeros((n, size), F32)
                key_grad = jnp.zeros((n, size), F32)
                query_sum = jnp.zeros((1, size), F32)
                for h in range(mine):
                    span = slice(h * size, (h + 1) * size)
                    query_raw = qkv_v[slot, :n, span]
                    query = turned(query_raw * head_norm(query_raw) * gains_ref[0:1], cos, sin).astype(BF16)
                    attention = weights_of(query, key, factor)
                    attention_low = attention.astype(BF16)
                    mixture = product(attention_low, values)
                    gate = jax.nn.sigmoid(logit_v[slot, :n, h : h + 1])
                    head_grad = gated_grad[:, span]
                    mixture_back = (head_grad * gate).astype(BF16)
                    one = jnp.sum(head_grad * mixture, axis=-1, keepdims=True) * gate * (1.0 - gate)
                    logit_back = jnp.where(lane == h, one, logit_back)
                    values_back += product_tn(attention_low, mixture_back)
                    attention_grad = product_nt(mixture_back, values)
                    scores_back = (
                        attention
                        * (attention_grad - jnp.sum(attention_grad * attention, axis=-1, keepdims=True))
                    ).astype(BF16)
                    query_grad = product(scores_back, key) * factor
                    key_grad += product_tn(scores_back, query)
                    back, total = head_back(query_grad, query_raw, gains_ref[0:1], cos, sin)
                    back_v[:n, span] = back.astype(BF16)
                    query_sum += total
                back, key_sum = head_back(key_grad * factor, key_raw, gains_ref[1:2], cos, sin)
                back_v[:n, q_cols : q_cols + size] = back.astype(BF16)
                back_v[:n, q_cols + size : cols] = values_back.astype(BF16)
                logit_back = logit_back.astype(BF16)
                back_v[:n, cols:] = logit_back
                gains_sum[0:1] += query_sum
                gains_sum[1:2] += key_sum
                part = product_nt(back_v[:n, :cols], wa_v[...]) + product(logit_back, wh_v[...])
                part_v[slot, :n] = part.astype(BF16)
                gain_sum[0:1] += jnp.sum(part * normed.astype(F32), axis=0, keepdims=True)
                attn_sum[...] += product_tn(back_v[:n], normed)
                if n < rows:
                    part_v[slot, n:] = jnp.zeros((rows - n, width), BF16)

            for_tiles(tiles_ref[r], rows // TILE, body)
            each_block(r, lambda k: store(slot, k).start())
            return carry

        lax.fori_loop(0, TEAM, step, 0)
        store(0).wait()
        store(1).wait()

    result = pl.pallas_call(
        kernel,
        out_shape=[struct((rows, width), BF16)] * TEAM
        + [
            struct((cols + TILE, width), F32),
            struct((q_cols, width), F32),
            struct((8, width), F32),
            struct((8, size), F32),
        ],
        in_specs=[SMEM] + [ANY] * (TEAM + 7) + [VMEM] * 3 + [ANY],
        out_specs=[ANY] * TEAM + [VMEM] * 4,
        scratch_shapes=[
            pltpu.VMEM((2, rows, width), BF16),
            pltpu.VMEM(weight_attn.shape, BF16),
            pltpu.VMEM(weight_head.shape, BF16),
            pltpu.VMEM(weight_out.shape, BF16),
            pltpu.VMEM((2, rows, width), BF16),
            pltpu.VMEM((2, rows, cols), F32),
            pltpu.VMEM((2, rows, TILE), F32),
            pltpu.VMEM((2, rows, q_cols), BF16),
            pltpu.VMEM((2, rows, width), BF16),
            pltpu.VMEM((rows, cols + TILE), BF16),
            pltpu.SemaphoreType.DMA((3,)),
            pltpu.SemaphoreType.DMA((5, 2)),
            pltpu.SemaphoreType.DMA((2,)),
        ],
        compiler_params=pltpu.CompilerParams(vmem_limit_bytes=56 << 20),
        cost_estimate=pl.CostEstimate(flops=45 << 30, bytes_accessed=70 << 20, transcendentals=1 << 20),
    )(tiles, *hidden, weight_attn, weight_head, weight_out, *saved, gains, cosine, sine, after)
    return result[:TEAM], result[TEAM], result[TEAM + 1], result[TEAM + 2][0], result[TEAM + 3][:2]


def tile_places(tiles_ref, rows):
    places, total = [], 0
    for r in range(TEAM):
        count = tiles_ref[r]
        for j in range(rows // TILE):
            places.append((r, j, j < count, total + j))
        total = total + count
    return places, total


def feed(tiles, twos, upstreams, weight_gate, weight_up, weight_down):
    rows, width = twos[0].shape
    ff_cols = weight_down.shape[0]
    whole = TEAM * rows
    chunk = 2 * TILE
    chunks = whole // chunk

    def kernel(*refs):
        tiles_ref, twos_ref, ups_ref = refs[0], refs[1 : 1 + TEAM], refs[1 + TEAM : 1 + 2 * TEAM]
        weights_ref = refs[1 + 2 * TEAM : 4 + 2 * TEAM]
        outs_ref = refs[4 + 2 * TEAM : 4 + 3 * TEAM]
        grads_ref = refs[4 + 3 * TEAM : 4 + 4 * TEAM]
        inner_all, back_all, two_all, ups_all = refs[4 + 4 * TEAM : 8 + 4 * TEAM]
        (
            two_v, ups_v, wg_v, wu_v, wd_v, inner_v, back_v, out_v, grad_v, zero_v,
            w_sem, load_sem, keep_sem, tile_sem, dead_sem,
        ) = refs[8 + 4 * TEAM :]
        places, total = tile_places(tiles_ref, rows)
        used = (total + 1) // 2

        def loads(sources, packed, which):
            for k, (r, j, live, place) in enumerate(places):
                yield live, pltpu.make_async_copy(
                    sources[r].at[rows_of(j)], packed.at[rows_of(place)], load_sem.at[which, k]
                )

        weights = [
            pltpu.make_async_copy(src, dst, w_sem.at[j])
            for j, (src, dst) in enumerate(zip(weights_ref, (wg_v, wu_v, wd_v)))
        ]
        for live, copy in loads(twos_ref, two_v, 0):
            pl.when(live)(copy.start)
        for copy in weights:
            copy.start()
        for live, copy in loads(ups_ref, ups_v, 1):
            pl.when(live)(copy.start)
        zero_v[...] = jnp.zeros_like(zero_v)

        def dead(k, r, j):
            zeros = zero_v.at[:TILE]
            yield pltpu.make_async_copy(zeros, grads_ref[r].at[rows_of(j)], dead_sem.at[0, k])
            yield pltpu.make_async_copy(zeros, outs_ref[r].at[rows_of(j)], dead_sem.at[1, k])

        for k, (r, j, live, place) in enumerate(places):

            @pl.when(jnp.logical_not(live))
            def _(k=k, r=r, j=j):
                for copy in dead(k, r, j):
                    copy.start()

        def keeps(c, sources):
            for j, (src, dst) in enumerate(zip(sources, (two_all, ups_all, inner_all, back_all))):
                yield pltpu.make_async_copy(src, dst.at[rows_of(c, chunk)], keep_sem.at[j, c])

        zeros = (zero_v, zero_v, zero_v.at[:, :ff_cols], zero_v.at[:, : 2 * ff_cols])
        for c in range(TEAM // 2, chunks):

            @pl.when(c >= used)
            def _(c=c):
                for copy in keeps(c, zeros):
                    copy.start()

        @pl.when(total % 2 == 1)
        def _():
            two_v[rows_of(total)] = jnp.zeros((TILE, width), BF16)
            ups_v[rows_of(total)] = jnp.zeros((TILE, width), BF16)

        for live, copy in loads(twos_ref, two_v, 0):
            pl.when(live)(copy.wait)
        for copy in weights:
            copy.wait()
        for live, copy in loads(ups_ref, ups_v, 1):
            pl.when(live)(copy.wait)

        def tile_stores(r, j, slot, side):
            here = pl.ds(side * TILE, TILE)
            yield pltpu.make_async_copy(
                grad_v.at[slot, here], grads_ref[r].at[rows_of(j)], tile_sem.at[0, slot, side]
            )
            yield pltpu.make_async_copy(
                out_v.at[slot, here], outs_ref[r].at[rows_of(j)], tile_sem.at[1, slot, side]
            )

        def wait_tiles(c, slot):
            for side in range(2):

                @pl.when(2 * c + side < total)
                def _(side=side):
                    for copy in tile_stores(0, 0, slot, side):
                        copy.wait()

        def body(c, carry):
            slot = c % 2
            span = rows_of(c, chunk)

            @pl.when(c >= 2)
            def _():
                wait_tiles(c - 2, slot)
                for j, copy in enumerate(keeps(c - 2, zeros)):
                    if j >= 2:
                        copy.wait()

            gate_part = product(two_v[span], wg_v[...])
            up_part = product(two_v[span], wu_v[...])
            sig = jax.nn.sigmoid(gate_part)
            silu = gate_part * sig
            inner_v[slot] = (silu * up_part).astype(BF16)
            inner_grad = product_nt(ups_v[span], wd_v[...])
            back_v[slot, :, :ff_cols] = (inner_grad * up_part * (sig + silu * (1.0 - sig))).astype(BF16)
            back_v[slot, :, ff_cols:] = (inner_grad * silu).astype(BF16)
            for copy in keeps(c, (two_v.at[span], ups_v.at[span], inner_v.at[slot], back_v.at[slot])):
                copy.start()
            grad = product_nt(back_v[slot, :, :ff_cols], wg_v[...]) + product_nt(
                back_v[slot, :, ff_cols:], wu_v[...]
            )
            grad_v[slot] = grad.astype(BF16)
            out_v[slot] = product(inner_v[slot], wd_v[...]).astype(BF16)
            for k, (r, j, live, place) in enumerate(places):
                for side in range(2):

                    @pl.when(jnp.logical_and(live, place == 2 * c + side))
                    def _(r=r, j=j, side=side):
                        for copy in tile_stores(r, j, slot, side):
                            copy.start()

            return carry

        lax.fori_loop(0, used, body, 0)
        wait_tiles(used - 2, used % 2)
        wait_tiles(used - 1, (used - 1) % 2)
        for k, (r, j, live, place) in enumerate(places):

            @pl.when(jnp.logical_not(live))
            def _(k=k, r=r, j=j):
                for copy in dead(k, r, j):
                    copy.wait()

        for c in range(chunks):
            for j, copy in enumerate(keeps(c, zeros)):
                if j < 2:
                    copy.wait()
                else:
                    pl.when(c >= used - 2)(copy.wait)

    count = whole // TILE
    result = pl.pallas_call(
        kernel,
        out_shape=[struct((rows, width), BF16)] * (2 * TEAM)
        + [
            struct((whole, ff_cols), BF16),
            struct((whole, 2 * ff_cols), BF16),
            struct((whole, width), BF16),
            struct((whole, width), BF16),
        ],
        in_specs=[SMEM] + [ANY] * (3 + 2 * TEAM),
        out_specs=[ANY] * (2 * TEAM + 4),
        scratch_shapes=[
            pltpu.VMEM((whole, width), BF16),
            pltpu.VMEM((whole, width), BF16),
            pltpu.VMEM(weight_gate.shape, BF16),
            pltpu.VMEM(weight_up.shape, BF16),
            pltpu.VMEM(weight_down.shape, BF16),
            pltpu.VMEM((2, chunk, ff_cols), BF16),
            pltpu.VMEM((2, chunk, 2 * ff_cols), BF16),
            pltpu.VMEM((2, chunk, width), BF16),
            pltpu.VMEM((2, chunk, width), BF16),
            pltpu.VMEM((chunk, width), BF16),
            pltpu.SemaphoreType.DMA((3,)),
            pltpu.SemaphoreType.DMA((2, count)),
            pltpu.SemaphoreType.DMA((4, chunks)),
            pltpu.SemaphoreType.DMA((2, 2, 2)),
            pltpu.SemaphoreType.DMA((2, count)),
        ],
        compiler_params=pltpu.CompilerParams(vmem_limit_bytes=60 << 20),
        cost_estimate=pl.CostEstimate(flops=58 << 30, bytes_accessed=100 << 20, transcendentals=1 << 20),
    )(tiles, *twos, *upstreams, weight_gate, weight_up, weight_down)
    return result[:TEAM], result[TEAM : 2 * TEAM], result[2 * TEAM :]


def local(
    groups,
    tokens,
    lengths,
    cotangent,
    attention_gain,
    query_weight,
    key_matrix,
    value_matrix,
    head_gate_weight,
    output_weight,
    query_key_gain,
    feedforward_gain,
    gate_weight,
    up_weight,
    down_weight,
):
    t = member()
    everyone = groups * TEAM
    rows, width = tokens.shape
    rho = query_weight.shape[0]
    phi = down_weight.shape[0]
    ff = gate_weight.shape[1]
    pair_cols = query_key_gain.shape[1]
    size = pair_cols * everyone
    heads = query_weight.shape[1] // size
    mine = heads // TEAM
    q_cols = query_weight.shape[1] // TEAM
    k_cols = key_matrix.shape[1] // TEAM
    ff_cols = ff // TEAM

    def everyone_in_team(vector):
        return jnp.broadcast_to(vector.reshape(1, -1), (TEAM, vector.size))

    live_tiles = (lengths + (TILE - 1)) // TILE
    row = jnp.concatenate(
        [
            head_gate_weight.reshape(rho, TEAM, mine).transpose(1, 2, 0).reshape(TEAM, -1),
            everyone_in_team(attention_gain),
            everyone_in_team(feedforward_gain),
            everyone_in_team(query_key_gain),
            everyone_in_team(live_tiles.astype(BF16)),
        ],
        axis=1,
    )
    cols = q_cols + 2 * k_cols
    row = jnp.pad(row, ((0, 0), (0, cols - row.shape[1])))[:, None, :]
    attn = jnp.concatenate(
        [
            query_weight.reshape(rho, TEAM, q_cols),
            key_matrix.reshape(rho, TEAM, k_cols),
            value_matrix.reshape(rho, TEAM, k_cols),
        ],
        axis=2,
    ).transpose(1, 0, 2)
    attn = jnp.concatenate([attn, jnp.pad(row, ((0, 0), (0, 7), (0, 0)))], axis=1)
    attn = exchange(attn)
    head_lanes = mine * rho
    at_one, at_two, at_pair = head_lanes, head_lanes + rho, head_lanes + 2 * rho
    at_tiles = at_pair + 2 * pair_cols
    team_tiles = attn[:, rho, at_tiles].astype(jnp.int32)
    order = jnp.arange(TEAM, dtype=jnp.int32)
    tiles = jnp.sum(jnp.where((order[:, None] ^ t) == order[None, :], team_tiles[None, :], 0), axis=1)
    attn = line_gather(attn.reshape(TEAM * (rho + 8), cols)).reshape(everyone, rho + 8, cols)
    weight_attn = attn[:, :rho].reshape(width, cols)
    rows_small = attn[:, rho]
    weight_head = jnp.pad(
        rows_small[:, :head_lanes].reshape(everyone, mine, rho).transpose(1, 0, 2).reshape(mine, width),
        ((0, TILE - mine), (0, 0)),
    )
    gain_one = rows_small[:, at_one:at_two].reshape(1, width).astype(F32)
    gain_two = rows_small[:, at_two:at_pair].reshape(1, width).astype(F32)
    gain_pair = (
        rows_small[:, at_pair:at_tiles]
        .reshape(everyone, 2, pair_cols)
        .transpose(1, 0, 2)
        .reshape(2, size)
        .astype(F32)
    )
    weight_out = out_weight_in(output_weight, groups)

    def ff_split(w):
        return w.reshape(rho, groups, TEAM, phi).transpose(2, 0, 1, 3).reshape(TEAM, rho, ff_cols)

    feed_shard = jnp.concatenate([ff_split(gate_weight), ff_split(up_weight)], axis=2)
    feed_shard = exchange(feed_shard).reshape(TEAM * rho, -1)
    weight_gate = line_gather(feed_shard[:, :ff_cols])

    exponent = jnp.arange(size // 2, dtype=F32) * (-2.0 / size)
    frequency = jnp.power(ROPE_BASE, exponent)
    angles = jnp.arange(rows, dtype=F32)[:, None] * frequency[None, :]
    cosine = jnp.concatenate([jnp.cos(angles), jnp.cos(angles)], axis=1)
    sine = jnp.concatenate([-jnp.sin(angles), jnp.sin(angles)], axis=1)
    consts = (weight_attn, weight_head, weight_out, gain_one, gain_pair, cosine, sine)
    team_tokens = team_gather(tokens)
    live = lax.broadcasted_iota(jnp.int32, (rows, 1), 0) < lengths[0]
    live_rows = live.astype(F32)
    upstream = cotangent.astype(F32) * live_rows
    tick = mark([team_tokens[6]])
    later = lax.broadcasted_iota(jnp.int32, (rows, 1), 0) < lengths[0] + tick[0, 0]
    upstream_low = jnp.where(later, cotangent, jnp.zeros_like(cotangent))
    upstream_levels = TeamGather(upstream_low)
    parts, kept, tick = attend(tiles, team_tokens, consts, mine, mark([feed_shard, upstream_low]))
    normed, qkv, logit, gated = kept
    weight_up = line_gather(hold([feed_shard[:, ff_cols:]], tick)[0])
    parts = hold(parts, mark([upstream_levels.a1, upstream_levels.a2, upstream_levels.a4, weight_gate]))
    arrived = TeamSum(parts)
    arrived.first()
    weight_down = line_gather(hold([down_weight], arrived.low6)[0])
    team_upstream = upstream_levels.blocks()
    inputs = tokens.astype(F32)
    hidden_state = inputs + arrived.total()

    normed_two = rms(hidden_state, gain_two).astype(BF16)
    normed_two = hold([normed_two], mark(team_upstream + [weight_up]))[0]
    team_two = team_gather(normed_two)
    outs, grads, saved = feed(tiles, team_two, team_upstream, weight_gate, weight_up, weight_down)
    inner, feed_back, two_all, ups_all = saved
    arrived = TeamSum(grads)
    arrived.first()
    two_grad = arrived.total()
    inner, feed_back = hold([inner, feed_back], arrived.low6)
    down_part = product_tn(inner, ups_all).astype(BF16)
    gate_part = product_tn(two_all, feed_back[:, :ff_cols]).astype(BF16)
    up_part = product_tn(two_all, feed_back[:, ff_cols:]).astype(BF16)
    parts_made = mark([gate_part, up_part])
    down_grad = line_sum(down_part)
    gate_grad = line_sum(hold([gate_part], down_grad)[0])
    up_grad = line_sum(hold([up_part], gate_grad)[0])
    feed_done = up_grad
    hidden_grad = upstream + rms_pull(hidden_state, gain_two, two_grad)

    fed = TeamSum(outs)
    team_hidden = team_gather(hidden_grad.astype(BF16))
    two_scale = lax.rsqrt(jnp.mean(hidden_state * hidden_state, axis=-1, keepdims=True) + EPSILON)
    two_sum = jnp.sum(two_grad * hidden_state * two_scale, axis=0)
    first_hop = fed.first(mark(team_hidden + [parts_made]))
    parts, attn_sum, out_sum, one_sum, pair_sum = attend_back(
        tiles, team_hidden, consts, (normed, qkv, logit, gated), mine, mark(fed.sent + [down_grad])
    )
    parts = hold(parts, mark(first_hop + [gate_grad]))
    arrived = TeamSum(parts)
    arrived.first()
    normed_grad = arrived.total()
    layer_output = ((hidden_state + fed.total()) * live_rows).astype(BF16)
    tokens_grad = (hidden_grad + rms_pull(inputs, gain_one, normed_grad)).astype(BF16)
    head_part = attn_sum[cols : cols + mine]
    row = jnp.concatenate(
        [
            head_part.reshape(mine, everyone, rho).transpose(1, 0, 2).reshape(everyone, -1),
            (one_sum / gain_one[0]).reshape(everyone, rho),
            two_sum.reshape(everyone, rho),
            pair_sum.reshape(2, everyone, pair_cols).transpose(1, 0, 2).reshape(everyone, -1),
        ],
        axis=1,
    ).astype(BF16)
    row = jnp.pad(row, ((0, 0), (0, cols - row.shape[1])))[:, None, :]
    attn_part = attn_sum[:cols].astype(BF16).T
    packed = jnp.concatenate(
        [attn_part.reshape(everyone, rho, cols), jnp.pad(row, ((0, 0), (0, 7), (0, 0)))], axis=1
    )
    packed = packed.reshape(everyone * (rho + 8), cols)
    packed = line_sum(hold([packed], feed_done)[0])
    output_grad, packed = out_weight_back(out_sum.astype(BF16), groups, packed)
    packed = exchange(packed.reshape(TEAM, rho + 8, cols))
    feed_grad = jnp.concatenate([gate_grad, hold([up_grad], normed_grad)[0]], axis=1)
    feed_grad = exchange(feed_grad.reshape(TEAM, rho, 2 * ff_cols))

    def ff_join(w):
        return w.reshape(TEAM, rho, groups, phi).transpose(1, 2, 0, 3).reshape(rho, ff)

    gate_grad, up_grad = hold(
        [ff_join(feed_grad[:, :, :ff_cols]), ff_join(feed_grad[:, :, ff_cols:])], normed_grad
    )
    attn_grad = packed[:, :rho].transpose(1, 0, 2)
    rows_small = packed[:, rho].astype(F32)
    sums = jnp.sum(rows_small[:, head_lanes:], axis=0)
    head_gate_grad = rows_small[:, :head_lanes].reshape(heads, rho).T
    return (
        layer_output,
        tokens_grad,
        sums[:rho],
        attn_grad[:, :, :q_cols].reshape(rho, -1).astype(F32),
        attn_grad[:, :, q_cols : q_cols + k_cols].reshape(rho, -1).astype(F32),
        attn_grad[:, :, q_cols + k_cols :].reshape(rho, -1).astype(F32),
        head_gate_grad,
        output_grad.astype(F32),
        sums[2 * rho : 2 * rho + 2 * pair_cols].reshape(2, pair_cols),
        sums[rho : 2 * rho],
        gate_grad.astype(F32),
        up_grad.astype(F32),
        down_grad.astype(F32),
    )


def solution(mesh):
    groups = mesh.size // TEAM
    rows, vector, columns = P(ALL, None), P(ALL), P(None, ALL)

    def step(*args):
        return local(groups, *args)

    return jax.shard_map(
        step,
        mesh=mesh,
        in_specs=(
            rows, vector, rows, vector, rows, rows, rows, rows, rows, columns, vector, rows, rows, rows,
        ),
        out_specs=(
            rows, rows, vector, rows, rows, rows, rows, rows, columns, vector, rows, rows, rows,
        ),
        check_vma=False,
    )
```

```python
import jax
import jax.numpy as jnp
from jax import lax
from jax.experimental import pallas as pl
from jax.experimental.pallas import tpu as pltpu
from jax.sharding import PartitionSpec as P

EPSILON = 1e-06
ROPE_BASE = 1000000.0
TEAM = 8
ALL = ("dp", "fsdp")
F32 = jnp.float32
BF16 = jnp.bfloat16
TILE = 128
ANY = pl.BlockSpec(memory_space=pl.ANY)
VMEM = pl.BlockSpec(memory_space=pltpu.VMEM)
SMEM = pl.BlockSpec(memory_space=pltpu.SMEM)


def product(left, right):
    return jnp.dot(left, right, preferred_element_type=F32)


def product_nt(left, right):
    return lax.dot_general(left, right, (((1,), (1,)), ((), ())), preferred_element_type=F32)


def product_tn(left, right):
    return lax.dot_general(left, right, (((0,), (0,)), ((), ())), preferred_element_type=F32)


def world():
    return lax.axis_size(ALL)


def member():
    return lax.axis_index(ALL) % TEAM


def teams():
    return [[first + t for t in range(TEAM)] for first in range(0, world(), TEAM)]


def lines():
    return [list(range(t, world(), TEAM)) for t in range(TEAM)]


def permute(array, pairs):
    return lax.ppermute(
        array, ALL, [(team[a], team[b]) for team in teams() for a, b in pairs]
    )


def swap(array, bits):
    return permute(array, [(i, i ^ bits) for i in range(TEAM)])


def exchange(blocks):
    if lax.axis_size("fsdp") == TEAM:
        return lax.all_to_all(blocks, "fsdp", 0, 0, tiled=True)
    return lax.all_to_all(blocks, ALL, 0, 0, tiled=True, axis_index_groups=teams())


def line_gather(shard):
    if lax.axis_size("fsdp") == TEAM:
        return lax.all_gather(shard, "dp", axis=0, tiled=True)
    return lax.all_gather(shard, ALL, axis=0, tiled=True, axis_index_groups=lines())


def line_sum(array):
    if lax.axis_size("fsdp") == TEAM:
        return lax.psum_scatter(array, "dp", scatter_dimension=0, tiled=True)
    return lax.psum_scatter(array, ALL, scatter_dimension=0, tiled=True, axis_index_groups=lines())


class TeamGather:
    def __init__(self, own):
        self.own = own
        self.a1 = swap(own, 1)
        self.a2 = swap(own, 2)
        self.a4 = swap(own, 4)

    def blocks(self, tick=None):
        a2, a4 = self.a2, self.a4
        if tick is not None:
            a2, a4 = hold([a2, a4], tick)
        half = self.own.shape[0] // 2
        a6 = jnp.concatenate([swap(a4[:half], 2), swap(a2[half:], 4)], axis=0)
        return [self.own, self.a1, a2, swap(a2, 1), a4, swap(a4, 1), a6, swap(a6, 1)]


def team_gather(own):
    return TeamGather(own).blocks()


class TeamSum:
    def __init__(self, parts):
        half = parts[0].shape[0] // 2
        odd = {r: swap(parts[r + 1], 1) for r in (6, 2, 4, 0)}
        self.total6, self.total2, self.total4, self.total0 = (
            parts[r].astype(F32) + odd[r].astype(F32) for r in (6, 2, 4, 0)
        )
        self.half = half
        self.low6 = self.total6.astype(BF16)
        self.ready = [self.low6, self.total2[:half].astype(BF16), self.total4[half:].astype(BF16)]

    def first(self, tick=None):
        half = self.half
        low6, x_top, y_low = self.ready if tick is None else hold(self.ready, tick)
        self.u4 = swap(low6[:half], 2)
        self.u2 = swap(low6[half:], 4)
        self.x_top = swap(x_top, 2)
        self.y_low = swap(y_low, 4)
        self.sent = [low6, x_top, y_low]
        return [self.u4, self.u2, self.x_top, self.y_low]

    def total(self):
        half = self.half
        x_low = swap((self.total2[half:] + self.u2.astype(F32)).astype(BF16), 2).astype(F32)
        y_top = swap((self.total4[:half] + self.u4.astype(F32)).astype(BF16), 4).astype(F32)
        top = self.x_top.astype(F32) + y_top
        low = x_low + self.y_low.astype(F32)
        return self.total0 + jnp.concatenate([top, low], axis=0)


def out_weight_in(shard, groups):
    t = member()
    if groups < TEAM:
        gathered = line_gather(shard[None])
        per = TEAM // groups
        b, z = t % groups, t // per
        result = jnp.zeros_like(gathered)
        for j in range(groups):
            perm = [(i, per * ((i % groups + j) % groups) + i // groups) for i in range(TEAM)]
            piece = lax.dynamic_index_in_dim(gathered, (b + j) % groups, 0, keepdims=True)
            piece = permute(piece, perm)
            result = lax.dynamic_update_slice_in_dim(result, piece, (z - j + groups) % groups, 0)
        return result.reshape(-1, shard.shape[1])
    full = lax.all_gather(shard, ALL, axis=0, tiled=True)
    rows = full.shape[0] // TEAM
    return lax.dynamic_slice_in_dim(full, t * rows, rows, 0)


def out_weight_back(grad, groups, done):
    t = member()
    if groups < TEAM:
        per = TEAM // groups
        b, z = t % groups, t // per
        grad = grad.reshape(groups, -1, grad.shape[1])
        placed = jnp.zeros_like(grad)
        for j in range(groups):
            perm = [(per * ((i % groups + j) % groups) + i // groups, i) for i in range(TEAM)]
            piece = lax.dynamic_index_in_dim(grad, (z - j + groups) % groups, 0, keepdims=True)
            piece = permute(piece, perm)
            placed = lax.dynamic_update_slice_in_dim(placed, piece, (b + j) % groups, 0)
        placed = hold([placed], done)[0]
        return line_sum(placed)[0], hold([done], placed)[0]
    whole = jnp.zeros((grad.shape[0] * TEAM, grad.shape[1]), grad.dtype)
    whole = lax.dynamic_update_slice_in_dim(whole, grad, t * grad.shape[0], 0)
    return lax.psum_scatter(whole, ALL, scatter_dimension=0, tiled=True), done


def rms_pull(value, gain, grad):
    scale = lax.rsqrt(jnp.mean(value * value, axis=-1, keepdims=True) + EPSILON)
    weighted = grad * gain
    mean = jnp.mean(weighted * value, axis=-1, keepdims=True)
    return scale * weighted - scale * scale * scale * value * mean


def rms(value, gain):
    return value * lax.rsqrt(jnp.mean(value * value, axis=-1, keepdims=True) + EPSILON) * gain


def struct(shape, dtype):
    return jax.ShapeDtypeStruct(shape, dtype)


def hold(arrays, tick):
    def kernel(*refs):
        del refs

    count = len(arrays)
    return pl.pallas_call(
        kernel,
        out_shape=[struct(a.shape, a.dtype) for a in arrays],
        in_specs=[ANY] * count + [ANY],
        out_specs=[ANY] * count,
        input_output_aliases={i: i for i in range(count)},
    )(*arrays, tick)


def mark(arrays):
    def kernel(*refs):
        refs[-1][...] = jnp.zeros_like(refs[-1])

    return pl.pallas_call(
        kernel,
        out_shape=struct((8, 128), jnp.int32),
        in_specs=[ANY] * len(arrays),
        out_specs=VMEM,
    )(*arrays)


def for_tiles(tiles, most, body):
    for m in range(1, most + 1):

        @pl.when(tiles == m)
        def _(m=m):
            body(m * TILE)


def turned(u, cosine, sine):
    return u * cosine + pltpu.roll(u, u.shape[-1] // 2, 1) * sine


def head_norm(u):
    return lax.rsqrt(jnp.mean(u * u, axis=-1, keepdims=True) + EPSILON)


def head_back(grad, raw, gain, cosine, sine):
    e = turned(grad, cosine, -sine)
    scale = head_norm(raw)
    weighted = e * gain
    mean = jnp.mean(weighted * raw, axis=-1, keepdims=True)
    back = scale * weighted - scale * scale * scale * raw * mean
    return back, jnp.sum(e * raw * scale, axis=0, keepdims=True)


def weights_of(query, key, factor):
    scores = product_nt(query, key) * factor
    n = scores.shape[0]
    causal = lax.broadcasted_iota(jnp.int32, (n, n), 1) <= lax.broadcasted_iota(jnp.int32, (n, n), 0)
    scores = jnp.where(causal, scores, -jnp.inf)
    terms = jnp.exp(scores - jnp.max(scores, axis=-1, keepdims=True))
    return terms * (1.0 / jnp.sum(terms, axis=-1, keepdims=True))


def rows_of(tile, size=TILE):
    return pl.ds(pl.multiple_of(tile * size, size), size)


def each_block(r, body):
    for k in range(TEAM):
        pl.when(r == k)(lambda k=k: body(k))


def attend(tiles, tokens, consts, mine, after):
    weight_attn, weight_head, weight_out, gain, gains, cosine, sine = consts
    rows, width = tokens[0].shape
    size = gains.shape[1]
    q_cols = mine * size
    cols = weight_attn.shape[1]
    factor = size ** (-0.5)

    def kernel(*refs):
        tiles_ref, toks = refs[0], refs[1 : 1 + TEAM]
        wa, wh, wo, gain_ref, gains_ref, cos_ref, sin_ref, _ = refs[1 + TEAM : 9 + TEAM]
        parts = refs[9 + TEAM : 9 + 2 * TEAM]
        normed_all, qkv_all, logit_all, gated_all, tick = refs[9 + 2 * TEAM : 14 + 2 * TEAM]
        (
            tok_v, wa_v, wh_v, wo_v, part_v, normed_v, qkv_v, logit_v, gated_v, w_sem, in_sem, out_sem,
        ) = refs[14 + 2 * TEAM :]
        tick[...] = jnp.zeros_like(tick)

        def load(k, slot):
            return pltpu.make_async_copy(toks[k], tok_v.at[slot], in_sem.at[slot])

        def store(r, slot, j, k=0):
            src = (part_v, normed_v, qkv_v, logit_v, gated_v)[j].at[slot]
            dst = parts[k] if j == 0 else (normed_all, qkv_all, logit_all, gated_all)[j - 1].at[rows_of(r, rows)]
            return pltpu.make_async_copy(src, dst, out_sem.at[j, slot])

        load(0, 0).start()
        weights = [
            pltpu.make_async_copy(src, dst, w_sem.at[j])
            for j, (src, dst) in enumerate(((wa, wa_v), (wh, wh_v), (wo, wo_v)))
        ]
        for copy in weights:
            copy.start()
        for copy in weights:
            copy.wait()

        def step(r, carry):
            slot = r % 2

            @pl.when(r + 1 < TEAM)
            def _():
                each_block(r + 1, lambda k: load(k, 1 - slot).start())

            load(0, slot).wait()

            @pl.when(r >= 2)
            def _():
                for j in range(5):
                    store(r - 2, slot, j).wait()

            def body(n):
                value = tok_v[slot, :n].astype(F32)
                normed = rms(value, gain_ref[...]).astype(BF16)
                normed_v[slot, :n] = normed
                qkv = product(normed, wa_v[...])
                qkv_v[slot, :n] = qkv
                logit = product_nt(normed, wh_v[...])
                logit_v[slot, :n] = logit
                cos, sin = cos_ref[:n], sin_ref[:n]
                key = qkv[:, q_cols : q_cols + size]
                key = turned(key * head_norm(key) * gains_ref[1:2], cos, sin).astype(BF16)
                values = qkv[:, q_cols + size :].astype(BF16)
                for h in range(mine):
                    query = qkv[:, h * size : (h + 1) * size]
                    query = turned(query * head_norm(query) * gains_ref[0:1], cos, sin).astype(BF16)
                    attention = weights_of(query, key, factor)
                    mixture = product(attention.astype(BF16), values)
                    gate = jax.nn.sigmoid(logit[:, h : h + 1])
                    gated_v[slot, :n, h * size : (h + 1) * size] = (mixture * gate).astype(BF16)
                part_v[slot, :n] = product(gated_v[slot, :n], wo_v[...]).astype(BF16)
                if n < rows:
                    part_v[slot, n:] = jnp.zeros((rows - n, width), BF16)
                    normed_v[slot, n:] = jnp.zeros((rows - n, width), BF16)
                    gated_v[slot, n:] = jnp.zeros((rows - n, q_cols), BF16)

            for_tiles(tiles_ref[r], rows // TILE, body)
            each_block(r, lambda k: store(r, slot, 0, k).start())
            for j in range(1, 5):
                store(r, slot, j).start()
            return carry

        lax.fori_loop(0, TEAM, step, 0)
        for r in (TEAM - 2, TEAM - 1):
            for j in range(5):
                store(r, r % 2, j).wait()

    whole = TEAM * rows
    result = pl.pallas_call(
        kernel,
        out_shape=[struct((rows, width), BF16)] * TEAM
        + [
            struct((whole, width), BF16),
            struct((whole, cols), F32),
            struct((whole, TILE), F32),
            struct((whole, q_cols), BF16),
            struct((8, 128), jnp.int32),
        ],
        in_specs=[SMEM] + [ANY] * (TEAM + 3) + [VMEM] * 4 + [ANY],
        out_specs=[ANY] * (TEAM + 4) + [VMEM],
        scratch_shapes=[
            pltpu.VMEM((2, rows, width), BF16),
            pltpu.VMEM(weight_attn.shape, BF16),
            pltpu.VMEM(weight_head.shape, BF16),
            pltpu.VMEM(weight_out.shape, BF16),
            pltpu.VMEM((2, rows, width), BF16),
            pltpu.VMEM((2, rows, width), BF16),
            pltpu.VMEM((2, rows, cols), F32),
            pltpu.VMEM((2, rows, TILE), F32),
            pltpu.VMEM((2, rows, q_cols), BF16),
            pltpu.SemaphoreType.DMA((3,)),
            pltpu.SemaphoreType.DMA((2,)),
            pltpu.SemaphoreType.DMA((5, 2)),
        ],
        compiler_params=pltpu.CompilerParams(vmem_limit_bytes=48 << 20),
        cost_estimate=pl.CostEstimate(flops=30 << 30, bytes_accessed=60 << 20, transcendentals=1 << 20),
    )(tiles, *tokens, weight_attn, weight_head, weight_out, gain, gains, cosine, sine, after)
    return result[:TEAM], result[TEAM : TEAM + 4], result[TEAM + 4]


def attend_back(tiles, hidden, consts, saved, mine, after):
    weight_attn, weight_head, weight_out, gain, gains, cosine, sine = consts
    rows, width = hidden[0].shape
    size = gains.shape[1]
    q_cols = mine * size
    cols = weight_attn.shape[1]
    factor = size ** (-0.5)

    def kernel(*refs):
        tiles_ref, hids = refs[0], refs[1 : 1 + TEAM]
        wa, wh, wo, normed_all, qkv_all, logit_all, gated_all = refs[1 + TEAM : 8 + TEAM]
        gains_ref, cos_ref, sin_ref, _ = refs[8 + TEAM : 12 + TEAM]
        parts = refs[12 + TEAM : 12 + 2 * TEAM]
        attn_part, head_sum, out_part, gain_sum, gains_sum = refs[12 + 2 * TEAM : 17 + 2 * TEAM]
        (
            hid_v, wa_v, wh_v, wo_v, normed_v, qkv_v, logit_v, gated_v, part_v, back_v, attn_sum, out_sum,
            w_sem, in_sem, out_sem,
        ) = refs[17 + 2 * TEAM :]

        def loads(r, slot, k):
            yield pltpu.make_async_copy(hids[k], hid_v.at[slot], in_sem.at[0, slot])
            here = rows_of(r, rows)
            for j, (src, dst) in enumerate(
                ((qkv_all, qkv_v), (logit_all, logit_v), (normed_all, normed_v), (gated_all, gated_v))
            ):
                yield pltpu.make_async_copy(src.at[here], dst.at[slot], in_sem.at[1 + j, slot])

        def start_loads(r, slot):
            def body(k):
                for copy in loads(r, slot, k):
                    copy.start()

            each_block(r, body)

        def store(slot, k=0):
            return pltpu.make_async_copy(part_v.at[slot], parts[k], out_sem.at[slot])

        for copy in loads(0, 0, 0):
            copy.start()
        weights = [
            pltpu.make_async_copy(src, dst, w_sem.at[j])
            for j, (src, dst) in enumerate(((wo, wo_v), (wa, wa_v), (wh, wh_v)))
        ]
        for copy in weights:
            copy.start()
        for ref in (attn_sum, out_sum, gain_sum, gains_sum):
            ref[...] = jnp.zeros_like(ref)
        for copy in weights:
            copy.wait()

        def step(r, carry):
            slot = r % 2

            @pl.when(r + 1 < TEAM)
            def _():
                start_loads(r + 1, 1 - slot)

            for copy in loads(r, slot, 0):
                copy.wait()

            @pl.when(r >= 2)
            def _():
                store(slot).wait()

            def body(n):
                hidden_low = hid_v[slot, :n]
                normed = normed_v[slot, :n]
                out_sum[...] += product_tn(gated_v[slot, :n], hidden_low)
                gated_grad = product_nt(hidden_low, wo_v[...])
                cos, sin = cos_ref[:n], sin_ref[:n]
                key_raw = qkv_v[slot, :n, q_cols : q_cols + size]
                key = turned(key_raw * head_norm(key_raw) * gains_ref[1:2], cos, sin).astype(BF16)
                values = qkv_v[slot, :n, q_cols + size :].astype(BF16)
                lane = lax.broadcasted_iota(jnp.int32, (n, TILE), 1)
                logit_back = jnp.zeros((n, TILE), F32)
                values_back = jnp.zeros((n, size), F32)
                key_grad = jnp.zeros((n, size), F32)
                query_sum = jnp.zeros((1, size), F32)
                for h in range(mine):
                    span = slice(h * size, (h + 1) * size)
                    query_raw = qkv_v[slot, :n, span]
                    query = turned(query_raw * head_norm(query_raw) * gains_ref[0:1], cos, sin).astype(BF16)
                    attention = weights_of(query, key, factor)
                    attention_low = attention.astype(BF16)
                    mixture = product(attention_low, values)
                    gate = jax.nn.sigmoid(logit_v[slot, :n, h : h + 1])
                    head_grad = gated_grad[:, span]
                    mixture_back = (head_grad * gate).astype(BF16)
                    one = jnp.sum(head_grad * mixture, axis=-1, keepdims=True) * gate * (1.0 - gate)
                    logit_back = jnp.where(lane == h, one, logit_back)
                    values_back += product_tn(attention_low, mixture_back)
                    attention_grad = product_nt(mixture_back, values)
                    scores_back = (
                        attention
                        * (attention_grad - jnp.sum(attention_grad * attention, axis=-1, keepdims=True))
                    ).astype(BF16)
                    query_grad = product(scores_back, key) * factor
                    key_grad += product_tn(scores_back, query)
                    back, total = head_back(query_grad, query_raw, gains_ref[0:1], cos, sin)
                    back_v[:n, span] = back.astype(BF16)
                    query_sum += total
                back, key_sum = head_back(key_grad * factor, key_raw, gains_ref[1:2], cos, sin)
                back_v[:n, q_cols : q_cols + size] = back.astype(BF16)
                back_v[:n, q_cols + size : cols] = values_back.astype(BF16)
                logit_back = logit_back.astype(BF16)
                back_v[:n, cols:] = logit_back
                gains_sum[0:1] += query_sum
                gains_sum[1:2] += key_sum
                part = product_nt(back_v[:n, :cols], wa_v[...]) + product(logit_back, wh_v[...])
                part_v[slot, :n] = part.astype(BF16)
                gain_sum[0:1] += jnp.sum(part * normed.astype(F32), axis=0, keepdims=True)
                attn_sum[...] += product_tn(back_v[:n], normed)
                if n < rows:
                    part_v[slot, n:] = jnp.zeros((rows - n, width), BF16)

            for_tiles(tiles_ref[r], rows // TILE, body)
            each_block(r, lambda k: store(slot, k).start())
            return carry

        lax.fori_loop(0, TEAM, step, 0)
        attn_part[...] = attn_sum[:cols].T.astype(BF16)
        head_sum[...] = attn_sum[cols : cols + 8]
        out_part[...] = out_sum[...].astype(BF16)
        store(0).wait()
        store(1).wait()

    result = pl.pallas_call(
        kernel,
        out_shape=[struct((rows, width), BF16)] * TEAM
        + [
            struct((width, cols), BF16),
            struct((8, width), F32),
            struct((q_cols, width), BF16),
            struct((8, width), F32),
            struct((8, size), F32),
        ],
        in_specs=[SMEM] + [ANY] * (TEAM + 7) + [VMEM] * 3 + [ANY],
        out_specs=[ANY] * TEAM + [VMEM] * 5,
        scratch_shapes=[
            pltpu.VMEM((2, rows, width), BF16),
            pltpu.VMEM(weight_attn.shape, BF16),
            pltpu.VMEM(weight_head.shape, BF16),
            pltpu.VMEM(weight_out.shape, BF16),
            pltpu.VMEM((2, rows, width), BF16),
            pltpu.VMEM((2, rows, cols), F32),
            pltpu.VMEM((2, rows, TILE), F32),
            pltpu.VMEM((2, rows, q_cols), BF16),
            pltpu.VMEM((2, rows, width), BF16),
            pltpu.VMEM((rows, cols + TILE), BF16),
            pltpu.VMEM((cols + TILE, width), F32),
            pltpu.VMEM((q_cols, width), F32),
            pltpu.SemaphoreType.DMA((3,)),
            pltpu.SemaphoreType.DMA((5, 2)),
            pltpu.SemaphoreType.DMA((2,)),
        ],
        compiler_params=pltpu.CompilerParams(vmem_limit_bytes=56 << 20),
        cost_estimate=pl.CostEstimate(flops=45 << 30, bytes_accessed=70 << 20, transcendentals=1 << 20),
    )(tiles, *hidden, weight_attn, weight_head, weight_out, *saved, gains, cosine, sine, after)
    return result[:TEAM], *result[TEAM : TEAM + 3], result[TEAM + 3][0], result[TEAM + 4][:2]


def tile_places(tiles_ref, rows):
    places, total = [], 0
    for r in range(TEAM):
        count = tiles_ref[r]
        for j in range(rows // TILE):
            places.append((r, j, j < count, total + j))
        total = total + count
    return places, total


def feed(tiles, twos, upstreams, weight_gate, weight_up, weight_down):
    rows, width = twos[0].shape
    ff_cols = weight_down.shape[0]
    whole = TEAM * rows
    chunk = 2 * TILE
    chunks = whole // chunk

    def kernel(*refs):
        tiles_ref, twos_ref, ups_ref = refs[0], refs[1 : 1 + TEAM], refs[1 + TEAM : 1 + 2 * TEAM]
        weights_ref = refs[1 + 2 * TEAM : 4 + 2 * TEAM]
        outs_ref = refs[4 + 2 * TEAM : 4 + 3 * TEAM]
        grads_ref = refs[4 + 3 * TEAM : 4 + 4 * TEAM]
        inner_all, back_all, two_all, ups_all = refs[4 + 4 * TEAM : 8 + 4 * TEAM]
        (
            two_v, ups_v, wg_v, wu_v, wd_v, inner_v, back_v, out_v, grad_v, zero_v,
            w_sem, load_sem, keep_sem, tile_sem, dead_sem,
        ) = refs[8 + 4 * TEAM :]
        places, total = tile_places(tiles_ref, rows)
        used = (total + 1) // 2

        def loads(sources, packed, which):
            for k, (r, j, live, place) in enumerate(places):
                yield live, pltpu.make_async_copy(
                    sources[r].at[rows_of(j)], packed.at[rows_of(place)], load_sem.at[which, k]
                )

        weights = [
            pltpu.make_async_copy(src, dst, w_sem.at[j])
            for j, (src, dst) in enumerate(zip(weights_ref, (wg_v, wu_v, wd_v)))
        ]
        for live, copy in loads(twos_ref, two_v, 0):
            pl.when(live)(copy.start)
        for copy in weights:
            copy.start()
        for live, copy in loads(ups_ref, ups_v, 1):
            pl.when(live)(copy.start)
        zero_v[...] = jnp.zeros_like(zero_v)

        def dead(k, r, j):
            zeros = zero_v.at[:TILE]
            yield pltpu.make_async_copy(zeros, grads_ref[r].at[rows_of(j)], dead_sem.at[0, k])
            yield pltpu.make_async_copy(zeros, outs_ref[r].at[rows_of(j)], dead_sem.at[1, k])

        for k, (r, j, live, place) in enumerate(places):

            @pl.when(jnp.logical_not(live))
            def _(k=k, r=r, j=j):
                for copy in dead(k, r, j):
                    copy.start()

        def keeps(c, sources):
            for j, (src, dst) in enumerate(zip(sources, (two_all, ups_all, inner_all, back_all))):
                yield pltpu.make_async_copy(src, dst.at[rows_of(c, chunk)], keep_sem.at[j, c])

        zeros = (zero_v, zero_v, zero_v.at[:, :ff_cols], zero_v.at[:, : 2 * ff_cols])
        for c in range(TEAM // 2, chunks):

            @pl.when(c >= used)
            def _(c=c):
                for copy in keeps(c, zeros):
                    copy.start()

        @pl.when(total % 2 == 1)
        def _():
            two_v[rows_of(total)] = jnp.zeros((TILE, width), BF16)
            ups_v[rows_of(total)] = jnp.zeros((TILE, width), BF16)

        for live, copy in loads(twos_ref, two_v, 0):
            pl.when(live)(copy.wait)
        for copy in weights:
            copy.wait()
        for live, copy in loads(ups_ref, ups_v, 1):
            pl.when(live)(copy.wait)

        def tile_stores(r, j, slot, side):
            here = pl.ds(side * TILE, TILE)
            yield pltpu.make_async_copy(
                grad_v.at[slot, here], grads_ref[r].at[rows_of(j)], tile_sem.at[0, slot, side]
            )
            yield pltpu.make_async_copy(
                out_v.at[slot, here], outs_ref[r].at[rows_of(j)], tile_sem.at[1, slot, side]
            )

        def wait_tiles(c, slot):
            for side in range(2):

                @pl.when(2 * c + side < total)
                def _(side=side):
                    for copy in tile_stores(0, 0, slot, side):
                        copy.wait()

        def body(c, carry):
            slot = c % 2
            span = rows_of(c, chunk)

            @pl.when(c >= 2)
            def _():
                wait_tiles(c - 2, slot)
                for j, copy in enumerate(keeps(c - 2, zeros)):
                    if j >= 2:
                        copy.wait()

            gate_part = product(two_v[span], wg_v[...])
            up_part = product(two_v[span], wu_v[...])
            sig = jax.nn.sigmoid(gate_part)
            silu = gate_part * sig
            inner_v[slot] = (silu * up_part).astype(BF16)
            inner_grad = product_nt(ups_v[span], wd_v[...])
            back_v[slot, :, :ff_cols] = (inner_grad * up_part * (sig + silu * (1.0 - sig))).astype(BF16)
            back_v[slot, :, ff_cols:] = (inner_grad * silu).astype(BF16)
            for copy in keeps(c, (two_v.at[span], ups_v.at[span], inner_v.at[slot], back_v.at[slot])):
                copy.start()
            grad = product_nt(back_v[slot, :, :ff_cols], wg_v[...]) + product_nt(
                back_v[slot, :, ff_cols:], wu_v[...]
            )
            grad_v[slot] = grad.astype(BF16)
            out_v[slot] = product(inner_v[slot], wd_v[...]).astype(BF16)
            for k, (r, j, live, place) in enumerate(places):
                for side in range(2):

                    @pl.when(jnp.logical_and(live, place == 2 * c + side))
                    def _(r=r, j=j, side=side):
                        for copy in tile_stores(r, j, slot, side):
                            copy.start()

            return carry

        lax.fori_loop(0, used, body, 0)
        wait_tiles(used - 2, used % 2)
        wait_tiles(used - 1, (used - 1) % 2)
        for k, (r, j, live, place) in enumerate(places):

            @pl.when(jnp.logical_not(live))
            def _(k=k, r=r, j=j):
                for copy in dead(k, r, j):
                    copy.wait()

        for c in range(chunks):
            for j, copy in enumerate(keeps(c, zeros)):
                if j < 2:
                    copy.wait()
                else:
                    pl.when(c >= used - 2)(copy.wait)

    count = whole // TILE
    result = pl.pallas_call(
        kernel,
        out_shape=[struct((rows, width), BF16)] * (2 * TEAM)
        + [
            struct((whole, ff_cols), BF16),
            struct((whole, 2 * ff_cols), BF16),
            struct((whole, width), BF16),
            struct((whole, width), BF16),
        ],
        in_specs=[SMEM] + [ANY] * (3 + 2 * TEAM),
        out_specs=[ANY] * (2 * TEAM + 4),
        scratch_shapes=[
            pltpu.VMEM((whole, width), BF16),
            pltpu.VMEM((whole, width), BF16),
            pltpu.VMEM(weight_gate.shape, BF16),
            pltpu.VMEM(weight_up.shape, BF16),
            pltpu.VMEM(weight_down.shape, BF16),
            pltpu.VMEM((2, chunk, ff_cols), BF16),
            pltpu.VMEM((2, chunk, 2 * ff_cols), BF16),
            pltpu.VMEM((2, chunk, width), BF16),
            pltpu.VMEM((2, chunk, width), BF16),
            pltpu.VMEM((chunk, width), BF16),
            pltpu.SemaphoreType.DMA((3,)),
            pltpu.SemaphoreType.DMA((2, count)),
            pltpu.SemaphoreType.DMA((4, chunks)),
            pltpu.SemaphoreType.DMA((2, 2, 2)),
            pltpu.SemaphoreType.DMA((2, count)),
        ],
        compiler_params=pltpu.CompilerParams(vmem_limit_bytes=60 << 20),
        cost_estimate=pl.CostEstimate(flops=58 << 30, bytes_accessed=100 << 20, transcendentals=1 << 20),
    )(tiles, *twos, *upstreams, weight_gate, weight_up, weight_down)
    return result[:TEAM], result[TEAM : 2 * TEAM], result[2 * TEAM :]


def local(
    groups,
    tokens,
    lengths,
    cotangent,
    attention_gain,
    query_weight,
    key_matrix,
    value_matrix,
    head_gate_weight,
    output_weight,
    query_key_gain,
    feedforward_gain,
    gate_weight,
    up_weight,
    down_weight,
):
    t = member()
    everyone = groups * TEAM
    rows, width = tokens.shape
    rho = query_weight.shape[0]
    phi = down_weight.shape[0]
    ff = gate_weight.shape[1]
    pair_cols = query_key_gain.shape[1]
    size = pair_cols * everyone
    heads = query_weight.shape[1] // size
    mine = heads // TEAM
    q_cols = query_weight.shape[1] // TEAM
    k_cols = key_matrix.shape[1] // TEAM
    ff_cols = ff // TEAM

    def everyone_in_team(vector):
        return jnp.broadcast_to(vector.reshape(1, -1), (TEAM, vector.size))

    live_tiles = (lengths + (TILE - 1)) // TILE
    row = jnp.concatenate(
        [
            head_gate_weight.reshape(rho, TEAM, mine).transpose(1, 2, 0).reshape(TEAM, -1),
            everyone_in_team(attention_gain),
            everyone_in_team(feedforward_gain),
            everyone_in_team(query_key_gain),
            everyone_in_team(live_tiles.astype(BF16)),
        ],
        axis=1,
    )
    cols = q_cols + 2 * k_cols
    row = jnp.pad(row, ((0, 0), (0, cols - row.shape[1])))[:, None, :]
    attn = jnp.concatenate(
        [
            query_weight.reshape(rho, TEAM, q_cols),
            key_matrix.reshape(rho, TEAM, k_cols),
            value_matrix.reshape(rho, TEAM, k_cols),
        ],
        axis=2,
    ).transpose(1, 0, 2)
    attn = jnp.concatenate([attn, jnp.pad(row, ((0, 0), (0, 7), (0, 0)))], axis=1)
    attn = exchange(attn)
    head_lanes = mine * rho
    at_one, at_two, at_pair = head_lanes, head_lanes + rho, head_lanes + 2 * rho
    at_tiles = at_pair + 2 * pair_cols
    team_tiles = attn[:, rho, at_tiles].astype(jnp.int32)
    order = jnp.arange(TEAM, dtype=jnp.int32)
    tiles = jnp.sum(jnp.where((order[:, None] ^ t) == order[None, :], team_tiles[None, :], 0), axis=1)
    attn = line_gather(attn.reshape(TEAM * (rho + 8), cols)).reshape(everyone, rho + 8, cols)
    weight_attn = attn[:, :rho].reshape(width, cols)
    rows_small = attn[:, rho]
    weight_head = jnp.pad(
        rows_small[:, :head_lanes].reshape(everyone, mine, rho).transpose(1, 0, 2).reshape(mine, width),
        ((0, TILE - mine), (0, 0)),
    )
    gain_one = rows_small[:, at_one:at_two].reshape(1, width).astype(F32)
    gain_two = rows_small[:, at_two:at_pair].reshape(1, width).astype(F32)
    gain_pair = (
        rows_small[:, at_pair:at_tiles]
        .reshape(everyone, 2, pair_cols)
        .transpose(1, 0, 2)
        .reshape(2, size)
        .astype(F32)
    )
    weight_out = out_weight_in(output_weight, groups)

    def ff_split(w):
        return w.reshape(rho, groups, TEAM, phi).transpose(2, 0, 1, 3).reshape(TEAM, rho, ff_cols)

    feed_shard = jnp.concatenate([ff_split(gate_weight), ff_split(up_weight)], axis=2)
    feed_shard = exchange(hold([feed_shard], weight_out)[0]).reshape(TEAM * rho, -1)
    weight_gate = line_gather(feed_shard[:, :ff_cols])

    exponent = jnp.arange(size // 2, dtype=F32) * (-2.0 / size)
    frequency = jnp.power(ROPE_BASE, exponent)
    angles = jnp.arange(rows, dtype=F32)[:, None] * frequency[None, :]
    cosine = jnp.concatenate([jnp.cos(angles), jnp.cos(angles)], axis=1)
    sine = jnp.concatenate([-jnp.sin(angles), jnp.sin(angles)], axis=1)
    consts = (weight_attn, weight_head, weight_out, gain_one, gain_pair, cosine, sine)
    team_tokens = team_gather(tokens)
    live = lax.broadcasted_iota(jnp.int32, (rows, 1), 0) < lengths[0]
    live_rows = live.astype(F32)
    upstream = cotangent.astype(F32) * live_rows
    tick = mark([team_tokens[6]])
    later = lax.broadcasted_iota(jnp.int32, (rows, 1), 0) < lengths[0] + tick[0, 0]
    upstream_low = jnp.where(later, cotangent, jnp.zeros_like(cotangent))
    upstream_levels = TeamGather(upstream_low)
    parts, kept, tick = attend(tiles, team_tokens, consts, mine, mark([feed_shard, upstream_low]))
    normed, qkv, logit, gated = kept
    weight_up = line_gather(hold([feed_shard[:, ff_cols:]], tick)[0])
    parts = hold(parts, mark([upstream_levels.a1, upstream_levels.a2, upstream_levels.a4, weight_gate]))
    arrived = TeamSum(parts)
    arrived.first()
    weight_down = line_gather(hold([down_weight], arrived.low6)[0])
    team_upstream = upstream_levels.blocks()
    inputs = tokens.astype(F32)
    hidden_state = inputs + arrived.total()

    normed_two = rms(hidden_state, gain_two).astype(BF16)
    normed_two = hold([normed_two], mark(team_upstream))[0]
    team_two = TeamGather(normed_two).blocks(mark([weight_up]))
    outs, grads, saved = feed(tiles, team_two, team_upstream, weight_gate, weight_up, weight_down)
    inner, feed_back, two_all, ups_all = saved
    arrived = TeamSum(grads)
    arrived.first()
    two_grad = arrived.total()
    inner, feed_back = hold([inner, feed_back], mark(arrived.ready))
    down_part = product_tn(inner, ups_all).astype(BF16)
    gate_part = product_tn(two_all, feed_back[:, :ff_cols]).astype(BF16)
    up_part = product_tn(two_all, feed_back[:, ff_cols:]).astype(BF16)
    parts_made = mark([gate_part, up_part])
    down_grad = line_sum(down_part)
    gate_grad = line_sum(hold([gate_part], down_grad)[0])
    up_grad = line_sum(hold([up_part], gate_grad)[0])
    feed_done = up_grad
    hidden_grad = upstream + rms_pull(hidden_state, gain_two, two_grad)

    fed = TeamSum(outs)
    team_hidden = TeamGather(hidden_grad.astype(BF16)).blocks(mark(fed.ready + [gate_part]))
    two_scale = lax.rsqrt(jnp.mean(hidden_state * hidden_state, axis=-1, keepdims=True) + EPSILON)
    two_sum = jnp.sum(two_grad * hidden_state * two_scale, axis=0)
    first_hop = fed.first(mark(team_hidden + [parts_made]))
    parts, attn_part, head_sum, out_part, one_sum, pair_sum = attend_back(
        tiles, team_hidden, consts, (normed, qkv, logit, gated), mine, mark(fed.sent + [down_grad])
    )
    row = jnp.concatenate(
        [
            head_sum[:mine].reshape(mine, everyone, rho).transpose(1, 0, 2).reshape(everyone, -1),
            (one_sum / gain_one[0]).reshape(everyone, rho),
            two_sum.reshape(everyone, rho),
            pair_sum.reshape(2, everyone, pair_cols).transpose(1, 0, 2).reshape(everyone, -1),
        ],
        axis=1,
    ).astype(BF16)
    row = jnp.pad(row, ((0, 0), (0, cols - row.shape[1])))[:, None, :]
    packed = jnp.concatenate(
        [attn_part.reshape(everyone, rho, cols), jnp.pad(row, ((0, 0), (0, 7), (0, 0)))], axis=1
    )
    packed = hold([packed.reshape(everyone * (rho + 8), cols)], feed_done)[0]
    parts = hold(parts, mark(first_hop + [gate_grad]))
    arrived = TeamSum(parts)
    arrived.first(packed)
    packed = line_sum(packed)
    normed_grad = arrived.total()
    layer_output = ((hidden_state + fed.total()) * live_rows).astype(BF16)
    tokens_grad = (hidden_grad + rms_pull(inputs, gain_one, normed_grad)).astype(BF16)
    output_grad, packed = out_weight_back(hold([out_part], arrived.u4)[0], groups, packed)
    packed = exchange(packed.reshape(TEAM, rho + 8, cols))
    feed_grad = jnp.concatenate([gate_grad, hold([up_grad], normed_grad)[0]], axis=1)
    feed_grad = exchange(feed_grad.reshape(TEAM, rho, 2 * ff_cols))

    def ff_join(w):
        return w.reshape(TEAM, rho, groups, phi).transpose(1, 2, 0, 3).reshape(rho, ff)

    gate_grad, up_grad = hold(
        [ff_join(feed_grad[:, :, :ff_cols]), ff_join(feed_grad[:, :, ff_cols:])], normed_grad
    )
    attn_grad = packed[:, :rho].transpose(1, 0, 2)
    rows_small = packed[:, rho].astype(F32)
    sums = jnp.sum(rows_small[:, head_lanes:], axis=0)
    head_gate_grad = rows_small[:, :head_lanes].reshape(heads, rho).T
    return (
        layer_output,
        tokens_grad,
        sums[:rho],
        attn_grad[:, :, :q_cols].reshape(rho, -1).astype(F32),
        attn_grad[:, :, q_cols : q_cols + k_cols].reshape(rho, -1).astype(F32),
        attn_grad[:, :, q_cols + k_cols :].reshape(rho, -1).astype(F32),
        head_gate_grad,
        output_grad.astype(F32),
        sums[2 * rho : 2 * rho + 2 * pair_cols].reshape(2, pair_cols),
        sums[rho : 2 * rho],
        gate_grad.astype(F32),
        up_grad.astype(F32),
        down_grad.astype(F32),
    )


def solution(mesh):
    groups = mesh.size // TEAM
    rows, vector, columns = P(ALL, None), P(ALL), P(None, ALL)

    def step(*args):
        return local(groups, *args)

    return jax.shard_map(
        step,
        mesh=mesh,
        in_specs=(
            rows, vector, rows, vector, rows, rows, rows, rows, rows, columns, vector, rows, rows, rows,
        ),
        out_specs=(
            rows, rows, vector, rows, rows, rows, rows, rows, columns, vector, rows, rows, rows,
        ),
        check_vma=False,
    )
```

```python
import jax
import jax.numpy as jnp
from jax import lax
from jax.experimental import pallas as pl
from jax.experimental.pallas import tpu as pltpu
from jax.sharding import PartitionSpec as P

EPSILON = 1e-06
ROPE_BASE = 1000000.0
TEAM = 8
ALL = ("dp", "fsdp")
F32 = jnp.float32
BF16 = jnp.bfloat16
TILE = 128
ANY = pl.BlockSpec(memory_space=pl.ANY)
VMEM = pl.BlockSpec(memory_space=pltpu.VMEM)
SMEM = pl.BlockSpec(memory_space=pltpu.SMEM)


def product(left, right):
    return jnp.dot(left, right, preferred_element_type=F32)


def product_nt(left, right):
    return lax.dot_general(left, right, (((1,), (1,)), ((), ())), preferred_element_type=F32)


def product_tn(left, right):
    return lax.dot_general(left, right, (((0,), (0,)), ((), ())), preferred_element_type=F32)


def world():
    return lax.axis_size(ALL)


def member():
    return lax.axis_index(ALL) % TEAM


def teams():
    return [[first + t for t in range(TEAM)] for first in range(0, world(), TEAM)]


def lines():
    return [list(range(t, world(), TEAM)) for t in range(TEAM)]


def permute(array, pairs):
    return lax.ppermute(
        array, ALL, [(team[a], team[b]) for team in teams() for a, b in pairs]
    )


def swap(array, bits):
    return permute(array, [(i, i ^ bits) for i in range(TEAM)])


def exchange(blocks):
    if lax.axis_size("fsdp") == TEAM:
        return lax.all_to_all(blocks, "fsdp", 0, 0, tiled=True)
    return lax.all_to_all(blocks, ALL, 0, 0, tiled=True, axis_index_groups=teams())


def line_gather(shard):
    if lax.axis_size("fsdp") == TEAM:
        return lax.all_gather(shard, "dp", axis=0, tiled=True)
    return lax.all_gather(shard, ALL, axis=0, tiled=True, axis_index_groups=lines())


def line_sum(array):
    if lax.axis_size("fsdp") == TEAM:
        return lax.psum_scatter(array, "dp", scatter_dimension=0, tiled=True)
    return lax.psum_scatter(array, ALL, scatter_dimension=0, tiled=True, axis_index_groups=lines())


class TeamGather:
    def __init__(self, own):
        self.own = own
        self.a1 = swap(own, 1)
        self.a2 = swap(own, 2)
        self.a4 = swap(own, 4)

    def blocks(self, tick=None):
        a2, a4 = self.a2, self.a4
        if tick is not None:
            a2, a4 = hold([a2, a4], tick)
        half = self.own.shape[0] // 2
        a6 = jnp.concatenate([swap(a4[:half], 2), swap(a2[half:], 4)], axis=0)
        return [self.own, self.a1, a2, swap(a2, 1), a4, swap(a4, 1), a6, swap(a6, 1)]


def team_gather(own):
    return TeamGather(own).blocks()


class TeamSum:
    def __init__(self, parts):
        half = parts[0].shape[0] // 2
        odd = {r: swap(parts[r + 1], 1) for r in (6, 2, 4, 0)}
        self.total6, self.total2, self.total4, self.total0 = (
            parts[r].astype(F32) + odd[r].astype(F32) for r in (6, 2, 4, 0)
        )
        self.half = half
        self.low6 = self.total6.astype(BF16)
        self.ready = [self.low6, self.total2[:half].astype(BF16), self.total4[half:].astype(BF16)]

    def first(self, tick=None):
        half = self.half
        low6, x_top, y_low = self.ready if tick is None else hold(self.ready, tick)
        self.u4 = swap(low6[:half], 2)
        self.u2 = swap(low6[half:], 4)
        self.x_top = swap(x_top, 2)
        self.y_low = swap(y_low, 4)
        self.sent = [low6, x_top, y_low]
        return [self.u4, self.u2, self.x_top, self.y_low]

    def total(self, tick=None):
        half = self.half
        lasts = [
            (self.total2[half:] + self.u2.astype(F32)).astype(BF16),
            (self.total4[:half] + self.u4.astype(F32)).astype(BF16),
        ]
        x_low, y_top = lasts if tick is None else hold(lasts, tick)
        x_low = swap(x_low, 2).astype(F32)
        y_top = swap(y_top, 4).astype(F32)
        top = self.x_top.astype(F32) + y_top
        low = x_low + self.y_low.astype(F32)
        return self.total0 + jnp.concatenate([top, low], axis=0)


def out_weight_routes(groups):
    return [(i, TEAM * (i % groups) + i // groups) for i in range(groups * TEAM)]


def out_weight_in(shard, groups, after):
    routed = lax.ppermute(shard, ALL, out_weight_routes(groups))
    return line_gather(hold([routed], after)[0]), routed


def out_weight_back(grad, groups, done):
    grad = hold([grad], done)[0]
    routes = [(user, owner) for owner, user in out_weight_routes(groups)]
    return lax.ppermute(line_sum(grad), ALL, routes), hold([done], grad)[0]


def rms_pull(value, gain, grad):
    scale = lax.rsqrt(jnp.mean(value * value, axis=-1, keepdims=True) + EPSILON)
    weighted = grad * gain
    mean = jnp.mean(weighted * value, axis=-1, keepdims=True)
    return scale * weighted - scale * scale * scale * value * mean


def rms(value, gain):
    return value * lax.rsqrt(jnp.mean(value * value, axis=-1, keepdims=True) + EPSILON) * gain


def struct(shape, dtype):
    return jax.ShapeDtypeStruct(shape, dtype)


def hold(arrays, tick):
    def kernel(*refs):
        del refs

    count = len(arrays)
    return pl.pallas_call(
        kernel,
        out_shape=[struct(a.shape, a.dtype) for a in arrays],
        in_specs=[ANY] * count + [ANY],
        out_specs=[ANY] * count,
        input_output_aliases={i: i for i in range(count)},
    )(*arrays, tick)


def mark(arrays):
    def kernel(*refs):
        refs[-1][...] = jnp.zeros_like(refs[-1])

    return pl.pallas_call(
        kernel,
        out_shape=struct((8, 128), jnp.int32),
        in_specs=[ANY] * len(arrays),
        out_specs=VMEM,
    )(*arrays)


def for_tiles(tiles, most, body):
    for m in range(1, most + 1):

        @pl.when(tiles == m)
        def _(m=m):
            body(m * TILE)


def turned(u, cosine, sine):
    return u * cosine + pltpu.roll(u, u.shape[-1] // 2, 1) * sine


def head_norm(u):
    return lax.rsqrt(jnp.mean(u * u, axis=-1, keepdims=True) + EPSILON)


def head_back(grad, raw, gain, cosine, sine):
    e = turned(grad, cosine, -sine)
    scale = head_norm(raw)
    weighted = e * gain
    mean = jnp.mean(weighted * raw, axis=-1, keepdims=True)
    back = scale * weighted - scale * scale * scale * raw * mean
    return back, jnp.sum(e * raw * scale, axis=0, keepdims=True)


def weights_of(query, key, factor):
    scores = product_nt(query, key) * factor
    n = scores.shape[0]
    causal = lax.broadcasted_iota(jnp.int32, (n, n), 1) <= lax.broadcasted_iota(jnp.int32, (n, n), 0)
    scores = jnp.where(causal, scores, -jnp.inf)
    terms = jnp.exp(scores - jnp.max(scores, axis=-1, keepdims=True))
    return terms * (1.0 / jnp.sum(terms, axis=-1, keepdims=True))


def rows_of(tile, size=TILE):
    return pl.ds(pl.multiple_of(tile * size, size), size)


def each_block(r, body):
    for k in range(TEAM):
        pl.when(r == k)(lambda k=k: body(k))


def attend(tiles, tokens, consts, mine, after):
    weight_attn, weight_head, weight_out, gain, gains, cosine, sine = consts
    rows, width = tokens[0].shape
    size = gains.shape[1]
    q_cols = mine * size
    cols = weight_attn.shape[1]
    factor = size ** (-0.5)

    def kernel(*refs):
        tiles_ref, toks = refs[0], refs[1 : 1 + TEAM]
        wa, wh, wo, gain_ref, gains_ref, cos_ref, sin_ref, _ = refs[1 + TEAM : 9 + TEAM]
        parts = refs[9 + TEAM : 9 + 2 * TEAM]
        normed_all, qkv_all, logit_all, gated_all, tick = refs[9 + 2 * TEAM : 14 + 2 * TEAM]
        (
            tok_v, wa_v, wh_v, wo_v, part_v, normed_v, qkv_v, logit_v, gated_v, w_sem, in_sem, out_sem,
        ) = refs[14 + 2 * TEAM :]
        tick[...] = jnp.zeros_like(tick)

        def load(k, slot):
            return pltpu.make_async_copy(toks[k], tok_v.at[slot], in_sem.at[slot])

        def store(r, slot, j, k=0):
            src = (part_v, normed_v, qkv_v, logit_v, gated_v)[j].at[slot]
            dst = parts[k] if j == 0 else (normed_all, qkv_all, logit_all, gated_all)[j - 1].at[rows_of(r, rows)]
            return pltpu.make_async_copy(src, dst, out_sem.at[j, slot])

        load(0, 0).start()
        weights = [
            pltpu.make_async_copy(src, dst, w_sem.at[j])
            for j, (src, dst) in enumerate(((wa, wa_v), (wh, wh_v), (wo, wo_v)))
        ]
        for copy in weights:
            copy.start()
        for copy in weights:
            copy.wait()

        def step(r, carry):
            slot = r % 2

            @pl.when(r + 1 < TEAM)
            def _():
                each_block(r + 1, lambda k: load(k, 1 - slot).start())

            load(0, slot).wait()

            @pl.when(r >= 2)
            def _():
                for j in range(5):
                    store(r - 2, slot, j).wait()

            def body(n):
                value = tok_v[slot, :n].astype(F32)
                normed = rms(value, gain_ref[...]).astype(BF16)
                normed_v[slot, :n] = normed
                qkv = product(normed, wa_v[...])
                qkv_v[slot, :n] = qkv
                logit = product_nt(normed, wh_v[...])
                logit_v[slot, :n] = logit
                cos, sin = cos_ref[:n], sin_ref[:n]
                key = qkv[:, q_cols : q_cols + size]
                key = turned(key * head_norm(key) * gains_ref[1:2], cos, sin).astype(BF16)
                values = qkv[:, q_cols + size :].astype(BF16)
                for h in range(mine):
                    query = qkv[:, h * size : (h + 1) * size]
                    query = turned(query * head_norm(query) * gains_ref[0:1], cos, sin).astype(BF16)
                    attention = weights_of(query, key, factor)
                    mixture = product(attention.astype(BF16), values)
                    gate = jax.nn.sigmoid(logit[:, h : h + 1])
                    gated_v[slot, :n, h * size : (h + 1) * size] = (mixture * gate).astype(BF16)
                part_v[slot, :n] = product(gated_v[slot, :n], wo_v[...]).astype(BF16)
                if n < rows:
                    part_v[slot, n:] = jnp.zeros((rows - n, width), BF16)
                    normed_v[slot, n:] = jnp.zeros((rows - n, width), BF16)
                    gated_v[slot, n:] = jnp.zeros((rows - n, q_cols), BF16)

            for_tiles(tiles_ref[r], rows // TILE, body)
            each_block(r, lambda k: store(r, slot, 0, k).start())
            for j in range(1, 5):
                store(r, slot, j).start()
            return carry

        lax.fori_loop(0, TEAM, step, 0)
        for r in (TEAM - 2, TEAM - 1):
            for j in range(5):
                store(r, r % 2, j).wait()

    whole = TEAM * rows
    result = pl.pallas_call(
        kernel,
        out_shape=[struct((rows, width), BF16)] * TEAM
        + [
            struct((whole, width), BF16),
            struct((whole, cols), F32),
            struct((whole, TILE), F32),
            struct((whole, q_cols), BF16),
            struct((8, 128), jnp.int32),
        ],
        in_specs=[SMEM] + [ANY] * (TEAM + 3) + [VMEM] * 4 + [ANY],
        out_specs=[ANY] * (TEAM + 4) + [VMEM],
        scratch_shapes=[
            pltpu.VMEM((2, rows, width), BF16),
            pltpu.VMEM(weight_attn.shape, BF16),
            pltpu.VMEM(weight_head.shape, BF16),
            pltpu.VMEM(weight_out.shape, BF16),
            pltpu.VMEM((2, rows, width), BF16),
            pltpu.VMEM((2, rows, width), BF16),
            pltpu.VMEM((2, rows, cols), F32),
            pltpu.VMEM((2, rows, TILE), F32),
            pltpu.VMEM((2, rows, q_cols), BF16),
            pltpu.SemaphoreType.DMA((3,)),
            pltpu.SemaphoreType.DMA((2,)),
            pltpu.SemaphoreType.DMA((5, 2)),
        ],
        compiler_params=pltpu.CompilerParams(vmem_limit_bytes=48 << 20),
        cost_estimate=pl.CostEstimate(flops=30 << 30, bytes_accessed=60 << 20, transcendentals=1 << 20),
    )(tiles, *tokens, weight_attn, weight_head, weight_out, gain, gains, cosine, sine, after)
    return result[:TEAM], result[TEAM : TEAM + 4], result[TEAM + 4]


def attend_back(tiles, hidden, consts, saved, mine, after):
    weight_attn, weight_head, weight_out, gain, gains, cosine, sine = consts
    rows, width = hidden[0].shape
    size = gains.shape[1]
    q_cols = mine * size
    cols = weight_attn.shape[1]
    factor = size ** (-0.5)

    def kernel(*refs):
        tiles_ref, hids = refs[0], refs[1 : 1 + TEAM]
        wa, wh, wo, normed_all, qkv_all, logit_all, gated_all = refs[1 + TEAM : 8 + TEAM]
        gains_ref, cos_ref, sin_ref, _ = refs[8 + TEAM : 12 + TEAM]
        parts = refs[12 + TEAM : 12 + 2 * TEAM]
        attn_part, head_sum, out_part, gain_sum, gains_sum = refs[12 + 2 * TEAM : 17 + 2 * TEAM]
        (
            hid_v, wa_v, wh_v, wo_v, normed_v, qkv_v, logit_v, gated_v, part_v, back_v, attn_sum, out_sum,
            w_sem, in_sem, out_sem,
        ) = refs[17 + 2 * TEAM :]

        def loads(r, slot, k):
            yield pltpu.make_async_copy(hids[k], hid_v.at[slot], in_sem.at[0, slot])
            here = rows_of(r, rows)
            for j, (src, dst) in enumerate(
                ((qkv_all, qkv_v), (logit_all, logit_v), (normed_all, normed_v), (gated_all, gated_v))
            ):
                yield pltpu.make_async_copy(src.at[here], dst.at[slot], in_sem.at[1 + j, slot])

        def start_loads(r, slot):
            def body(k):
                for copy in loads(r, slot, k):
                    copy.start()

            each_block(r, body)

        def store(slot, k=0):
            return pltpu.make_async_copy(part_v.at[slot], parts[k], out_sem.at[slot])

        for copy in loads(0, 0, 0):
            copy.start()
        weights = [
            pltpu.make_async_copy(src, dst, w_sem.at[j])
            for j, (src, dst) in enumerate(((wo, wo_v), (wa, wa_v), (wh, wh_v)))
        ]
        for copy in weights:
            copy.start()
        for ref in (attn_sum, out_sum, gain_sum, gains_sum):
            ref[...] = jnp.zeros_like(ref)
        for copy in weights:
            copy.wait()

        def step(r, carry):
            slot = r % 2

            @pl.when(r + 1 < TEAM)
            def _():
                start_loads(r + 1, 1 - slot)

            for copy in loads(r, slot, 0):
                copy.wait()

            @pl.when(r >= 2)
            def _():
                store(slot).wait()

            def body(n):
                hidden_low = hid_v[slot, :n]
                normed = normed_v[slot, :n]
                out_sum[...] += product_tn(gated_v[slot, :n], hidden_low)
                gated_grad = product_nt(hidden_low, wo_v[...])
                cos, sin = cos_ref[:n], sin_ref[:n]
                key_raw = qkv_v[slot, :n, q_cols : q_cols + size]
                key = turned(key_raw * head_norm(key_raw) * gains_ref[1:2], cos, sin).astype(BF16)
                values = qkv_v[slot, :n, q_cols + size :].astype(BF16)
                lane = lax.broadcasted_iota(jnp.int32, (n, TILE), 1)
                logit_back = jnp.zeros((n, TILE), F32)
                values_back = jnp.zeros((n, size), F32)
                key_grad = jnp.zeros((n, size), F32)
                query_sum = jnp.zeros((1, size), F32)
                for h in range(mine):
                    span = slice(h * size, (h + 1) * size)
                    query_raw = qkv_v[slot, :n, span]
                    query = turned(query_raw * head_norm(query_raw) * gains_ref[0:1], cos, sin).astype(BF16)
                    attention = weights_of(query, key, factor)
                    attention_low = attention.astype(BF16)
                    mixture = product(attention_low, values)
                    gate = jax.nn.sigmoid(logit_v[slot, :n, h : h + 1])
                    head_grad = gated_grad[:, span]
                    mixture_back = (head_grad * gate).astype(BF16)
                    one = jnp.sum(head_grad * mixture, axis=-1, keepdims=True) * gate * (1.0 - gate)
                    logit_back = jnp.where(lane == h, one, logit_back)
                    values_back += product_tn(attention_low, mixture_back)
                    attention_grad = product_nt(mixture_back, values)
                    scores_back = (
                        attention
                        * (attention_grad - jnp.sum(attention_grad * attention, axis=-1, keepdims=True))
                    ).astype(BF16)
                    query_grad = product(scores_back, key) * factor
                    key_grad += product_tn(scores_back, query)
                    back, total = head_back(query_grad, query_raw, gains_ref[0:1], cos, sin)
                    back_v[:n, span] = back.astype(BF16)
                    query_sum += total
                back, key_sum = head_back(key_grad * factor, key_raw, gains_ref[1:2], cos, sin)
                back_v[:n, q_cols : q_cols + size] = back.astype(BF16)
                back_v[:n, q_cols + size : cols] = values_back.astype(BF16)
                logit_back = logit_back.astype(BF16)
                back_v[:n, cols:] = logit_back
                gains_sum[0:1] += query_sum
                gains_sum[1:2] += key_sum
                part = product_nt(back_v[:n, :cols], wa_v[...]) + product(logit_back, wh_v[...])
                part_v[slot, :n] = part.astype(BF16)
                gain_sum[0:1] += jnp.sum(part * normed.astype(F32), axis=0, keepdims=True)
                attn_sum[...] += product_tn(back_v[:n], normed)
                if n < rows:
                    part_v[slot, n:] = jnp.zeros((rows - n, width), BF16)

            for_tiles(tiles_ref[r], rows // TILE, body)
            each_block(r, lambda k: store(slot, k).start())
            return carry

        lax.fori_loop(0, TEAM, step, 0)
        attn_part[...] = attn_sum[:cols].T.astype(BF16)
        head_sum[...] = attn_sum[cols : cols + 8]
        out_part[...] = out_sum[...].astype(BF16)
        store(0).wait()
        store(1).wait()

    result = pl.pallas_call(
        kernel,
        out_shape=[struct((rows, width), BF16)] * TEAM
        + [
            struct((width, cols), BF16),
            struct((8, width), F32),
            struct((q_cols, width), BF16),
            struct((8, width), F32),
            struct((8, size), F32),
        ],
        in_specs=[SMEM] + [ANY] * (TEAM + 7) + [VMEM] * 3 + [ANY],
        out_specs=[ANY] * TEAM + [VMEM] * 5,
        scratch_shapes=[
            pltpu.VMEM((2, rows, width), BF16),
            pltpu.VMEM(weight_attn.shape, BF16),
            pltpu.VMEM(weight_head.shape, BF16),
            pltpu.VMEM(weight_out.shape, BF16),
            pltpu.VMEM((2, rows, width), BF16),
            pltpu.VMEM((2, rows, cols), F32),
            pltpu.VMEM((2, rows, TILE), F32),
            pltpu.VMEM((2, rows, q_cols), BF16),
            pltpu.VMEM((2, rows, width), BF16),
            pltpu.VMEM((rows, cols + TILE), BF16),
            pltpu.VMEM((cols + TILE, width), F32),
            pltpu.VMEM((q_cols, width), F32),
            pltpu.SemaphoreType.DMA((3,)),
            pltpu.SemaphoreType.DMA((5, 2)),
            pltpu.SemaphoreType.DMA((2,)),
        ],
        compiler_params=pltpu.CompilerParams(vmem_limit_bytes=56 << 20),
        cost_estimate=pl.CostEstimate(flops=45 << 30, bytes_accessed=70 << 20, transcendentals=1 << 20),
    )(tiles, *hidden, weight_attn, weight_head, weight_out, *saved, gains, cosine, sine, after)
    return result[:TEAM], *result[TEAM : TEAM + 3], result[TEAM + 3][0], result[TEAM + 4][:2]


def tile_places(tiles_ref, rows):
    places, total = [], 0
    for r in range(TEAM):
        count = tiles_ref[r]
        for j in range(rows // TILE):
            places.append((r, j, j < count, total + j))
        total = total + count
    return places, total


def feed(tiles, twos, upstreams, weight_gate, weight_up, weight_down):
    rows, width = twos[0].shape
    ff_cols = weight_down.shape[0]
    whole = TEAM * rows
    chunk = 2 * TILE
    chunks = whole // chunk

    def kernel(*refs):
        tiles_ref, twos_ref, ups_ref = refs[0], refs[1 : 1 + TEAM], refs[1 + TEAM : 1 + 2 * TEAM]
        weights_ref = refs[1 + 2 * TEAM : 4 + 2 * TEAM]
        outs_ref = refs[4 + 2 * TEAM : 4 + 3 * TEAM]
        grads_ref = refs[4 + 3 * TEAM : 4 + 4 * TEAM]
        inner_all, back_all, two_all, ups_all = refs[4 + 4 * TEAM : 8 + 4 * TEAM]
        (
            two_v, ups_v, wg_v, wu_v, wd_v, inner_v, back_v, out_v, grad_v, zero_v,
            w_sem, load_sem, keep_sem, tile_sem, dead_sem,
        ) = refs[8 + 4 * TEAM :]
        places, total = tile_places(tiles_ref, rows)
        used = (total + 1) // 2

        def loads(sources, packed, which):
            for k, (r, j, live, place) in enumerate(places):
                yield live, pltpu.make_async_copy(
                    sources[r].at[rows_of(j)], packed.at[rows_of(place)], load_sem.at[which, k]
                )

        weights = [
            pltpu.make_async_copy(src, dst, w_sem.at[j])
            for j, (src, dst) in enumerate(zip(weights_ref, (wg_v, wu_v, wd_v)))
        ]
        for live, copy in loads(twos_ref, two_v, 0):
            pl.when(live)(copy.start)
        for copy in weights:
            copy.start()
        for live, copy in loads(ups_ref, ups_v, 1):
            pl.when(live)(copy.start)
        zero_v[...] = jnp.zeros_like(zero_v)

        def dead(k, r, j):
            zeros = zero_v.at[:TILE]
            yield pltpu.make_async_copy(zeros, grads_ref[r].at[rows_of(j)], dead_sem.at[0, k])
            yield pltpu.make_async_copy(zeros, outs_ref[r].at[rows_of(j)], dead_sem.at[1, k])

        for k, (r, j, live, place) in enumerate(places):

            @pl.when(jnp.logical_not(live))
            def _(k=k, r=r, j=j):
                for copy in dead(k, r, j):
                    copy.start()

        def keeps(c, sources):
            for j, (src, dst) in enumerate(zip(sources, (two_all, ups_all, inner_all, back_all))):
                yield pltpu.make_async_copy(src, dst.at[rows_of(c, chunk)], keep_sem.at[j, c])

        zeros = (zero_v, zero_v, zero_v.at[:, :ff_cols], zero_v.at[:, : 2 * ff_cols])
        for c in range(TEAM // 2, chunks):

            @pl.when(c >= used)
            def _(c=c):
                for copy in keeps(c, zeros):
                    copy.start()

        @pl.when(total % 2 == 1)
        def _():
            two_v[rows_of(total)] = jnp.zeros((TILE, width), BF16)
            ups_v[rows_of(total)] = jnp.zeros((TILE, width), BF16)

        for live, copy in loads(twos_ref, two_v, 0):
            pl.when(live)(copy.wait)
        for copy in weights:
            copy.wait()
        for live, copy in loads(ups_ref, ups_v, 1):
            pl.when(live)(copy.wait)

        def tile_stores(r, j, slot, side):
            here = pl.ds(side * TILE, TILE)
            yield pltpu.make_async_copy(
                grad_v.at[slot, here], grads_ref[r].at[rows_of(j)], tile_sem.at[0, slot, side]
            )
            yield pltpu.make_async_copy(
                out_v.at[slot, here], outs_ref[r].at[rows_of(j)], tile_sem.at[1, slot, side]
            )

        def wait_tiles(c, slot):
            for side in range(2):

                @pl.when(2 * c + side < total)
                def _(side=side):
                    for copy in tile_stores(0, 0, slot, side):
                        copy.wait()

        def body(c, carry):
            slot = c % 2
            span = rows_of(c, chunk)

            @pl.when(c >= 2)
            def _():
                wait_tiles(c - 2, slot)
                for j, copy in enumerate(keeps(c - 2, zeros)):
                    if j >= 2:
                        copy.wait()

            gate_part = product(two_v[span], wg_v[...])
            up_part = product(two_v[span], wu_v[...])
            sig = jax.nn.sigmoid(gate_part)
            silu = gate_part * sig
            inner_v[slot] = (silu * up_part).astype(BF16)
            inner_grad = product_nt(ups_v[span], wd_v[...])
            back_v[slot, :, :ff_cols] = (inner_grad * up_part * (sig + silu * (1.0 - sig))).astype(BF16)
            back_v[slot, :, ff_cols:] = (inner_grad * silu).astype(BF16)
            for copy in keeps(c, (two_v.at[span], ups_v.at[span], inner_v.at[slot], back_v.at[slot])):
                copy.start()
            grad = product_nt(back_v[slot, :, :ff_cols], wg_v[...]) + product_nt(
                back_v[slot, :, ff_cols:], wu_v[...]
            )
            grad_v[slot] = grad.astype(BF16)
            out_v[slot] = product(inner_v[slot], wd_v[...]).astype(BF16)
            for k, (r, j, live, place) in enumerate(places):
                for side in range(2):

                    @pl.when(jnp.logical_and(live, place == 2 * c + side))
                    def _(r=r, j=j, side=side):
                        for copy in tile_stores(r, j, slot, side):
                            copy.start()

            return carry

        lax.fori_loop(0, used, body, 0)
        wait_tiles(used - 2, used % 2)
        wait_tiles(used - 1, (used - 1) % 2)
        for k, (r, j, live, place) in enumerate(places):

            @pl.when(jnp.logical_not(live))
            def _(k=k, r=r, j=j):
                for copy in dead(k, r, j):
                    copy.wait()

        for c in range(chunks):
            for j, copy in enumerate(keeps(c, zeros)):
                if j < 2:
                    copy.wait()
                else:
                    pl.when(c >= used - 2)(copy.wait)

    count = whole // TILE
    result = pl.pallas_call(
        kernel,
        out_shape=[struct((rows, width), BF16)] * (2 * TEAM)
        + [
            struct((whole, ff_cols), BF16),
            struct((whole, 2 * ff_cols), BF16),
            struct((whole, width), BF16),
            struct((whole, width), BF16),
        ],
        in_specs=[SMEM] + [ANY] * (3 + 2 * TEAM),
        out_specs=[ANY] * (2 * TEAM + 4),
        scratch_shapes=[
            pltpu.VMEM((whole, width), BF16),
            pltpu.VMEM((whole, width), BF16),
            pltpu.VMEM(weight_gate.shape, BF16),
            pltpu.VMEM(weight_up.shape, BF16),
            pltpu.VMEM(weight_down.shape, BF16),
            pltpu.VMEM((2, chunk, ff_cols), BF16),
            pltpu.VMEM((2, chunk, 2 * ff_cols), BF16),
            pltpu.VMEM((2, chunk, width), BF16),
            pltpu.VMEM((2, chunk, width), BF16),
            pltpu.VMEM((chunk, width), BF16),
            pltpu.SemaphoreType.DMA((3,)),
            pltpu.SemaphoreType.DMA((2, count)),
            pltpu.SemaphoreType.DMA((4, chunks)),
            pltpu.SemaphoreType.DMA((2, 2, 2)),
            pltpu.SemaphoreType.DMA((2, count)),
        ],
        compiler_params=pltpu.CompilerParams(vmem_limit_bytes=60 << 20),
        cost_estimate=pl.CostEstimate(flops=58 << 30, bytes_accessed=100 << 20, transcendentals=1 << 20),
    )(tiles, *twos, *upstreams, weight_gate, weight_up, weight_down)
    return result[:TEAM], result[TEAM : 2 * TEAM], result[2 * TEAM :]


def local(
    groups,
    tokens,
    lengths,
    cotangent,
    attention_gain,
    query_weight,
    key_matrix,
    value_matrix,
    head_gate_weight,
    output_weight,
    query_key_gain,
    feedforward_gain,
    gate_weight,
    up_weight,
    down_weight,
):
    t = member()
    everyone = groups * TEAM
    rows, width = tokens.shape
    rho = query_weight.shape[0]
    phi = down_weight.shape[0]
    ff = gate_weight.shape[1]
    pair_cols = query_key_gain.shape[1]
    size = pair_cols * everyone
    heads = query_weight.shape[1] // size
    mine = heads // TEAM
    q_cols = query_weight.shape[1] // TEAM
    k_cols = key_matrix.shape[1] // TEAM
    ff_cols = ff // TEAM

    def everyone_in_team(vector):
        return jnp.broadcast_to(vector.reshape(1, -1), (TEAM, vector.size))

    live_tiles = (lengths + (TILE - 1)) // TILE
    row = jnp.concatenate(
        [
            head_gate_weight.reshape(rho, TEAM, mine).transpose(1, 2, 0).reshape(TEAM, -1),
            everyone_in_team(attention_gain),
            everyone_in_team(feedforward_gain),
            everyone_in_team(query_key_gain),
            everyone_in_team(live_tiles.astype(BF16)),
        ],
        axis=1,
    )
    cols = q_cols + 2 * k_cols
    row = jnp.pad(row, ((0, 0), (0, cols - row.shape[1])))[:, None, :]
    attn = jnp.concatenate(
        [
            query_weight.reshape(rho, TEAM, q_cols),
            key_matrix.reshape(rho, TEAM, k_cols),
            value_matrix.reshape(rho, TEAM, k_cols),
        ],
        axis=2,
    ).transpose(1, 0, 2)
    attn = jnp.concatenate([attn, jnp.pad(row, ((0, 0), (0, 7), (0, 0)))], axis=1)
    attn = exchange(attn)
    exchanged = attn
    head_lanes = mine * rho
    at_one, at_two, at_pair = head_lanes, head_lanes + rho, head_lanes + 2 * rho
    at_tiles = at_pair + 2 * pair_cols
    team_tiles = attn[:, rho, at_tiles].astype(jnp.int32)
    order = jnp.arange(TEAM, dtype=jnp.int32)
    tiles = jnp.sum(jnp.where((order[:, None] ^ t) == order[None, :], team_tiles[None, :], 0), axis=1)
    attn = line_gather(attn.reshape(TEAM * (rho + 8), cols)).reshape(everyone, rho + 8, cols)
    weight_attn = attn[:, :rho].reshape(width, cols)
    rows_small = attn[:, rho]
    weight_head = jnp.pad(
        rows_small[:, :head_lanes].reshape(everyone, mine, rho).transpose(1, 0, 2).reshape(mine, width),
        ((0, TILE - mine), (0, 0)),
    )
    gain_one = rows_small[:, at_one:at_two].reshape(1, width).astype(F32)
    gain_two = rows_small[:, at_two:at_pair].reshape(1, width).astype(F32)
    gain_pair = (
        rows_small[:, at_pair:at_tiles]
        .reshape(everyone, 2, pair_cols)
        .transpose(1, 0, 2)
        .reshape(2, size)
        .astype(F32)
    )
    weight_out, routed = out_weight_in(output_weight, groups, exchanged)

    def ff_split(w):
        return w.reshape(rho, groups, TEAM, phi).transpose(2, 0, 1, 3).reshape(TEAM, rho, ff_cols)

    feed_shard = jnp.concatenate([ff_split(gate_weight), ff_split(up_weight)], axis=2)
    feed_shard = exchange(hold([feed_shard], routed)[0]).reshape(TEAM * rho, -1)
    weight_gate = line_gather(feed_shard[:, :ff_cols])

    exponent = jnp.arange(size // 2, dtype=F32) * (-2.0 / size)
    frequency = jnp.power(ROPE_BASE, exponent)
    angles = jnp.arange(rows, dtype=F32)[:, None] * frequency[None, :]
    cosine = jnp.concatenate([jnp.cos(angles), jnp.cos(angles)], axis=1)
    sine = jnp.concatenate([-jnp.sin(angles), jnp.sin(angles)], axis=1)
    consts = (weight_attn, weight_head, weight_out, gain_one, gain_pair, cosine, sine)
    team_tokens = team_gather(tokens)
    live = lax.broadcasted_iota(jnp.int32, (rows, 1), 0) < lengths[0]
    live_rows = live.astype(F32)
    upstream = cotangent.astype(F32) * live_rows
    tick = mark([team_tokens[6], feed_shard])
    later = lax.broadcasted_iota(jnp.int32, (rows, 1), 0) < lengths[0] + tick[0, 0]
    upstream_low = jnp.where(later, cotangent, jnp.zeros_like(cotangent))
    upstream_levels = TeamGather(upstream_low)
    parts, kept, tick = attend(tiles, team_tokens, consts, mine, mark([feed_shard, upstream_low]))
    normed, qkv, logit, gated = kept
    weight_up = line_gather(hold([feed_shard[:, ff_cols:]], tick)[0])
    parts = hold(parts, mark([upstream_levels.a1, upstream_levels.a2, upstream_levels.a4, tick]))
    arrived = TeamSum(parts)
    arrived.first()
    weight_down = line_gather(hold([down_weight], arrived.low6)[0])
    team_upstream = upstream_levels.blocks(mark([arrived.u4, arrived.u2]))
    inputs = tokens.astype(F32)
    hidden_state = inputs + arrived.total(weight_gate)

    normed_two = rms(hidden_state, gain_two).astype(BF16)
    normed_two = hold([normed_two], mark(team_upstream))[0]
    team_two = TeamGather(normed_two).blocks(mark([weight_up]))
    outs, grads, saved = feed(tiles, team_two, team_upstream, weight_gate, weight_up, weight_down)
    inner, feed_back, two_all, ups_all = saved
    arrived = TeamSum(grads)
    arrived.first()
    two_grad = arrived.total()
    down_part = product_tn(inner, ups_all).astype(BF16)
    feed_back = hold([feed_back], mark([arrived.x_top, arrived.y_low]))[0]
    gate_part = product_tn(two_all, feed_back[:, :ff_cols]).astype(BF16)
    up_part = product_tn(two_all, feed_back[:, ff_cols:]).astype(BF16)
    parts_made = mark([gate_part, up_part])
    down_grad = line_sum(down_part)
    gate_grad = line_sum(hold([gate_part], down_grad)[0])
    up_grad = line_sum(hold([up_part], gate_grad)[0])
    feed_done = up_grad
    hidden_grad = upstream + rms_pull(hidden_state, gain_two, two_grad)

    fed = TeamSum(outs)
    team_hidden = TeamGather(hidden_grad.astype(BF16)).blocks(mark(fed.ready + [gate_part, up_part]))
    two_scale = lax.rsqrt(jnp.mean(hidden_state * hidden_state, axis=-1, keepdims=True) + EPSILON)
    two_sum = jnp.sum(two_grad * hidden_state * two_scale, axis=0)
    first_hop = fed.first(mark(team_hidden + [parts_made]))
    parts, attn_part, head_sum, out_part, one_sum, pair_sum = attend_back(
        tiles, team_hidden, consts, (normed, qkv, logit, gated), mine, mark(fed.sent + [down_grad])
    )
    row = jnp.concatenate(
        [
            head_sum[:mine].reshape(mine, everyone, rho).transpose(1, 0, 2).reshape(everyone, -1),
            (one_sum / gain_one[0]).reshape(everyone, rho),
            two_sum.reshape(everyone, rho),
            pair_sum.reshape(2, everyone, pair_cols).transpose(1, 0, 2).reshape(everyone, -1),
        ],
        axis=1,
    ).astype(BF16)
    row = jnp.pad(row, ((0, 0), (0, cols - row.shape[1])))[:, None, :]
    packed = jnp.concatenate(
        [attn_part.reshape(everyone, rho, cols), jnp.pad(row, ((0, 0), (0, 7), (0, 0)))], axis=1
    )
    packed = hold([packed.reshape(everyone * (rho + 8), cols)], feed_done)[0]
    parts = hold(parts, mark(first_hop + [gate_grad]))
    arrived = TeamSum(parts)
    arrived.first(packed)
    packed = line_sum(packed)
    normed_grad = arrived.total()
    layer_output = ((hidden_state + fed.total()) * live_rows).astype(BF16)
    tokens_grad = (hidden_grad + rms_pull(inputs, gain_one, normed_grad)).astype(BF16)
    output_grad, packed = out_weight_back(out_part, groups, packed)
    packed = exchange(packed.reshape(TEAM, rho + 8, cols))
    feed_grad = jnp.concatenate([gate_grad, hold([up_grad], arrived.u4)[0]], axis=1)
    feed_grad = exchange(feed_grad.reshape(TEAM, rho, 2 * ff_cols))

    def ff_join(w):
        return w.reshape(TEAM, rho, groups, phi).transpose(1, 2, 0, 3).reshape(rho, ff)

    gate_grad, up_grad = hold(
        [ff_join(feed_grad[:, :, :ff_cols]), ff_join(feed_grad[:, :, ff_cols:])], normed_grad
    )
    attn_grad = packed[:, :rho].transpose(1, 0, 2)
    rows_small = packed[:, rho].astype(F32)
    sums = jnp.sum(rows_small[:, head_lanes:], axis=0)
    head_gate_grad = rows_small[:, :head_lanes].reshape(heads, rho).T
    return (
        layer_output,
        tokens_grad,
        sums[:rho],
        attn_grad[:, :, :q_cols].reshape(rho, -1).astype(F32),
        attn_grad[:, :, q_cols : q_cols + k_cols].reshape(rho, -1).astype(F32),
        attn_grad[:, :, q_cols + k_cols :].reshape(rho, -1).astype(F32),
        head_gate_grad,
        output_grad.astype(F32),
        sums[2 * rho : 2 * rho + 2 * pair_cols].reshape(2, pair_cols),
        sums[rho : 2 * rho],
        gate_grad.astype(F32),
        up_grad.astype(F32),
        down_grad.astype(F32),
    )


def solution(mesh):
    groups = mesh.size // TEAM
    rows, vector, columns = P(ALL, None), P(ALL), P(None, ALL)

    def step(*args):
        return local(groups, *args)

    return jax.shard_map(
        step,
        mesh=mesh,
        in_specs=(
            rows, vector, rows, vector, rows, rows, rows, rows, rows, columns, vector, rows, rows, rows,
        ),
        out_specs=(
            rows, rows, vector, rows, rows, rows, rows, rows, columns, vector, rows, rows, rows,
        ),
        check_vma=False,
    )
```

```python
import jax
import jax.numpy as jnp
from jax import lax
from jax.experimental import pallas as pl
from jax.experimental.pallas import tpu as pltpu
from jax.sharding import PartitionSpec as P

EPSILON = 1e-06
ROPE_BASE = 1000000.0
TEAM = 8
ALL = ("dp", "fsdp")
F32 = jnp.float32
BF16 = jnp.bfloat16
TILE = 128
ANY = pl.BlockSpec(memory_space=pl.ANY)
VMEM = pl.BlockSpec(memory_space=pltpu.VMEM)
SMEM = pl.BlockSpec(memory_space=pltpu.SMEM)


def product(left, right):
    return jnp.dot(left, right, preferred_element_type=F32)


def product_nt(left, right):
    return lax.dot_general(left, right, (((1,), (1,)), ((), ())), preferred_element_type=F32)


def product_tn(left, right):
    return lax.dot_general(left, right, (((0,), (0,)), ((), ())), preferred_element_type=F32)


def world():
    return lax.axis_size(ALL)


def member():
    return lax.axis_index(ALL) % TEAM


def teams():
    return [[first + t for t in range(TEAM)] for first in range(0, world(), TEAM)]


def lines():
    return [list(range(t, world(), TEAM)) for t in range(TEAM)]


def permute(array, pairs):
    return lax.ppermute(
        array, ALL, [(team[a], team[b]) for team in teams() for a, b in pairs]
    )


def swap(array, bits):
    return permute(array, [(i, i ^ bits) for i in range(TEAM)])


def exchange(blocks):
    if lax.axis_size("fsdp") == TEAM:
        return lax.all_to_all(blocks, "fsdp", 0, 0, tiled=True)
    return lax.all_to_all(blocks, ALL, 0, 0, tiled=True, axis_index_groups=teams())


def line_gather(shard):
    if lax.axis_size("fsdp") == TEAM:
        return lax.all_gather(shard, "dp", axis=0, tiled=True)
    return lax.all_gather(shard, ALL, axis=0, tiled=True, axis_index_groups=lines())


def line_sum(array):
    if lax.axis_size("fsdp") == TEAM:
        return lax.psum_scatter(array, "dp", scatter_dimension=0, tiled=True)
    return lax.psum_scatter(array, ALL, scatter_dimension=0, tiled=True, axis_index_groups=lines())


class TeamGather:
    def __init__(self, own):
        self.own = own
        self.a1 = swap(own, 1)
        self.a2 = swap(own, 2)
        self.a4 = swap(own, 4)

    def blocks(self, tick=None):
        a2, a4 = self.a2, self.a4
        if tick is not None:
            a2, a4 = hold([a2, a4], tick)
        half = self.own.shape[0] // 2
        a6 = jnp.concatenate([swap(a4[:half], 2), swap(a2[half:], 4)], axis=0)
        return [self.own, self.a1, a2, swap(a2, 1), a4, swap(a4, 1), a6, swap(a6, 1)]


def team_gather(own):
    return TeamGather(own).blocks()


class TeamSum:
    def __init__(self, parts):
        half = parts[0].shape[0] // 2
        odd = {r: swap(parts[r + 1], 1) for r in (6, 2, 4, 0)}
        self.total6, self.total2, self.total4, self.total0 = (
            (parts[r].astype(F32) + odd[r].astype(F32)).astype(BF16) for r in (6, 2, 4, 0)
        )
        self.half = half
        self.low6 = self.total6
        self.ready = [self.low6, self.total2[:half], self.total4[half:]]

    def first(self, tick=None):
        half = self.half
        low6, x_top, y_low = self.ready if tick is None else hold(self.ready, tick)
        self.u4 = swap(low6[:half], 2)
        self.u2 = swap(low6[half:], 4)
        self.x_top = swap(x_top, 2)
        self.y_low = swap(y_low, 4)
        self.sent = [low6, x_top, y_low]
        return [self.u4, self.u2, self.x_top, self.y_low]

    def total(self, tick=None):
        half = self.half
        lasts = [
            (self.total2[half:].astype(F32) + self.u2.astype(F32)).astype(BF16),
            (self.total4[:half].astype(F32) + self.u4.astype(F32)).astype(BF16),
        ]
        x_low, y_top = lasts if tick is None else hold(lasts, tick)
        self.last_sent = [x_low, y_top]
        x_low = swap(x_low, 2).astype(F32)
        y_top = swap(y_top, 4).astype(F32)
        top = self.x_top.astype(F32) + y_top
        low = x_low + self.y_low.astype(F32)
        return self.total0.astype(F32) + jnp.concatenate([top, low], axis=0)


def out_weight_routes(groups):
    return [(i, TEAM * (i % groups) + i // groups) for i in range(groups * TEAM)]


def rms_pull(value, gain, grad):
    scale = lax.rsqrt(jnp.mean(value * value, axis=-1, keepdims=True) + EPSILON)
    weighted = grad * gain
    mean = jnp.mean(weighted * value, axis=-1, keepdims=True)
    return scale * weighted - scale * scale * scale * value * mean


def rms(value, gain):
    return value * lax.rsqrt(jnp.mean(value * value, axis=-1, keepdims=True) + EPSILON) * gain


def struct(shape, dtype):
    return jax.ShapeDtypeStruct(shape, dtype)


def hold(arrays, tick):
    def kernel(*refs):
        del refs

    count = len(arrays)
    return pl.pallas_call(
        kernel,
        out_shape=[struct(a.shape, a.dtype) for a in arrays],
        in_specs=[ANY] * count + [ANY],
        out_specs=[ANY] * count,
        input_output_aliases={i: i for i in range(count)},
    )(*arrays, tick)


def mark(arrays):
    def kernel(*refs):
        refs[-1][...] = jnp.zeros_like(refs[-1])

    return pl.pallas_call(
        kernel,
        out_shape=struct((8, 128), jnp.int32),
        in_specs=[ANY] * len(arrays),
        out_specs=VMEM,
    )(*arrays)


def for_tiles(tiles, most, body):
    for m in range(1, most + 1):

        @pl.when(tiles == m)
        def _(m=m):
            body(m * TILE)


def turned(u, cosine, sine):
    return u * cosine + pltpu.roll(u, u.shape[-1] // 2, 1) * sine


def head_norm(u):
    return lax.rsqrt(jnp.mean(u * u, axis=-1, keepdims=True) + EPSILON)


def head_back(grad, raw, gain, cosine, sine):
    e = turned(grad, cosine, -sine)
    scale = head_norm(raw)
    weighted = e * gain
    mean = jnp.mean(weighted * raw, axis=-1, keepdims=True)
    back = scale * weighted - scale * scale * scale * raw * mean
    return back, jnp.sum(e * raw * scale, axis=0, keepdims=True)


def weights_of(query, key, factor):
    scores = product_nt(query, key) * factor
    n = scores.shape[0]
    causal = lax.broadcasted_iota(jnp.int32, (n, n), 1) <= lax.broadcasted_iota(jnp.int32, (n, n), 0)
    scores = jnp.where(causal, scores, -jnp.inf)
    terms = jnp.exp(scores - jnp.max(scores, axis=-1, keepdims=True))
    return terms * (1.0 / jnp.sum(terms, axis=-1, keepdims=True))


def rows_of(tile, size=TILE):
    return pl.ds(pl.multiple_of(tile * size, size), size)


def each_block(r, body):
    for k in range(TEAM):
        pl.when(r == k)(lambda k=k: body(k))


def attend(tiles, tokens, consts, mine, after):
    weight_attn, weight_head, weight_out, gain, gains, cosine, sine = consts
    rows, width = tokens[0].shape
    size = gains.shape[1]
    q_cols = mine * size
    cols = weight_attn.shape[1]
    factor = size ** (-0.5)

    def kernel(*refs):
        tiles_ref, toks = refs[0], refs[1 : 1 + TEAM]
        wa, wh, wo, gain_ref, gains_ref, cos_ref, sin_ref, _ = refs[1 + TEAM : 9 + TEAM]
        parts = refs[9 + TEAM : 9 + 2 * TEAM]
        normed_all, qkv_all, logit_all, gated_all, tick = refs[9 + 2 * TEAM : 14 + 2 * TEAM]
        (
            tok_v, wa_v, wh_v, wo_v, part_v, normed_v, qkv_v, logit_v, gated_v, w_sem, in_sem, out_sem,
        ) = refs[14 + 2 * TEAM :]
        tick[...] = jnp.zeros_like(tick)

        def load(k, slot):
            return pltpu.make_async_copy(toks[k], tok_v.at[slot], in_sem.at[slot])

        def store(r, slot, j, k=0):
            src = (part_v, normed_v, qkv_v, logit_v, gated_v)[j].at[slot]
            dst = parts[k] if j == 0 else (normed_all, qkv_all, logit_all, gated_all)[j - 1].at[rows_of(r, rows)]
            return pltpu.make_async_copy(src, dst, out_sem.at[j, slot])

        load(0, 0).start()
        weights = [
            pltpu.make_async_copy(src, dst, w_sem.at[j])
            for j, (src, dst) in enumerate(((wa, wa_v), (wh, wh_v), (wo, wo_v)))
        ]
        for copy in weights:
            copy.start()
        for copy in weights:
            copy.wait()

        def step(r, carry):
            slot = r % 2

            @pl.when(r + 1 < TEAM)
            def _():
                each_block(r + 1, lambda k: load(k, 1 - slot).start())

            load(0, slot).wait()

            @pl.when(r >= 2)
            def _():
                for j in range(5):
                    store(r - 2, slot, j).wait()

            def body(n):
                value = tok_v[slot, :n].astype(F32)
                normed = rms(value, gain_ref[...]).astype(BF16)
                normed_v[slot, :n] = normed
                qkv = product(normed, wa_v[...])
                qkv_v[slot, :n] = qkv
                logit = product_nt(normed, wh_v[...])
                logit_v[slot, :n] = logit
                cos, sin = cos_ref[:n], sin_ref[:n]
                key = qkv[:, q_cols : q_cols + size]
                key = turned(key * head_norm(key) * gains_ref[1:2], cos, sin).astype(BF16)
                values = qkv[:, q_cols + size :].astype(BF16)
                for h in range(mine):
                    query = qkv[:, h * size : (h + 1) * size]
                    query = turned(query * head_norm(query) * gains_ref[0:1], cos, sin).astype(BF16)
                    attention = weights_of(query, key, factor)
                    mixture = product(attention.astype(BF16), values)
                    gate = jax.nn.sigmoid(logit[:, h : h + 1])
                    gated_v[slot, :n, h * size : (h + 1) * size] = (mixture * gate).astype(BF16)
                part_v[slot, :n] = product(gated_v[slot, :n], wo_v[...]).astype(BF16)
                if n < rows:
                    part_v[slot, n:] = jnp.zeros((rows - n, width), BF16)
                    normed_v[slot, n:] = jnp.zeros((rows - n, width), BF16)
                    gated_v[slot, n:] = jnp.zeros((rows - n, q_cols), BF16)

            for_tiles(tiles_ref[r], rows // TILE, body)
            each_block(r, lambda k: store(r, slot, 0, k).start())
            for j in range(1, 5):
                store(r, slot, j).start()
            return carry

        lax.fori_loop(0, TEAM, step, 0)
        for r in (TEAM - 2, TEAM - 1):
            for j in range(5):
                store(r, r % 2, j).wait()

    whole = TEAM * rows
    result = pl.pallas_call(
        kernel,
        out_shape=[struct((rows, width), BF16)] * TEAM
        + [
            struct((whole, width), BF16),
            struct((whole, cols), F32),
            struct((whole, TILE), F32),
            struct((whole, q_cols), BF16),
            struct((8, 128), jnp.int32),
        ],
        in_specs=[SMEM] + [ANY] * (TEAM + 3) + [VMEM] * 4 + [ANY],
        out_specs=[ANY] * (TEAM + 4) + [VMEM],
        scratch_shapes=[
            pltpu.VMEM((2, rows, width), BF16),
            pltpu.VMEM(weight_attn.shape, BF16),
            pltpu.VMEM(weight_head.shape, BF16),
            pltpu.VMEM(weight_out.shape, BF16),
            pltpu.VMEM((2, rows, width), BF16),
            pltpu.VMEM((2, rows, width), BF16),
            pltpu.VMEM((2, rows, cols), F32),
            pltpu.VMEM((2, rows, TILE), F32),
            pltpu.VMEM((2, rows, q_cols), BF16),
            pltpu.SemaphoreType.DMA((3,)),
            pltpu.SemaphoreType.DMA((2,)),
            pltpu.SemaphoreType.DMA((5, 2)),
        ],
        compiler_params=pltpu.CompilerParams(vmem_limit_bytes=48 << 20),
        cost_estimate=pl.CostEstimate(flops=30 << 30, bytes_accessed=60 << 20, transcendentals=1 << 20),
    )(tiles, *tokens, weight_attn, weight_head, weight_out, gain, gains, cosine, sine, after)
    return result[:TEAM], result[TEAM : TEAM + 4], result[TEAM + 4]


def attend_back(tiles, hidden, consts, saved, mine, after):
    weight_attn, weight_head, weight_out, gain, gains, cosine, sine = consts
    rows, width = hidden[0].shape
    size = gains.shape[1]
    q_cols = mine * size
    cols = weight_attn.shape[1]
    factor = size ** (-0.5)

    def kernel(*refs):
        tiles_ref, hids = refs[0], refs[1 : 1 + TEAM]
        wa, wh, wo, normed_all, qkv_all, logit_all, gated_all = refs[1 + TEAM : 8 + TEAM]
        gains_ref, cos_ref, sin_ref, _ = refs[8 + TEAM : 12 + TEAM]
        parts = refs[12 + TEAM : 12 + 2 * TEAM]
        attn_part, head_sum, out_part, gain_sum, gains_sum = refs[12 + 2 * TEAM : 17 + 2 * TEAM]
        (
            hid_v, wa_v, wh_v, wo_v, normed_v, qkv_v, logit_v, gated_v, part_v, back_v, attn_sum, out_sum,
            w_sem, in_sem, out_sem,
        ) = refs[17 + 2 * TEAM :]

        def loads(r, slot, k):
            yield pltpu.make_async_copy(hids[k], hid_v.at[slot], in_sem.at[0, slot])
            here = rows_of(r, rows)
            for j, (src, dst) in enumerate(
                ((qkv_all, qkv_v), (logit_all, logit_v), (normed_all, normed_v), (gated_all, gated_v))
            ):
                yield pltpu.make_async_copy(src.at[here], dst.at[slot], in_sem.at[1 + j, slot])

        def start_loads(r, slot):
            def body(k):
                for copy in loads(r, slot, k):
                    copy.start()

            each_block(r, body)

        def store(slot, k=0):
            return pltpu.make_async_copy(part_v.at[slot], parts[k], out_sem.at[slot])

        for copy in loads(0, 0, 0):
            copy.start()
        weights = [
            pltpu.make_async_copy(src, dst, w_sem.at[j])
            for j, (src, dst) in enumerate(((wo, wo_v), (wa, wa_v), (wh, wh_v)))
        ]
        for copy in weights:
            copy.start()
        for ref in (attn_sum, out_sum, gain_sum, gains_sum):
            ref[...] = jnp.zeros_like(ref)
        for copy in weights:
            copy.wait()

        def step(r, carry):
            slot = r % 2

            @pl.when(r + 1 < TEAM)
            def _():
                start_loads(r + 1, 1 - slot)

            for copy in loads(r, slot, 0):
                copy.wait()

            @pl.when(r >= 2)
            def _():
                store(slot).wait()

            def body(n):
                hidden_low = hid_v[slot, :n]
                normed = normed_v[slot, :n]
                out_sum[...] += product_tn(gated_v[slot, :n], hidden_low)
                gated_grad = product_nt(hidden_low, wo_v[...])
                cos, sin = cos_ref[:n], sin_ref[:n]
                key_raw = qkv_v[slot, :n, q_cols : q_cols + size]
                key = turned(key_raw * head_norm(key_raw) * gains_ref[1:2], cos, sin).astype(BF16)
                values = qkv_v[slot, :n, q_cols + size :].astype(BF16)
                lane = lax.broadcasted_iota(jnp.int32, (n, TILE), 1)
                logit_back = jnp.zeros((n, TILE), F32)
                values_back = jnp.zeros((n, size), F32)
                key_grad = jnp.zeros((n, size), F32)
                query_sum = jnp.zeros((1, size), F32)
                for h in range(mine):
                    span = slice(h * size, (h + 1) * size)
                    query_raw = qkv_v[slot, :n, span]
                    query = turned(query_raw * head_norm(query_raw) * gains_ref[0:1], cos, sin).astype(BF16)
                    attention = weights_of(query, key, factor)
                    attention_low = attention.astype(BF16)
                    mixture = product(attention_low, values)
                    gate = jax.nn.sigmoid(logit_v[slot, :n, h : h + 1])
                    head_grad = gated_grad[:, span]
                    mixture_back = (head_grad * gate).astype(BF16)
                    one = jnp.sum(head_grad * mixture, axis=-1, keepdims=True) * gate * (1.0 - gate)
                    logit_back = jnp.where(lane == h, one, logit_back)
                    values_back += product_tn(attention_low, mixture_back)
                    attention_grad = product_nt(mixture_back, values)
                    scores_back = (
                        attention
                        * (attention_grad - jnp.sum(attention_grad * attention, axis=-1, keepdims=True))
                    ).astype(BF16)
                    query_grad = product(scores_back, key) * factor
                    key_grad += product_tn(scores_back, query)
                    back, total = head_back(query_grad, query_raw, gains_ref[0:1], cos, sin)
                    back_v[:n, span] = back.astype(BF16)
                    query_sum += total
                back, key_sum = head_back(key_grad * factor, key_raw, gains_ref[1:2], cos, sin)
                back_v[:n, q_cols : q_cols + size] = back.astype(BF16)
                back_v[:n, q_cols + size : cols] = values_back.astype(BF16)
                logit_back = logit_back.astype(BF16)
                back_v[:n, cols:] = logit_back
                gains_sum[0:1] += query_sum
                gains_sum[1:2] += key_sum
                part = product_nt(back_v[:n, :cols], wa_v[...]) + product(logit_back, wh_v[...])
                part_v[slot, :n] = part.astype(BF16)
                gain_sum[0:1] += jnp.sum(part * normed.astype(F32), axis=0, keepdims=True)
                attn_sum[...] += product_tn(back_v[:n], normed)
                if n < rows:
                    part_v[slot, n:] = jnp.zeros((rows - n, width), BF16)

            for_tiles(tiles_ref[r], rows // TILE, body)
            each_block(r, lambda k: store(slot, k).start())
            return carry

        lax.fori_loop(0, TEAM, step, 0)
        attn_part[...] = attn_sum[:cols].T.astype(BF16)
        head_sum[...] = attn_sum[cols : cols + 8]
        out_part[...] = out_sum[...].astype(BF16)
        store(0).wait()
        store(1).wait()

    result = pl.pallas_call(
        kernel,
        out_shape=[struct((rows, width), BF16)] * TEAM
        + [
            struct((width, cols), BF16),
            struct((8, width), F32),
            struct((q_cols, width), BF16),
            struct((8, width), F32),
            struct((8, size), F32),
        ],
        in_specs=[SMEM] + [ANY] * (TEAM + 7) + [VMEM] * 3 + [ANY],
        out_specs=[ANY] * TEAM + [VMEM] * 5,
        scratch_shapes=[
            pltpu.VMEM((2, rows, width), BF16),
            pltpu.VMEM(weight_attn.shape, BF16),
            pltpu.VMEM(weight_head.shape, BF16),
            pltpu.VMEM(weight_out.shape, BF16),
            pltpu.VMEM((2, rows, width), BF16),
            pltpu.VMEM((2, rows, cols), F32),
            pltpu.VMEM((2, rows, TILE), F32),
            pltpu.VMEM((2, rows, q_cols), BF16),
            pltpu.VMEM((2, rows, width), BF16),
            pltpu.VMEM((rows, cols + TILE), BF16),
            pltpu.VMEM((cols + TILE, width), F32),
            pltpu.VMEM((q_cols, width), F32),
            pltpu.SemaphoreType.DMA((3,)),
            pltpu.SemaphoreType.DMA((5, 2)),
            pltpu.SemaphoreType.DMA((2,)),
        ],
        compiler_params=pltpu.CompilerParams(vmem_limit_bytes=56 << 20),
        cost_estimate=pl.CostEstimate(flops=45 << 30, bytes_accessed=70 << 20, transcendentals=1 << 20),
    )(tiles, *hidden, weight_attn, weight_head, weight_out, *saved, gains, cosine, sine, after)
    return result[:TEAM], *result[TEAM : TEAM + 3], result[TEAM + 3][0], result[TEAM + 4][:2]


def tile_places(tiles_ref, rows):
    places, total = [], 0
    for r in range(TEAM):
        count = tiles_ref[r]
        for j in range(rows // TILE):
            places.append((r, j, j < count, total + j))
        total = total + count
    return places, total


def feed(tiles, twos, upstreams, weight_gate, weight_up, weight_down):
    rows, width = twos[0].shape
    ff_cols = weight_down.shape[0]
    whole = TEAM * rows
    chunk = 2 * TILE
    chunks = whole // chunk

    def kernel(*refs):
        tiles_ref, twos_ref, ups_ref = refs[0], refs[1 : 1 + TEAM], refs[1 + TEAM : 1 + 2 * TEAM]
        weights_ref = refs[1 + 2 * TEAM : 4 + 2 * TEAM]
        outs_ref = refs[4 + 2 * TEAM : 4 + 3 * TEAM]
        grads_ref = refs[4 + 3 * TEAM : 4 + 4 * TEAM]
        inner_all, back_all, two_all, ups_all = refs[4 + 4 * TEAM : 8 + 4 * TEAM]
        (
            two_v, ups_v, wg_v, wu_v, wd_v, inner_v, back_v, out_v, grad_v, zero_v,
            w_sem, load_sem, keep_sem, tile_sem, dead_sem,
        ) = refs[8 + 4 * TEAM :]
        places, total = tile_places(tiles_ref, rows)
        used = (total + 1) // 2

        def loads(sources, packed, which):
            for k, (r, j, live, place) in enumerate(places):
                yield live, pltpu.make_async_copy(
                    sources[r].at[rows_of(j)], packed.at[rows_of(place)], load_sem.at[which, k]
                )

        weights = [
            pltpu.make_async_copy(src, dst, w_sem.at[j])
            for j, (src, dst) in enumerate(zip(weights_ref, (wg_v, wu_v, wd_v)))
        ]
        for live, copy in loads(twos_ref, two_v, 0):
            pl.when(live)(copy.start)
        for copy in weights:
            copy.start()
        for live, copy in loads(ups_ref, ups_v, 1):
            pl.when(live)(copy.start)
        zero_v[...] = jnp.zeros_like(zero_v)

        def dead(k, r, j):
            zeros = zero_v.at[:TILE]
            yield pltpu.make_async_copy(zeros, grads_ref[r].at[rows_of(j)], dead_sem.at[0, k])
            yield pltpu.make_async_copy(zeros, outs_ref[r].at[rows_of(j)], dead_sem.at[1, k])

        for k, (r, j, live, place) in enumerate(places):

            @pl.when(jnp.logical_not(live))
            def _(k=k, r=r, j=j):
                for copy in dead(k, r, j):
                    copy.start()

        def keeps(c, sources):
            for j, (src, dst) in enumerate(zip(sources, (two_all, ups_all, inner_all, back_all))):
                yield pltpu.make_async_copy(src, dst.at[rows_of(c, chunk)], keep_sem.at[j, c])

        zeros = (zero_v, zero_v, zero_v.at[:, :ff_cols], zero_v.at[:, : 2 * ff_cols])
        for c in range(TEAM // 2, chunks):

            @pl.when(c >= used)
            def _(c=c):
                for copy in keeps(c, zeros):
                    copy.start()

        @pl.when(total % 2 == 1)
        def _():
            two_v[rows_of(total)] = jnp.zeros((TILE, width), BF16)
            ups_v[rows_of(total)] = jnp.zeros((TILE, width), BF16)

        for live, copy in loads(twos_ref, two_v, 0):
            pl.when(live)(copy.wait)
        for copy in weights:
            copy.wait()
        for live, copy in loads(ups_ref, ups_v, 1):
            pl.when(live)(copy.wait)

        def tile_stores(r, j, slot, side):
            here = pl.ds(side * TILE, TILE)
            yield pltpu.make_async_copy(
                grad_v.at[slot, here], grads_ref[r].at[rows_of(j)], tile_sem.at[0, slot, side]
            )
            yield pltpu.make_async_copy(
                out_v.at[slot, here], outs_ref[r].at[rows_of(j)], tile_sem.at[1, slot, side]
            )

        def wait_tiles(c, slot):
            for side in range(2):

                @pl.when(2 * c + side < total)
                def _(side=side):
                    for copy in tile_stores(0, 0, slot, side):
                        copy.wait()

        def body(c, carry):
            slot = c % 2
            span = rows_of(c, chunk)

            @pl.when(c >= 2)
            def _():
                wait_tiles(c - 2, slot)
                for j, copy in enumerate(keeps(c - 2, zeros)):
                    if j >= 2:
                        copy.wait()

            gate_part = product(two_v[span], wg_v[...])
            up_part = product(two_v[span], wu_v[...])
            sig = jax.nn.sigmoid(gate_part)
            silu = gate_part * sig
            inner_v[slot] = (silu * up_part).astype(BF16)
            inner_grad = product_nt(ups_v[span], wd_v[...])
            back_v[slot, :, :ff_cols] = (inner_grad * up_part * (sig + silu * (1.0 - sig))).astype(BF16)
            back_v[slot, :, ff_cols:] = (inner_grad * silu).astype(BF16)
            for copy in keeps(c, (two_v.at[span], ups_v.at[span], inner_v.at[slot], back_v.at[slot])):
                copy.start()
            grad = product_nt(back_v[slot, :, :ff_cols], wg_v[...]) + product_nt(
                back_v[slot, :, ff_cols:], wu_v[...]
            )
            grad_v[slot] = grad.astype(BF16)
            out_v[slot] = product(inner_v[slot], wd_v[...]).astype(BF16)
            for k, (r, j, live, place) in enumerate(places):
                for side in range(2):

                    @pl.when(jnp.logical_and(live, place == 2 * c + side))
                    def _(r=r, j=j, side=side):
                        for copy in tile_stores(r, j, slot, side):
                            copy.start()

            return carry

        lax.fori_loop(0, used, body, 0)
        wait_tiles(used - 2, used % 2)
        wait_tiles(used - 1, (used - 1) % 2)
        for k, (r, j, live, place) in enumerate(places):

            @pl.when(jnp.logical_not(live))
            def _(k=k, r=r, j=j):
                for copy in dead(k, r, j):
                    copy.wait()

        for c in range(chunks):
            for j, copy in enumerate(keeps(c, zeros)):
                if j < 2:
                    copy.wait()
                else:
                    pl.when(c >= used - 2)(copy.wait)

    count = whole // TILE
    result = pl.pallas_call(
        kernel,
        out_shape=[struct((rows, width), BF16)] * (2 * TEAM)
        + [
            struct((whole, ff_cols), BF16),
            struct((whole, 2 * ff_cols), BF16),
            struct((whole, width), BF16),
            struct((whole, width), BF16),
        ],
        in_specs=[SMEM] + [ANY] * (3 + 2 * TEAM),
        out_specs=[ANY] * (2 * TEAM + 4),
        scratch_shapes=[
            pltpu.VMEM((whole, width), BF16),
            pltpu.VMEM((whole, width), BF16),
            pltpu.VMEM(weight_gate.shape, BF16),
            pltpu.VMEM(weight_up.shape, BF16),
            pltpu.VMEM(weight_down.shape, BF16),
            pltpu.VMEM((2, chunk, ff_cols), BF16),
            pltpu.VMEM((2, chunk, 2 * ff_cols), BF16),
            pltpu.VMEM((2, chunk, width), BF16),
            pltpu.VMEM((2, chunk, width), BF16),
            pltpu.VMEM((chunk, width), BF16),
            pltpu.SemaphoreType.DMA((3,)),
            pltpu.SemaphoreType.DMA((2, count)),
            pltpu.SemaphoreType.DMA((4, chunks)),
            pltpu.SemaphoreType.DMA((2, 2, 2)),
            pltpu.SemaphoreType.DMA((2, count)),
        ],
        compiler_params=pltpu.CompilerParams(vmem_limit_bytes=60 << 20),
        cost_estimate=pl.CostEstimate(flops=58 << 30, bytes_accessed=100 << 20, transcendentals=1 << 20),
    )(tiles, *twos, *upstreams, weight_gate, weight_up, weight_down)
    return result[:TEAM], result[TEAM : 2 * TEAM], result[2 * TEAM :]


def local(
    groups,
    tokens,
    lengths,
    cotangent,
    attention_gain,
    query_weight,
    key_matrix,
    value_matrix,
    head_gate_weight,
    output_weight,
    query_key_gain,
    feedforward_gain,
    gate_weight,
    up_weight,
    down_weight,
):
    t = member()
    everyone = groups * TEAM
    rows, width = tokens.shape
    rho = query_weight.shape[0]
    phi = down_weight.shape[0]
    ff = gate_weight.shape[1]
    pair_cols = query_key_gain.shape[1]
    size = pair_cols * everyone
    heads = query_weight.shape[1] // size
    mine = heads // TEAM
    q_cols = query_weight.shape[1] // TEAM
    k_cols = key_matrix.shape[1] // TEAM
    ff_cols = ff // TEAM

    def everyone_in_team(vector):
        return jnp.broadcast_to(vector.reshape(1, -1), (TEAM, vector.size))

    live_tiles = (lengths + (TILE - 1)) // TILE
    row = jnp.concatenate(
        [
            head_gate_weight.reshape(rho, TEAM, mine).transpose(1, 2, 0).reshape(TEAM, -1),
            everyone_in_team(attention_gain),
            everyone_in_team(feedforward_gain),
            everyone_in_team(query_key_gain),
            everyone_in_team(live_tiles.astype(BF16)),
        ],
        axis=1,
    )
    cols = q_cols + 2 * k_cols
    row = jnp.pad(row, ((0, 0), (0, cols - row.shape[1])))[:, None, :]
    attn = jnp.concatenate(
        [
            query_weight.reshape(rho, TEAM, q_cols),
            key_matrix.reshape(rho, TEAM, k_cols),
            value_matrix.reshape(rho, TEAM, k_cols),
        ],
        axis=2,
    ).transpose(1, 0, 2)
    attn = jnp.concatenate([attn, jnp.pad(row, ((0, 0), (0, 7), (0, 0)))], axis=1)
    attn = exchange(attn)
    head_lanes = mine * rho
    at_one, at_two, at_pair = head_lanes, head_lanes + rho, head_lanes + 2 * rho
    at_tiles = at_pair + 2 * pair_cols
    team_tiles = attn[:, rho, at_tiles].astype(jnp.int32)
    order = jnp.arange(TEAM, dtype=jnp.int32)
    tiles = jnp.sum(jnp.where((order[:, None] ^ t) == order[None, :], team_tiles[None, :], 0), axis=1)
    routed = lax.ppermute(output_weight, ALL, out_weight_routes(groups))
    team_rows = TEAM * (rho + 8)
    attn = jnp.concatenate([attn.reshape(team_rows, cols), routed.reshape(-1, cols)], axis=0)
    attn = line_gather(attn).reshape(groups, -1, cols)
    weight_out = attn[:, team_rows:].reshape(-1, width)
    attn = attn[:, :team_rows].reshape(everyone, rho + 8, cols)
    weight_attn = attn[:, :rho].reshape(width, cols)
    rows_small = attn[:, rho]
    weight_head = jnp.pad(
        rows_small[:, :head_lanes].reshape(everyone, mine, rho).transpose(1, 0, 2).reshape(mine, width),
        ((0, TILE - mine), (0, 0)),
    )
    gain_one = rows_small[:, at_one:at_two].reshape(1, width).astype(F32)
    gain_two = rows_small[:, at_two:at_pair].reshape(1, width).astype(F32)
    gain_pair = (
        rows_small[:, at_pair:at_tiles]
        .reshape(everyone, 2, pair_cols)
        .transpose(1, 0, 2)
        .reshape(2, size)
        .astype(F32)
    )
    def ff_split(w):
        return w.reshape(rho, groups, TEAM, phi).transpose(2, 0, 1, 3).reshape(TEAM, rho, ff_cols)

    feed_shard = jnp.concatenate([ff_split(gate_weight), ff_split(up_weight)], axis=2)

    exponent = jnp.arange(size // 2, dtype=F32) * (-2.0 / size)
    frequency = jnp.power(ROPE_BASE, exponent)
    angles = jnp.arange(rows, dtype=F32)[:, None] * frequency[None, :]
    cosine = jnp.concatenate([jnp.cos(angles), jnp.cos(angles)], axis=1)
    sine = jnp.concatenate([-jnp.sin(angles), jnp.sin(angles)], axis=1)
    consts = (weight_attn, weight_head, weight_out, gain_one, gain_pair, cosine, sine)
    team_tokens = team_gather(tokens)
    feed_shard = exchange(hold([feed_shard], team_tokens[6])[0]).reshape(TEAM * rho, -1)
    weight_gate = line_gather(feed_shard[:, :ff_cols])
    live = lax.broadcasted_iota(jnp.int32, (rows, 1), 0) < lengths[0]
    live_rows = live.astype(F32)
    upstream = cotangent.astype(F32) * live_rows
    tick = mark([team_tokens[6]])
    later = lax.broadcasted_iota(jnp.int32, (rows, 1), 0) < lengths[0] + tick[0, 0]
    upstream_low = jnp.where(later, cotangent, jnp.zeros_like(cotangent))
    upstream_levels = TeamGather(upstream_low)
    parts, kept, tick = attend(tiles, team_tokens, consts, mine, mark([upstream_low]))
    normed, qkv, logit, gated = kept
    weight_up = line_gather(hold([feed_shard[:, ff_cols:]], tick)[0])
    parts = hold(parts, mark([upstream_levels.a1, upstream_levels.a2, upstream_levels.a4, tick]))
    arrived = TeamSum(parts)
    arrived.first()
    weight_down = line_gather(hold([down_weight], arrived.low6)[0])
    inputs = tokens.astype(F32)
    hidden_state = inputs + arrived.total(weight_gate)
    team_upstream = upstream_levels.blocks(mark(arrived.last_sent))

    normed_two = rms(hidden_state, gain_two).astype(BF16)
    team_two = TeamGather(normed_two).blocks(mark(team_upstream + [weight_up]))
    outs, grads, saved = feed(tiles, team_two, team_upstream, weight_gate, weight_up, weight_down)
    inner, feed_back, two_all, ups_all = saved
    arrived = TeamSum(grads)
    arrived.first()
    two_grad = arrived.total()
    down_part = product_tn(inner, ups_all).astype(BF16)
    feed_back = hold([feed_back], mark([arrived.x_top, arrived.y_low]))[0]
    gate_part = product_tn(two_all, feed_back[:, :ff_cols]).astype(BF16)
    up_part = product_tn(two_all, feed_back[:, ff_cols:]).astype(BF16)
    parts_made = mark([gate_part, up_part])
    down_grad = line_sum(down_part)
    gate_grad = line_sum(hold([gate_part], down_grad)[0])
    up_grad = line_sum(hold([up_part], gate_grad)[0])
    feed_done = up_grad
    hidden_grad = upstream + rms_pull(hidden_state, gain_two, two_grad)

    fed = TeamSum(outs)
    team_hidden = TeamGather(hidden_grad.astype(BF16)).blocks(mark(fed.ready + [gate_part, up_part]))
    two_scale = lax.rsqrt(jnp.mean(hidden_state * hidden_state, axis=-1, keepdims=True) + EPSILON)
    two_sum = jnp.sum(two_grad * hidden_state * two_scale, axis=0)
    first_hop = fed.first(mark(team_hidden + [parts_made]))
    parts, attn_part, head_sum, out_part, one_sum, pair_sum = attend_back(
        tiles, team_hidden, consts, (normed, qkv, logit, gated), mine, mark(fed.sent + [down_grad])
    )
    row = jnp.concatenate(
        [
            head_sum[:mine].reshape(mine, everyone, rho).transpose(1, 0, 2).reshape(everyone, -1),
            (one_sum / gain_one[0]).reshape(everyone, rho),
            two_sum.reshape(everyone, rho),
            pair_sum.reshape(2, everyone, pair_cols).transpose(1, 0, 2).reshape(everyone, -1),
        ],
        axis=1,
    ).astype(BF16)
    row = jnp.pad(row, ((0, 0), (0, cols - row.shape[1])))[:, None, :]
    packed = jnp.concatenate(
        [attn_part.reshape(everyone, rho, cols), jnp.pad(row, ((0, 0), (0, 7), (0, 0)))], axis=1
    )
    packed = jnp.concatenate(
        [packed.reshape(groups, team_rows, cols), out_part.reshape(groups, -1, cols)], axis=1
    )
    parts = hold(parts, mark(first_hop + [gate_grad]))
    arrived = TeamSum(parts)
    arrived.first()
    packed = hold([packed.reshape(-1, cols)], mark([feed_done, arrived.u4, arrived.u2] + arrived.sent))[0]
    normed_grad = arrived.total(packed)
    packed = line_sum(packed)
    layer_output = ((hidden_state + fed.total()) * live_rows).astype(BF16)
    tokens_grad = (hidden_grad + rms_pull(inputs, gain_one, normed_grad)).astype(BF16)
    routes = [(user, owner) for owner, user in out_weight_routes(groups)]
    output_grad = lax.ppermute(packed[team_rows:].reshape(rho, width), ALL, routes)
    packed = exchange(packed[:team_rows].reshape(TEAM, rho + 8, cols))
    feed_grad = jnp.concatenate([gate_grad, hold([up_grad], arrived.u4)[0]], axis=1)
    feed_grad = exchange(feed_grad.reshape(TEAM, rho, 2 * ff_cols))

    def ff_join(w):
        return w.reshape(TEAM, rho, groups, phi).transpose(1, 2, 0, 3).reshape(rho, ff)

    gate_grad, up_grad = hold(
        [ff_join(feed_grad[:, :, :ff_cols]), ff_join(feed_grad[:, :, ff_cols:])], normed_grad
    )
    attn_grad = packed[:, :rho].transpose(1, 0, 2)
    rows_small = packed[:, rho].astype(F32)
    sums = jnp.sum(rows_small[:, head_lanes:], axis=0)
    head_gate_grad = rows_small[:, :head_lanes].reshape(heads, rho).T
    return (
        layer_output,
        tokens_grad,
        sums[:rho],
        attn_grad[:, :, :q_cols].reshape(rho, -1).astype(F32),
        attn_grad[:, :, q_cols : q_cols + k_cols].reshape(rho, -1).astype(F32),
        attn_grad[:, :, q_cols + k_cols :].reshape(rho, -1).astype(F32),
        head_gate_grad,
        output_grad.astype(F32),
        sums[2 * rho : 2 * rho + 2 * pair_cols].reshape(2, pair_cols),
        sums[rho : 2 * rho],
        gate_grad.astype(F32),
        up_grad.astype(F32),
        down_grad.astype(F32),
    )


def solution(mesh):
    groups = mesh.size // TEAM
    rows, vector, columns = P(ALL, None), P(ALL), P(None, ALL)

    def step(*args):
        return local(groups, *args)

    return jax.shard_map(
        step,
        mesh=mesh,
        in_specs=(
            rows, vector, rows, vector, rows, rows, rows, rows, rows, columns, vector, rows, rows, rows,
        ),
        out_specs=(
            rows, rows, vector, rows, rows, rows, rows, rows, columns, vector, rows, rows, rows,
        ),
        check_vma=False,
    )
```

```python
import jax
import jax.numpy as jnp
from jax import lax
from jax.experimental import pallas as pl
from jax.experimental.pallas import tpu as pltpu
from jax.sharding import PartitionSpec as P

EPSILON = 1e-06
ROPE_BASE = 1000000.0
TEAM = 8
ALL = ("dp", "fsdp")
F32 = jnp.float32
BF16 = jnp.bfloat16
TILE = 128
ANY = pl.BlockSpec(memory_space=pl.ANY)
VMEM = pl.BlockSpec(memory_space=pltpu.VMEM)
SMEM = pl.BlockSpec(memory_space=pltpu.SMEM)


def product(left, right):
    return jnp.dot(left, right, preferred_element_type=F32)


def product_nt(left, right):
    return lax.dot_general(left, right, (((1,), (1,)), ((), ())), preferred_element_type=F32)


def product_tn(left, right):
    return lax.dot_general(left, right, (((0,), (0,)), ((), ())), preferred_element_type=F32)


def world():
    return lax.axis_size(ALL)


def member():
    return lax.axis_index(ALL) % TEAM


def teams():
    return [[first + t for t in range(TEAM)] for first in range(0, world(), TEAM)]


def lines():
    return [list(range(t, world(), TEAM)) for t in range(TEAM)]


def permute(array, pairs):
    return lax.ppermute(
        array, ALL, [(team[a], team[b]) for team in teams() for a, b in pairs]
    )


def swap(array, bits):
    return permute(array, [(i, i ^ bits) for i in range(TEAM)])


def exchange(blocks):
    if lax.axis_size("fsdp") == TEAM:
        return lax.all_to_all(blocks, "fsdp", 0, 0, tiled=True)
    return lax.all_to_all(blocks, ALL, 0, 0, tiled=True, axis_index_groups=teams())


def line_gather(shard):
    if lax.axis_size("fsdp") == TEAM:
        return lax.all_gather(shard, "dp", axis=0, tiled=True)
    return lax.all_gather(shard, ALL, axis=0, tiled=True, axis_index_groups=lines())


def line_sum(array):
    if lax.axis_size("fsdp") == TEAM:
        return lax.psum_scatter(array, "dp", scatter_dimension=0, tiled=True)
    return lax.psum_scatter(array, ALL, scatter_dimension=0, tiled=True, axis_index_groups=lines())


class TeamGather:
    def __init__(self, own):
        self.own = own
        self.a1 = swap(own, 1)
        self.a2 = swap(own, 2)
        self.a4 = swap(own, 4)

    def blocks(self, tick=None):
        a2, a4 = self.a2, self.a4
        if tick is not None:
            a2, a4 = hold([a2, a4], tick)
        half = self.own.shape[0] // 2
        a6 = jnp.concatenate([swap(a4[:half], 2), swap(a2[half:], 4)], axis=0)
        return [self.own, self.a1, a2, swap(a2, 1), a4, swap(a4, 1), a6, swap(a6, 1)]


def team_gather(own):
    return TeamGather(own).blocks()


class TeamSum:
    def __init__(self, parts):
        half = parts[0].shape[0] // 2
        odd = {r: swap(parts[r + 1], 1) for r in (6, 2, 4, 0)}
        self.total6, self.total2, self.total4, self.total0 = (
            (parts[r].astype(F32) + odd[r].astype(F32)).astype(BF16) for r in (6, 2, 4, 0)
        )
        self.half = half
        self.low6 = self.total6
        self.ready = [self.low6, self.total2[:half], self.total4[half:]]

    def first(self, tick=None):
        half = self.half
        low6, x_top, y_low = self.ready if tick is None else hold(self.ready, tick)
        self.u4 = swap(low6[:half], 2)
        self.u2 = swap(low6[half:], 4)
        self.x_top = swap(x_top, 2)
        self.y_low = swap(y_low, 4)
        self.sent = [low6, x_top, y_low]
        return [self.u4, self.u2, self.x_top, self.y_low]

    def total(self, tick=None):
        half = self.half
        lasts = [
            (self.total2[half:].astype(F32) + self.u2.astype(F32)).astype(BF16),
            (self.total4[:half].astype(F32) + self.u4.astype(F32)).astype(BF16),
        ]
        x_low, y_top = lasts if tick is None else hold(lasts, tick)
        self.last_sent = [x_low, y_top]
        x_low = swap(x_low, 2).astype(F32)
        y_top = swap(y_top, 4).astype(F32)
        top = self.x_top.astype(F32) + y_top
        low = x_low + self.y_low.astype(F32)
        return self.total0.astype(F32) + jnp.concatenate([top, low], axis=0)


def out_weight_routes(groups):
    return [(i, TEAM * (i % groups) + i // groups) for i in range(groups * TEAM)]


def rms_pull(value, gain, grad):
    scale = lax.rsqrt(jnp.mean(value * value, axis=-1, keepdims=True) + EPSILON)
    weighted = grad * gain
    mean = jnp.mean(weighted * value, axis=-1, keepdims=True)
    return scale * weighted - scale * scale * scale * value * mean


def rms(value, gain):
    return value * lax.rsqrt(jnp.mean(value * value, axis=-1, keepdims=True) + EPSILON) * gain


def struct(shape, dtype):
    return jax.ShapeDtypeStruct(shape, dtype)


def hold(arrays, tick):
    def kernel(*refs):
        del refs

    count = len(arrays)
    return pl.pallas_call(
        kernel,
        out_shape=[struct(a.shape, a.dtype) for a in arrays],
        in_specs=[ANY] * count + [ANY],
        out_specs=[ANY] * count,
        input_output_aliases={i: i for i in range(count)},
    )(*arrays, tick)


def mark(arrays):
    def kernel(*refs):
        refs[-1][...] = jnp.zeros_like(refs[-1])

    return pl.pallas_call(
        kernel,
        out_shape=struct((8, 128), jnp.int32),
        in_specs=[ANY] * len(arrays),
        out_specs=VMEM,
    )(*arrays)


def for_tiles(tiles, most, body):
    for m in range(1, most + 1):

        @pl.when(tiles == m)
        def _(m=m):
            body(m * TILE)


def turned(u, cosine, sine):
    return u * cosine + pltpu.roll(u, u.shape[-1] // 2, 1) * sine


def head_norm(u):
    return lax.rsqrt(jnp.mean(u * u, axis=-1, keepdims=True) + EPSILON)


def head_back(grad, raw, gain, cosine, sine):
    e = turned(grad, cosine, -sine)
    scale = head_norm(raw)
    weighted = e * gain
    mean = jnp.mean(weighted * raw, axis=-1, keepdims=True)
    back = scale * weighted - scale * scale * scale * raw * mean
    return back, jnp.sum(e * raw * scale, axis=0, keepdims=True)


def weights_of(query, key, factor):
    scores = product_nt(query, key) * factor
    n = scores.shape[0]
    causal = lax.broadcasted_iota(jnp.int32, (n, n), 1) <= lax.broadcasted_iota(jnp.int32, (n, n), 0)
    scores = jnp.where(causal, scores, -jnp.inf)
    terms = jnp.exp(scores - jnp.max(scores, axis=-1, keepdims=True))
    return terms * (1.0 / jnp.sum(terms, axis=-1, keepdims=True))


def rows_of(tile, size=TILE):
    return pl.ds(pl.multiple_of(tile * size, size), size)


def each_block(r, body):
    for k in range(TEAM):
        pl.when(r == k)(lambda k=k: body(k))


def load_weights(gathered, weight_head, wa_v, wo_v, wh_v, sems):
    groups, _, cols = gathered.shape
    width = wo_v.shape[1]
    rho = width // (groups * TEAM)
    copies = [pltpu.make_async_copy(weight_head, wh_v, sems.at[0])]
    for g in range(groups):
        copies.append(
            pltpu.make_async_copy(
                gathered.at[g, pl.ds(0, TEAM * rho)],
                wa_v.at[pl.ds(g * TEAM * rho, TEAM * rho)],
                sems.at[len(copies)],
            )
        )
        for k in range(width // cols):
            copies.append(
                pltpu.make_async_copy(
                    gathered.at[g, pl.ds(TEAM * rho + k * rho, rho)],
                    wo_v.at[pl.ds(g * rho, rho), pl.ds(k * cols, cols)],
                    sems.at[len(copies)],
                )
            )
    return copies


def attend(tiles, tokens, consts, mine, after):
    gathered, weight_head, gain, gains, cosine, sine = consts
    rows, width = tokens[0].shape
    size = gains.shape[1]
    q_cols = mine * size
    cols = gathered.shape[2]
    factor = size ** (-0.5)

    def kernel(*refs):
        tiles_ref, toks = refs[0], refs[1 : 1 + TEAM]
        wa, wh, gain_ref, gains_ref, cos_ref, sin_ref, _ = refs[1 + TEAM : 8 + TEAM]
        parts = refs[8 + TEAM : 8 + 2 * TEAM]
        normed_all, qkv_all, logit_all, gated_all, tick = refs[8 + 2 * TEAM : 13 + 2 * TEAM]
        (
            tok_v, wa_v, wh_v, wo_v, part_v, normed_v, qkv_v, logit_v, gated_v, w_sem, in_sem, out_sem,
        ) = refs[13 + 2 * TEAM :]
        tick[...] = jnp.zeros_like(tick)

        def load(k, slot):
            return pltpu.make_async_copy(toks[k], tok_v.at[slot], in_sem.at[slot])

        def store(r, slot, j, k=0):
            src = (part_v, normed_v, qkv_v, logit_v, gated_v)[j].at[slot]
            dst = parts[k] if j == 0 else (normed_all, qkv_all, logit_all, gated_all)[j - 1].at[rows_of(r, rows)]
            return pltpu.make_async_copy(src, dst, out_sem.at[j, slot])

        load(0, 0).start()
        weights = load_weights(wa, wh, wa_v, wo_v, wh_v, w_sem)
        for copy in weights:
            copy.start()
        for copy in weights:
            copy.wait()

        def step(r, carry):
            slot = r % 2

            @pl.when(r + 1 < TEAM)
            def _():
                each_block(r + 1, lambda k: load(k, 1 - slot).start())

            load(0, slot).wait()

            @pl.when(r >= 2)
            def _():
                for j in range(5):
                    store(r - 2, slot, j).wait()

            def body(n):
                value = tok_v[slot, :n].astype(F32)
                normed = rms(value, gain_ref[...]).astype(BF16)
                normed_v[slot, :n] = normed
                qkv = product(normed, wa_v[...])
                qkv_v[slot, :n] = qkv
                logit = product_nt(normed, wh_v[...])
                logit_v[slot, :n] = logit
                cos, sin = cos_ref[:n], sin_ref[:n]
                key = qkv[:, q_cols : q_cols + size]
                key = turned(key * head_norm(key) * gains_ref[1:2], cos, sin).astype(BF16)
                values = qkv[:, q_cols + size :].astype(BF16)
                for h in range(mine):
                    query = qkv[:, h * size : (h + 1) * size]
                    query = turned(query * head_norm(query) * gains_ref[0:1], cos, sin).astype(BF16)
                    attention = weights_of(query, key, factor)
                    mixture = product(attention.astype(BF16), values)
                    gate = jax.nn.sigmoid(logit[:, h : h + 1])
                    gated_v[slot, :n, h * size : (h + 1) * size] = (mixture * gate).astype(BF16)
                part_v[slot, :n] = product(gated_v[slot, :n], wo_v[...]).astype(BF16)
                if n < rows:
                    part_v[slot, n:] = jnp.zeros((rows - n, width), BF16)
                    normed_v[slot, n:] = jnp.zeros((rows - n, width), BF16)
                    gated_v[slot, n:] = jnp.zeros((rows - n, q_cols), BF16)

            for_tiles(tiles_ref[r], rows // TILE, body)
            each_block(r, lambda k: store(r, slot, 0, k).start())
            for j in range(1, 5):
                store(r, slot, j).start()
            return carry

        lax.fori_loop(0, TEAM, step, 0)
        for r in (TEAM - 2, TEAM - 1):
            for j in range(5):
                store(r, r % 2, j).wait()

    whole = TEAM * rows
    result = pl.pallas_call(
        kernel,
        out_shape=[struct((rows, width), BF16)] * TEAM
        + [
            struct((whole, width), BF16),
            struct((whole, cols), F32),
            struct((whole, TILE), F32),
            struct((whole, q_cols), BF16),
            struct((8, 128), jnp.int32),
        ],
        in_specs=[SMEM] + [ANY] * (TEAM + 2) + [VMEM] * 4 + [ANY],
        out_specs=[ANY] * (TEAM + 4) + [VMEM],
        scratch_shapes=[
            pltpu.VMEM((2, rows, width), BF16),
            pltpu.VMEM((width, cols), BF16),
            pltpu.VMEM(weight_head.shape, BF16),
            pltpu.VMEM((q_cols, width), BF16),
            pltpu.VMEM((2, rows, width), BF16),
            pltpu.VMEM((2, rows, width), BF16),
            pltpu.VMEM((2, rows, cols), F32),
            pltpu.VMEM((2, rows, TILE), F32),
            pltpu.VMEM((2, rows, q_cols), BF16),
            pltpu.SemaphoreType.DMA((1 + gathered.shape[0] * (1 + width // cols),)),
            pltpu.SemaphoreType.DMA((2,)),
            pltpu.SemaphoreType.DMA((5, 2)),
        ],
        compiler_params=pltpu.CompilerParams(vmem_limit_bytes=48 << 20),
        cost_estimate=pl.CostEstimate(flops=30 << 30, bytes_accessed=60 << 20, transcendentals=1 << 20),
    )(tiles, *tokens, gathered, weight_head, gain, gains, cosine, sine, after)
    return result[:TEAM], result[TEAM : TEAM + 4], result[TEAM + 4]


def attend_back(tiles, hidden, consts, saved, mine, after):
    gathered, weight_head, gain, gains, cosine, sine = consts
    rows, width = hidden[0].shape
    size = gains.shape[1]
    q_cols = mine * size
    cols = gathered.shape[2]
    factor = size ** (-0.5)

    def kernel(*refs):
        tiles_ref, hids = refs[0], refs[1 : 1 + TEAM]
        wa, wh, normed_all, qkv_all, logit_all, gated_all = refs[1 + TEAM : 7 + TEAM]
        gains_ref, cos_ref, sin_ref, _ = refs[7 + TEAM : 11 + TEAM]
        parts = refs[11 + TEAM : 11 + 2 * TEAM]
        packed, head_sum, gain_sum, gains_sum = refs[11 + 2 * TEAM : 15 + 2 * TEAM]
        (
            hid_v, wa_v, wh_v, wo_v, normed_v, qkv_v, logit_v, gated_v, part_v, back_v, attn_sum, out_sum,
            w_sem, in_sem, out_sem,
        ) = refs[15 + 2 * TEAM :]

        def loads(r, slot, k):
            yield pltpu.make_async_copy(hids[k], hid_v.at[slot], in_sem.at[0, slot])
            here = rows_of(r, rows)
            for j, (src, dst) in enumerate(
                ((qkv_all, qkv_v), (logit_all, logit_v), (normed_all, normed_v), (gated_all, gated_v))
            ):
                yield pltpu.make_async_copy(src.at[here], dst.at[slot], in_sem.at[1 + j, slot])

        def start_loads(r, slot):
            def body(k):
                for copy in loads(r, slot, k):
                    copy.start()

            each_block(r, body)

        def store(slot, k=0):
            return pltpu.make_async_copy(part_v.at[slot], parts[k], out_sem.at[slot])

        for copy in loads(0, 0, 0):
            copy.start()
        weights = load_weights(wa, wh, wa_v, wo_v, wh_v, w_sem)
        for copy in weights:
            copy.start()
        for ref in (attn_sum, out_sum, gain_sum, gains_sum):
            ref[...] = jnp.zeros_like(ref)
        for copy in weights:
            copy.wait()

        def step(r, carry):
            slot = r % 2

            @pl.when(r + 1 < TEAM)
            def _():
                start_loads(r + 1, 1 - slot)

            for copy in loads(r, slot, 0):
                copy.wait()

            @pl.when(r >= 2)
            def _():
                store(slot).wait()

            def body(n):
                hidden_low = hid_v[slot, :n]
                normed = normed_v[slot, :n]
                out_sum[...] += product_tn(gated_v[slot, :n], hidden_low)
                gated_grad = product_nt(hidden_low, wo_v[...])
                cos, sin = cos_ref[:n], sin_ref[:n]
                key_raw = qkv_v[slot, :n, q_cols : q_cols + size]
                key = turned(key_raw * head_norm(key_raw) * gains_ref[1:2], cos, sin).astype(BF16)
                values = qkv_v[slot, :n, q_cols + size :].astype(BF16)
                lane = lax.broadcasted_iota(jnp.int32, (n, TILE), 1)
                logit_back = jnp.zeros((n, TILE), F32)
                values_back = jnp.zeros((n, size), F32)
                key_grad = jnp.zeros((n, size), F32)
                query_sum = jnp.zeros((1, size), F32)
                for h in range(mine):
                    span = slice(h * size, (h + 1) * size)
                    query_raw = qkv_v[slot, :n, span]
                    query = turned(query_raw * head_norm(query_raw) * gains_ref[0:1], cos, sin).astype(BF16)
                    attention = weights_of(query, key, factor)
                    attention_low = attention.astype(BF16)
                    mixture = product(attention_low, values)
                    gate = jax.nn.sigmoid(logit_v[slot, :n, h : h + 1])
                    head_grad = gated_grad[:, span]
                    mixture_back = (head_grad * gate).astype(BF16)
                    one = jnp.sum(head_grad * mixture, axis=-1, keepdims=True) * gate * (1.0 - gate)
                    logit_back = jnp.where(lane == h, one, logit_back)
                    values_back += product_tn(attention_low, mixture_back)
                    attention_grad = product_nt(mixture_back, values)
                    scores_back = (
                        attention
                        * (attention_grad - jnp.sum(attention_grad * attention, axis=-1, keepdims=True))
                    ).astype(BF16)
                    query_grad = product(scores_back, key) * factor
                    key_grad += product_tn(scores_back, query)
                    back, total = head_back(query_grad, query_raw, gains_ref[0:1], cos, sin)
                    back_v[:n, span] = back.astype(BF16)
                    query_sum += total
                back, key_sum = head_back(key_grad * factor, key_raw, gains_ref[1:2], cos, sin)
                back_v[:n, q_cols : q_cols + size] = back.astype(BF16)
                back_v[:n, q_cols + size : cols] = values_back.astype(BF16)
                logit_back = logit_back.astype(BF16)
                back_v[:n, cols:] = logit_back
                gains_sum[0:1] += query_sum
                gains_sum[1:2] += key_sum
                part = product_nt(back_v[:n, :cols], wa_v[...]) + product(logit_back, wh_v[...])
                part_v[slot, :n] = part.astype(BF16)
                gain_sum[0:1] += jnp.sum(part * normed.astype(F32), axis=0, keepdims=True)
                attn_sum[...] += product_tn(back_v[:n], normed)
                if n < rows:
                    part_v[slot, n:] = jnp.zeros((rows - n, width), BF16)

            for_tiles(tiles_ref[r], rows // TILE, body)
            each_block(r, lambda k: store(slot, k).start())
            return carry

        lax.fori_loop(0, TEAM, step, 0)
        head_sum[...] = attn_sum[cols : cols + 8]
        turned_sum = attn_sum[:cols].T.astype(BF16)
        groups, height, _ = packed.shape
        rho = width // (groups * TEAM)
        for g in range(groups):
            packed[g, : TEAM * rho] = turned_sum[g * TEAM * rho : (g + 1) * TEAM * rho]
            for k in range(width // cols):
                top = TEAM * rho + k * rho
                packed[g, top : top + rho] = out_sum[
                    g * rho : (g + 1) * rho, k * cols : (k + 1) * cols
                ].astype(BF16)
            packed[g, height - 16 :] = jnp.zeros((16, cols), BF16)
        store(0).wait()
        store(1).wait()

    result = pl.pallas_call(
        kernel,
        out_shape=[struct((rows, width), BF16)] * TEAM
        + [
            struct(gathered.shape, BF16),
            struct((8, width), F32),
            struct((8, width), F32),
            struct((8, size), F32),
        ],
        in_specs=[SMEM] + [ANY] * (TEAM + 6) + [VMEM] * 3 + [ANY],
        out_specs=[ANY] * TEAM + [VMEM] * 4,
        scratch_shapes=[
            pltpu.VMEM((2, rows, width), BF16),
            pltpu.VMEM((width, cols), BF16),
            pltpu.VMEM(weight_head.shape, BF16),
            pltpu.VMEM((q_cols, width), BF16),
            pltpu.VMEM((2, rows, width), BF16),
            pltpu.VMEM((2, rows, cols), F32),
            pltpu.VMEM((2, rows, TILE), F32),
            pltpu.VMEM((2, rows, q_cols), BF16),
            pltpu.VMEM((2, rows, width), BF16),
            pltpu.VMEM((rows, cols + TILE), BF16),
            pltpu.VMEM((cols + TILE, width), F32),
            pltpu.VMEM((q_cols, width), F32),
            pltpu.SemaphoreType.DMA((1 + gathered.shape[0] * (1 + width // cols),)),
            pltpu.SemaphoreType.DMA((5, 2)),
            pltpu.SemaphoreType.DMA((2,)),
        ],
        compiler_params=pltpu.CompilerParams(vmem_limit_bytes=56 << 20),
        cost_estimate=pl.CostEstimate(flops=45 << 30, bytes_accessed=70 << 20, transcendentals=1 << 20),
    )(tiles, *hidden, gathered, weight_head, *saved, gains, cosine, sine, after)
    return result[:TEAM], *result[TEAM : TEAM + 2], result[TEAM + 2][0], result[TEAM + 3][:2]


def tile_places(tiles_ref, rows):
    places, total = [], 0
    for r in range(TEAM):
        count = tiles_ref[r]
        for j in range(rows // TILE):
            places.append((r, j, j < count, total + j))
        total = total + count
    return places, total


def feed(tiles, twos, upstreams, weight_gate, weight_up, weight_down):
    rows, width = twos[0].shape
    ff_cols = weight_down.shape[0]
    whole = TEAM * rows
    chunk = 2 * TILE
    chunks = whole // chunk

    def kernel(*refs):
        tiles_ref, twos_ref, ups_ref = refs[0], refs[1 : 1 + TEAM], refs[1 + TEAM : 1 + 2 * TEAM]
        weights_ref = refs[1 + 2 * TEAM : 4 + 2 * TEAM]
        outs_ref = refs[4 + 2 * TEAM : 4 + 3 * TEAM]
        grads_ref = refs[4 + 3 * TEAM : 4 + 4 * TEAM]
        inner_all, back_all, two_all, ups_all = refs[4 + 4 * TEAM : 8 + 4 * TEAM]
        (
            two_v, ups_v, wg_v, wu_v, wd_v, inner_v, back_v, out_v, grad_v, zero_v,
            w_sem, load_sem, keep_sem, tile_sem, dead_sem,
        ) = refs[8 + 4 * TEAM :]
        places, total = tile_places(tiles_ref, rows)
        used = (total + 1) // 2

        def loads(sources, packed, which):
            for k, (r, j, live, place) in enumerate(places):
                yield live, pltpu.make_async_copy(
                    sources[r].at[rows_of(j)], packed.at[rows_of(place)], load_sem.at[which, k]
                )

        weights = [
            pltpu.make_async_copy(src, dst, w_sem.at[j])
            for j, (src, dst) in enumerate(zip(weights_ref, (wg_v, wu_v, wd_v)))
        ]
        for live, copy in loads(twos_ref, two_v, 0):
            pl.when(live)(copy.start)
        for copy in weights:
            copy.start()
        for live, copy in loads(ups_ref, ups_v, 1):
            pl.when(live)(copy.start)
        zero_v[...] = jnp.zeros_like(zero_v)

        def dead(k, r, j):
            zeros = zero_v.at[:TILE]
            yield pltpu.make_async_copy(zeros, grads_ref[r].at[rows_of(j)], dead_sem.at[0, k])
            yield pltpu.make_async_copy(zeros, outs_ref[r].at[rows_of(j)], dead_sem.at[1, k])

        for k, (r, j, live, place) in enumerate(places):

            @pl.when(jnp.logical_not(live))
            def _(k=k, r=r, j=j):
                for copy in dead(k, r, j):
                    copy.start()

        def keeps(c, sources):
            for j, (src, dst) in enumerate(zip(sources, (two_all, ups_all, inner_all, back_all))):
                yield pltpu.make_async_copy(src, dst.at[rows_of(c, chunk)], keep_sem.at[j, c])

        zeros = (zero_v, zero_v, zero_v.at[:, :ff_cols], zero_v.at[:, : 2 * ff_cols])
        for c in range(TEAM // 2, chunks):

            @pl.when(c >= used)
            def _(c=c):
                for copy in keeps(c, zeros):
                    copy.start()

        @pl.when(total % 2 == 1)
        def _():
            two_v[rows_of(total)] = jnp.zeros((TILE, width), BF16)
            ups_v[rows_of(total)] = jnp.zeros((TILE, width), BF16)

        for live, copy in loads(twos_ref, two_v, 0):
            pl.when(live)(copy.wait)
        for copy in weights:
            copy.wait()
        for live, copy in loads(ups_ref, ups_v, 1):
            pl.when(live)(copy.wait)

        def tile_stores(r, j, slot, side):
            here = pl.ds(side * TILE, TILE)
            yield pltpu.make_async_copy(
                grad_v.at[slot, here], grads_ref[r].at[rows_of(j)], tile_sem.at[0, slot, side]
            )
            yield pltpu.make_async_copy(
                out_v.at[slot, here], outs_ref[r].at[rows_of(j)], tile_sem.at[1, slot, side]
            )

        def wait_tiles(c, slot):
            for side in range(2):

                @pl.when(2 * c + side < total)
                def _(side=side):
                    for copy in tile_stores(0, 0, slot, side):
                        copy.wait()

        def body(c, carry):
            slot = c % 2
            span = rows_of(c, chunk)

            @pl.when(c >= 2)
            def _():
                wait_tiles(c - 2, slot)
                for j, copy in enumerate(keeps(c - 2, zeros)):
                    if j >= 2:
                        copy.wait()

            gate_part = product(two_v[span], wg_v[...])
            up_part = product(two_v[span], wu_v[...])
            sig = jax.nn.sigmoid(gate_part)
            silu = gate_part * sig
            inner_v[slot] = (silu * up_part).astype(BF16)
            inner_grad = product_nt(ups_v[span], wd_v[...])
            back_v[slot, :, :ff_cols] = (inner_grad * up_part * (sig + silu * (1.0 - sig))).astype(BF16)
            back_v[slot, :, ff_cols:] = (inner_grad * silu).astype(BF16)
            for copy in keeps(c, (two_v.at[span], ups_v.at[span], inner_v.at[slot], back_v.at[slot])):
                copy.start()
            grad = product_nt(back_v[slot, :, :ff_cols], wg_v[...]) + product_nt(
                back_v[slot, :, ff_cols:], wu_v[...]
            )
            grad_v[slot] = grad.astype(BF16)
            out_v[slot] = product(inner_v[slot], wd_v[...]).astype(BF16)
            for k, (r, j, live, place) in enumerate(places):
                for side in range(2):

                    @pl.when(jnp.logical_and(live, place == 2 * c + side))
                    def _(r=r, j=j, side=side):
                        for copy in tile_stores(r, j, slot, side):
                            copy.start()

            return carry

        lax.fori_loop(0, used, body, 0)
        wait_tiles(used - 2, used % 2)
        wait_tiles(used - 1, (used - 1) % 2)
        for k, (r, j, live, place) in enumerate(places):

            @pl.when(jnp.logical_not(live))
            def _(k=k, r=r, j=j):
                for copy in dead(k, r, j):
                    copy.wait()

        for c in range(chunks):
            for j, copy in enumerate(keeps(c, zeros)):
                if j < 2:
                    copy.wait()
                else:
                    pl.when(c >= used - 2)(copy.wait)

    count = whole // TILE
    result = pl.pallas_call(
        kernel,
        out_shape=[struct((rows, width), BF16)] * (2 * TEAM)
        + [
            struct((whole, ff_cols), BF16),
            struct((whole, 2 * ff_cols), BF16),
            struct((whole, width), BF16),
            struct((whole, width), BF16),
        ],
        in_specs=[SMEM] + [ANY] * (3 + 2 * TEAM),
        out_specs=[ANY] * (2 * TEAM + 4),
        scratch_shapes=[
            pltpu.VMEM((whole, width), BF16),
            pltpu.VMEM((whole, width), BF16),
            pltpu.VMEM(weight_gate.shape, BF16),
            pltpu.VMEM(weight_up.shape, BF16),
            pltpu.VMEM(weight_down.shape, BF16),
            pltpu.VMEM((2, chunk, ff_cols), BF16),
            pltpu.VMEM((2, chunk, 2 * ff_cols), BF16),
            pltpu.VMEM((2, chunk, width), BF16),
            pltpu.VMEM((2, chunk, width), BF16),
            pltpu.VMEM((chunk, width), BF16),
            pltpu.SemaphoreType.DMA((3,)),
            pltpu.SemaphoreType.DMA((2, count)),
            pltpu.SemaphoreType.DMA((4, chunks)),
            pltpu.SemaphoreType.DMA((2, 2, 2)),
            pltpu.SemaphoreType.DMA((2, count)),
        ],
        compiler_params=pltpu.CompilerParams(vmem_limit_bytes=60 << 20),
        cost_estimate=pl.CostEstimate(flops=58 << 30, bytes_accessed=100 << 20, transcendentals=1 << 20),
    )(tiles, *twos, *upstreams, weight_gate, weight_up, weight_down)
    return result[:TEAM], result[TEAM : 2 * TEAM], result[2 * TEAM :]


def local(
    groups,
    tokens,
    lengths,
    cotangent,
    attention_gain,
    query_weight,
    key_matrix,
    value_matrix,
    head_gate_weight,
    output_weight,
    query_key_gain,
    feedforward_gain,
    gate_weight,
    up_weight,
    down_weight,
):
    t = member()
    everyone = groups * TEAM
    rows, width = tokens.shape
    rho = query_weight.shape[0]
    phi = down_weight.shape[0]
    ff = gate_weight.shape[1]
    pair_cols = query_key_gain.shape[1]
    size = pair_cols * everyone
    heads = query_weight.shape[1] // size
    mine = heads // TEAM
    q_cols = query_weight.shape[1] // TEAM
    k_cols = key_matrix.shape[1] // TEAM
    ff_cols = ff // TEAM

    def everyone_in_team(vector):
        return jnp.broadcast_to(vector.reshape(1, -1), (TEAM, vector.size))

    live_tiles = (lengths + (TILE - 1)) // TILE
    row = jnp.concatenate(
        [
            head_gate_weight.reshape(rho, TEAM, mine).transpose(1, 2, 0).reshape(TEAM, -1),
            everyone_in_team(attention_gain),
            everyone_in_team(feedforward_gain),
            everyone_in_team(query_key_gain),
            everyone_in_team(live_tiles.astype(BF16)),
        ],
        axis=1,
    )
    cols = q_cols + 2 * k_cols
    row = jnp.pad(row, ((0, 0), (0, cols - row.shape[1])))[:, None, :]
    attn = jnp.concatenate(
        [
            query_weight.reshape(rho, TEAM, q_cols),
            key_matrix.reshape(rho, TEAM, k_cols),
            value_matrix.reshape(rho, TEAM, k_cols),
        ],
        axis=2,
    ).transpose(1, 0, 2)
    attn = jnp.concatenate([attn, jnp.pad(row, ((0, 0), (0, 7), (0, 0)))], axis=1)
    attn = exchange(attn)
    head_lanes = mine * rho
    at_one, at_two, at_pair = head_lanes, head_lanes + rho, head_lanes + 2 * rho
    at_tiles = at_pair + 2 * pair_cols
    team_tiles = attn[:, rho, at_tiles].astype(jnp.int32)
    order = jnp.arange(TEAM, dtype=jnp.int32)
    tiles = jnp.sum(jnp.where((order[:, None] ^ t) == order[None, :], team_tiles[None, :], 0), axis=1)
    routed = lax.ppermute(output_weight, ALL, out_weight_routes(groups))
    team_rows = TEAM * rho
    small_at = team_rows + (width // cols) * rho
    stacked = jnp.concatenate(
        [attn[:, :rho].reshape(team_rows, cols)]
        + [routed[:, k : k + cols] for k in range(0, width, cols)]
        + [attn[:, rho], jnp.zeros((16 - TEAM, cols), BF16)],
        axis=0,
    )
    gathered = line_gather(stacked).reshape(groups, -1, cols)
    rows_small = gathered[:, small_at : small_at + TEAM].reshape(everyone, cols)
    weight_head = jnp.pad(
        rows_small[:, :head_lanes].reshape(everyone, mine, rho).transpose(1, 0, 2).reshape(mine, width),
        ((0, TILE - mine), (0, 0)),
    )
    gain_one = rows_small[:, at_one:at_two].reshape(1, width).astype(F32)
    gain_two = rows_small[:, at_two:at_pair].reshape(1, width).astype(F32)
    gain_pair = (
        rows_small[:, at_pair:at_tiles]
        .reshape(everyone, 2, pair_cols)
        .transpose(1, 0, 2)
        .reshape(2, size)
        .astype(F32)
    )
    def ff_split(w):
        return w.reshape(rho, groups, TEAM, phi).transpose(2, 0, 1, 3).reshape(TEAM, rho, ff_cols)

    feed_shard = jnp.concatenate([ff_split(gate_weight), ff_split(up_weight)], axis=2)

    exponent = jnp.arange(size // 2, dtype=F32) * (-2.0 / size)
    frequency = jnp.power(ROPE_BASE, exponent)
    angles = jnp.arange(rows, dtype=F32)[:, None] * frequency[None, :]
    cosine = jnp.concatenate([jnp.cos(angles), jnp.cos(angles)], axis=1)
    sine = jnp.concatenate([-jnp.sin(angles), jnp.sin(angles)], axis=1)
    consts = (gathered, weight_head, gain_one, gain_pair, cosine, sine)
    team_tokens = team_gather(tokens)
    feed_shard = exchange(feed_shard).reshape(TEAM * rho, -1)
    weight_gate = line_gather(feed_shard[:, :ff_cols])
    live = lax.broadcasted_iota(jnp.int32, (rows, 1), 0) < lengths[0]
    live_rows = live.astype(F32)
    upstream = cotangent.astype(F32) * live_rows
    tick = mark([team_tokens[6]])
    later = lax.broadcasted_iota(jnp.int32, (rows, 1), 0) < lengths[0] + tick[0, 0]
    upstream_low = jnp.where(later, cotangent, jnp.zeros_like(cotangent))
    upstream_levels = TeamGather(upstream_low)
    parts, kept, tick = attend(tiles, team_tokens, consts, mine, mark([upstream_low]))
    normed, qkv, logit, gated = kept
    weight_up = line_gather(hold([feed_shard[:, ff_cols:]], tick)[0])
    parts = hold(parts, mark([upstream_levels.a1, upstream_levels.a2, upstream_levels.a4, tick]))
    arrived = TeamSum(parts)
    arrived.first()
    weight_down = line_gather(hold([down_weight], arrived.low6)[0])
    inputs = tokens.astype(F32)
    hidden_state = inputs + arrived.total(weight_gate)
    team_upstream = upstream_levels.blocks(mark(arrived.last_sent))

    normed_two = rms(hidden_state, gain_two).astype(BF16)
    team_two = TeamGather(normed_two).blocks(mark(team_upstream + [weight_up]))
    outs, grads, saved = feed(tiles, team_two, team_upstream, weight_gate, weight_up, weight_down)
    inner, feed_back, two_all, ups_all = saved
    arrived = TeamSum(grads)
    arrived.first()
    two_grad = arrived.total()
    down_part = product_tn(inner, ups_all).astype(BF16)
    feed_back = hold([feed_back], mark([arrived.x_top, arrived.y_low]))[0]
    gate_part = product_tn(two_all, feed_back[:, :ff_cols]).astype(BF16)
    up_part = product_tn(two_all, feed_back[:, ff_cols:]).astype(BF16)
    parts_made = mark([gate_part, up_part])
    down_grad = line_sum(down_part)
    gate_grad = line_sum(hold([gate_part], down_grad)[0])
    up_grad = line_sum(hold([up_part], gate_grad)[0])
    feed_done = up_grad
    hidden_grad = upstream + rms_pull(hidden_state, gain_two, two_grad)

    fed = TeamSum(outs)
    team_hidden = TeamGather(hidden_grad.astype(BF16)).blocks(mark(fed.ready + [gate_part, up_part]))
    two_scale = lax.rsqrt(jnp.mean(hidden_state * hidden_state, axis=-1, keepdims=True) + EPSILON)
    two_sum = jnp.sum(two_grad * hidden_state * two_scale, axis=0)
    first_hop = fed.first(mark(team_hidden + [parts_made]))
    parts, packed, head_sum, one_sum, pair_sum = attend_back(
        tiles, team_hidden, consts, (normed, qkv, logit, gated), mine, mark(fed.sent + [down_grad])
    )
    row = jnp.concatenate(
        [
            head_sum[:mine].reshape(mine, everyone, rho).transpose(1, 0, 2).reshape(everyone, -1),
            (one_sum / gain_one[0]).reshape(everyone, rho),
            two_sum.reshape(everyone, rho),
            pair_sum.reshape(2, everyone, pair_cols).transpose(1, 0, 2).reshape(everyone, -1),
        ],
        axis=1,
    ).astype(BF16)
    row = jnp.pad(row, ((0, 0), (0, cols - row.shape[1]))).reshape(groups, TEAM, cols)
    packed = lax.dynamic_update_slice(packed, row, (0, small_at, 0))
    parts = hold(parts, mark(first_hop + [gate_grad]))
    arrived = TeamSum(parts)
    arrived.first()
    packed = hold([packed.reshape(-1, cols)], mark([feed_done, arrived.u4, arrived.u2] + arrived.sent))[0]
    normed_grad = arrived.total(packed)
    packed = line_sum(packed)
    layer_output = ((hidden_state + fed.total()) * live_rows).astype(BF16)
    tokens_grad = (hidden_grad + rms_pull(inputs, gain_one, normed_grad)).astype(BF16)
    feed_grad = jnp.concatenate([gate_grad, hold([up_grad], arrived.u4)[0]], axis=1)
    feed_grad = exchange(feed_grad.reshape(TEAM, rho, 2 * ff_cols))

    def ff_join(w):
        return w.reshape(TEAM, rho, groups, phi).transpose(1, 2, 0, 3).reshape(rho, ff)

    gate_grad, up_grad = hold(
        [ff_join(feed_grad[:, :, :ff_cols]), ff_join(feed_grad[:, :, ff_cols:])], arrived.u4
    )
    packed = hold([packed], mark([gate_grad, up_grad]))[0]
    routes = [(user, owner) for owner, user in out_weight_routes(groups)]
    output_grad = packed[team_rows:small_at].reshape(-1, rho, cols).transpose(1, 0, 2).reshape(rho, width)
    output_grad = lax.ppermute(output_grad, ALL, routes)
    packed = jnp.concatenate(
        [
            packed[:team_rows].reshape(TEAM, rho, cols),
            jnp.pad(packed[small_at : small_at + TEAM][:, None], ((0, 0), (0, 7), (0, 0))),
        ],
        axis=1,
    )
    packed = exchange(packed)
    attn_grad = packed[:, :rho].transpose(1, 0, 2)
    rows_small = packed[:, rho].astype(F32)
    sums = jnp.sum(rows_small[:, head_lanes:], axis=0)
    head_gate_grad = rows_small[:, :head_lanes].reshape(heads, rho).T
    return (
        layer_output,
        tokens_grad,
        sums[:rho],
        attn_grad[:, :, :q_cols].reshape(rho, -1).astype(F32),
        attn_grad[:, :, q_cols : q_cols + k_cols].reshape(rho, -1).astype(F32),
        attn_grad[:, :, q_cols + k_cols :].reshape(rho, -1).astype(F32),
        head_gate_grad,
        output_grad.astype(F32),
        sums[2 * rho : 2 * rho + 2 * pair_cols].reshape(2, pair_cols),
        sums[rho : 2 * rho],
        gate_grad.astype(F32),
        up_grad.astype(F32),
        down_grad.astype(F32),
    )


def solution(mesh):
    groups = mesh.size // TEAM
    rows, vector, columns = P(ALL, None), P(ALL), P(None, ALL)

    def step(*args):
        return local(groups, *args)

    return jax.shard_map(
        step,
        mesh=mesh,
        in_specs=(
            rows, vector, rows, vector, rows, rows, rows, rows, rows, columns, vector, rows, rows, rows,
        ),
        out_specs=(
            rows, rows, vector, rows, rows, rows, rows, rows, columns, vector, rows, rows, rows,
        ),
        check_vma=False,
    )
```

```python
import jax
import jax.numpy as jnp
from jax import lax
from jax.experimental import pallas as pl
from jax.experimental.pallas import tpu as pltpu
from jax.sharding import PartitionSpec as P

EPSILON = 1e-06
ROPE_BASE = 1000000.0
TEAM = 8
ALL = ("dp", "fsdp")
F32 = jnp.float32
BF16 = jnp.bfloat16
TILE = 128
ANY = pl.BlockSpec(memory_space=pl.ANY)
VMEM = pl.BlockSpec(memory_space=pltpu.VMEM)
SMEM = pl.BlockSpec(memory_space=pltpu.SMEM)


def product(left, right):
    return jnp.dot(left, right, preferred_element_type=F32)


def product_nt(left, right):
    return lax.dot_general(left, right, (((1,), (1,)), ((), ())), preferred_element_type=F32)


def product_tn(left, right):
    return lax.dot_general(left, right, (((0,), (0,)), ((), ())), preferred_element_type=F32)


def world():
    return lax.axis_size(ALL)


def member():
    return lax.axis_index(ALL) % TEAM


def teams():
    return [[first + t for t in range(TEAM)] for first in range(0, world(), TEAM)]


def lines():
    return [list(range(t, world(), TEAM)) for t in range(TEAM)]


def permute(array, pairs):
    return lax.ppermute(
        array, ALL, [(team[a], team[b]) for team in teams() for a, b in pairs]
    )


def swap(array, bits):
    return permute(array, [(i, i ^ bits) for i in range(TEAM)])


def exchange(blocks):
    if lax.axis_size("fsdp") == TEAM:
        return lax.all_to_all(blocks, "fsdp", 0, 0, tiled=True)
    return lax.all_to_all(blocks, ALL, 0, 0, tiled=True, axis_index_groups=teams())


def line_gather(shard):
    if lax.axis_size("fsdp") == TEAM:
        return lax.all_gather(shard, "dp", axis=0, tiled=True)
    return lax.all_gather(shard, ALL, axis=0, tiled=True, axis_index_groups=lines())


def line_sum(array):
    if lax.axis_size("fsdp") == TEAM:
        return lax.psum_scatter(array, "dp", scatter_dimension=0, tiled=True)
    return lax.psum_scatter(array, ALL, scatter_dimension=0, tiled=True, axis_index_groups=lines())


class TeamGather:
    def __init__(self, own):
        self.own = own
        self.a1 = swap(own, 1)
        self.a2 = swap(own, 2)
        self.a4 = swap(own, 4)

    def blocks(self, tick=None):
        a2, a4 = self.a2, self.a4
        if tick is not None:
            a2, a4 = hold([a2, a4], tick)
        half = self.own.shape[0] // 2
        a6 = jnp.concatenate([swap(a4[:half], 2), swap(a2[half:], 4)], axis=0)
        return [self.own, self.a1, a2, swap(a2, 1), a4, swap(a4, 1), a6, swap(a6, 1)]


def team_gather(own):
    return TeamGather(own).blocks()


class TeamSum:
    def __init__(self, parts):
        half = parts[0].shape[0] // 2
        odd = {r: swap(parts[r + 1], 1) for r in (6, 2, 4, 0)}
        self.total6, self.total2, self.total4, self.total0 = (
            (parts[r].astype(F32) + odd[r].astype(F32)).astype(BF16) for r in (6, 2, 4, 0)
        )
        self.half = half
        self.ready = [
            jnp.concatenate([self.total6[:half], self.total2[:half]], axis=0),
            jnp.concatenate([self.total6[half:], self.total4[half:]], axis=0),
        ]

    def first(self, tick=None):
        self.sent = self.ready if tick is None else list(hold(self.ready, tick))
        self.over_x, self.over_y = swap(self.sent[0], 2), swap(self.sent[1], 4)
        return [self.over_x, self.over_y]

    def total(self, tick=None):
        half = self.half
        lasts = [
            (self.total2[half:].astype(F32) + self.over_y[:half].astype(F32)).astype(BF16),
            (self.total4[:half].astype(F32) + self.over_x[:half].astype(F32)).astype(BF16),
        ]
        x_low, y_top = lasts if tick is None else hold(lasts, tick)
        self.last_sent = [x_low, y_top]
        x_low = swap(x_low, 2).astype(F32)
        y_top = swap(y_top, 4).astype(F32)
        top = self.over_x[half:].astype(F32) + y_top
        low = x_low + self.over_y[half:].astype(F32)
        return self.total0.astype(F32) + jnp.concatenate([top, low], axis=0)


def out_weight_routes(groups):
    return [(i, TEAM * (i % groups) + i // groups) for i in range(groups * TEAM)]


def rms_pull(value, gain, grad):
    scale = lax.rsqrt(jnp.mean(value * value, axis=-1, keepdims=True) + EPSILON)
    weighted = grad * gain
    mean = jnp.mean(weighted * value, axis=-1, keepdims=True)
    return scale * weighted - scale * scale * scale * value * mean


def rms(value, gain):
    return value * lax.rsqrt(jnp.mean(value * value, axis=-1, keepdims=True) + EPSILON) * gain


def struct(shape, dtype):
    return jax.ShapeDtypeStruct(shape, dtype)


def hold(arrays, tick):
    def kernel(*refs):
        del refs

    count = len(arrays)
    return pl.pallas_call(
        kernel,
        out_shape=[struct(a.shape, a.dtype) for a in arrays],
        in_specs=[ANY] * count + [ANY],
        out_specs=[ANY] * count,
        input_output_aliases={i: i for i in range(count)},
    )(*arrays, tick)


def mark(arrays):
    def kernel(*refs):
        refs[-1][...] = jnp.zeros_like(refs[-1])

    return pl.pallas_call(
        kernel,
        out_shape=struct((8, 128), jnp.int32),
        in_specs=[ANY] * len(arrays),
        out_specs=VMEM,
    )(*arrays)


def for_tiles(tiles, most, body):
    for m in range(1, most + 1):

        @pl.when(tiles == m)
        def _(m=m):
            body(m * TILE)


def turned(u, cosine, sine):
    return u * cosine + pltpu.roll(u, u.shape[-1] // 2, 1) * sine


def head_norm(u):
    return lax.rsqrt(jnp.mean(u * u, axis=-1, keepdims=True) + EPSILON)


def head_back(grad, raw, gain, cosine, sine):
    e = turned(grad, cosine, -sine)
    scale = head_norm(raw)
    weighted = e * gain
    mean = jnp.mean(weighted * raw, axis=-1, keepdims=True)
    back = scale * weighted - scale * scale * scale * raw * mean
    return back, jnp.sum(e * raw * scale, axis=0, keepdims=True)


def weights_of(query, key, factor):
    scores = product_nt(query, key) * factor
    n = scores.shape[0]
    causal = lax.broadcasted_iota(jnp.int32, (n, n), 1) <= lax.broadcasted_iota(jnp.int32, (n, n), 0)
    scores = jnp.where(causal, scores, -jnp.inf)
    terms = jnp.exp(scores - jnp.max(scores, axis=-1, keepdims=True))
    return terms * (1.0 / jnp.sum(terms, axis=-1, keepdims=True))


def rows_of(tile, size=TILE):
    return pl.ds(pl.multiple_of(tile * size, size), size)


def each_block(r, body):
    for k in range(TEAM):
        pl.when(r == k)(lambda k=k: body(k))


def load_weights(gathered, weight_head, wa_v, wo_v, wh_v, sems):
    groups, _, cols = gathered.shape
    width = wo_v.shape[1]
    rho = width // (groups * TEAM)
    copies = [pltpu.make_async_copy(weight_head, wh_v, sems.at[0])]
    for g in range(groups):
        copies.append(
            pltpu.make_async_copy(
                gathered.at[g, pl.ds(0, TEAM * rho)],
                wa_v.at[pl.ds(g * TEAM * rho, TEAM * rho)],
                sems.at[len(copies)],
            )
        )
        for k in range(width // cols):
            copies.append(
                pltpu.make_async_copy(
                    gathered.at[g, pl.ds(TEAM * rho + k * rho, rho)],
                    wo_v.at[pl.ds(g * rho, rho), pl.ds(k * cols, cols)],
                    sems.at[len(copies)],
                )
            )
    return copies


def attend(tiles, tokens, consts, mine, after):
    gathered, weight_head, gain, gains, cosine, sine = consts
    rows, width = tokens[0].shape
    size = gains.shape[1]
    q_cols = mine * size
    cols = gathered.shape[2]
    factor = size ** (-0.5)

    def kernel(*refs):
        tiles_ref, toks = refs[0], refs[1 : 1 + TEAM]
        wa, wh, gain_ref, gains_ref, cos_ref, sin_ref, _ = refs[1 + TEAM : 8 + TEAM]
        parts = refs[8 + TEAM : 8 + 2 * TEAM]
        normed_all, qkv_all, logit_all, gated_all, tick = refs[8 + 2 * TEAM : 13 + 2 * TEAM]
        (
            tok_v, wa_v, wh_v, wo_v, part_v, normed_v, qkv_v, logit_v, gated_v, w_sem, in_sem, out_sem,
        ) = refs[13 + 2 * TEAM :]
        tick[...] = jnp.zeros_like(tick)

        def load(k, slot):
            return pltpu.make_async_copy(toks[k], tok_v.at[slot], in_sem.at[slot])

        def store(r, slot, j, k=0):
            src = (part_v, normed_v, qkv_v, logit_v, gated_v)[j].at[slot]
            dst = parts[k] if j == 0 else (normed_all, qkv_all, logit_all, gated_all)[j - 1].at[rows_of(r, rows)]
            return pltpu.make_async_copy(src, dst, out_sem.at[j, slot])

        load(0, 0).start()
        weights = load_weights(wa, wh, wa_v, wo_v, wh_v, w_sem)
        for copy in weights:
            copy.start()
        for copy in weights:
            copy.wait()

        def step(r, carry):
            slot = r % 2

            @pl.when(r + 1 < TEAM)
            def _():
                each_block(r + 1, lambda k: load(k, 1 - slot).start())

            load(0, slot).wait()

            @pl.when(r >= 2)
            def _():
                for j in range(5):
                    store(r - 2, slot, j).wait()

            def body(n):
                value = tok_v[slot, :n].astype(F32)
                normed = rms(value, gain_ref[...]).astype(BF16)
                normed_v[slot, :n] = normed
                qkv = product(normed, wa_v[...])
                qkv_v[slot, :n] = qkv
                logit = product_nt(normed, wh_v[...])
                logit_v[slot, :n] = logit
                cos, sin = cos_ref[:n], sin_ref[:n]
                key = qkv[:, q_cols : q_cols + size]
                key = turned(key * head_norm(key) * gains_ref[1:2], cos, sin).astype(BF16)
                values = qkv[:, q_cols + size :].astype(BF16)
                for h in range(mine):
                    query = qkv[:, h * size : (h + 1) * size]
                    query = turned(query * head_norm(query) * gains_ref[0:1], cos, sin).astype(BF16)
                    attention = weights_of(query, key, factor)
                    mixture = product(attention.astype(BF16), values)
                    gate = jax.nn.sigmoid(logit[:, h : h + 1])
                    gated_v[slot, :n, h * size : (h + 1) * size] = (mixture * gate).astype(BF16)
                part_v[slot, :n] = product(gated_v[slot, :n], wo_v[...]).astype(BF16)
                if n < rows:
                    part_v[slot, n:] = jnp.zeros((rows - n, width), BF16)
                    normed_v[slot, n:] = jnp.zeros((rows - n, width), BF16)
                    gated_v[slot, n:] = jnp.zeros((rows - n, q_cols), BF16)

            for_tiles(tiles_ref[r], rows // TILE, body)
            each_block(r, lambda k: store(r, slot, 0, k).start())
            for j in range(1, 5):
                store(r, slot, j).start()
            return carry

        lax.fori_loop(0, TEAM, step, 0)
        for r in (TEAM - 2, TEAM - 1):
            for j in range(5):
                store(r, r % 2, j).wait()

    whole = TEAM * rows
    result = pl.pallas_call(
        kernel,
        out_shape=[struct((rows, width), BF16)] * TEAM
        + [
            struct((whole, width), BF16),
            struct((whole, cols), F32),
            struct((whole, TILE), F32),
            struct((whole, q_cols), BF16),
            struct((8, 128), jnp.int32),
        ],
        in_specs=[SMEM] + [ANY] * (TEAM + 2) + [VMEM] * 4 + [ANY],
        out_specs=[ANY] * (TEAM + 4) + [VMEM],
        scratch_shapes=[
            pltpu.VMEM((2, rows, width), BF16),
            pltpu.VMEM((width, cols), BF16),
            pltpu.VMEM(weight_head.shape, BF16),
            pltpu.VMEM((q_cols, width), BF16),
            pltpu.VMEM((2, rows, width), BF16),
            pltpu.VMEM((2, rows, width), BF16),
            pltpu.VMEM((2, rows, cols), F32),
            pltpu.VMEM((2, rows, TILE), F32),
            pltpu.VMEM((2, rows, q_cols), BF16),
            pltpu.SemaphoreType.DMA((1 + gathered.shape[0] * (1 + width // cols),)),
            pltpu.SemaphoreType.DMA((2,)),
            pltpu.SemaphoreType.DMA((5, 2)),
        ],
        compiler_params=pltpu.CompilerParams(vmem_limit_bytes=48 << 20),
        cost_estimate=pl.CostEstimate(flops=30 << 30, bytes_accessed=60 << 20, transcendentals=1 << 20),
    )(tiles, *tokens, gathered, weight_head, gain, gains, cosine, sine, after)
    return result[:TEAM], result[TEAM : TEAM + 4], result[TEAM + 4]


def attend_back(tiles, hidden, consts, saved, mine, after):
    gathered, weight_head, gain, gains, cosine, sine = consts
    rows, width = hidden[0].shape
    size = gains.shape[1]
    q_cols = mine * size
    cols = gathered.shape[2]
    factor = size ** (-0.5)

    def kernel(*refs):
        tiles_ref, hids = refs[0], refs[1 : 1 + TEAM]
        wa, wh, normed_all, qkv_all, logit_all, gated_all = refs[1 + TEAM : 7 + TEAM]
        gains_ref, cos_ref, sin_ref, _ = refs[7 + TEAM : 11 + TEAM]
        parts = refs[11 + TEAM : 11 + 2 * TEAM]
        packed, head_sum, gain_sum, gains_sum = refs[11 + 2 * TEAM : 15 + 2 * TEAM]
        (
            hid_v, wa_v, wh_v, wo_v, normed_v, qkv_v, logit_v, gated_v, part_v, back_v, attn_sum, out_sum,
            w_sem, in_sem, out_sem,
        ) = refs[15 + 2 * TEAM :]

        def loads(r, slot, k):
            yield pltpu.make_async_copy(hids[k], hid_v.at[slot], in_sem.at[0, slot])
            here = rows_of(r, rows)
            for j, (src, dst) in enumerate(
                ((qkv_all, qkv_v), (logit_all, logit_v), (normed_all, normed_v), (gated_all, gated_v))
            ):
                yield pltpu.make_async_copy(src.at[here], dst.at[slot], in_sem.at[1 + j, slot])

        def start_loads(r, slot):
            def body(k):
                for copy in loads(r, slot, k):
                    copy.start()

            each_block(r, body)

        def store(slot, k=0):
            return pltpu.make_async_copy(part_v.at[slot], parts[k], out_sem.at[slot])

        for copy in loads(0, 0, 0):
            copy.start()
        weights = load_weights(wa, wh, wa_v, wo_v, wh_v, w_sem)
        for copy in weights:
            copy.start()
        for ref in (attn_sum, out_sum, gain_sum, gains_sum):
            ref[...] = jnp.zeros_like(ref)
        for copy in weights:
            copy.wait()

        def step(r, carry):
            slot = r % 2

            @pl.when(r + 1 < TEAM)
            def _():
                start_loads(r + 1, 1 - slot)

            for copy in loads(r, slot, 0):
                copy.wait()

            @pl.when(r >= 2)
            def _():
                store(slot).wait()

            def body(n):
                hidden_low = hid_v[slot, :n]
                normed = normed_v[slot, :n]
                out_sum[...] += product_tn(gated_v[slot, :n], hidden_low)
                gated_grad = product_nt(hidden_low, wo_v[...])
                cos, sin = cos_ref[:n], sin_ref[:n]
                key_raw = qkv_v[slot, :n, q_cols : q_cols + size]
                key = turned(key_raw * head_norm(key_raw) * gains_ref[1:2], cos, sin).astype(BF16)
                values = qkv_v[slot, :n, q_cols + size :].astype(BF16)
                lane = lax.broadcasted_iota(jnp.int32, (n, TILE), 1)
                logit_back = jnp.zeros((n, TILE), F32)
                values_back = jnp.zeros((n, size), F32)
                key_grad = jnp.zeros((n, size), F32)
                query_sum = jnp.zeros((1, size), F32)
                for h in range(mine):
                    span = slice(h * size, (h + 1) * size)
                    query_raw = qkv_v[slot, :n, span]
                    query = turned(query_raw * head_norm(query_raw) * gains_ref[0:1], cos, sin).astype(BF16)
                    attention = weights_of(query, key, factor)
                    attention_low = attention.astype(BF16)
                    mixture = product(attention_low, values)
                    gate = jax.nn.sigmoid(logit_v[slot, :n, h : h + 1])
                    head_grad = gated_grad[:, span]
                    mixture_back = (head_grad * gate).astype(BF16)
                    one = jnp.sum(head_grad * mixture, axis=-1, keepdims=True) * gate * (1.0 - gate)
                    logit_back = jnp.where(lane == h, one, logit_back)
                    values_back += product_tn(attention_low, mixture_back)
                    attention_grad = product_nt(mixture_back, values)
                    scores_back = (
                        attention
                        * (attention_grad - jnp.sum(attention_grad * attention, axis=-1, keepdims=True))
                    ).astype(BF16)
                    query_grad = product(scores_back, key) * factor
                    key_grad += product_tn(scores_back, query)
                    back, total = head_back(query_grad, query_raw, gains_ref[0:1], cos, sin)
                    back_v[:n, span] = back.astype(BF16)
                    query_sum += total
                back, key_sum = head_back(key_grad * factor, key_raw, gains_ref[1:2], cos, sin)
                back_v[:n, q_cols : q_cols + size] = back.astype(BF16)
                back_v[:n, q_cols + size : cols] = values_back.astype(BF16)
                logit_back = logit_back.astype(BF16)
                back_v[:n, cols:] = logit_back
                gains_sum[0:1] += query_sum
                gains_sum[1:2] += key_sum
                part = product_nt(back_v[:n, :cols], wa_v[...]) + product(logit_back, wh_v[...])
                part_v[slot, :n] = part.astype(BF16)
                gain_sum[0:1] += jnp.sum(part * normed.astype(F32), axis=0, keepdims=True)
                attn_sum[...] += product_tn(back_v[:n], normed)
                if n < rows:
                    part_v[slot, n:] = jnp.zeros((rows - n, width), BF16)

            for_tiles(tiles_ref[r], rows // TILE, body)
            each_block(r, lambda k: store(slot, k).start())
            return carry

        lax.fori_loop(0, TEAM, step, 0)
        head_sum[...] = attn_sum[cols : cols + 8]
        turned_sum = attn_sum[:cols].T.astype(BF16)
        groups, height, _ = packed.shape
        rho = width // (groups * TEAM)
        for g in range(groups):
            packed[g, : TEAM * rho] = turned_sum[g * TEAM * rho : (g + 1) * TEAM * rho]
            for k in range(width // cols):
                top = TEAM * rho + k * rho
                packed[g, top : top + rho] = out_sum[
                    g * rho : (g + 1) * rho, k * cols : (k + 1) * cols
                ].astype(BF16)
            packed[g, height - 16 :] = jnp.zeros((16, cols), BF16)
        store(0).wait()
        store(1).wait()

    result = pl.pallas_call(
        kernel,
        out_shape=[struct((rows, width), BF16)] * TEAM
        + [
            struct(gathered.shape, BF16),
            struct((8, width), F32),
            struct((8, width), F32),
            struct((8, size), F32),
        ],
        in_specs=[SMEM] + [ANY] * (TEAM + 6) + [VMEM] * 3 + [ANY],
        out_specs=[ANY] * TEAM + [VMEM] * 4,
        scratch_shapes=[
            pltpu.VMEM((2, rows, width), BF16),
            pltpu.VMEM((width, cols), BF16),
            pltpu.VMEM(weight_head.shape, BF16),
            pltpu.VMEM((q_cols, width), BF16),
            pltpu.VMEM((2, rows, width), BF16),
            pltpu.VMEM((2, rows, cols), F32),
            pltpu.VMEM((2, rows, TILE), F32),
            pltpu.VMEM((2, rows, q_cols), BF16),
            pltpu.VMEM((2, rows, width), BF16),
            pltpu.VMEM((rows, cols + TILE), BF16),
            pltpu.VMEM((cols + TILE, width), F32),
            pltpu.VMEM((q_cols, width), F32),
            pltpu.SemaphoreType.DMA((1 + gathered.shape[0] * (1 + width // cols),)),
            pltpu.SemaphoreType.DMA((5, 2)),
            pltpu.SemaphoreType.DMA((2,)),
        ],
        compiler_params=pltpu.CompilerParams(vmem_limit_bytes=56 << 20),
        cost_estimate=pl.CostEstimate(flops=45 << 30, bytes_accessed=70 << 20, transcendentals=1 << 20),
    )(tiles, *hidden, gathered, weight_head, *saved, gains, cosine, sine, after)
    return result[:TEAM], *result[TEAM : TEAM + 2], result[TEAM + 2][0], result[TEAM + 3][:2]


def tile_places(tiles_ref, rows):
    places, total = [], 0
    for r in range(TEAM):
        count = tiles_ref[r]
        for j in range(rows // TILE):
            places.append((r, j, j < count, total + j))
        total = total + count
    return places, total


def feed(tiles, twos, upstreams, weight_gate, weight_up, weight_down):
    rows, width = twos[0].shape
    ff_cols = weight_down.shape[0]
    whole = TEAM * rows
    chunk = 2 * TILE
    chunks = whole // chunk

    def kernel(*refs):
        tiles_ref, twos_ref, ups_ref = refs[0], refs[1 : 1 + TEAM], refs[1 + TEAM : 1 + 2 * TEAM]
        weights_ref = refs[1 + 2 * TEAM : 4 + 2 * TEAM]
        outs_ref = refs[4 + 2 * TEAM : 4 + 3 * TEAM]
        grads_ref = refs[4 + 3 * TEAM : 4 + 4 * TEAM]
        inner_all, back_all, two_all, ups_all = refs[4 + 4 * TEAM : 8 + 4 * TEAM]
        (
            two_v, ups_v, wg_v, wu_v, wd_v, inner_v, back_v, out_v, grad_v, zero_v,
            w_sem, load_sem, keep_sem, tile_sem, dead_sem,
        ) = refs[8 + 4 * TEAM :]
        places, total = tile_places(tiles_ref, rows)
        used = (total + 1) // 2

        def loads(sources, packed, which):
            for k, (r, j, live, place) in enumerate(places):
                yield live, pltpu.make_async_copy(
                    sources[r].at[rows_of(j)], packed.at[rows_of(place)], load_sem.at[which, k]
                )

        weights = [
            pltpu.make_async_copy(src, dst, w_sem.at[j])
            for j, (src, dst) in enumerate(zip(weights_ref, (wg_v, wu_v, wd_v)))
        ]
        for live, copy in loads(twos_ref, two_v, 0):
            pl.when(live)(copy.start)
        for copy in weights:
            copy.start()
        for live, copy in loads(ups_ref, ups_v, 1):
            pl.when(live)(copy.start)
        zero_v[...] = jnp.zeros_like(zero_v)

        def dead(k, r, j):
            zeros = zero_v.at[:TILE]
            yield pltpu.make_async_copy(zeros, grads_ref[r].at[rows_of(j)], dead_sem.at[0, k])
            yield pltpu.make_async_copy(zeros, outs_ref[r].at[rows_of(j)], dead_sem.at[1, k])

        for k, (r, j, live, place) in enumerate(places):

            @pl.when(jnp.logical_not(live))
            def _(k=k, r=r, j=j):
                for copy in dead(k, r, j):
                    copy.start()

        def keeps(c, sources):
            for j, (src, dst) in enumerate(zip(sources, (two_all, ups_all, inner_all, back_all))):
                yield pltpu.make_async_copy(src, dst.at[rows_of(c, chunk)], keep_sem.at[j, c])

        zeros = (zero_v, zero_v, zero_v.at[:, :ff_cols], zero_v.at[:, : 2 * ff_cols])
        for c in range(TEAM // 2, chunks):

            @pl.when(c >= used)
            def _(c=c):
                for copy in keeps(c, zeros):
                    copy.start()

        @pl.when(total % 2 == 1)
        def _():
            two_v[rows_of(total)] = jnp.zeros((TILE, width), BF16)
            ups_v[rows_of(total)] = jnp.zeros((TILE, width), BF16)

        for live, copy in loads(twos_ref, two_v, 0):
            pl.when(live)(copy.wait)
        for copy in weights:
            copy.wait()
        for live, copy in loads(ups_ref, ups_v, 1):
            pl.when(live)(copy.wait)

        def tile_stores(r, j, slot, side):
            here = pl.ds(side * TILE, TILE)
            yield pltpu.make_async_copy(
                grad_v.at[slot, here], grads_ref[r].at[rows_of(j)], tile_sem.at[0, slot, side]
            )
            yield pltpu.make_async_copy(
                out_v.at[slot, here], outs_ref[r].at[rows_of(j)], tile_sem.at[1, slot, side]
            )

        def wait_tiles(c, slot):
            for side in range(2):

                @pl.when(2 * c + side < total)
                def _(side=side):
                    for copy in tile_stores(0, 0, slot, side):
                        copy.wait()

        def body(c, carry):
            slot = c % 2
            span = rows_of(c, chunk)

            @pl.when(c >= 2)
            def _():
                wait_tiles(c - 2, slot)
                for j, copy in enumerate(keeps(c - 2, zeros)):
                    if j >= 2:
                        copy.wait()

            gate_part = product(two_v[span], wg_v[...])
            up_part = product(two_v[span], wu_v[...])
            sig = jax.nn.sigmoid(gate_part)
            silu = gate_part * sig
            inner_v[slot] = (silu * up_part).astype(BF16)
            inner_grad = product_nt(ups_v[span], wd_v[...])
            back_v[slot, :, :ff_cols] = (inner_grad * up_part * (sig + silu * (1.0 - sig))).astype(BF16)
            back_v[slot, :, ff_cols:] = (inner_grad * silu).astype(BF16)
            for copy in keeps(c, (two_v.at[span], ups_v.at[span], inner_v.at[slot], back_v.at[slot])):
                copy.start()
            grad = product_nt(back_v[slot, :, :ff_cols], wg_v[...]) + product_nt(
                back_v[slot, :, ff_cols:], wu_v[...]
            )
            grad_v[slot] = grad.astype(BF16)
            out_v[slot] = product(inner_v[slot], wd_v[...]).astype(BF16)
            for k, (r, j, live, place) in enumerate(places):
                for side in range(2):

                    @pl.when(jnp.logical_and(live, place == 2 * c + side))
                    def _(r=r, j=j, side=side):
                        for copy in tile_stores(r, j, slot, side):
                            copy.start()

            return carry

        lax.fori_loop(0, used, body, 0)
        wait_tiles(used - 2, used % 2)
        wait_tiles(used - 1, (used - 1) % 2)
        for k, (r, j, live, place) in enumerate(places):

            @pl.when(jnp.logical_not(live))
            def _(k=k, r=r, j=j):
                for copy in dead(k, r, j):
                    copy.wait()

        for c in range(chunks):
            for j, copy in enumerate(keeps(c, zeros)):
                if j < 2:
                    copy.wait()
                else:
                    pl.when(c >= used - 2)(copy.wait)

    count = whole // TILE
    result = pl.pallas_call(
        kernel,
        out_shape=[struct((rows, width), BF16)] * (2 * TEAM)
        + [
            struct((whole, ff_cols), BF16),
            struct((whole, 2 * ff_cols), BF16),
            struct((whole, width), BF16),
            struct((whole, width), BF16),
        ],
        in_specs=[SMEM] + [ANY] * (3 + 2 * TEAM),
        out_specs=[ANY] * (2 * TEAM + 4),
        scratch_shapes=[
            pltpu.VMEM((whole, width), BF16),
            pltpu.VMEM((whole, width), BF16),
            pltpu.VMEM(weight_gate.shape, BF16),
            pltpu.VMEM(weight_up.shape, BF16),
            pltpu.VMEM(weight_down.shape, BF16),
            pltpu.VMEM((2, chunk, ff_cols), BF16),
            pltpu.VMEM((2, chunk, 2 * ff_cols), BF16),
            pltpu.VMEM((2, chunk, width), BF16),
            pltpu.VMEM((2, chunk, width), BF16),
            pltpu.VMEM((chunk, width), BF16),
            pltpu.SemaphoreType.DMA((3,)),
            pltpu.SemaphoreType.DMA((2, count)),
            pltpu.SemaphoreType.DMA((4, chunks)),
            pltpu.SemaphoreType.DMA((2, 2, 2)),
            pltpu.SemaphoreType.DMA((2, count)),
        ],
        compiler_params=pltpu.CompilerParams(vmem_limit_bytes=60 << 20),
        cost_estimate=pl.CostEstimate(flops=58 << 30, bytes_accessed=100 << 20, transcendentals=1 << 20),
    )(tiles, *twos, *upstreams, weight_gate, weight_up, weight_down)
    return result[:TEAM], result[TEAM : 2 * TEAM], result[2 * TEAM :]


def local(
    groups,
    tokens,
    lengths,
    cotangent,
    attention_gain,
    query_weight,
    key_matrix,
    value_matrix,
    head_gate_weight,
    output_weight,
    query_key_gain,
    feedforward_gain,
    gate_weight,
    up_weight,
    down_weight,
):
    t = member()
    everyone = groups * TEAM
    rows, width = tokens.shape
    rho = query_weight.shape[0]
    phi = down_weight.shape[0]
    ff = gate_weight.shape[1]
    pair_cols = query_key_gain.shape[1]
    size = pair_cols * everyone
    heads = query_weight.shape[1] // size
    mine = heads // TEAM
    q_cols = query_weight.shape[1] // TEAM
    k_cols = key_matrix.shape[1] // TEAM
    ff_cols = ff // TEAM

    def everyone_in_team(vector):
        return jnp.broadcast_to(vector.reshape(1, -1), (TEAM, vector.size))

    live_tiles = (lengths + (TILE - 1)) // TILE
    row = jnp.concatenate(
        [
            head_gate_weight.reshape(rho, TEAM, mine).transpose(1, 2, 0).reshape(TEAM, -1),
            everyone_in_team(attention_gain),
            everyone_in_team(feedforward_gain),
            everyone_in_team(query_key_gain),
            everyone_in_team(live_tiles.astype(BF16)),
        ],
        axis=1,
    )
    cols = q_cols + 2 * k_cols
    row = jnp.pad(row, ((0, 0), (0, cols - row.shape[1])))[:, None, :]
    attn = jnp.concatenate(
        [
            query_weight.reshape(rho, TEAM, q_cols),
            key_matrix.reshape(rho, TEAM, k_cols),
            value_matrix.reshape(rho, TEAM, k_cols),
        ],
        axis=2,
    ).transpose(1, 0, 2)
    attn = jnp.concatenate([attn, jnp.pad(row, ((0, 0), (0, 7), (0, 0)))], axis=1)
    attn = exchange(attn)
    head_lanes = mine * rho
    at_one, at_two, at_pair = head_lanes, head_lanes + rho, head_lanes + 2 * rho
    at_tiles = at_pair + 2 * pair_cols
    team_tiles = attn[:, rho, at_tiles].astype(jnp.int32)
    order = jnp.arange(TEAM, dtype=jnp.int32)
    tiles = jnp.sum(jnp.where((order[:, None] ^ t) == order[None, :], team_tiles[None, :], 0), axis=1)
    routed = lax.ppermute(output_weight, ALL, out_weight_routes(groups))
    team_rows = TEAM * rho
    small_at = team_rows + (width // cols) * rho
    stacked = jnp.concatenate(
        [attn[:, :rho].reshape(team_rows, cols)]
        + [routed[:, k : k + cols] for k in range(0, width, cols)]
        + [attn[:, rho], jnp.zeros((16 - TEAM, cols), BF16)],
        axis=0,
    )
    gathered = line_gather(stacked).reshape(groups, -1, cols)
    rows_small = gathered[:, small_at : small_at + TEAM].reshape(everyone, cols)
    weight_head = jnp.pad(
        rows_small[:, :head_lanes].reshape(everyone, mine, rho).transpose(1, 0, 2).reshape(mine, width),
        ((0, TILE - mine), (0, 0)),
    )
    gain_one = rows_small[:, at_one:at_two].reshape(1, width).astype(F32)
    gain_two = rows_small[:, at_two:at_pair].reshape(1, width).astype(F32)
    gain_pair = (
        rows_small[:, at_pair:at_tiles]
        .reshape(everyone, 2, pair_cols)
        .transpose(1, 0, 2)
        .reshape(2, size)
        .astype(F32)
    )
    def ff_split(w):
        return w.reshape(rho, groups, TEAM, phi).transpose(2, 0, 1, 3).reshape(TEAM, rho, ff_cols)

    feed_shard = jnp.concatenate([ff_split(gate_weight), ff_split(up_weight)], axis=2)

    exponent = jnp.arange(size // 2, dtype=F32) * (-2.0 / size)
    frequency = jnp.power(ROPE_BASE, exponent)
    angles = jnp.arange(rows, dtype=F32)[:, None] * frequency[None, :]
    cosine = jnp.concatenate([jnp.cos(angles), jnp.cos(angles)], axis=1)
    sine = jnp.concatenate([-jnp.sin(angles), jnp.sin(angles)], axis=1)
    consts = (gathered, weight_head, gain_one, gain_pair, cosine, sine)
    team_tokens = team_gather(tokens)
    feed_shard = exchange(feed_shard).reshape(TEAM * rho, -1)
    weight_gate = line_gather(feed_shard[:, :ff_cols])
    live = lax.broadcasted_iota(jnp.int32, (rows, 1), 0) < lengths[0]
    live_rows = live.astype(F32)
    upstream = cotangent.astype(F32) * live_rows
    tick = mark([team_tokens[6]])
    later = lax.broadcasted_iota(jnp.int32, (rows, 1), 0) < lengths[0] + tick[0, 0]
    upstream_low = jnp.where(later, cotangent, jnp.zeros_like(cotangent))
    upstream_levels = TeamGather(upstream_low)
    parts, kept, tick = attend(tiles, team_tokens, consts, mine, mark([upstream_low]))
    normed, qkv, logit, gated = kept
    weight_up = line_gather(hold([feed_shard[:, ff_cols:]], tick)[0])
    parts = hold(parts, mark([upstream_levels.a1, upstream_levels.a2, upstream_levels.a4, tick]))
    arrived = TeamSum(parts)
    arrived.first()
    weight_down = line_gather(hold([down_weight], arrived.sent[0])[0])
    inputs = tokens.astype(F32)
    hidden_state = inputs + arrived.total(weight_gate)

    normed_two = rms(hidden_state, gain_two).astype(BF16)
    team_upstream = upstream_levels.blocks(normed_two)
    team_two = TeamGather(normed_two).blocks(weight_up)
    outs, grads, saved = feed(tiles, team_two, team_upstream, weight_gate, weight_up, weight_down)
    inner, feed_back, two_all, ups_all = saved
    arrived = TeamSum(grads)
    arrived.first()
    two_grad = arrived.total()
    down_part = product_tn(inner, ups_all).astype(BF16)
    feed_back = hold([feed_back], mark([arrived.over_x, arrived.over_y]))[0]
    gate_part = product_tn(two_all, feed_back[:, :ff_cols]).astype(BF16)
    up_part = product_tn(two_all, feed_back[:, ff_cols:]).astype(BF16)
    parts_made = mark([gate_part, up_part])
    down_grad = line_sum(down_part)
    gate_grad = line_sum(hold([gate_part], down_grad)[0])
    up_grad = line_sum(hold([up_part], gate_grad)[0])
    feed_done = up_grad
    hidden_grad = upstream + rms_pull(hidden_state, gain_two, two_grad)

    fed = TeamSum(outs)
    team_hidden = TeamGather(hidden_grad.astype(BF16)).blocks(mark(fed.ready + [gate_part, up_part]))
    two_scale = lax.rsqrt(jnp.mean(hidden_state * hidden_state, axis=-1, keepdims=True) + EPSILON)
    two_sum = jnp.sum(two_grad * hidden_state * two_scale, axis=0)
    first_hop = fed.first(mark(team_hidden + [parts_made]))
    parts, packed, head_sum, one_sum, pair_sum = attend_back(
        tiles, team_hidden, consts, (normed, qkv, logit, gated), mine, mark(fed.sent + [down_grad])
    )
    row = jnp.concatenate(
        [
            head_sum[:mine].reshape(mine, everyone, rho).transpose(1, 0, 2).reshape(everyone, -1),
            (one_sum / gain_one[0]).reshape(everyone, rho),
            two_sum.reshape(everyone, rho),
            pair_sum.reshape(2, everyone, pair_cols).transpose(1, 0, 2).reshape(everyone, -1),
        ],
        axis=1,
    ).astype(BF16)
    row = jnp.pad(row, ((0, 0), (0, cols - row.shape[1]))).reshape(groups, TEAM, cols)
    packed = lax.dynamic_update_slice(packed, row, (0, small_at, 0))
    parts = hold(parts, mark(first_hop + [gate_grad]))
    arrived = TeamSum(parts)
    arrived.first()
    packed = hold([packed.reshape(-1, cols)], mark([feed_done] + arrived.sent))[0]
    normed_grad = arrived.total(packed)
    packed = line_sum(packed)
    layer_output = ((hidden_state + fed.total(mark(arrived.last_sent))) * live_rows).astype(BF16)
    tokens_grad = (hidden_grad + rms_pull(inputs, gain_one, normed_grad)).astype(BF16)
    feed_grad = jnp.concatenate([gate_grad, hold([up_grad], mark(arrived.last_sent))[0]], axis=1)
    feed_grad = exchange(feed_grad.reshape(TEAM, rho, 2 * ff_cols))

    def ff_join(w):
        return w.reshape(TEAM, rho, groups, phi).transpose(1, 2, 0, 3).reshape(rho, ff)

    gate_grad, up_grad = hold(
        [ff_join(feed_grad[:, :, :ff_cols]), ff_join(feed_grad[:, :, ff_cols:])], normed_grad
    )
    routes = [(user, owner) for owner, user in out_weight_routes(groups)]
    output_grad = packed[team_rows:small_at].reshape(-1, rho, cols).transpose(1, 0, 2).reshape(rho, width)
    output_grad = lax.ppermute(output_grad, ALL, routes)
    packed = jnp.concatenate(
        [
            packed[:team_rows].reshape(TEAM, rho, cols),
            jnp.pad(packed[small_at : small_at + TEAM][:, None], ((0, 0), (0, 7), (0, 0))),
        ],
        axis=1,
    )
    packed = exchange(packed)
    attn_grad = packed[:, :rho].transpose(1, 0, 2)
    rows_small = packed[:, rho].astype(F32)
    sums = jnp.sum(rows_small[:, head_lanes:], axis=0)
    head_gate_grad = rows_small[:, :head_lanes].reshape(heads, rho).T
    return (
        layer_output,
        tokens_grad,
        sums[:rho],
        attn_grad[:, :, :q_cols].reshape(rho, -1).astype(F32),
        attn_grad[:, :, q_cols : q_cols + k_cols].reshape(rho, -1).astype(F32),
        attn_grad[:, :, q_cols + k_cols :].reshape(rho, -1).astype(F32),
        head_gate_grad,
        output_grad.astype(F32),
        sums[2 * rho : 2 * rho + 2 * pair_cols].reshape(2, pair_cols),
        sums[rho : 2 * rho],
        gate_grad.astype(F32),
        up_grad.astype(F32),
        down_grad.astype(F32),
    )


def solution(mesh):
    groups = mesh.size // TEAM
    rows, vector, columns = P(ALL, None), P(ALL), P(None, ALL)

    def step(*args):
        return local(groups, *args)

    return jax.shard_map(
        step,
        mesh=mesh,
        in_specs=(
            rows, vector, rows, vector, rows, rows, rows, rows, rows, columns, vector, rows, rows, rows,
        ),
        out_specs=(
            rows, rows, vector, rows, rows, rows, rows, rows, columns, vector, rows, rows, rows,
        ),
        check_vma=False,
    )
```

```python
import jax
import jax.numpy as jnp
from jax import lax
from jax.experimental import pallas as pl
from jax.experimental.pallas import tpu as pltpu
from jax.sharding import PartitionSpec as P

EPSILON = 1e-06
ROPE_BASE = 1000000.0
TEAM = 8
ALL = ("dp", "fsdp")
F32 = jnp.float32
BF16 = jnp.bfloat16
TILE = 128
ANY = pl.BlockSpec(memory_space=pl.ANY)
VMEM = pl.BlockSpec(memory_space=pltpu.VMEM)
SMEM = pl.BlockSpec(memory_space=pltpu.SMEM)


def product(left, right):
    return jnp.dot(left, right, preferred_element_type=F32)


def product_nt(left, right):
    return lax.dot_general(left, right, (((1,), (1,)), ((), ())), preferred_element_type=F32)


def product_tn(left, right):
    return lax.dot_general(left, right, (((0,), (0,)), ((), ())), preferred_element_type=F32)


def world():
    return lax.axis_size(ALL)


def member():
    return lax.axis_index(ALL) % TEAM


def teams():
    return [[first + t for t in range(TEAM)] for first in range(0, world(), TEAM)]


def lines():
    return [list(range(t, world(), TEAM)) for t in range(TEAM)]


def permute(array, pairs):
    return lax.ppermute(
        array, ALL, [(team[a], team[b]) for team in teams() for a, b in pairs]
    )


def swap(array, bits):
    return permute(array, [(i, i ^ bits) for i in range(TEAM)])


def exchange(blocks):
    if lax.axis_size("fsdp") == TEAM:
        return lax.all_to_all(blocks, "fsdp", 0, 0, tiled=True)
    return lax.all_to_all(blocks, ALL, 0, 0, tiled=True, axis_index_groups=teams())


def line_gather(shard):
    if lax.axis_size("fsdp") == TEAM:
        return lax.all_gather(shard, "dp", axis=0, tiled=True)
    return lax.all_gather(shard, ALL, axis=0, tiled=True, axis_index_groups=lines())


def line_sum(array):
    if lax.axis_size("fsdp") == TEAM:
        return lax.psum_scatter(array, "dp", scatter_dimension=0, tiled=True)
    return lax.psum_scatter(array, ALL, scatter_dimension=0, tiled=True, axis_index_groups=lines())


class TeamGather:
    def __init__(self, own):
        self.own = own
        self.a1 = swap(own, 1)
        self.a2 = swap(own, 2)
        self.a4 = swap(own, 4)

    def blocks(self, tick=None):
        a2, a4 = self.a2, self.a4
        if tick is not None:
            a2, a4 = hold([a2, a4], tick)
        half = self.own.shape[0] // 2
        a6 = jnp.concatenate([swap(a4[:half], 2), swap(a2[half:], 4)], axis=0)
        return [self.own, self.a1, a2, swap(a2, 1), a4, swap(a4, 1), a6, swap(a6, 1)]


def team_gather(own):
    return TeamGather(own).blocks()


class TeamSum:
    def __init__(self, parts):
        half = parts[0].shape[0] // 2
        odd = {r: swap(parts[r + 1], 1) for r in (6, 2, 4, 0)}
        self.total6, self.total2, self.total4, self.total0 = (
            (parts[r].astype(F32) + odd[r].astype(F32)).astype(BF16) for r in (6, 2, 4, 0)
        )
        self.half = half
        self.ready = [
            jnp.concatenate([self.total6[:half], self.total2[:half]], axis=0),
            jnp.concatenate([self.total6[half:], self.total4[half:]], axis=0),
        ]

    def first(self, tick=None):
        self.sent = self.ready if tick is None else list(hold(self.ready, tick))
        self.over_x, self.over_y = swap(self.sent[0], 2), swap(self.sent[1], 4)
        return [self.over_x, self.over_y]

    def total(self, tick=None):
        half = self.half
        lasts = [
            (self.total2[half:].astype(F32) + self.over_y[:half].astype(F32)).astype(BF16),
            (self.total4[:half].astype(F32) + self.over_x[:half].astype(F32)).astype(BF16),
        ]
        x_low, y_top = lasts if tick is None else hold(lasts, tick)
        self.last_sent = [x_low, y_top]
        x_low = swap(x_low, 2).astype(F32)
        y_top = swap(y_top, 4).astype(F32)
        top = self.over_x[half:].astype(F32) + y_top
        low = x_low + self.over_y[half:].astype(F32)
        return self.total0.astype(F32) + jnp.concatenate([top, low], axis=0)


def out_weight_routes(groups):
    return [(i, TEAM * (i % groups) + i // groups) for i in range(groups * TEAM)]


def rms_pull(value, gain, grad):
    scale = lax.rsqrt(jnp.mean(value * value, axis=-1, keepdims=True) + EPSILON)
    weighted = grad * gain
    mean = jnp.mean(weighted * value, axis=-1, keepdims=True)
    return scale * weighted - scale * scale * scale * value * mean


def rms(value, gain):
    return value * lax.rsqrt(jnp.mean(value * value, axis=-1, keepdims=True) + EPSILON) * gain


def struct(shape, dtype):
    return jax.ShapeDtypeStruct(shape, dtype)


def hold(arrays, tick):
    def kernel(*refs):
        del refs

    count = len(arrays)
    return pl.pallas_call(
        kernel,
        out_shape=[struct(a.shape, a.dtype) for a in arrays],
        in_specs=[ANY] * count + [ANY],
        out_specs=[ANY] * count,
        input_output_aliases={i: i for i in range(count)},
    )(*arrays, tick)


def mark(arrays):
    def kernel(*refs):
        refs[-1][...] = jnp.zeros_like(refs[-1])

    return pl.pallas_call(
        kernel,
        out_shape=struct((8, 128), jnp.int32),
        in_specs=[ANY] * len(arrays),
        out_specs=VMEM,
    )(*arrays)


def for_tiles(tiles, most, body):
    for m in range(1, most + 1):

        @pl.when(tiles == m)
        def _(m=m):
            body(m * TILE)


def turned(u, cosine, sine):
    return u * cosine + pltpu.roll(u, u.shape[-1] // 2, 1) * sine


def head_norm(u):
    return lax.rsqrt(jnp.mean(u * u, axis=-1, keepdims=True) + EPSILON)


def head_back(grad, raw, gain, cosine, sine):
    e = turned(grad, cosine, -sine)
    scale = head_norm(raw)
    weighted = e * gain
    mean = jnp.mean(weighted * raw, axis=-1, keepdims=True)
    back = scale * weighted - scale * scale * scale * raw * mean
    return back, jnp.sum(e * raw * scale, axis=0, keepdims=True)


def weights_of(query, key, factor):
    scores = product_nt(query, key) * factor
    n = scores.shape[0]
    causal = lax.broadcasted_iota(jnp.int32, (n, n), 1) <= lax.broadcasted_iota(jnp.int32, (n, n), 0)
    scores = jnp.where(causal, scores, -jnp.inf)
    terms = jnp.exp(scores - jnp.max(scores, axis=-1, keepdims=True))
    return terms * (1.0 / jnp.sum(terms, axis=-1, keepdims=True))


def rows_of(tile, size=TILE):
    return pl.ds(pl.multiple_of(tile * size, size), size)


def each_block(r, body):
    for k in range(TEAM):
        pl.when(r == k)(lambda k=k: body(k))


def load_weights(gathered, weight_head, wa_v, wo_v, wh_v, sems):
    groups, _, cols = gathered.shape
    width = wo_v.shape[1]
    rho = width // (groups * TEAM)
    copies = [pltpu.make_async_copy(weight_head, wh_v, sems.at[0])]
    for g in range(groups):
        copies.append(
            pltpu.make_async_copy(
                gathered.at[g, pl.ds(0, TEAM * rho)],
                wa_v.at[pl.ds(g * TEAM * rho, TEAM * rho)],
                sems.at[len(copies)],
            )
        )
        for k in range(width // cols):
            copies.append(
                pltpu.make_async_copy(
                    gathered.at[g, pl.ds(TEAM * rho + k * rho, rho)],
                    wo_v.at[pl.ds(g * rho, rho), pl.ds(k * cols, cols)],
                    sems.at[len(copies)],
                )
            )
    return copies


def attend(tiles, tokens, consts, mine, after):
    gathered, weight_head, gain, gains, cosine, sine = consts
    rows, width = tokens[0].shape
    size = gains.shape[1]
    q_cols = mine * size
    cols = gathered.shape[2]
    factor = size ** (-0.5)

    def kernel(*refs):
        tiles_ref, toks = refs[0], refs[1 : 1 + TEAM]
        wa, wh, gain_ref, gains_ref, cos_ref, sin_ref, _ = refs[1 + TEAM : 8 + TEAM]
        parts = refs[8 + TEAM : 8 + 2 * TEAM]
        normed_all, qkv_all, logit_all, gated_all, tick = refs[8 + 2 * TEAM : 13 + 2 * TEAM]
        (
            tok_v, wa_v, wh_v, wo_v, part_v, normed_v, qkv_v, logit_v, gated_v, w_sem, in_sem, out_sem,
        ) = refs[13 + 2 * TEAM :]
        tick[...] = jnp.zeros_like(tick)

        def load(k, slot):
            return pltpu.make_async_copy(toks[k], tok_v.at[slot], in_sem.at[slot])

        def store(r, slot, j, k=0):
            src = (part_v, normed_v, qkv_v, logit_v, gated_v)[j].at[slot]
            dst = parts[k] if j == 0 else (normed_all, qkv_all, logit_all, gated_all)[j - 1].at[rows_of(r, rows)]
            return pltpu.make_async_copy(src, dst, out_sem.at[j, slot])

        load(0, 0).start()
        weights = load_weights(wa, wh, wa_v, wo_v, wh_v, w_sem)
        for copy in weights:
            copy.start()
        for copy in weights:
            copy.wait()

        def step(r, carry):
            slot = r % 2

            @pl.when(r + 1 < TEAM)
            def _():
                each_block(r + 1, lambda k: load(k, 1 - slot).start())

            load(0, slot).wait()

            @pl.when(r >= 2)
            def _():
                for j in range(5):
                    store(r - 2, slot, j).wait()

            def body(n):
                value = tok_v[slot, :n].astype(F32)
                normed = rms(value, gain_ref[...]).astype(BF16)
                normed_v[slot, :n] = normed
                qkv = product(normed, wa_v[...])
                qkv_v[slot, :n] = qkv
                logit = product_nt(normed, wh_v[...])
                logit_v[slot, :n] = logit
                cos, sin = cos_ref[:n], sin_ref[:n]
                key = qkv[:, q_cols : q_cols + size]
                key = turned(key * head_norm(key) * gains_ref[1:2], cos, sin).astype(BF16)
                values = qkv[:, q_cols + size :].astype(BF16)
                for h in range(mine):
                    query = qkv[:, h * size : (h + 1) * size]
                    query = turned(query * head_norm(query) * gains_ref[0:1], cos, sin).astype(BF16)
                    attention = weights_of(query, key, factor)
                    mixture = product(attention.astype(BF16), values)
                    gate = jax.nn.sigmoid(logit[:, h : h + 1])
                    gated_v[slot, :n, h * size : (h + 1) * size] = (mixture * gate).astype(BF16)
                part_v[slot, :n] = product(gated_v[slot, :n], wo_v[...]).astype(BF16)
                if n < rows:
                    part_v[slot, n:] = jnp.zeros((rows - n, width), BF16)
                    normed_v[slot, n:] = jnp.zeros((rows - n, width), BF16)
                    gated_v[slot, n:] = jnp.zeros((rows - n, q_cols), BF16)

            for_tiles(tiles_ref[r], rows // TILE, body)
            each_block(r, lambda k: store(r, slot, 0, k).start())
            for j in range(1, 5):
                store(r, slot, j).start()
            return carry

        lax.fori_loop(0, TEAM, step, 0)
        for r in (TEAM - 2, TEAM - 1):
            for j in range(5):
                store(r, r % 2, j).wait()

    whole = TEAM * rows
    result = pl.pallas_call(
        kernel,
        out_shape=[struct((rows, width), BF16)] * TEAM
        + [
            struct((whole, width), BF16),
            struct((whole, cols), F32),
            struct((whole, TILE), F32),
            struct((whole, q_cols), BF16),
            struct((8, 128), jnp.int32),
        ],
        in_specs=[SMEM] + [ANY] * (TEAM + 2) + [VMEM] * 4 + [ANY],
        out_specs=[ANY] * (TEAM + 4) + [VMEM],
        scratch_shapes=[
            pltpu.VMEM((2, rows, width), BF16),
            pltpu.VMEM((width, cols), BF16),
            pltpu.VMEM(weight_head.shape, BF16),
            pltpu.VMEM((q_cols, width), BF16),
            pltpu.VMEM((2, rows, width), BF16),
            pltpu.VMEM((2, rows, width), BF16),
            pltpu.VMEM((2, rows, cols), F32),
            pltpu.VMEM((2, rows, TILE), F32),
            pltpu.VMEM((2, rows, q_cols), BF16),
            pltpu.SemaphoreType.DMA((1 + gathered.shape[0] * (1 + width // cols),)),
            pltpu.SemaphoreType.DMA((2,)),
            pltpu.SemaphoreType.DMA((5, 2)),
        ],
        compiler_params=pltpu.CompilerParams(vmem_limit_bytes=48 << 20),
        cost_estimate=pl.CostEstimate(flops=30 << 30, bytes_accessed=60 << 20, transcendentals=1 << 20),
    )(tiles, *tokens, gathered, weight_head, gain, gains, cosine, sine, after)
    return result[:TEAM], result[TEAM : TEAM + 4], result[TEAM + 4]


def attend_back(tiles, hidden, consts, saved, mine, after):
    gathered, weight_head, gain, gains, cosine, sine = consts
    rows, width = hidden[0].shape
    size = gains.shape[1]
    q_cols = mine * size
    cols = gathered.shape[2]
    factor = size ** (-0.5)

    def kernel(*refs):
        tiles_ref, hids = refs[0], refs[1 : 1 + TEAM]
        wa, wh, normed_all, qkv_all, logit_all, gated_all = refs[1 + TEAM : 7 + TEAM]
        gains_ref, cos_ref, sin_ref, _ = refs[7 + TEAM : 11 + TEAM]
        parts = refs[11 + TEAM : 11 + 2 * TEAM]
        packed, head_sum, gain_sum, gains_sum = refs[11 + 2 * TEAM : 15 + 2 * TEAM]
        (
            hid_v, wa_v, wh_v, wo_v, normed_v, qkv_v, logit_v, gated_v, part_v, back_v, attn_sum, out_sum,
            w_sem, in_sem, out_sem,
        ) = refs[15 + 2 * TEAM :]

        def loads(r, slot, k):
            yield pltpu.make_async_copy(hids[k], hid_v.at[slot], in_sem.at[0, slot])
            here = rows_of(r, rows)
            for j, (src, dst) in enumerate(
                ((qkv_all, qkv_v), (logit_all, logit_v), (normed_all, normed_v), (gated_all, gated_v))
            ):
                yield pltpu.make_async_copy(src.at[here], dst.at[slot], in_sem.at[1 + j, slot])

        def start_loads(r, slot):
            def body(k):
                for copy in loads(r, slot, k):
                    copy.start()

            each_block(r, body)

        def store(slot, k=0):
            return pltpu.make_async_copy(part_v.at[slot], parts[k], out_sem.at[slot])

        for copy in loads(0, 0, 0):
            copy.start()
        weights = load_weights(wa, wh, wa_v, wo_v, wh_v, w_sem)
        for copy in weights:
            copy.start()
        for ref in (attn_sum, out_sum, gain_sum, gains_sum):
            ref[...] = jnp.zeros_like(ref)
        for copy in weights:
            copy.wait()

        def step(r, carry):
            slot = r % 2

            @pl.when(r + 1 < TEAM)
            def _():
                start_loads(r + 1, 1 - slot)

            for copy in loads(r, slot, 0):
                copy.wait()

            @pl.when(r >= 2)
            def _():
                store(slot).wait()

            def body(n):
                hidden_low = hid_v[slot, :n]
                normed = normed_v[slot, :n]
                out_sum[...] += product_tn(gated_v[slot, :n], hidden_low)
                gated_grad = product_nt(hidden_low, wo_v[...])
                cos, sin = cos_ref[:n], sin_ref[:n]
                key_raw = qkv_v[slot, :n, q_cols : q_cols + size]
                key = turned(key_raw * head_norm(key_raw) * gains_ref[1:2], cos, sin).astype(BF16)
                values = qkv_v[slot, :n, q_cols + size :].astype(BF16)
                lane = lax.broadcasted_iota(jnp.int32, (n, TILE), 1)
                logit_back = jnp.zeros((n, TILE), F32)
                values_back = jnp.zeros((n, size), F32)
                key_grad = jnp.zeros((n, size), F32)
                query_sum = jnp.zeros((1, size), F32)
                for h in range(mine):
                    span = slice(h * size, (h + 1) * size)
                    query_raw = qkv_v[slot, :n, span]
                    query = turned(query_raw * head_norm(query_raw) * gains_ref[0:1], cos, sin).astype(BF16)
                    attention = weights_of(query, key, factor)
                    attention_low = attention.astype(BF16)
                    mixture = product(attention_low, values)
                    gate = jax.nn.sigmoid(logit_v[slot, :n, h : h + 1])
                    head_grad = gated_grad[:, span]
                    mixture_back = (head_grad * gate).astype(BF16)
                    one = jnp.sum(head_grad * mixture, axis=-1, keepdims=True) * gate * (1.0 - gate)
                    logit_back = jnp.where(lane == h, one, logit_back)
                    values_back += product_tn(attention_low, mixture_back)
                    attention_grad = product_nt(mixture_back, values)
                    scores_back = (
                        attention
                        * (attention_grad - jnp.sum(attention_grad * attention, axis=-1, keepdims=True))
                    ).astype(BF16)
                    query_grad = product(scores_back, key) * factor
                    key_grad += product_tn(scores_back, query)
                    back, total = head_back(query_grad, query_raw, gains_ref[0:1], cos, sin)
                    back_v[:n, span] = back.astype(BF16)
                    query_sum += total
                back, key_sum = head_back(key_grad * factor, key_raw, gains_ref[1:2], cos, sin)
                back_v[:n, q_cols : q_cols + size] = back.astype(BF16)
                back_v[:n, q_cols + size : cols] = values_back.astype(BF16)
                logit_back = logit_back.astype(BF16)
                back_v[:n, cols:] = logit_back
                gains_sum[0:1] += query_sum
                gains_sum[1:2] += key_sum
                part = product_nt(back_v[:n, :cols], wa_v[...]) + product(logit_back, wh_v[...])
                part_v[slot, :n] = part.astype(BF16)
                gain_sum[0:1] += jnp.sum(part * normed.astype(F32), axis=0, keepdims=True)
                attn_sum[...] += product_tn(back_v[:n], normed)
                if n < rows:
                    part_v[slot, n:] = jnp.zeros((rows - n, width), BF16)

            for_tiles(tiles_ref[r], rows // TILE, body)
            each_block(r, lambda k: store(slot, k).start())
            return carry

        lax.fori_loop(0, TEAM, step, 0)
        head_sum[...] = attn_sum[cols : cols + 8]
        turned_sum = attn_sum[:cols].T.astype(BF16)
        groups, height, _ = packed.shape
        rho = width // (groups * TEAM)
        for g in range(groups):
            packed[g, : TEAM * rho] = turned_sum[g * TEAM * rho : (g + 1) * TEAM * rho]
            for k in range(width // cols):
                top = TEAM * rho + k * rho
                packed[g, top : top + rho] = out_sum[
                    g * rho : (g + 1) * rho, k * cols : (k + 1) * cols
                ].astype(BF16)
            packed[g, height - 16 :] = jnp.zeros((16, cols), BF16)
        store(0).wait()
        store(1).wait()

    result = pl.pallas_call(
        kernel,
        out_shape=[struct((rows, width), BF16)] * TEAM
        + [
            struct(gathered.shape, BF16),
            struct((8, width), F32),
            struct((8, width), F32),
            struct((8, size), F32),
        ],
        in_specs=[SMEM] + [ANY] * (TEAM + 6) + [VMEM] * 3 + [ANY],
        out_specs=[ANY] * TEAM + [VMEM] * 4,
        scratch_shapes=[
            pltpu.VMEM((2, rows, width), BF16),
            pltpu.VMEM((width, cols), BF16),
            pltpu.VMEM(weight_head.shape, BF16),
            pltpu.VMEM((q_cols, width), BF16),
            pltpu.VMEM((2, rows, width), BF16),
            pltpu.VMEM((2, rows, cols), F32),
            pltpu.VMEM((2, rows, TILE), F32),
            pltpu.VMEM((2, rows, q_cols), BF16),
            pltpu.VMEM((2, rows, width), BF16),
            pltpu.VMEM((rows, cols + TILE), BF16),
            pltpu.VMEM((cols + TILE, width), F32),
            pltpu.VMEM((q_cols, width), F32),
            pltpu.SemaphoreType.DMA((1 + gathered.shape[0] * (1 + width // cols),)),
            pltpu.SemaphoreType.DMA((5, 2)),
            pltpu.SemaphoreType.DMA((2,)),
        ],
        compiler_params=pltpu.CompilerParams(vmem_limit_bytes=56 << 20),
        cost_estimate=pl.CostEstimate(flops=45 << 30, bytes_accessed=70 << 20, transcendentals=1 << 20),
    )(tiles, *hidden, gathered, weight_head, *saved, gains, cosine, sine, after)
    return result[:TEAM], *result[TEAM : TEAM + 2], result[TEAM + 2][0], result[TEAM + 3][:2]


def tile_places(tiles_ref, rows):
    places, total = [], 0
    for r in range(TEAM):
        count = tiles_ref[r]
        for j in range(rows // TILE):
            places.append((r, j, j < count, total + j))
        total = total + count
    return places, total


def feed(tiles, twos, upstreams, weight_gate, weight_up, weight_down):
    rows, width = twos[0].shape
    ff_cols = weight_down.shape[0]
    whole = TEAM * rows
    chunk = 2 * TILE
    chunks = whole // chunk

    def kernel(*refs):
        tiles_ref, twos_ref, ups_ref = refs[0], refs[1 : 1 + TEAM], refs[1 + TEAM : 1 + 2 * TEAM]
        weights_ref = refs[1 + 2 * TEAM : 4 + 2 * TEAM]
        outs_ref = refs[4 + 2 * TEAM : 4 + 3 * TEAM]
        grads_ref = refs[4 + 3 * TEAM : 4 + 4 * TEAM]
        inner_all, back_all, two_all, ups_all = refs[4 + 4 * TEAM : 8 + 4 * TEAM]
        (
            two_v, ups_v, wg_v, wu_v, wd_v, inner_v, back_v, out_v, grad_v, zero_v,
            w_sem, load_sem, keep_sem, tile_sem, dead_sem,
        ) = refs[8 + 4 * TEAM :]
        places, total = tile_places(tiles_ref, rows)
        used = (total + 1) // 2

        def loads(sources, packed, which):
            for k, (r, j, live, place) in enumerate(places):
                yield live, pltpu.make_async_copy(
                    sources[r].at[rows_of(j)], packed.at[rows_of(place)], load_sem.at[which, k]
                )

        weights = [
            pltpu.make_async_copy(src, dst, w_sem.at[j])
            for j, (src, dst) in enumerate(zip(weights_ref, (wg_v, wu_v, wd_v)))
        ]
        for live, copy in loads(twos_ref, two_v, 0):
            pl.when(live)(copy.start)
        for copy in weights:
            copy.start()
        for live, copy in loads(ups_ref, ups_v, 1):
            pl.when(live)(copy.start)
        zero_v[...] = jnp.zeros_like(zero_v)

        def dead(k, r, j):
            zeros = zero_v.at[:TILE]
            yield pltpu.make_async_copy(zeros, grads_ref[r].at[rows_of(j)], dead_sem.at[0, k])
            yield pltpu.make_async_copy(zeros, outs_ref[r].at[rows_of(j)], dead_sem.at[1, k])

        for k, (r, j, live, place) in enumerate(places):

            @pl.when(jnp.logical_not(live))
            def _(k=k, r=r, j=j):
                for copy in dead(k, r, j):
                    copy.start()

        def keeps(c, sources):
            for j, (src, dst) in enumerate(zip(sources, (two_all, ups_all, inner_all, back_all))):
                yield pltpu.make_async_copy(src, dst.at[rows_of(c, chunk)], keep_sem.at[j, c])

        zeros = (zero_v, zero_v, zero_v.at[:, :ff_cols], zero_v.at[:, : 2 * ff_cols])
        for c in range(TEAM // 2, chunks):

            @pl.when(c >= used)
            def _(c=c):
                for copy in keeps(c, zeros):
                    copy.start()

        @pl.when(total % 2 == 1)
        def _():
            two_v[rows_of(total)] = jnp.zeros((TILE, width), BF16)
            ups_v[rows_of(total)] = jnp.zeros((TILE, width), BF16)

        for live, copy in loads(twos_ref, two_v, 0):
            pl.when(live)(copy.wait)
        for copy in weights:
            copy.wait()
        for live, copy in loads(ups_ref, ups_v, 1):
            pl.when(live)(copy.wait)

        def tile_stores(r, j, slot, side):
            here = pl.ds(side * TILE, TILE)
            yield pltpu.make_async_copy(
                grad_v.at[slot, here], grads_ref[r].at[rows_of(j)], tile_sem.at[0, slot, side]
            )
            yield pltpu.make_async_copy(
                out_v.at[slot, here], outs_ref[r].at[rows_of(j)], tile_sem.at[1, slot, side]
            )

        def wait_tiles(c, slot):
            for side in range(2):

                @pl.when(2 * c + side < total)
                def _(side=side):
                    for copy in tile_stores(0, 0, slot, side):
                        copy.wait()

        def body(c, carry):
            slot = c % 2
            span = rows_of(c, chunk)

            @pl.when(c >= 2)
            def _():
                wait_tiles(c - 2, slot)
                for j, copy in enumerate(keeps(c - 2, zeros)):
                    if j >= 2:
                        copy.wait()

            gate_part = product(two_v[span], wg_v[...])
            up_part = product(two_v[span], wu_v[...])
            sig = jax.nn.sigmoid(gate_part)
            silu = gate_part * sig
            inner_v[slot] = (silu * up_part).astype(BF16)
            inner_grad = product_nt(ups_v[span], wd_v[...])
            back_v[slot, :, :ff_cols] = (inner_grad * up_part * (sig + silu * (1.0 - sig))).astype(BF16)
            back_v[slot, :, ff_cols:] = (inner_grad * silu).astype(BF16)
            for copy in keeps(c, (two_v.at[span], ups_v.at[span], inner_v.at[slot], back_v.at[slot])):
                copy.start()
            grad = product_nt(back_v[slot, :, :ff_cols], wg_v[...]) + product_nt(
                back_v[slot, :, ff_cols:], wu_v[...]
            )
            grad_v[slot] = grad.astype(BF16)
            out_v[slot] = product(inner_v[slot], wd_v[...]).astype(BF16)
            for k, (r, j, live, place) in enumerate(places):
                for side in range(2):

                    @pl.when(jnp.logical_and(live, place == 2 * c + side))
                    def _(r=r, j=j, side=side):
                        for copy in tile_stores(r, j, slot, side):
                            copy.start()

            return carry

        lax.fori_loop(0, used, body, 0)
        wait_tiles(used - 2, used % 2)
        wait_tiles(used - 1, (used - 1) % 2)
        for k, (r, j, live, place) in enumerate(places):

            @pl.when(jnp.logical_not(live))
            def _(k=k, r=r, j=j):
                for copy in dead(k, r, j):
                    copy.wait()

        for c in range(chunks):
            for j, copy in enumerate(keeps(c, zeros)):
                if j < 2:
                    copy.wait()
                else:
                    pl.when(c >= used - 2)(copy.wait)

    count = whole // TILE
    result = pl.pallas_call(
        kernel,
        out_shape=[struct((rows, width), BF16)] * (2 * TEAM)
        + [
            struct((whole, ff_cols), BF16),
            struct((whole, 2 * ff_cols), BF16),
            struct((whole, width), BF16),
            struct((whole, width), BF16),
        ],
        in_specs=[SMEM] + [ANY] * (3 + 2 * TEAM),
        out_specs=[ANY] * (2 * TEAM + 4),
        scratch_shapes=[
            pltpu.VMEM((whole, width), BF16),
            pltpu.VMEM((whole, width), BF16),
            pltpu.VMEM(weight_gate.shape, BF16),
            pltpu.VMEM(weight_up.shape, BF16),
            pltpu.VMEM(weight_down.shape, BF16),
            pltpu.VMEM((2, chunk, ff_cols), BF16),
            pltpu.VMEM((2, chunk, 2 * ff_cols), BF16),
            pltpu.VMEM((2, chunk, width), BF16),
            pltpu.VMEM((2, chunk, width), BF16),
            pltpu.VMEM((chunk, width), BF16),
            pltpu.SemaphoreType.DMA((3,)),
            pltpu.SemaphoreType.DMA((2, count)),
            pltpu.SemaphoreType.DMA((4, chunks)),
            pltpu.SemaphoreType.DMA((2, 2, 2)),
            pltpu.SemaphoreType.DMA((2, count)),
        ],
        compiler_params=pltpu.CompilerParams(vmem_limit_bytes=60 << 20),
        cost_estimate=pl.CostEstimate(flops=58 << 30, bytes_accessed=100 << 20, transcendentals=1 << 20),
    )(tiles, *twos, *upstreams, weight_gate, weight_up, weight_down)
    return result[:TEAM], result[TEAM : 2 * TEAM], result[2 * TEAM :]


def local(
    groups,
    tokens,
    lengths,
    cotangent,
    attention_gain,
    query_weight,
    key_matrix,
    value_matrix,
    head_gate_weight,
    output_weight,
    query_key_gain,
    feedforward_gain,
    gate_weight,
    up_weight,
    down_weight,
):
    t = member()
    everyone = groups * TEAM
    rows, width = tokens.shape
    rho = query_weight.shape[0]
    phi = down_weight.shape[0]
    ff = gate_weight.shape[1]
    pair_cols = query_key_gain.shape[1]
    size = pair_cols * everyone
    heads = query_weight.shape[1] // size
    mine = heads // TEAM
    q_cols = query_weight.shape[1] // TEAM
    k_cols = key_matrix.shape[1] // TEAM
    ff_cols = ff // TEAM

    def everyone_in_team(vector):
        return jnp.broadcast_to(vector.reshape(1, -1), (TEAM, vector.size))

    live_tiles = (lengths + (TILE - 1)) // TILE
    row = jnp.concatenate(
        [
            head_gate_weight.reshape(rho, TEAM, mine).transpose(1, 2, 0).reshape(TEAM, -1),
            everyone_in_team(attention_gain),
            everyone_in_team(feedforward_gain),
            everyone_in_team(query_key_gain),
            everyone_in_team(live_tiles.astype(BF16)),
        ],
        axis=1,
    )
    cols = q_cols + 2 * k_cols
    row = jnp.pad(row, ((0, 0), (0, cols - row.shape[1])))[:, None, :]
    attn = jnp.concatenate(
        [
            query_weight.reshape(rho, TEAM, q_cols),
            key_matrix.reshape(rho, TEAM, k_cols),
            value_matrix.reshape(rho, TEAM, k_cols),
        ],
        axis=2,
    ).transpose(1, 0, 2)
    attn = jnp.concatenate([attn, jnp.pad(row, ((0, 0), (0, 7), (0, 0)))], axis=1)
    attn = exchange(attn)
    head_lanes = mine * rho
    at_one, at_two, at_pair = head_lanes, head_lanes + rho, head_lanes + 2 * rho
    at_tiles = at_pair + 2 * pair_cols
    team_tiles = attn[:, rho, at_tiles].astype(jnp.int32)
    order = jnp.arange(TEAM, dtype=jnp.int32)
    tiles = jnp.sum(jnp.where((order[:, None] ^ t) == order[None, :], team_tiles[None, :], 0), axis=1)
    routed = lax.ppermute(output_weight, ALL, out_weight_routes(groups))
    team_rows = TEAM * rho
    small_at = team_rows + (width // cols) * rho
    stacked = jnp.concatenate(
        [attn[:, :rho].reshape(team_rows, cols)]
        + [routed[:, k : k + cols] for k in range(0, width, cols)]
        + [attn[:, rho], jnp.zeros((16 - TEAM, cols), BF16)],
        axis=0,
    )
    gathered = line_gather(stacked).reshape(groups, -1, cols)
    rows_small = gathered[:, small_at : small_at + TEAM].reshape(everyone, cols)
    weight_head = jnp.pad(
        rows_small[:, :head_lanes].reshape(everyone, mine, rho).transpose(1, 0, 2).reshape(mine, width),
        ((0, TILE - mine), (0, 0)),
    )
    gain_one = rows_small[:, at_one:at_two].reshape(1, width).astype(F32)
    gain_two = rows_small[:, at_two:at_pair].reshape(1, width).astype(F32)
    gain_pair = (
        rows_small[:, at_pair:at_tiles]
        .reshape(everyone, 2, pair_cols)
        .transpose(1, 0, 2)
        .reshape(2, size)
        .astype(F32)
    )
    def ff_split(w):
        return w.reshape(rho, groups, TEAM, phi).transpose(2, 0, 1, 3).reshape(TEAM, rho, ff_cols)

    feed_shard = jnp.concatenate([ff_split(gate_weight), ff_split(up_weight)], axis=2)

    exponent = jnp.arange(size // 2, dtype=F32) * (-2.0 / size)
    frequency = jnp.power(ROPE_BASE, exponent)
    angles = jnp.arange(rows, dtype=F32)[:, None] * frequency[None, :]
    cosine = jnp.concatenate([jnp.cos(angles), jnp.cos(angles)], axis=1)
    sine = jnp.concatenate([-jnp.sin(angles), jnp.sin(angles)], axis=1)
    consts = (gathered, weight_head, gain_one, gain_pair, cosine, sine)
    team_tokens = team_gather(tokens)
    feed_shard = exchange(feed_shard).reshape(TEAM * rho, -1)
    weight_gate = line_gather(feed_shard[:, :ff_cols])
    live = lax.broadcasted_iota(jnp.int32, (rows, 1), 0) < lengths[0]
    live_rows = live.astype(F32)
    upstream = cotangent.astype(F32) * live_rows
    tick = mark([team_tokens[6]])
    later = lax.broadcasted_iota(jnp.int32, (rows, 1), 0) < lengths[0] + tick[0, 0]
    upstream_low = jnp.where(later, cotangent, jnp.zeros_like(cotangent))
    upstream_levels = TeamGather(upstream_low)
    parts, kept, tick = attend(tiles, team_tokens, consts, mine, mark([upstream_low]))
    normed, qkv, logit, gated = kept
    weight_up = line_gather(hold([feed_shard[:, ff_cols:]], tick)[0])
    parts = hold(parts, mark([upstream_levels.a1, upstream_levels.a2, upstream_levels.a4, tick]))
    arrived = TeamSum(parts)
    arrived.first()
    weight_down = line_gather(hold([down_weight], arrived.sent[0])[0])
    inputs = tokens.astype(F32)
    hidden_state = inputs + arrived.total(weight_gate)

    normed_two = rms(hidden_state, gain_two).astype(BF16)
    team_upstream = upstream_levels.blocks(normed_two)
    team_two = TeamGather(normed_two).blocks(weight_up)
    outs, grads, saved = feed(tiles, team_two, team_upstream, weight_gate, weight_up, weight_down)
    inner, feed_back, two_all, ups_all = saved
    arrived = TeamSum(grads)
    arrived.first()
    two_grad = arrived.total()
    inner = hold([inner], mark(arrived.sent))[0]
    down_part = product_tn(inner, ups_all).astype(BF16)
    feed_back = hold([feed_back], mark([arrived.over_x, arrived.over_y]))[0]
    gate_part = product_tn(two_all, feed_back[:, :ff_cols]).astype(BF16)
    up_part = product_tn(two_all, feed_back[:, ff_cols:]).astype(BF16)
    parts_made = mark([gate_part, up_part])
    down_grad = line_sum(down_part)
    gate_grad = line_sum(hold([gate_part], down_grad)[0])
    up_grad = line_sum(hold([up_part], gate_grad)[0])
    feed_done = up_grad
    hidden_grad = upstream + rms_pull(hidden_state, gain_two, two_grad)

    fed = TeamSum(hold(outs, arrived.over_x))
    team_hidden = TeamGather(hidden_grad.astype(BF16)).blocks(mark(fed.ready + [gate_part, up_part]))
    two_scale = lax.rsqrt(jnp.mean(hidden_state * hidden_state, axis=-1, keepdims=True) + EPSILON)
    two_sum = jnp.sum(two_grad * hidden_state * two_scale, axis=0)
    first_hop = fed.first(mark(team_hidden + [parts_made]))
    parts, packed, head_sum, one_sum, pair_sum = attend_back(
        tiles, team_hidden, consts, (normed, qkv, logit, gated), mine, mark(fed.sent + [down_grad])
    )
    row = jnp.concatenate(
        [
            head_sum[:mine].reshape(mine, everyone, rho).transpose(1, 0, 2).reshape(everyone, -1),
            (one_sum / gain_one[0]).reshape(everyone, rho),
            two_sum.reshape(everyone, rho),
            pair_sum.reshape(2, everyone, pair_cols).transpose(1, 0, 2).reshape(everyone, -1),
        ],
        axis=1,
    ).astype(BF16)
    row = jnp.pad(row, ((0, 0), (0, cols - row.shape[1]))).reshape(groups, TEAM, cols)
    packed = lax.dynamic_update_slice(packed, row, (0, small_at, 0))
    parts = hold(parts, mark(first_hop + [gate_grad]))
    arrived = TeamSum(parts)
    arrived.first()
    packed = hold([packed.reshape(-1, cols)], mark([feed_done] + arrived.sent))[0]
    normed_grad = arrived.total(packed)
    packed = line_sum(packed)
    layer_output = ((hidden_state + fed.total(packed)) * live_rows).astype(BF16)
    tokens_grad = (hidden_grad + rms_pull(inputs, gain_one, normed_grad)).astype(BF16)
    feed_grad = jnp.concatenate([gate_grad, hold([up_grad], mark(arrived.last_sent))[0]], axis=1)
    feed_grad = exchange(feed_grad.reshape(TEAM, rho, 2 * ff_cols))

    def ff_join(w):
        return w.reshape(TEAM, rho, groups, phi).transpose(1, 2, 0, 3).reshape(rho, ff)

    gate_grad, up_grad = hold(
        [ff_join(feed_grad[:, :, :ff_cols]), ff_join(feed_grad[:, :, ff_cols:])], normed_grad
    )
    routes = [(user, owner) for owner, user in out_weight_routes(groups)]
    output_grad = packed[team_rows:small_at].reshape(-1, rho, cols).transpose(1, 0, 2).reshape(rho, width)
    output_grad = lax.ppermute(output_grad, ALL, routes)
    packed = jnp.concatenate(
        [
            packed[:team_rows].reshape(TEAM, rho, cols),
            jnp.pad(packed[small_at : small_at + TEAM][:, None], ((0, 0), (0, 7), (0, 0))),
        ],
        axis=1,
    )
    packed = exchange(packed)
    attn_grad = packed[:, :rho].transpose(1, 0, 2)
    rows_small = packed[:, rho].astype(F32)
    sums = jnp.sum(rows_small[:, head_lanes:], axis=0)
    head_gate_grad = rows_small[:, :head_lanes].reshape(heads, rho).T
    return (
        layer_output,
        tokens_grad,
        sums[:rho],
        attn_grad[:, :, :q_cols].reshape(rho, -1).astype(F32),
        attn_grad[:, :, q_cols : q_cols + k_cols].reshape(rho, -1).astype(F32),
        attn_grad[:, :, q_cols + k_cols :].reshape(rho, -1).astype(F32),
        head_gate_grad,
        output_grad.astype(F32),
        sums[2 * rho : 2 * rho + 2 * pair_cols].reshape(2, pair_cols),
        sums[rho : 2 * rho],
        gate_grad.astype(F32),
        up_grad.astype(F32),
        down_grad.astype(F32),
    )


def solution(mesh):
    groups = mesh.size // TEAM
    rows, vector, columns = P(ALL, None), P(ALL), P(None, ALL)

    def step(*args):
        return local(groups, *args)

    return jax.shard_map(
        step,
        mesh=mesh,
        in_specs=(
            rows, vector, rows, vector, rows, rows, rows, rows, rows, columns, vector, rows, rows, rows,
        ),
        out_specs=(
            rows, rows, vector, rows, rows, rows, rows, rows, columns, vector, rows, rows, rows,
        ),
        check_vma=False,
    )
```

```python
import jax
import jax.numpy as jnp
from jax import lax
from jax.experimental import pallas as pl
from jax.experimental.pallas import tpu as pltpu
from jax.sharding import PartitionSpec as P

EPSILON = 1e-06
ROPE_BASE = 1000000.0
TEAM = 8
ALL = ("dp", "fsdp")
F32 = jnp.float32
BF16 = jnp.bfloat16
TILE = 128
ANY = pl.BlockSpec(memory_space=pl.ANY)
VMEM = pl.BlockSpec(memory_space=pltpu.VMEM)
SMEM = pl.BlockSpec(memory_space=pltpu.SMEM)


def product(left, right):
    return jnp.dot(left, right, preferred_element_type=F32)


def product_nt(left, right):
    return lax.dot_general(left, right, (((1,), (1,)), ((), ())), preferred_element_type=F32)


def product_tn(left, right):
    return lax.dot_general(left, right, (((0,), (0,)), ((), ())), preferred_element_type=F32)


def world():
    return lax.axis_size(ALL)


def member():
    return lax.axis_index(ALL) % TEAM


def teams():
    return [[first + t for t in range(TEAM)] for first in range(0, world(), TEAM)]


def lines():
    return [list(range(t, world(), TEAM)) for t in range(TEAM)]


def permute(array, pairs):
    return lax.ppermute(
        array, ALL, [(team[a], team[b]) for team in teams() for a, b in pairs]
    )


def swap(array, bits):
    return permute(array, [(i, i ^ bits) for i in range(TEAM)])


def exchange(blocks):
    if lax.axis_size("fsdp") == TEAM:
        return lax.all_to_all(blocks, "fsdp", 0, 0, tiled=True)
    return lax.all_to_all(blocks, ALL, 0, 0, tiled=True, axis_index_groups=teams())


def line_gather(shard):
    if lax.axis_size("fsdp") == TEAM:
        return lax.all_gather(shard, "dp", axis=0, tiled=True)
    return lax.all_gather(shard, ALL, axis=0, tiled=True, axis_index_groups=lines())


def line_sum(array):
    if lax.axis_size("fsdp") == TEAM:
        return lax.psum_scatter(array, "dp", scatter_dimension=0, tiled=True)
    return lax.psum_scatter(array, ALL, scatter_dimension=0, tiled=True, axis_index_groups=lines())


class TeamGather:
    def __init__(self, own):
        self.own = own
        self.a1 = swap(own, 1)
        self.a2 = swap(own, 2)
        self.a4 = swap(own, 4)

    def blocks(self, tick=None):
        a2, a4 = self.a2, self.a4
        if tick is not None:
            a2, a4 = hold([a2, a4], tick)
        half = self.own.shape[0] // 2
        a6 = jnp.concatenate([swap(a4[:half], 2), swap(a2[half:], 4)], axis=0)
        return [self.own, self.a1, a2, swap(a2, 1), a4, swap(a4, 1), a6, swap(a6, 1)]


def team_gather(own):
    return TeamGather(own).blocks()


class TeamSum:
    def __init__(self, parts):
        half = parts[0].shape[0] // 2
        odd = {r: swap(parts[r + 1], 1) for r in (6, 2, 4, 0)}
        self.total6, self.total2, self.total4, self.total0 = (
            (parts[r].astype(F32) + odd[r].astype(F32)).astype(BF16) for r in (6, 2, 4, 0)
        )
        self.half = half
        self.ready = [
            jnp.concatenate([self.total6[:half], self.total2[:half]], axis=0),
            jnp.concatenate([self.total6[half:], self.total4[half:]], axis=0),
        ]

    def first(self, tick=None):
        self.sent = self.ready if tick is None else list(hold(self.ready, tick))
        self.over_x, self.over_y = swap(self.sent[0], 2), swap(self.sent[1], 4)
        return [self.over_x, self.over_y]

    def total(self, tick=None):
        half = self.half
        lasts = [
            (self.total2[half:].astype(F32) + self.over_y[:half].astype(F32)).astype(BF16),
            (self.total4[:half].astype(F32) + self.over_x[:half].astype(F32)).astype(BF16),
        ]
        x_low, y_top = lasts if tick is None else hold(lasts, tick)
        self.last_sent = [x_low, y_top]
        x_low = swap(x_low, 2).astype(F32)
        y_top = swap(y_top, 4).astype(F32)
        top = self.over_x[half:].astype(F32) + y_top
        low = x_low + self.over_y[half:].astype(F32)
        return self.total0.astype(F32) + jnp.concatenate([top, low], axis=0)


def out_weight_routes(groups):
    return [(i, TEAM * (i % groups) + i // groups) for i in range(groups * TEAM)]


def rms_pull(value, gain, grad):
    scale = lax.rsqrt(jnp.mean(value * value, axis=-1, keepdims=True) + EPSILON)
    weighted = grad * gain
    mean = jnp.mean(weighted * value, axis=-1, keepdims=True)
    return scale * weighted - scale * scale * scale * value * mean


def rms(value, gain):
    return value * lax.rsqrt(jnp.mean(value * value, axis=-1, keepdims=True) + EPSILON) * gain


def struct(shape, dtype):
    return jax.ShapeDtypeStruct(shape, dtype)


def hold(arrays, tick):
    def kernel(*refs):
        del refs

    count = len(arrays)
    return pl.pallas_call(
        kernel,
        out_shape=[struct(a.shape, a.dtype) for a in arrays],
        in_specs=[ANY] * count + [ANY],
        out_specs=[ANY] * count,
        input_output_aliases={i: i for i in range(count)},
    )(*arrays, tick)


def mark(arrays):
    def kernel(*refs):
        refs[-1][...] = jnp.zeros_like(refs[-1])

    return pl.pallas_call(
        kernel,
        out_shape=struct((8, 128), jnp.int32),
        in_specs=[ANY] * len(arrays),
        out_specs=VMEM,
    )(*arrays)


def for_tiles(tiles, most, body):
    for m in range(1, most + 1):

        @pl.when(tiles == m)
        def _(m=m):
            body(m * TILE)


def turned(u, cosine, sine):
    return u * cosine + pltpu.roll(u, u.shape[-1] // 2, 1) * sine


def head_norm(u):
    return lax.rsqrt(jnp.mean(u * u, axis=-1, keepdims=True) + EPSILON)


def head_back(grad, raw, gain, cosine, sine):
    e = turned(grad, cosine, -sine)
    scale = head_norm(raw)
    weighted = e * gain
    mean = jnp.mean(weighted * raw, axis=-1, keepdims=True)
    back = scale * weighted - scale * scale * scale * raw * mean
    return back, jnp.sum(e * raw * scale, axis=0, keepdims=True)


def weights_of(query, key, factor):
    scores = product_nt(query, key) * factor
    n = scores.shape[0]
    causal = lax.broadcasted_iota(jnp.int32, (n, n), 1) <= lax.broadcasted_iota(jnp.int32, (n, n), 0)
    scores = jnp.where(causal, scores, -jnp.inf)
    terms = jnp.exp(scores - jnp.max(scores, axis=-1, keepdims=True))
    return terms * (1.0 / jnp.sum(terms, axis=-1, keepdims=True))


def rows_of(tile, size=TILE):
    return pl.ds(pl.multiple_of(tile * size, size), size)


def each_block(r, body):
    for k in range(TEAM):
        pl.when(r == k)(lambda k=k: body(k))


def load_weights(gathered, weight_head, wa_v, wo_v, wh_v, sems):
    groups, _, cols = gathered.shape
    width = wo_v.shape[1]
    rho = width // (groups * TEAM)
    copies = [pltpu.make_async_copy(weight_head, wh_v, sems.at[0])]
    for g in range(groups):
        copies.append(
            pltpu.make_async_copy(
                gathered.at[g, pl.ds(0, TEAM * rho)],
                wa_v.at[pl.ds(g * TEAM * rho, TEAM * rho)],
                sems.at[len(copies)],
            )
        )
        for k in range(width // cols):
            copies.append(
                pltpu.make_async_copy(
                    gathered.at[g, pl.ds(TEAM * rho + k * rho, rho)],
                    wo_v.at[pl.ds(g * rho, rho), pl.ds(k * cols, cols)],
                    sems.at[len(copies)],
                )
            )
    return copies


def attend(tiles, tokens, consts, mine, after):
    gathered, weight_head, gain, gains, cosine, sine = consts
    rows, width = tokens[0].shape
    size = gains.shape[1]
    q_cols = mine * size
    cols = gathered.shape[2]
    factor = size ** (-0.5)

    def kernel(*refs):
        tiles_ref, toks = refs[0], refs[1 : 1 + TEAM]
        wa, wh, gain_ref, gains_ref, cos_ref, sin_ref, _ = refs[1 + TEAM : 8 + TEAM]
        parts = refs[8 + TEAM : 8 + 2 * TEAM]
        normed_all, qkv_all, logit_all, gated_all, tick = refs[8 + 2 * TEAM : 13 + 2 * TEAM]
        (
            tok_v, wa_v, wh_v, wo_v, part_v, normed_v, qkv_v, logit_v, gated_v, w_sem, in_sem, out_sem,
        ) = refs[13 + 2 * TEAM :]
        tick[...] = jnp.zeros_like(tick)

        def load(k, slot):
            return pltpu.make_async_copy(toks[k], tok_v.at[slot], in_sem.at[slot])

        def store(r, slot, j, k=0):
            src = (part_v, normed_v, qkv_v, logit_v, gated_v)[j].at[slot]
            dst = parts[k] if j == 0 else (normed_all, qkv_all, logit_all, gated_all)[j - 1].at[rows_of(r, rows)]
            return pltpu.make_async_copy(src, dst, out_sem.at[j, slot])

        load(0, 0).start()
        weights = load_weights(wa, wh, wa_v, wo_v, wh_v, w_sem)
        for copy in weights:
            copy.start()
        for copy in weights:
            copy.wait()

        def step(r, carry):
            slot = r % 2

            @pl.when(r + 1 < TEAM)
            def _():
                each_block(r + 1, lambda k: load(k, 1 - slot).start())

            load(0, slot).wait()

            @pl.when(r >= 2)
            def _():
                for j in range(5):
                    store(r - 2, slot, j).wait()

            def body(n):
                value = tok_v[slot, :n].astype(F32)
                normed = rms(value, gain_ref[...]).astype(BF16)
                normed_v[slot, :n] = normed
                qkv = product(normed, wa_v[...])
                qkv_v[slot, :n] = qkv
                logit = product_nt(normed, wh_v[...])
                logit_v[slot, :n] = logit
                cos, sin = cos_ref[:n], sin_ref[:n]
                key = qkv[:, q_cols : q_cols + size]
                key = turned(key * head_norm(key) * gains_ref[1:2], cos, sin).astype(BF16)
                values = qkv[:, q_cols + size :].astype(BF16)
                for h in range(mine):
                    query = qkv[:, h * size : (h + 1) * size]
                    query = turned(query * head_norm(query) * gains_ref[0:1], cos, sin).astype(BF16)
                    attention = weights_of(query, key, factor)
                    mixture = product(attention.astype(BF16), values)
                    gate = jax.nn.sigmoid(logit[:, h : h + 1])
                    gated_v[slot, :n, h * size : (h + 1) * size] = (mixture * gate).astype(BF16)
                part_v[slot, :n] = product(gated_v[slot, :n], wo_v[...]).astype(BF16)
                if n < rows:
                    part_v[slot, n:] = jnp.zeros((rows - n, width), BF16)
                    normed_v[slot, n:] = jnp.zeros((rows - n, width), BF16)
                    gated_v[slot, n:] = jnp.zeros((rows - n, q_cols), BF16)

            for_tiles(tiles_ref[r], rows // TILE, body)
            each_block(r, lambda k: store(r, slot, 0, k).start())
            for j in range(1, 5):
                store(r, slot, j).start()
            return carry

        lax.fori_loop(0, TEAM, step, 0)
        for r in (TEAM - 2, TEAM - 1):
            for j in range(5):
                store(r, r % 2, j).wait()

    whole = TEAM * rows
    result = pl.pallas_call(
        kernel,
        out_shape=[struct((rows, width), BF16)] * TEAM
        + [
            struct((whole, width), BF16),
            struct((whole, cols), F32),
            struct((whole, TILE), F32),
            struct((whole, q_cols), BF16),
            struct((8, 128), jnp.int32),
        ],
        in_specs=[SMEM] + [ANY] * (TEAM + 2) + [VMEM] * 4 + [ANY],
        out_specs=[ANY] * (TEAM + 4) + [VMEM],
        scratch_shapes=[
            pltpu.VMEM((2, rows, width), BF16),
            pltpu.VMEM((width, cols), BF16),
            pltpu.VMEM(weight_head.shape, BF16),
            pltpu.VMEM((q_cols, width), BF16),
            pltpu.VMEM((2, rows, width), BF16),
            pltpu.VMEM((2, rows, width), BF16),
            pltpu.VMEM((2, rows, cols), F32),
            pltpu.VMEM((2, rows, TILE), F32),
            pltpu.VMEM((2, rows, q_cols), BF16),
            pltpu.SemaphoreType.DMA((1 + gathered.shape[0] * (1 + width // cols),)),
            pltpu.SemaphoreType.DMA((2,)),
            pltpu.SemaphoreType.DMA((5, 2)),
        ],
        compiler_params=pltpu.CompilerParams(vmem_limit_bytes=48 << 20),
        cost_estimate=pl.CostEstimate(flops=30 << 30, bytes_accessed=60 << 20, transcendentals=1 << 20),
    )(tiles, *tokens, gathered, weight_head, gain, gains, cosine, sine, after)
    return result[:TEAM], result[TEAM : TEAM + 4], result[TEAM + 4]


def attend_back(tiles, hidden, consts, saved, mine, after):
    gathered, weight_head, gain, gains, cosine, sine = consts
    rows, width = hidden[0].shape
    size = gains.shape[1]
    q_cols = mine * size
    cols = gathered.shape[2]
    factor = size ** (-0.5)

    def kernel(*refs):
        tiles_ref, hids = refs[0], refs[1 : 1 + TEAM]
        wa, wh, normed_all, qkv_all, logit_all, gated_all = refs[1 + TEAM : 7 + TEAM]
        gains_ref, cos_ref, sin_ref, _ = refs[7 + TEAM : 11 + TEAM]
        parts = refs[11 + TEAM : 11 + 2 * TEAM]
        packed, head_sum, gain_sum, gains_sum = refs[11 + 2 * TEAM : 15 + 2 * TEAM]
        (
            hid_v, wa_v, wh_v, wo_v, normed_v, qkv_v, logit_v, gated_v, part_v, back_v, attn_sum, out_sum,
            w_sem, in_sem, out_sem,
        ) = refs[15 + 2 * TEAM :]

        def loads(r, slot, k):
            yield pltpu.make_async_copy(hids[k], hid_v.at[slot], in_sem.at[0, slot])
            here = rows_of(r, rows)
            for j, (src, dst) in enumerate(
                ((qkv_all, qkv_v), (logit_all, logit_v), (normed_all, normed_v), (gated_all, gated_v))
            ):
                yield pltpu.make_async_copy(src.at[here], dst.at[slot], in_sem.at[1 + j, slot])

        def start_loads(r, slot):
            def body(k):
                for copy in loads(r, slot, k):
                    copy.start()

            each_block(r, body)

        def store(slot, k=0):
            return pltpu.make_async_copy(part_v.at[slot], parts[k], out_sem.at[slot])

        for copy in loads(0, 0, 0):
            copy.start()
        weights = load_weights(wa, wh, wa_v, wo_v, wh_v, w_sem)
        for copy in weights:
            copy.start()
        for ref in (attn_sum, out_sum, gain_sum, gains_sum):
            ref[...] = jnp.zeros_like(ref)
        for copy in weights:
            copy.wait()

        def step(r, carry):
            slot = r % 2

            @pl.when(r + 1 < TEAM)
            def _():
                start_loads(r + 1, 1 - slot)

            for copy in loads(r, slot, 0):
                copy.wait()

            @pl.when(r >= 2)
            def _():
                store(slot).wait()

            def body(n):
                hidden_low = hid_v[slot, :n]
                normed = normed_v[slot, :n]
                out_sum[...] += product_tn(gated_v[slot, :n], hidden_low)
                gated_grad = product_nt(hidden_low, wo_v[...])
                cos, sin = cos_ref[:n], sin_ref[:n]
                key_raw = qkv_v[slot, :n, q_cols : q_cols + size]
                key = turned(key_raw * head_norm(key_raw) * gains_ref[1:2], cos, sin).astype(BF16)
                values = qkv_v[slot, :n, q_cols + size :].astype(BF16)
                lane = lax.broadcasted_iota(jnp.int32, (n, TILE), 1)
                logit_back = jnp.zeros((n, TILE), F32)
                values_back = jnp.zeros((n, size), F32)
                key_grad = jnp.zeros((n, size), F32)
                query_sum = jnp.zeros((1, size), F32)
                for h in range(mine):
                    span = slice(h * size, (h + 1) * size)
                    query_raw = qkv_v[slot, :n, span]
                    query = turned(query_raw * head_norm(query_raw) * gains_ref[0:1], cos, sin).astype(BF16)
                    attention = weights_of(query, key, factor)
                    attention_low = attention.astype(BF16)
                    mixture = product(attention_low, values)
                    gate = jax.nn.sigmoid(logit_v[slot, :n, h : h + 1])
                    head_grad = gated_grad[:, span]
                    mixture_back = (head_grad * gate).astype(BF16)
                    one = jnp.sum(head_grad * mixture, axis=-1, keepdims=True) * gate * (1.0 - gate)
                    logit_back = jnp.where(lane == h, one, logit_back)
                    values_back += product_tn(attention_low, mixture_back)
                    attention_grad = product_nt(mixture_back, values)
                    scores_back = (
                        attention
                        * (attention_grad - jnp.sum(attention_grad * attention, axis=-1, keepdims=True))
                    ).astype(BF16)
                    query_grad = product(scores_back, key) * factor
                    key_grad += product_tn(scores_back, query)
                    back, total = head_back(query_grad, query_raw, gains_ref[0:1], cos, sin)
                    back_v[:n, span] = back.astype(BF16)
                    query_sum += total
                back, key_sum = head_back(key_grad * factor, key_raw, gains_ref[1:2], cos, sin)
                back_v[:n, q_cols : q_cols + size] = back.astype(BF16)
                back_v[:n, q_cols + size : cols] = values_back.astype(BF16)
                logit_back = logit_back.astype(BF16)
                back_v[:n, cols:] = logit_back
                gains_sum[0:1] += query_sum
                gains_sum[1:2] += key_sum
                part = product_nt(back_v[:n, :cols], wa_v[...]) + product(logit_back, wh_v[...])
                part_v[slot, :n] = part.astype(BF16)
                gain_sum[0:1] += jnp.sum(part * normed.astype(F32), axis=0, keepdims=True)
                attn_sum[...] += product_tn(back_v[:n], normed)
                if n < rows:
                    part_v[slot, n:] = jnp.zeros((rows - n, width), BF16)

            for_tiles(tiles_ref[r], rows // TILE, body)
            each_block(r, lambda k: store(slot, k).start())
            return carry

        lax.fori_loop(0, TEAM, step, 0)
        head_sum[...] = attn_sum[cols : cols + 8]
        turned_sum = attn_sum[:cols].T.astype(BF16)
        groups, height, _ = packed.shape
        rho = width // (groups * TEAM)
        for g in range(groups):
            packed[g, : TEAM * rho] = turned_sum[g * TEAM * rho : (g + 1) * TEAM * rho]
            for k in range(width // cols):
                top = TEAM * rho + k * rho
                packed[g, top : top + rho] = out_sum[
                    g * rho : (g + 1) * rho, k * cols : (k + 1) * cols
                ].astype(BF16)
            packed[g, height - 16 :] = jnp.zeros((16, cols), BF16)
        store(0).wait()
        store(1).wait()

    result = pl.pallas_call(
        kernel,
        out_shape=[struct((rows, width), BF16)] * TEAM
        + [
            struct(gathered.shape, BF16),
            struct((8, width), F32),
            struct((8, width), F32),
            struct((8, size), F32),
        ],
        in_specs=[SMEM] + [ANY] * (TEAM + 6) + [VMEM] * 3 + [ANY],
        out_specs=[ANY] * TEAM + [VMEM] * 4,
        scratch_shapes=[
            pltpu.VMEM((2, rows, width), BF16),
            pltpu.VMEM((width, cols), BF16),
            pltpu.VMEM(weight_head.shape, BF16),
            pltpu.VMEM((q_cols, width), BF16),
            pltpu.VMEM((2, rows, width), BF16),
            pltpu.VMEM((2, rows, cols), F32),
            pltpu.VMEM((2, rows, TILE), F32),
            pltpu.VMEM((2, rows, q_cols), BF16),
            pltpu.VMEM((2, rows, width), BF16),
            pltpu.VMEM((rows, cols + TILE), BF16),
            pltpu.VMEM((cols + TILE, width), F32),
            pltpu.VMEM((q_cols, width), F32),
            pltpu.SemaphoreType.DMA((1 + gathered.shape[0] * (1 + width // cols),)),
            pltpu.SemaphoreType.DMA((5, 2)),
            pltpu.SemaphoreType.DMA((2,)),
        ],
        compiler_params=pltpu.CompilerParams(vmem_limit_bytes=56 << 20),
        cost_estimate=pl.CostEstimate(flops=45 << 30, bytes_accessed=70 << 20, transcendentals=1 << 20),
    )(tiles, *hidden, gathered, weight_head, *saved, gains, cosine, sine, after)
    return result[:TEAM], *result[TEAM : TEAM + 2], result[TEAM + 2][0], result[TEAM + 3][:2]


def tile_places(tiles_ref, rows):
    places, total = [], 0
    for r in range(TEAM):
        count = tiles_ref[r]
        for j in range(rows // TILE):
            places.append((r, j, j < count, total + j))
        total = total + count
    return places, total


def feed(tiles, twos, upstreams, weight_gate, weight_up, weight_down):
    rows, width = twos[0].shape
    ff_cols = weight_down.shape[0]
    whole = TEAM * rows
    chunk = 2 * TILE
    chunks = whole // chunk

    def kernel(*refs):
        tiles_ref, twos_ref, ups_ref = refs[0], refs[1 : 1 + TEAM], refs[1 + TEAM : 1 + 2 * TEAM]
        weights_ref = refs[1 + 2 * TEAM : 4 + 2 * TEAM]
        outs_ref = refs[4 + 2 * TEAM : 4 + 3 * TEAM]
        grads_ref = refs[4 + 3 * TEAM : 4 + 4 * TEAM]
        inner_all, back_all, two_all, ups_all = refs[4 + 4 * TEAM : 8 + 4 * TEAM]
        (
            two_v, ups_v, wg_v, wu_v, wd_v, inner_v, back_v, out_v, grad_v, zero_v,
            w_sem, load_sem, keep_sem, tile_sem, dead_sem,
        ) = refs[8 + 4 * TEAM :]
        places, total = tile_places(tiles_ref, rows)
        used = (total + 1) // 2

        def loads(sources, packed, which):
            for k, (r, j, live, place) in enumerate(places):
                yield live, pltpu.make_async_copy(
                    sources[r].at[rows_of(j)], packed.at[rows_of(place)], load_sem.at[which, k]
                )

        weights = [
            pltpu.make_async_copy(src, dst, w_sem.at[j])
            for j, (src, dst) in enumerate(zip(weights_ref, (wg_v, wu_v, wd_v)))
        ]
        for live, copy in loads(twos_ref, two_v, 0):
            pl.when(live)(copy.start)
        for copy in weights:
            copy.start()
        for live, copy in loads(ups_ref, ups_v, 1):
            pl.when(live)(copy.start)
        zero_v[...] = jnp.zeros_like(zero_v)

        def dead(k, r, j):
            zeros = zero_v.at[:TILE]
            yield pltpu.make_async_copy(zeros, grads_ref[r].at[rows_of(j)], dead_sem.at[0, k])
            yield pltpu.make_async_copy(zeros, outs_ref[r].at[rows_of(j)], dead_sem.at[1, k])

        for k, (r, j, live, place) in enumerate(places):

            @pl.when(jnp.logical_not(live))
            def _(k=k, r=r, j=j):
                for copy in dead(k, r, j):
                    copy.start()

        def keeps(c, sources):
            for j, (src, dst) in enumerate(zip(sources, (two_all, ups_all, inner_all, back_all))):
                yield pltpu.make_async_copy(src, dst.at[rows_of(c, chunk)], keep_sem.at[j, c])

        zeros = (zero_v, zero_v, zero_v.at[:, :ff_cols], zero_v.at[:, : 2 * ff_cols])
        for c in range(TEAM // 2, chunks):

            @pl.when(c >= used)
            def _(c=c):
                for copy in keeps(c, zeros):
                    copy.start()

        @pl.when(total % 2 == 1)
        def _():
            two_v[rows_of(total)] = jnp.zeros((TILE, width), BF16)
            ups_v[rows_of(total)] = jnp.zeros((TILE, width), BF16)

        for live, copy in loads(twos_ref, two_v, 0):
            pl.when(live)(copy.wait)
        for copy in weights:
            copy.wait()
        for live, copy in loads(ups_ref, ups_v, 1):
            pl.when(live)(copy.wait)

        def tile_stores(r, j, slot, side):
            here = pl.ds(side * TILE, TILE)
            yield pltpu.make_async_copy(
                grad_v.at[slot, here], grads_ref[r].at[rows_of(j)], tile_sem.at[0, slot, side]
            )
            yield pltpu.make_async_copy(
                out_v.at[slot, here], outs_ref[r].at[rows_of(j)], tile_sem.at[1, slot, side]
            )

        def wait_tiles(c, slot):
            for side in range(2):

                @pl.when(2 * c + side < total)
                def _(side=side):
                    for copy in tile_stores(0, 0, slot, side):
                        copy.wait()

        def body(c, carry):
            slot = c % 2
            span = rows_of(c, chunk)

            @pl.when(c >= 2)
            def _():
                wait_tiles(c - 2, slot)
                for j, copy in enumerate(keeps(c - 2, zeros)):
                    if j >= 2:
                        copy.wait()

            gate_part = product(two_v[span], wg_v[...])
            up_part = product(two_v[span], wu_v[...])
            sig = jax.nn.sigmoid(gate_part)
            silu = gate_part * sig
            inner_v[slot] = (silu * up_part).astype(BF16)
            inner_grad = product_nt(ups_v[span], wd_v[...])
            back_v[slot, :, :ff_cols] = (inner_grad * up_part * (sig + silu * (1.0 - sig))).astype(BF16)
            back_v[slot, :, ff_cols:] = (inner_grad * silu).astype(BF16)
            for copy in keeps(c, (two_v.at[span], ups_v.at[span], inner_v.at[slot], back_v.at[slot])):
                copy.start()
            grad = product_nt(back_v[slot, :, :ff_cols], wg_v[...]) + product_nt(
                back_v[slot, :, ff_cols:], wu_v[...]
            )
            grad_v[slot] = grad.astype(BF16)
            out_v[slot] = product(inner_v[slot], wd_v[...]).astype(BF16)
            for k, (r, j, live, place) in enumerate(places):
                for side in range(2):

                    @pl.when(jnp.logical_and(live, place == 2 * c + side))
                    def _(r=r, j=j, side=side):
                        for copy in tile_stores(r, j, slot, side):
                            copy.start()

            return carry

        lax.fori_loop(0, used, body, 0)
        wait_tiles(used - 2, used % 2)
        wait_tiles(used - 1, (used - 1) % 2)
        for k, (r, j, live, place) in enumerate(places):

            @pl.when(jnp.logical_not(live))
            def _(k=k, r=r, j=j):
                for copy in dead(k, r, j):
                    copy.wait()

        for c in range(chunks):
            for j, copy in enumerate(keeps(c, zeros)):
                if j < 2:
                    copy.wait()
                else:
                    pl.when(c >= used - 2)(copy.wait)

    count = whole // TILE
    result = pl.pallas_call(
        kernel,
        out_shape=[struct((rows, width), BF16)] * (2 * TEAM)
        + [
            struct((whole, ff_cols), BF16),
            struct((whole, 2 * ff_cols), BF16),
            struct((whole, width), BF16),
            struct((whole, width), BF16),
        ],
        in_specs=[SMEM] + [ANY] * (3 + 2 * TEAM),
        out_specs=[ANY] * (2 * TEAM + 4),
        scratch_shapes=[
            pltpu.VMEM((whole, width), BF16),
            pltpu.VMEM((whole, width), BF16),
            pltpu.VMEM(weight_gate.shape, BF16),
            pltpu.VMEM(weight_up.shape, BF16),
            pltpu.VMEM(weight_down.shape, BF16),
            pltpu.VMEM((2, chunk, ff_cols), BF16),
            pltpu.VMEM((2, chunk, 2 * ff_cols), BF16),
            pltpu.VMEM((2, chunk, width), BF16),
            pltpu.VMEM((2, chunk, width), BF16),
            pltpu.VMEM((chunk, width), BF16),
            pltpu.SemaphoreType.DMA((3,)),
            pltpu.SemaphoreType.DMA((2, count)),
            pltpu.SemaphoreType.DMA((4, chunks)),
            pltpu.SemaphoreType.DMA((2, 2, 2)),
            pltpu.SemaphoreType.DMA((2, count)),
        ],
        compiler_params=pltpu.CompilerParams(vmem_limit_bytes=60 << 20),
        cost_estimate=pl.CostEstimate(flops=58 << 30, bytes_accessed=100 << 20, transcendentals=1 << 20),
    )(tiles, *twos, *upstreams, weight_gate, weight_up, weight_down)
    return result[:TEAM], result[TEAM : 2 * TEAM], result[2 * TEAM :]


def local(
    groups,
    tokens,
    lengths,
    cotangent,
    attention_gain,
    query_weight,
    key_matrix,
    value_matrix,
    head_gate_weight,
    output_weight,
    query_key_gain,
    feedforward_gain,
    gate_weight,
    up_weight,
    down_weight,
):
    t = member()
    everyone = groups * TEAM
    rows, width = tokens.shape
    rho = query_weight.shape[0]
    phi = down_weight.shape[0]
    ff = gate_weight.shape[1]
    pair_cols = query_key_gain.shape[1]
    size = pair_cols * everyone
    heads = query_weight.shape[1] // size
    mine = heads // TEAM
    q_cols = query_weight.shape[1] // TEAM
    k_cols = key_matrix.shape[1] // TEAM
    ff_cols = ff // TEAM

    def everyone_in_team(vector):
        return jnp.broadcast_to(vector.reshape(1, -1), (TEAM, vector.size))

    live_tiles = (lengths + (TILE - 1)) // TILE
    row = jnp.concatenate(
        [
            head_gate_weight.reshape(rho, TEAM, mine).transpose(1, 2, 0).reshape(TEAM, -1),
            everyone_in_team(attention_gain),
            everyone_in_team(feedforward_gain),
            everyone_in_team(query_key_gain),
            everyone_in_team(live_tiles.astype(BF16)),
        ],
        axis=1,
    )
    cols = q_cols + 2 * k_cols
    row = jnp.pad(row, ((0, 0), (0, cols - row.shape[1])))[:, None, :]
    attn = jnp.concatenate(
        [
            query_weight.reshape(rho, TEAM, q_cols),
            key_matrix.reshape(rho, TEAM, k_cols),
            value_matrix.reshape(rho, TEAM, k_cols),
        ],
        axis=2,
    ).transpose(1, 0, 2)
    attn = jnp.concatenate([attn, jnp.pad(row, ((0, 0), (0, 7), (0, 0)))], axis=1)
    attn = exchange(attn)
    head_lanes = mine * rho
    at_one, at_two, at_pair = head_lanes, head_lanes + rho, head_lanes + 2 * rho
    at_tiles = at_pair + 2 * pair_cols
    team_tiles = attn[:, rho, at_tiles].astype(jnp.int32)
    order = jnp.arange(TEAM, dtype=jnp.int32)
    tiles = jnp.sum(jnp.where((order[:, None] ^ t) == order[None, :], team_tiles[None, :], 0), axis=1)
    routed = lax.ppermute(output_weight, ALL, out_weight_routes(groups))
    team_rows = TEAM * rho
    small_at = team_rows + (width // cols) * rho
    stacked = jnp.concatenate(
        [attn[:, :rho].reshape(team_rows, cols)]
        + [routed[:, k : k + cols] for k in range(0, width, cols)]
        + [attn[:, rho], jnp.zeros((16 - TEAM, cols), BF16)],
        axis=0,
    )
    gathered = line_gather(stacked).reshape(groups, -1, cols)
    rows_small = gathered[:, small_at : small_at + TEAM].reshape(everyone, cols)
    weight_head = jnp.pad(
        rows_small[:, :head_lanes].reshape(everyone, mine, rho).transpose(1, 0, 2).reshape(mine, width),
        ((0, TILE - mine), (0, 0)),
    )
    gain_one = rows_small[:, at_one:at_two].reshape(1, width).astype(F32)
    gain_two = rows_small[:, at_two:at_pair].reshape(1, width).astype(F32)
    gain_pair = (
        rows_small[:, at_pair:at_tiles]
        .reshape(everyone, 2, pair_cols)
        .transpose(1, 0, 2)
        .reshape(2, size)
        .astype(F32)
    )
    def ff_split(w):
        return w.reshape(rho, groups, TEAM, phi).transpose(2, 0, 1, 3).reshape(TEAM, rho, ff_cols)

    feed_shard = jnp.concatenate([ff_split(gate_weight), ff_split(up_weight)], axis=2)

    exponent = jnp.arange(size // 2, dtype=F32) * (-2.0 / size)
    frequency = jnp.power(ROPE_BASE, exponent)
    angles = jnp.arange(rows, dtype=F32)[:, None] * frequency[None, :]
    cosine = jnp.concatenate([jnp.cos(angles), jnp.cos(angles)], axis=1)
    sine = jnp.concatenate([-jnp.sin(angles), jnp.sin(angles)], axis=1)
    consts = (gathered, weight_head, gain_one, gain_pair, cosine, sine)
    team_tokens = team_gather(tokens)
    feed_shard = exchange(feed_shard).reshape(TEAM * rho, -1)
    weight_gate = line_gather(feed_shard[:, :ff_cols])
    live = lax.broadcasted_iota(jnp.int32, (rows, 1), 0) < lengths[0]
    live_rows = live.astype(F32)
    upstream = cotangent.astype(F32) * live_rows
    tick = mark([team_tokens[6]])
    later = lax.broadcasted_iota(jnp.int32, (rows, 1), 0) < lengths[0] + tick[0, 0]
    upstream_low = jnp.where(later, cotangent, jnp.zeros_like(cotangent))
    upstream_levels = TeamGather(upstream_low)
    parts, kept, tick = attend(tiles, team_tokens, consts, mine, mark([upstream_low]))
    normed, qkv, logit, gated = kept
    weight_up = line_gather(hold([feed_shard[:, ff_cols:]], tick)[0])
    parts = hold(parts, mark([upstream_levels.a1, upstream_levels.a2, upstream_levels.a4, tick]))
    arrived = TeamSum(parts)
    arrived.first()
    weight_down = line_gather(hold([down_weight], arrived.sent[0])[0])
    inputs = tokens.astype(F32)
    hidden_state = inputs + arrived.total(weight_gate)

    normed_two = rms(hidden_state, gain_two).astype(BF16)
    team_upstream = upstream_levels.blocks(normed_two)
    team_two = TeamGather(normed_two).blocks(weight_up)
    outs, grads, saved = feed(tiles, team_two, team_upstream, weight_gate, weight_up, weight_down)
    inner, feed_back, two_all, ups_all = saved
    arrived = TeamSum(grads)
    arrived.first()
    two_grad = arrived.total()
    inner = hold([inner], mark(arrived.sent))[0]
    down_part = product_tn(inner, ups_all).astype(BF16)
    feed_back = hold([feed_back], mark([arrived.over_x, arrived.over_y]))[0]
    gate_part = product_tn(two_all, feed_back[:, :ff_cols]).astype(BF16)
    hidden_grad = upstream + rms_pull(hidden_state, gain_two, two_grad)
    hidden_low = hidden_grad.astype(BF16)
    feed_back = hold([feed_back], mark([gate_part, hidden_low]))[0]
    up_part = product_tn(two_all, feed_back[:, ff_cols:]).astype(BF16)
    parts_made = mark([gate_part, up_part])
    down_grad = line_sum(down_part)
    gate_grad = line_sum(hold([gate_part], down_grad)[0])
    up_grad = line_sum(hold([up_part], gate_grad)[0])
    feed_done = up_grad

    fed = TeamSum(hold(outs, arrived.over_x))
    team_hidden = TeamGather(hidden_low).blocks(mark(fed.ready + [gate_part, up_part]))
    two_scale = lax.rsqrt(jnp.mean(hidden_state * hidden_state, axis=-1, keepdims=True) + EPSILON)
    two_sum = jnp.sum(two_grad * hidden_state * two_scale, axis=0)
    first_hop = fed.first(mark(team_hidden + [parts_made]))
    parts, packed, head_sum, one_sum, pair_sum = attend_back(
        tiles, team_hidden, consts, (normed, qkv, logit, gated), mine, mark(fed.sent + [down_grad])
    )
    row = jnp.concatenate(
        [
            head_sum[:mine].reshape(mine, everyone, rho).transpose(1, 0, 2).reshape(everyone, -1),
            (one_sum / gain_one[0]).reshape(everyone, rho),
            two_sum.reshape(everyone, rho),
            pair_sum.reshape(2, everyone, pair_cols).transpose(1, 0, 2).reshape(everyone, -1),
        ],
        axis=1,
    ).astype(BF16)
    row = jnp.pad(row, ((0, 0), (0, cols - row.shape[1]))).reshape(groups, TEAM, cols)
    packed = lax.dynamic_update_slice(packed, row, (0, small_at, 0))
    parts = hold(parts, mark(first_hop + [gate_grad]))
    arrived = TeamSum(parts)
    arrived.first()
    packed = hold([packed.reshape(-1, cols)], mark([feed_done] + arrived.sent))[0]
    normed_grad = arrived.total(packed)
    packed = line_sum(packed)
    layer_output = ((hidden_state + fed.total(normed_grad)) * live_rows).astype(BF16)
    tokens_grad = (hidden_grad + rms_pull(inputs, gain_one, normed_grad)).astype(BF16)
    feed_grad = jnp.concatenate([gate_grad, hold([up_grad], mark(arrived.last_sent))[0]], axis=1)
    feed_grad = exchange(feed_grad.reshape(TEAM, rho, 2 * ff_cols))

    def ff_join(w):
        return w.reshape(TEAM, rho, groups, phi).transpose(1, 2, 0, 3).reshape(rho, ff)

    gate_grad, up_grad = hold(
        [ff_join(feed_grad[:, :, :ff_cols]), ff_join(feed_grad[:, :, ff_cols:])], mark(fed.last_sent)
    )
    routes = [(user, owner) for owner, user in out_weight_routes(groups)]
    output_grad = packed[team_rows:small_at].reshape(-1, rho, cols).transpose(1, 0, 2).reshape(rho, width)
    output_grad = lax.ppermute(output_grad, ALL, routes)
    packed = jnp.concatenate(
        [
            packed[:team_rows].reshape(TEAM, rho, cols),
            jnp.pad(packed[small_at : small_at + TEAM][:, None], ((0, 0), (0, 7), (0, 0))),
        ],
        axis=1,
    )
    packed = exchange(packed)
    attn_grad = packed[:, :rho].transpose(1, 0, 2)
    rows_small = packed[:, rho].astype(F32)
    sums = jnp.sum(rows_small[:, head_lanes:], axis=0)
    head_gate_grad = rows_small[:, :head_lanes].reshape(heads, rho).T
    return (
        layer_output,
        tokens_grad,
        sums[:rho],
        attn_grad[:, :, :q_cols].reshape(rho, -1).astype(F32),
        attn_grad[:, :, q_cols : q_cols + k_cols].reshape(rho, -1).astype(F32),
        attn_grad[:, :, q_cols + k_cols :].reshape(rho, -1).astype(F32),
        head_gate_grad,
        output_grad.astype(F32),
        sums[2 * rho : 2 * rho + 2 * pair_cols].reshape(2, pair_cols),
        sums[rho : 2 * rho],
        gate_grad.astype(F32),
        up_grad.astype(F32),
        down_grad.astype(F32),
    )


def solution(mesh):
    groups = mesh.size // TEAM
    rows, vector, columns = P(ALL, None), P(ALL), P(None, ALL)

    def step(*args):
        return local(groups, *args)

    return jax.shard_map(
        step,
        mesh=mesh,
        in_specs=(
            rows, vector, rows, vector, rows, rows, rows, rows, rows, columns, vector, rows, rows, rows,
        ),
        out_specs=(
            rows, rows, vector, rows, rows, rows, rows, rows, columns, vector, rows, rows, rows,
        ),
        check_vma=False,
    )
```

```python
import jax
import jax.numpy as jnp
from jax import lax
from jax.experimental import pallas as pl
from jax.experimental.pallas import tpu as pltpu
from jax.sharding import PartitionSpec as P

EPSILON = 1e-06
ROPE_BASE = 1000000.0
TEAM = 8
ALL = ("dp", "fsdp")
F32 = jnp.float32
BF16 = jnp.bfloat16
TILE = 128
ANY = pl.BlockSpec(memory_space=pl.ANY)
VMEM = pl.BlockSpec(memory_space=pltpu.VMEM)
SMEM = pl.BlockSpec(memory_space=pltpu.SMEM)


def product(left, right):
    return jnp.dot(left, right, preferred_element_type=F32)


def product_nt(left, right):
    return lax.dot_general(left, right, (((1,), (1,)), ((), ())), preferred_element_type=F32)


def product_tn(left, right):
    return lax.dot_general(left, right, (((0,), (0,)), ((), ())), preferred_element_type=F32)


def world():
    return lax.axis_size(ALL)


def member():
    return lax.axis_index(ALL) % TEAM


def teams():
    return [[first + t for t in range(TEAM)] for first in range(0, world(), TEAM)]


def lines():
    return [list(range(t, world(), TEAM)) for t in range(TEAM)]


def permute(array, pairs):
    return lax.ppermute(
        array, ALL, [(team[a], team[b]) for team in teams() for a, b in pairs]
    )


def swap(array, bits):
    return permute(array, [(i, i ^ bits) for i in range(TEAM)])


def exchange(blocks):
    if lax.axis_size("fsdp") == TEAM:
        return lax.all_to_all(blocks, "fsdp", 0, 0, tiled=True)
    return lax.all_to_all(blocks, ALL, 0, 0, tiled=True, axis_index_groups=teams())


def line_gather(shard):
    if lax.axis_size("fsdp") == TEAM:
        return lax.all_gather(shard, "dp", axis=0, tiled=True)
    return lax.all_gather(shard, ALL, axis=0, tiled=True, axis_index_groups=lines())


def line_sum(array):
    if lax.axis_size("fsdp") == TEAM:
        return lax.psum_scatter(array, "dp", scatter_dimension=0, tiled=True)
    return lax.psum_scatter(array, ALL, scatter_dimension=0, tiled=True, axis_index_groups=lines())


class TeamGather:
    def __init__(self, own):
        self.own = own
        self.a1 = swap(own, 1)
        self.a2 = swap(own, 2)
        self.a4 = swap(own, 4)

    def blocks(self, tick=None):
        a2, a4 = self.a2, self.a4
        if tick is not None:
            a2, a4 = hold([a2, a4], tick)
        half = self.own.shape[0] // 2
        a6 = jnp.concatenate([swap(a4[:half], 2), swap(a2[half:], 4)], axis=0)
        return [self.own, self.a1, a2, swap(a2, 1), a4, swap(a4, 1), a6, swap(a6, 1)]


def team_gather(own):
    return TeamGather(own).blocks()


class TeamSum:
    def __init__(self, parts):
        half = parts[0].shape[0] // 2
        odd = {r: swap(parts[r + 1], 1) for r in (6, 2, 4, 0)}
        self.total6, self.total2, self.total4, self.total0 = (
            (parts[r].astype(F32) + odd[r].astype(F32)).astype(BF16) for r in (6, 2, 4, 0)
        )
        self.half = half
        self.ready = [
            jnp.concatenate([self.total6[:half], self.total2[:half]], axis=0),
            jnp.concatenate([self.total6[half:], self.total4[half:]], axis=0),
        ]

    def first(self, tick=None):
        self.sent = self.ready if tick is None else list(hold(self.ready, tick))
        self.over_x, self.over_y = swap(self.sent[0], 2), swap(self.sent[1], 4)
        return [self.over_x, self.over_y]

    def total(self, tick=None):
        half = self.half
        lasts = [
            (self.total2[half:].astype(F32) + self.over_y[:half].astype(F32)).astype(BF16),
            (self.total4[:half].astype(F32) + self.over_x[:half].astype(F32)).astype(BF16),
        ]
        x_low, y_top = lasts if tick is None else hold(lasts, tick)
        self.last_sent = [x_low, y_top]
        x_low = swap(x_low, 2).astype(F32)
        y_top = swap(y_top, 4).astype(F32)
        top = self.over_x[half:].astype(F32) + y_top
        low = x_low + self.over_y[half:].astype(F32)
        return self.total0.astype(F32) + jnp.concatenate([top, low], axis=0)


def out_weight_routes(groups):
    return [(i, TEAM * (i % groups) + i // groups) for i in range(groups * TEAM)]


def rms_pull(value, gain, grad):
    scale = lax.rsqrt(jnp.mean(value * value, axis=-1, keepdims=True) + EPSILON)
    weighted = grad * gain
    mean = jnp.mean(weighted * value, axis=-1, keepdims=True)
    return scale * weighted - scale * scale * scale * value * mean


def rms(value, gain):
    return value * lax.rsqrt(jnp.mean(value * value, axis=-1, keepdims=True) + EPSILON) * gain


def struct(shape, dtype):
    return jax.ShapeDtypeStruct(shape, dtype)


def hold(arrays, tick):
    def kernel(*refs):
        del refs

    count = len(arrays)
    return pl.pallas_call(
        kernel,
        out_shape=[struct(a.shape, a.dtype) for a in arrays],
        in_specs=[ANY] * count + [ANY],
        out_specs=[ANY] * count,
        input_output_aliases={i: i for i in range(count)},
    )(*arrays, tick)


def mark(arrays):
    def kernel(*refs):
        refs[-1][...] = jnp.zeros_like(refs[-1])

    return pl.pallas_call(
        kernel,
        out_shape=struct((8, 128), jnp.int32),
        in_specs=[ANY] * len(arrays),
        out_specs=VMEM,
    )(*arrays)


def for_tiles(tiles, most, body):
    for m in range(1, most + 1):

        @pl.when(tiles == m)
        def _(m=m):
            body(m * TILE)


def turned(u, cosine, sine):
    return u * cosine + pltpu.roll(u, u.shape[-1] // 2, 1) * sine


def head_norm(u):
    return lax.rsqrt(jnp.mean(u * u, axis=-1, keepdims=True) + EPSILON)


def head_back(grad, raw, gain, cosine, sine):
    e = turned(grad, cosine, -sine)
    scale = head_norm(raw)
    weighted = e * gain
    mean = jnp.mean(weighted * raw, axis=-1, keepdims=True)
    back = scale * weighted - scale * scale * scale * raw * mean
    return back, jnp.sum(e * raw * scale, axis=0, keepdims=True)


def weights_of(query, key, factor):
    scores = product_nt(query, key) * factor
    n = scores.shape[0]
    causal = lax.broadcasted_iota(jnp.int32, (n, n), 1) <= lax.broadcasted_iota(jnp.int32, (n, n), 0)
    scores = jnp.where(causal, scores, -jnp.inf)
    terms = jnp.exp(scores - jnp.max(scores, axis=-1, keepdims=True))
    return terms * (1.0 / jnp.sum(terms, axis=-1, keepdims=True))


def rows_of(tile, size=TILE):
    return pl.ds(pl.multiple_of(tile * size, size), size)


def each_block(r, body):
    for k in range(TEAM):
        pl.when(r == k)(lambda k=k: body(k))


def load_weights(gathered, weight_head, wa_v, wo_v, wh_v, sems):
    groups, _, cols = gathered.shape
    width = wo_v.shape[1]
    rho = width // (groups * TEAM)
    copies = [pltpu.make_async_copy(weight_head, wh_v, sems.at[0])]
    for g in range(groups):
        copies.append(
            pltpu.make_async_copy(
                gathered.at[g, pl.ds(0, TEAM * rho)],
                wa_v.at[pl.ds(g * TEAM * rho, TEAM * rho)],
                sems.at[len(copies)],
            )
        )
        for k in range(width // cols):
            copies.append(
                pltpu.make_async_copy(
                    gathered.at[g, pl.ds(TEAM * rho + k * rho, rho)],
                    wo_v.at[pl.ds(g * rho, rho), pl.ds(k * cols, cols)],
                    sems.at[len(copies)],
                )
            )
    return copies


def attend(tiles, tokens, consts, mine, after):
    gathered, weight_head, gain, gains, cosine, sine = consts
    rows, width = tokens[0].shape
    size = gains.shape[1]
    q_cols = mine * size
    cols = gathered.shape[2]
    factor = size ** (-0.5)

    def kernel(*refs):
        tiles_ref, toks = refs[0], refs[1 : 1 + TEAM]
        wa, wh, gain_ref, gains_ref, cos_ref, sin_ref, _ = refs[1 + TEAM : 8 + TEAM]
        parts = refs[8 + TEAM : 8 + 2 * TEAM]
        normed_all, qkv_all, logit_all, gated_all, tick = refs[8 + 2 * TEAM : 13 + 2 * TEAM]
        (
            tok_v, wa_v, wh_v, wo_v, part_v, normed_v, qkv_v, logit_v, gated_v, w_sem, in_sem, out_sem,
        ) = refs[13 + 2 * TEAM :]
        tick[...] = jnp.zeros_like(tick)

        def load(k, slot):
            return pltpu.make_async_copy(toks[k], tok_v.at[slot], in_sem.at[slot])

        def store(r, slot, j, k=0):
            src = (part_v, normed_v, qkv_v, logit_v, gated_v)[j].at[slot]
            dst = parts[k] if j == 0 else (normed_all, qkv_all, logit_all, gated_all)[j - 1].at[rows_of(r, rows)]
            return pltpu.make_async_copy(src, dst, out_sem.at[j, slot])

        load(0, 0).start()
        weights = load_weights(wa, wh, wa_v, wo_v, wh_v, w_sem)
        for copy in weights:
            copy.start()
        for copy in weights:
            copy.wait()

        def step(r, carry):
            slot = r % 2

            @pl.when(r + 1 < TEAM)
            def _():
                each_block(r + 1, lambda k: load(k, 1 - slot).start())

            load(0, slot).wait()

            @pl.when(r >= 2)
            def _():
                for j in range(5):
                    store(r - 2, slot, j).wait()

            def body(n):
                value = tok_v[slot, :n].astype(F32)
                normed = rms(value, gain_ref[...]).astype(BF16)
                normed_v[slot, :n] = normed
                qkv = product(normed, wa_v[...])
                qkv_v[slot, :n] = qkv
                logit = product_nt(normed, wh_v[...])
                logit_v[slot, :n] = logit
                cos, sin = cos_ref[:n], sin_ref[:n]
                key = qkv[:, q_cols : q_cols + size]
                key = turned(key * head_norm(key) * gains_ref[1:2], cos, sin).astype(BF16)
                values = qkv[:, q_cols + size :].astype(BF16)
                for h in range(mine):
                    query = qkv[:, h * size : (h + 1) * size]
                    query = turned(query * head_norm(query) * gains_ref[0:1], cos, sin).astype(BF16)
                    attention = weights_of(query, key, factor)
                    mixture = product(attention.astype(BF16), values)
                    gate = jax.nn.sigmoid(logit[:, h : h + 1])
                    gated_v[slot, :n, h * size : (h + 1) * size] = (mixture * gate).astype(BF16)
                part_v[slot, :n] = product(gated_v[slot, :n], wo_v[...]).astype(BF16)
                if n < rows:
                    part_v[slot, n:] = jnp.zeros((rows - n, width), BF16)
                    normed_v[slot, n:] = jnp.zeros((rows - n, width), BF16)
                    gated_v[slot, n:] = jnp.zeros((rows - n, q_cols), BF16)

            for_tiles(tiles_ref[r], rows // TILE, body)
            each_block(r, lambda k: store(r, slot, 0, k).start())
            for j in range(1, 5):
                store(r, slot, j).start()
            return carry

        lax.fori_loop(0, TEAM, step, 0)
        for r in (TEAM - 2, TEAM - 1):
            for j in range(5):
                store(r, r % 2, j).wait()

    whole = TEAM * rows
    result = pl.pallas_call(
        kernel,
        out_shape=[struct((rows, width), BF16)] * TEAM
        + [
            struct((whole, width), BF16),
            struct((whole, cols), F32),
            struct((whole, TILE), F32),
            struct((whole, q_cols), BF16),
            struct((8, 128), jnp.int32),
        ],
        in_specs=[SMEM] + [ANY] * (TEAM + 2) + [VMEM] * 4 + [ANY],
        out_specs=[ANY] * (TEAM + 4) + [VMEM],
        scratch_shapes=[
            pltpu.VMEM((2, rows, width), BF16),
            pltpu.VMEM((width, cols), BF16),
            pltpu.VMEM(weight_head.shape, BF16),
            pltpu.VMEM((q_cols, width), BF16),
            pltpu.VMEM((2, rows, width), BF16),
            pltpu.VMEM((2, rows, width), BF16),
            pltpu.VMEM((2, rows, cols), F32),
            pltpu.VMEM((2, rows, TILE), F32),
            pltpu.VMEM((2, rows, q_cols), BF16),
            pltpu.SemaphoreType.DMA((1 + gathered.shape[0] * (1 + width // cols),)),
            pltpu.SemaphoreType.DMA((2,)),
            pltpu.SemaphoreType.DMA((5, 2)),
        ],
        compiler_params=pltpu.CompilerParams(vmem_limit_bytes=48 << 20),
        cost_estimate=pl.CostEstimate(flops=30 << 30, bytes_accessed=60 << 20, transcendentals=1 << 20),
    )(tiles, *tokens, gathered, weight_head, gain, gains, cosine, sine, after)
    return result[:TEAM], result[TEAM : TEAM + 4], result[TEAM + 4]


def attend_back(tiles, hidden, consts, saved, mine, after):
    gathered, weight_head, gain, gains, cosine, sine = consts
    rows, width = hidden[0].shape
    size = gains.shape[1]
    q_cols = mine * size
    cols = gathered.shape[2]
    factor = size ** (-0.5)

    def kernel(*refs):
        tiles_ref, hids = refs[0], refs[1 : 1 + TEAM]
        wa, wh, normed_all, qkv_all, logit_all, gated_all = refs[1 + TEAM : 7 + TEAM]
        gains_ref, cos_ref, sin_ref, _ = refs[7 + TEAM : 11 + TEAM]
        parts = refs[11 + TEAM : 11 + 2 * TEAM]
        packed, head_sum, gain_sum, gains_sum = refs[11 + 2 * TEAM : 15 + 2 * TEAM]
        (
            hid_v, wa_v, wh_v, wo_v, normed_v, qkv_v, logit_v, gated_v, part_v, back_v, attn_sum, out_sum,
            w_sem, in_sem, out_sem,
        ) = refs[15 + 2 * TEAM :]

        def loads(r, slot, k):
            yield pltpu.make_async_copy(hids[k], hid_v.at[slot], in_sem.at[0, slot])
            here = rows_of(r, rows)
            for j, (src, dst) in enumerate(
                ((qkv_all, qkv_v), (logit_all, logit_v), (normed_all, normed_v), (gated_all, gated_v))
            ):
                yield pltpu.make_async_copy(src.at[here], dst.at[slot], in_sem.at[1 + j, slot])

        def start_loads(r, slot):
            def body(k):
                for copy in loads(r, slot, k):
                    copy.start()

            each_block(r, body)

        def store(slot, k=0):
            return pltpu.make_async_copy(part_v.at[slot], parts[k], out_sem.at[slot])

        for copy in loads(0, 0, 0):
            copy.start()
        weights = load_weights(wa, wh, wa_v, wo_v, wh_v, w_sem)
        for copy in weights:
            copy.start()
        for ref in (attn_sum, out_sum, gain_sum, gains_sum):
            ref[...] = jnp.zeros_like(ref)
        for copy in weights:
            copy.wait()

        def step(r, carry):
            slot = r % 2

            @pl.when(r + 1 < TEAM)
            def _():
                start_loads(r + 1, 1 - slot)

            for copy in loads(r, slot, 0):
                copy.wait()

            @pl.when(r >= 2)
            def _():
                store(slot).wait()

            def body(n):
                hidden_low = hid_v[slot, :n]
                normed = normed_v[slot, :n]
                out_sum[...] += product_tn(gated_v[slot, :n], hidden_low)
                gated_grad = product_nt(hidden_low, wo_v[...])
                cos, sin = cos_ref[:n], sin_ref[:n]
                key_raw = qkv_v[slot, :n, q_cols : q_cols + size]
                key = turned(key_raw * head_norm(key_raw) * gains_ref[1:2], cos, sin).astype(BF16)
                values = qkv_v[slot, :n, q_cols + size :].astype(BF16)
                lane = lax.broadcasted_iota(jnp.int32, (n, TILE), 1)
                logit_back = jnp.zeros((n, TILE), F32)
                values_back = jnp.zeros((n, size), F32)
                key_grad = jnp.zeros((n, size), F32)
                query_sum = jnp.zeros((1, size), F32)
                for h in range(mine):
                    span = slice(h * size, (h + 1) * size)
                    query_raw = qkv_v[slot, :n, span]
                    query = turned(query_raw * head_norm(query_raw) * gains_ref[0:1], cos, sin).astype(BF16)
                    attention = weights_of(query, key, factor)
                    attention_low = attention.astype(BF16)
                    mixture = product(attention_low, values)
                    gate = jax.nn.sigmoid(logit_v[slot, :n, h : h + 1])
                    head_grad = gated_grad[:, span]
                    mixture_back = (head_grad * gate).astype(BF16)
                    one = jnp.sum(head_grad * mixture, axis=-1, keepdims=True) * gate * (1.0 - gate)
                    logit_back = jnp.where(lane == h, one, logit_back)
                    values_back += product_tn(attention_low, mixture_back)
                    attention_grad = product_nt(mixture_back, values)
                    scores_back = (
                        attention
                        * (attention_grad - jnp.sum(attention_grad * attention, axis=-1, keepdims=True))
                    ).astype(BF16)
                    query_grad = product(scores_back, key) * factor
                    key_grad += product_tn(scores_back, query)
                    back, total = head_back(query_grad, query_raw, gains_ref[0:1], cos, sin)
                    back_v[:n, span] = back.astype(BF16)
                    query_sum += total
                back, key_sum = head_back(key_grad * factor, key_raw, gains_ref[1:2], cos, sin)
                back_v[:n, q_cols : q_cols + size] = back.astype(BF16)
                back_v[:n, q_cols + size : cols] = values_back.astype(BF16)
                logit_back = logit_back.astype(BF16)
                back_v[:n, cols:] = logit_back
                gains_sum[0:1] += query_sum
                gains_sum[1:2] += key_sum
                part = product_nt(back_v[:n, :cols], wa_v[...]) + product(logit_back, wh_v[...])
                part_v[slot, :n] = part.astype(BF16)
                gain_sum[0:1] += jnp.sum(part * normed.astype(F32), axis=0, keepdims=True)
                attn_sum[...] += product_tn(back_v[:n], normed)
                if n < rows:
                    part_v[slot, n:] = jnp.zeros((rows - n, width), BF16)

            for_tiles(tiles_ref[r], rows // TILE, body)
            each_block(r, lambda k: store(slot, k).start())
            return carry

        lax.fori_loop(0, TEAM, step, 0)
        head_sum[...] = attn_sum[cols : cols + 8]
        turned_sum = attn_sum[:cols].T.astype(BF16)
        groups, height, _ = packed.shape
        rho = width // (groups * TEAM)
        for g in range(groups):
            packed[g, : TEAM * rho] = turned_sum[g * TEAM * rho : (g + 1) * TEAM * rho]
            for k in range(width // cols):
                top = TEAM * rho + k * rho
                packed[g, top : top + rho] = out_sum[
                    g * rho : (g + 1) * rho, k * cols : (k + 1) * cols
                ].astype(BF16)
            packed[g, height - 16 :] = jnp.zeros((16, cols), BF16)
        store(0).wait()
        store(1).wait()

    result = pl.pallas_call(
        kernel,
        out_shape=[struct((rows, width), BF16)] * TEAM
        + [
            struct(gathered.shape, BF16),
            struct((8, width), F32),
            struct((8, width), F32),
            struct((8, size), F32),
        ],
        in_specs=[SMEM] + [ANY] * (TEAM + 6) + [VMEM] * 3 + [ANY],
        out_specs=[ANY] * TEAM + [VMEM] * 4,
        scratch_shapes=[
            pltpu.VMEM((2, rows, width), BF16),
            pltpu.VMEM((width, cols), BF16),
            pltpu.VMEM(weight_head.shape, BF16),
            pltpu.VMEM((q_cols, width), BF16),
            pltpu.VMEM((2, rows, width), BF16),
            pltpu.VMEM((2, rows, cols), F32),
            pltpu.VMEM((2, rows, TILE), F32),
            pltpu.VMEM((2, rows, q_cols), BF16),
            pltpu.VMEM((2, rows, width), BF16),
            pltpu.VMEM((rows, cols + TILE), BF16),
            pltpu.VMEM((cols + TILE, width), F32),
            pltpu.VMEM((q_cols, width), F32),
            pltpu.SemaphoreType.DMA((1 + gathered.shape[0] * (1 + width // cols),)),
            pltpu.SemaphoreType.DMA((5, 2)),
            pltpu.SemaphoreType.DMA((2,)),
        ],
        compiler_params=pltpu.CompilerParams(vmem_limit_bytes=56 << 20),
        cost_estimate=pl.CostEstimate(flops=45 << 30, bytes_accessed=70 << 20, transcendentals=1 << 20),
    )(tiles, *hidden, gathered, weight_head, *saved, gains, cosine, sine, after)
    return result[:TEAM], *result[TEAM : TEAM + 2], result[TEAM + 2][0], result[TEAM + 3][:2]


def tile_places(tiles_ref, rows):
    places, total = [], 0
    for r in range(TEAM):
        count = tiles_ref[r]
        for j in range(rows // TILE):
            places.append((r, j, j < count, total + j))
        total = total + count
    return places, total


def feed(tiles, twos, upstreams, weight_gate, weight_up, weight_down):
    rows, width = twos[0].shape
    ff_cols = weight_down.shape[0]
    whole = TEAM * rows
    chunk = 2 * TILE
    chunks = whole // chunk

    def kernel(*refs):
        tiles_ref, twos_ref, ups_ref = refs[0], refs[1 : 1 + TEAM], refs[1 + TEAM : 1 + 2 * TEAM]
        weights_ref = refs[1 + 2 * TEAM : 4 + 2 * TEAM]
        outs_ref = refs[4 + 2 * TEAM : 4 + 3 * TEAM]
        grads_ref = refs[4 + 3 * TEAM : 4 + 4 * TEAM]
        inner_all, back_all, two_all, ups_all = refs[4 + 4 * TEAM : 8 + 4 * TEAM]
        (
            two_v, ups_v, wg_v, wu_v, wd_v, inner_v, back_v, out_v, grad_v, zero_v,
            w_sem, load_sem, keep_sem, tile_sem, dead_sem,
        ) = refs[8 + 4 * TEAM :]
        places, total = tile_places(tiles_ref, rows)
        used = (total + 1) // 2

        def loads(sources, packed, which):
            for k, (r, j, live, place) in enumerate(places):
                yield live, pltpu.make_async_copy(
                    sources[r].at[rows_of(j)], packed.at[rows_of(place)], load_sem.at[which, k]
                )

        weights = [
            pltpu.make_async_copy(src, dst, w_sem.at[j])
            for j, (src, dst) in enumerate(zip(weights_ref, (wg_v, wu_v, wd_v)))
        ]
        for live, copy in loads(twos_ref, two_v, 0):
            pl.when(live)(copy.start)
        for copy in weights:
            copy.start()
        for live, copy in loads(ups_ref, ups_v, 1):
            pl.when(live)(copy.start)
        zero_v[...] = jnp.zeros_like(zero_v)

        def dead(k, r, j):
            zeros = zero_v.at[:TILE]
            yield pltpu.make_async_copy(zeros, grads_ref[r].at[rows_of(j)], dead_sem.at[0, k])
            yield pltpu.make_async_copy(zeros, outs_ref[r].at[rows_of(j)], dead_sem.at[1, k])

        for k, (r, j, live, place) in enumerate(places):

            @pl.when(jnp.logical_not(live))
            def _(k=k, r=r, j=j):
                for copy in dead(k, r, j):
                    copy.start()

        def keeps(c, sources):
            for j, (src, dst) in enumerate(zip(sources, (two_all, ups_all, inner_all, back_all))):
                yield pltpu.make_async_copy(src, dst.at[rows_of(c, chunk)], keep_sem.at[j, c])

        zeros = (zero_v, zero_v, zero_v.at[:, :ff_cols], zero_v.at[:, : 2 * ff_cols])
        for c in range(TEAM // 2, chunks):

            @pl.when(c >= used)
            def _(c=c):
                for copy in keeps(c, zeros):
                    copy.start()

        @pl.when(total % 2 == 1)
        def _():
            two_v[rows_of(total)] = jnp.zeros((TILE, width), BF16)
            ups_v[rows_of(total)] = jnp.zeros((TILE, width), BF16)

        for live, copy in loads(twos_ref, two_v, 0):
            pl.when(live)(copy.wait)
        for copy in weights:
            copy.wait()
        for live, copy in loads(ups_ref, ups_v, 1):
            pl.when(live)(copy.wait)

        def tile_stores(r, j, slot, side):
            here = pl.ds(side * TILE, TILE)
            yield pltpu.make_async_copy(
                grad_v.at[slot, here], grads_ref[r].at[rows_of(j)], tile_sem.at[0, slot, side]
            )
            yield pltpu.make_async_copy(
                out_v.at[slot, here], outs_ref[r].at[rows_of(j)], tile_sem.at[1, slot, side]
            )

        def wait_tiles(c, slot):
            for side in range(2):

                @pl.when(2 * c + side < total)
                def _(side=side):
                    for copy in tile_stores(0, 0, slot, side):
                        copy.wait()

        def body(c, carry):
            slot = c % 2
            span = rows_of(c, chunk)

            @pl.when(c >= 2)
            def _():
                wait_tiles(c - 2, slot)
                for j, copy in enumerate(keeps(c - 2, zeros)):
                    if j >= 2:
                        copy.wait()

            gate_part = product(two_v[span], wg_v[...])
            up_part = product(two_v[span], wu_v[...])
            sig = jax.nn.sigmoid(gate_part)
            silu = gate_part * sig
            inner_v[slot] = (silu * up_part).astype(BF16)
            inner_grad = product_nt(ups_v[span], wd_v[...])
            back_v[slot, :, :ff_cols] = (inner_grad * up_part * (sig + silu * (1.0 - sig))).astype(BF16)
            back_v[slot, :, ff_cols:] = (inner_grad * silu).astype(BF16)
            for copy in keeps(c, (two_v.at[span], ups_v.at[span], inner_v.at[slot], back_v.at[slot])):
                copy.start()
            grad = product_nt(back_v[slot, :, :ff_cols], wg_v[...]) + product_nt(
                back_v[slot, :, ff_cols:], wu_v[...]
            )
            grad_v[slot] = grad.astype(BF16)
            out_v[slot] = product(inner_v[slot], wd_v[...]).astype(BF16)
            for k, (r, j, live, place) in enumerate(places):
                for side in range(2):

                    @pl.when(jnp.logical_and(live, place == 2 * c + side))
                    def _(r=r, j=j, side=side):
                        for copy in tile_stores(r, j, slot, side):
                            copy.start()

            return carry

        lax.fori_loop(0, used, body, 0)
        wait_tiles(used - 2, used % 2)
        wait_tiles(used - 1, (used - 1) % 2)
        for k, (r, j, live, place) in enumerate(places):

            @pl.when(jnp.logical_not(live))
            def _(k=k, r=r, j=j):
                for copy in dead(k, r, j):
                    copy.wait()

        for c in range(chunks):
            for j, copy in enumerate(keeps(c, zeros)):
                if j < 2:
                    copy.wait()
                else:
                    pl.when(c >= used - 2)(copy.wait)

    count = whole // TILE
    result = pl.pallas_call(
        kernel,
        out_shape=[struct((rows, width), BF16)] * (2 * TEAM)
        + [
            struct((whole, ff_cols), BF16),
            struct((whole, 2 * ff_cols), BF16),
            struct((whole, width), BF16),
            struct((whole, width), BF16),
        ],
        in_specs=[SMEM] + [ANY] * (3 + 2 * TEAM),
        out_specs=[ANY] * (2 * TEAM + 4),
        scratch_shapes=[
            pltpu.VMEM((whole, width), BF16),
            pltpu.VMEM((whole, width), BF16),
            pltpu.VMEM(weight_gate.shape, BF16),
            pltpu.VMEM(weight_up.shape, BF16),
            pltpu.VMEM(weight_down.shape, BF16),
            pltpu.VMEM((2, chunk, ff_cols), BF16),
            pltpu.VMEM((2, chunk, 2 * ff_cols), BF16),
            pltpu.VMEM((2, chunk, width), BF16),
            pltpu.VMEM((2, chunk, width), BF16),
            pltpu.VMEM((chunk, width), BF16),
            pltpu.SemaphoreType.DMA((3,)),
            pltpu.SemaphoreType.DMA((2, count)),
            pltpu.SemaphoreType.DMA((4, chunks)),
            pltpu.SemaphoreType.DMA((2, 2, 2)),
            pltpu.SemaphoreType.DMA((2, count)),
        ],
        compiler_params=pltpu.CompilerParams(vmem_limit_bytes=60 << 20),
        cost_estimate=pl.CostEstimate(flops=58 << 30, bytes_accessed=100 << 20, transcendentals=1 << 20),
    )(tiles, *twos, *upstreams, weight_gate, weight_up, weight_down)
    return result[:TEAM], result[TEAM : 2 * TEAM], result[2 * TEAM :]


def local(
    groups,
    tokens,
    lengths,
    cotangent,
    attention_gain,
    query_weight,
    key_matrix,
    value_matrix,
    head_gate_weight,
    output_weight,
    query_key_gain,
    feedforward_gain,
    gate_weight,
    up_weight,
    down_weight,
):
    t = member()
    everyone = groups * TEAM
    rows, width = tokens.shape
    rho = query_weight.shape[0]
    phi = down_weight.shape[0]
    ff = gate_weight.shape[1]
    pair_cols = query_key_gain.shape[1]
    size = pair_cols * everyone
    heads = query_weight.shape[1] // size
    mine = heads // TEAM
    q_cols = query_weight.shape[1] // TEAM
    k_cols = key_matrix.shape[1] // TEAM
    ff_cols = ff // TEAM

    def everyone_in_team(vector):
        return jnp.broadcast_to(vector.reshape(1, -1), (TEAM, vector.size))

    live_tiles = (lengths + (TILE - 1)) // TILE
    row = jnp.concatenate(
        [
            head_gate_weight.reshape(rho, TEAM, mine).transpose(1, 2, 0).reshape(TEAM, -1),
            everyone_in_team(attention_gain),
            everyone_in_team(feedforward_gain),
            everyone_in_team(query_key_gain),
            everyone_in_team(live_tiles.astype(BF16)),
        ],
        axis=1,
    )
    cols = q_cols + 2 * k_cols
    row = jnp.pad(row, ((0, 0), (0, cols - row.shape[1])))[:, None, :]
    attn = jnp.concatenate(
        [
            query_weight.reshape(rho, TEAM, q_cols),
            key_matrix.reshape(rho, TEAM, k_cols),
            value_matrix.reshape(rho, TEAM, k_cols),
        ],
        axis=2,
    ).transpose(1, 0, 2)
    attn = jnp.concatenate([attn, jnp.pad(row, ((0, 0), (0, 7), (0, 0)))], axis=1)
    attn = exchange(attn)
    head_lanes = mine * rho
    at_one, at_two, at_pair = head_lanes, head_lanes + rho, head_lanes + 2 * rho
    at_tiles = at_pair + 2 * pair_cols
    team_tiles = attn[:, rho, at_tiles].astype(jnp.int32)
    order = jnp.arange(TEAM, dtype=jnp.int32)
    tiles = jnp.sum(jnp.where((order[:, None] ^ t) == order[None, :], team_tiles[None, :], 0), axis=1)
    routed = lax.ppermute(output_weight, ALL, out_weight_routes(groups))
    team_rows = TEAM * rho
    small_at = team_rows + (width // cols) * rho
    stacked = jnp.concatenate(
        [attn[:, :rho].reshape(team_rows, cols)]
        + [routed[:, k : k + cols] for k in range(0, width, cols)]
        + [attn[:, rho], jnp.zeros((16 - TEAM, cols), BF16)],
        axis=0,
    )
    gathered = line_gather(stacked).reshape(groups, -1, cols)
    rows_small = gathered[:, small_at : small_at + TEAM].reshape(everyone, cols)
    weight_head = jnp.pad(
        rows_small[:, :head_lanes].reshape(everyone, mine, rho).transpose(1, 0, 2).reshape(mine, width),
        ((0, TILE - mine), (0, 0)),
    )
    gain_one = rows_small[:, at_one:at_two].reshape(1, width).astype(F32)
    gain_two = rows_small[:, at_two:at_pair].reshape(1, width).astype(F32)
    gain_pair = (
        rows_small[:, at_pair:at_tiles]
        .reshape(everyone, 2, pair_cols)
        .transpose(1, 0, 2)
        .reshape(2, size)
        .astype(F32)
    )
    def ff_split(w):
        return w.reshape(rho, groups, TEAM, phi).transpose(2, 0, 1, 3).reshape(TEAM, rho, ff_cols)

    feed_shard = jnp.concatenate([ff_split(gate_weight), ff_split(up_weight)], axis=2)

    exponent = jnp.arange(size // 2, dtype=F32) * (-2.0 / size)
    frequency = jnp.power(ROPE_BASE, exponent)
    angles = jnp.arange(rows, dtype=F32)[:, None] * frequency[None, :]
    cosine = jnp.concatenate([jnp.cos(angles), jnp.cos(angles)], axis=1)
    sine = jnp.concatenate([-jnp.sin(angles), jnp.sin(angles)], axis=1)
    consts = (gathered, weight_head, gain_one, gain_pair, cosine, sine)
    team_tokens = team_gather(tokens)
    feed_shard = exchange(feed_shard).reshape(TEAM * rho, -1)
    weight_gate = line_gather(feed_shard[:, :ff_cols])
    live = lax.broadcasted_iota(jnp.int32, (rows, 1), 0) < lengths[0]
    live_rows = live.astype(F32)
    upstream = cotangent.astype(F32) * live_rows
    tick = mark([team_tokens[6]])
    later = lax.broadcasted_iota(jnp.int32, (rows, 1), 0) < lengths[0] + tick[0, 0]
    upstream_low = jnp.where(later, cotangent, jnp.zeros_like(cotangent))
    upstream_levels = TeamGather(upstream_low)
    parts, kept, tick = attend(tiles, team_tokens, consts, mine, mark([upstream_low]))
    normed, qkv, logit, gated = kept
    weight_up = line_gather(hold([feed_shard[:, ff_cols:]], tick)[0])
    parts = hold(parts, mark([upstream_levels.a1, upstream_levels.a2, upstream_levels.a4, tick]))
    arrived = TeamSum(parts)
    arrived.first()
    weight_down = line_gather(hold([down_weight], arrived.sent[0])[0])
    inputs = tokens.astype(F32)
    hidden_state = inputs + arrived.total(weight_gate)

    normed_two = rms(hidden_state, gain_two).astype(BF16)
    team_upstream = upstream_levels.blocks(normed_two)
    team_two = TeamGather(normed_two).blocks(weight_up)
    outs, grads, saved = feed(tiles, team_two, team_upstream, weight_gate, weight_up, weight_down)
    inner, feed_back, two_all, ups_all = saved
    arrived = TeamSum(grads)
    arrived.first()
    two_grad = arrived.total()
    inner = hold([inner], mark(arrived.sent))[0]
    down_part = product_tn(inner, ups_all).astype(BF16)
    feed_back = hold([feed_back], mark([arrived.over_x, arrived.over_y]))[0]
    gate_part = product_tn(two_all, feed_back[:, :ff_cols]).astype(BF16)
    hidden_grad = upstream + rms_pull(hidden_state, gain_two, two_grad)
    hidden_low = hidden_grad.astype(BF16)
    feed_back = hold([feed_back], mark([gate_part, hidden_low]))[0]
    up_part = product_tn(two_all, feed_back[:, ff_cols:]).astype(BF16)
    parts_made = mark([gate_part, up_part])
    down_grad = line_sum(down_part)
    gate_grad = line_sum(hold([gate_part], down_grad)[0])
    up_grad = line_sum(hold([up_part], gate_grad)[0])
    feed_done = up_grad

    fed = TeamSum(hold(outs, arrived.over_x))
    team_hidden = TeamGather(hidden_low).blocks(mark(fed.ready + [gate_part, up_part]))
    two_scale = lax.rsqrt(jnp.mean(hidden_state * hidden_state, axis=-1, keepdims=True) + EPSILON)
    two_sum = jnp.sum(two_grad * hidden_state * two_scale, axis=0)
    first_hop = fed.first(mark(team_hidden + [parts_made]))
    parts, packed, head_sum, one_sum, pair_sum = attend_back(
        tiles, team_hidden, consts, (normed, qkv, logit, gated), mine, mark(fed.sent + [down_grad])
    )
    row = jnp.concatenate(
        [
            head_sum[:mine].reshape(mine, everyone, rho).transpose(1, 0, 2).reshape(everyone, -1),
            (one_sum / gain_one[0]).reshape(everyone, rho),
            two_sum.reshape(everyone, rho),
            pair_sum.reshape(2, everyone, pair_cols).transpose(1, 0, 2).reshape(everyone, -1),
        ],
        axis=1,
    ).astype(BF16)
    row = jnp.pad(row, ((0, 0), (0, cols - row.shape[1]))).reshape(groups, TEAM, cols)
    packed = lax.dynamic_update_slice(packed, row, (0, small_at, 0))
    parts = hold(parts, mark(first_hop + [gate_grad]))
    arrived = TeamSum(parts)
    arrived.first()
    packed = hold([packed.reshape(-1, cols)], mark([feed_done] + arrived.sent))[0]
    normed_grad = arrived.total(packed)
    packed = line_sum(packed)
    summed = packed
    layer_output = ((hidden_state + fed.total(mark([normed_grad, summed]))) * live_rows).astype(BF16)
    tokens_grad = (hidden_grad + rms_pull(inputs, gain_one, normed_grad)).astype(BF16)
    feed_grad = jnp.concatenate([gate_grad, hold([up_grad], mark(arrived.last_sent))[0]], axis=1)
    feed_grad = exchange(feed_grad.reshape(TEAM, rho, 2 * ff_cols))
    feed_grad = hold([feed_grad], mark(fed.last_sent))[0]

    def ff_join(w):
        return w.reshape(TEAM, rho, groups, phi).transpose(1, 2, 0, 3).reshape(rho, ff)

    gate_grad, up_grad = hold(
        [ff_join(feed_grad[:, :, :ff_cols]), ff_join(feed_grad[:, :, ff_cols:])], summed
    )
    routes = [(user, owner) for owner, user in out_weight_routes(groups)]
    output_grad = packed[team_rows:small_at].reshape(-1, rho, cols).transpose(1, 0, 2).reshape(rho, width)
    output_grad = lax.ppermute(output_grad, ALL, routes)
    packed = jnp.concatenate(
        [
            packed[:team_rows].reshape(TEAM, rho, cols),
            jnp.pad(packed[small_at : small_at + TEAM][:, None], ((0, 0), (0, 7), (0, 0))),
        ],
        axis=1,
    )
    packed = exchange(packed)
    attn_grad = packed[:, :rho].transpose(1, 0, 2)
    rows_small = packed[:, rho].astype(F32)
    sums = jnp.sum(rows_small[:, head_lanes:], axis=0)
    head_gate_grad = rows_small[:, :head_lanes].reshape(heads, rho).T
    return (
        layer_output,
        tokens_grad,
        sums[:rho],
        attn_grad[:, :, :q_cols].reshape(rho, -1).astype(F32),
        attn_grad[:, :, q_cols : q_cols + k_cols].reshape(rho, -1).astype(F32),
        attn_grad[:, :, q_cols + k_cols :].reshape(rho, -1).astype(F32),
        head_gate_grad,
        output_grad.astype(F32),
        sums[2 * rho : 2 * rho + 2 * pair_cols].reshape(2, pair_cols),
        sums[rho : 2 * rho],
        gate_grad.astype(F32),
        up_grad.astype(F32),
        down_grad.astype(F32),
    )


def solution(mesh):
    groups = mesh.size // TEAM
    rows, vector, columns = P(ALL, None), P(ALL), P(None, ALL)

    def step(*args):
        return local(groups, *args)

    return jax.shard_map(
        step,
        mesh=mesh,
        in_specs=(
            rows, vector, rows, vector, rows, rows, rows, rows, rows, columns, vector, rows, rows, rows,
        ),
        out_specs=(
            rows, rows, vector, rows, rows, rows, rows, rows, columns, vector, rows, rows, rows,
        ),
        check_vma=False,
    )
```

```python
import jax
import jax.numpy as jnp
from jax import lax
from jax.experimental import pallas as pl
from jax.experimental.pallas import tpu as pltpu
from jax.sharding import PartitionSpec as P

EPSILON = 1e-06
ROPE_BASE = 1000000.0
TEAM = 8
ALL = ("dp", "fsdp")
F32 = jnp.float32
BF16 = jnp.bfloat16
TILE = 128
ANY = pl.BlockSpec(memory_space=pl.ANY)
VMEM = pl.BlockSpec(memory_space=pltpu.VMEM)
SMEM = pl.BlockSpec(memory_space=pltpu.SMEM)


def product(left, right):
    return jnp.dot(left, right, preferred_element_type=F32)


def product_nt(left, right):
    return lax.dot_general(left, right, (((1,), (1,)), ((), ())), preferred_element_type=F32)


def product_tn(left, right):
    return lax.dot_general(left, right, (((0,), (0,)), ((), ())), preferred_element_type=F32)


def world():
    return lax.axis_size(ALL)


def member():
    return lax.axis_index(ALL) % TEAM


def teams():
    return [[first + t for t in range(TEAM)] for first in range(0, world(), TEAM)]


def lines():
    return [list(range(t, world(), TEAM)) for t in range(TEAM)]


def permute(array, pairs):
    return lax.ppermute(
        array, ALL, [(team[a], team[b]) for team in teams() for a, b in pairs]
    )


def swap(array, bits):
    return permute(array, [(i, i ^ bits) for i in range(TEAM)])


def exchange(blocks):
    if lax.axis_size("fsdp") == TEAM:
        return lax.all_to_all(blocks, "fsdp", 0, 0, tiled=True)
    return lax.all_to_all(blocks, ALL, 0, 0, tiled=True, axis_index_groups=teams())


def line_gather(shard):
    if lax.axis_size("fsdp") == TEAM:
        return lax.all_gather(shard, "dp", axis=0, tiled=True)
    return lax.all_gather(shard, ALL, axis=0, tiled=True, axis_index_groups=lines())


def line_sum(array):
    if lax.axis_size("fsdp") == TEAM:
        return lax.psum_scatter(array, "dp", scatter_dimension=0, tiled=True)
    return lax.psum_scatter(array, ALL, scatter_dimension=0, tiled=True, axis_index_groups=lines())


class TeamGather:
    def __init__(self, own):
        self.own = own
        self.a1 = swap(own, 1)
        self.a2 = swap(own, 2)
        self.a4 = swap(own, 4)

    def blocks(self, tick=None):
        a2, a4 = self.a2, self.a4
        if tick is not None:
            a2, a4 = hold([a2, a4], tick)
        half = self.own.shape[0] // 2
        a6 = jnp.concatenate([swap(a4[:half], 2), swap(a2[half:], 4)], axis=0)
        return [self.own, self.a1, a2, swap(a2, 1), a4, swap(a4, 1), a6, swap(a6, 1)]


def team_gather(own):
    return TeamGather(own).blocks()


class TeamSum:
    def __init__(self, parts):
        half = parts[0].shape[0] // 2
        odd = {r: swap(parts[r + 1], 1) for r in (6, 2, 4, 0)}
        self.total6, self.total2, self.total4, self.total0 = (
            (parts[r].astype(F32) + odd[r].astype(F32)).astype(BF16) for r in (6, 2, 4, 0)
        )
        self.half = half
        self.ready = [
            jnp.concatenate([self.total6[:half], self.total2[:half]], axis=0),
            jnp.concatenate([self.total6[half:], self.total4[half:]], axis=0),
        ]

    def first(self, tick=None):
        self.sent = self.ready if tick is None else list(hold(self.ready, tick))
        self.over_x, self.over_y = swap(self.sent[0], 2), swap(self.sent[1], 4)
        return [self.over_x, self.over_y]

    def total(self, tick=None):
        half = self.half
        lasts = [
            (self.total2[half:].astype(F32) + self.over_y[:half].astype(F32)).astype(BF16),
            (self.total4[:half].astype(F32) + self.over_x[:half].astype(F32)).astype(BF16),
        ]
        x_low, y_top = lasts if tick is None else hold(lasts, tick)
        self.last_sent = [x_low, y_top]
        x_low = swap(x_low, 2).astype(F32)
        y_top = swap(y_top, 4).astype(F32)
        top = self.over_x[half:].astype(F32) + y_top
        low = x_low + self.over_y[half:].astype(F32)
        return self.total0.astype(F32) + jnp.concatenate([top, low], axis=0)


def out_weight_routes(groups):
    return [(i, TEAM * (i % groups) + i // groups) for i in range(groups * TEAM)]


def rms_pull(value, gain, grad):
    scale = lax.rsqrt(jnp.mean(value * value, axis=-1, keepdims=True) + EPSILON)
    weighted = grad * gain
    mean = jnp.mean(weighted * value, axis=-1, keepdims=True)
    return scale * weighted - scale * scale * scale * value * mean


def rms(value, gain):
    return value * lax.rsqrt(jnp.mean(value * value, axis=-1, keepdims=True) + EPSILON) * gain


def struct(shape, dtype):
    return jax.ShapeDtypeStruct(shape, dtype)


def hold(arrays, tick):
    def kernel(*refs):
        del refs

    count = len(arrays)
    return pl.pallas_call(
        kernel,
        out_shape=[struct(a.shape, a.dtype) for a in arrays],
        in_specs=[ANY] * count + [ANY],
        out_specs=[ANY] * count,
        input_output_aliases={i: i for i in range(count)},
    )(*arrays, tick)


def mark(arrays):
    def kernel(*refs):
        refs[-1][...] = jnp.zeros_like(refs[-1])

    return pl.pallas_call(
        kernel,
        out_shape=struct((8, 128), jnp.int32),
        in_specs=[ANY] * len(arrays),
        out_specs=VMEM,
    )(*arrays)


def for_tiles(tiles, most, body):
    for m in range(1, most + 1):

        @pl.when(tiles == m)
        def _(m=m):
            body(m * TILE)


def turned(u, cosine, sine):
    return u * cosine + pltpu.roll(u, u.shape[-1] // 2, 1) * sine


def head_norm(u):
    return lax.rsqrt(jnp.mean(u * u, axis=-1, keepdims=True) + EPSILON)


def head_back(grad, raw, gain, cosine, sine):
    e = turned(grad, cosine, -sine)
    scale = head_norm(raw)
    weighted = e * gain
    mean = jnp.mean(weighted * raw, axis=-1, keepdims=True)
    back = scale * weighted - scale * scale * scale * raw * mean
    return back, jnp.sum(e * raw * scale, axis=0, keepdims=True)


def weights_of(query, key, factor):
    scores = product_nt(query, key) * factor
    n = scores.shape[0]
    causal = lax.broadcasted_iota(jnp.int32, (n, n), 1) <= lax.broadcasted_iota(jnp.int32, (n, n), 0)
    scores = jnp.where(causal, scores, -jnp.inf)
    terms = jnp.exp(scores - jnp.max(scores, axis=-1, keepdims=True))
    return terms * (1.0 / jnp.sum(terms, axis=-1, keepdims=True))


def rows_of(tile, size=TILE):
    return pl.ds(pl.multiple_of(tile * size, size), size)


def each_block(r, body):
    for k in range(TEAM):
        pl.when(r == k)(lambda k=k: body(k))


def load_weights(gathered, weight_head, wa_v, wo_v, wh_v, sems):
    groups, _, cols = gathered.shape
    width = wo_v.shape[1]
    rho = width // (groups * TEAM)
    copies = [pltpu.make_async_copy(weight_head, wh_v, sems.at[0])]
    for g in range(groups):
        copies.append(
            pltpu.make_async_copy(
                gathered.at[g, pl.ds(0, TEAM * rho)],
                wa_v.at[pl.ds(g * TEAM * rho, TEAM * rho)],
                sems.at[len(copies)],
            )
        )
        for k in range(width // cols):
            copies.append(
                pltpu.make_async_copy(
                    gathered.at[g, pl.ds(TEAM * rho + k * rho, rho)],
                    wo_v.at[pl.ds(g * rho, rho), pl.ds(k * cols, cols)],
                    sems.at[len(copies)],
                )
            )
    return copies


def attend(tiles, tokens, consts, mine, after):
    gathered, weight_head, gain, gains, cosine, sine = consts
    rows, width = tokens[0].shape
    size = gains.shape[1]
    q_cols = mine * size
    cols = gathered.shape[2]
    factor = size ** (-0.5)

    def kernel(*refs):
        tiles_ref, toks = refs[0], refs[1 : 1 + TEAM]
        wa, wh, gain_ref, gains_ref, cos_ref, sin_ref, _ = refs[1 + TEAM : 8 + TEAM]
        parts = refs[8 + TEAM : 8 + 2 * TEAM]
        normed_all, qkv_all, logit_all, gated_all, tick = refs[8 + 2 * TEAM : 13 + 2 * TEAM]
        (
            tok_v, wa_v, wh_v, wo_v, part_v, normed_v, qkv_v, logit_v, gated_v, w_sem, in_sem, out_sem,
        ) = refs[13 + 2 * TEAM :]
        tick[...] = jnp.zeros_like(tick)

        def load(k, slot):
            return pltpu.make_async_copy(toks[k], tok_v.at[slot], in_sem.at[slot])

        def store(r, slot, j, k=0):
            src = (part_v, normed_v, qkv_v, logit_v, gated_v)[j].at[slot]
            dst = parts[k] if j == 0 else (normed_all, qkv_all, logit_all, gated_all)[j - 1].at[rows_of(r, rows)]
            return pltpu.make_async_copy(src, dst, out_sem.at[j, slot])

        load(0, 0).start()
        weights = load_weights(wa, wh, wa_v, wo_v, wh_v, w_sem)
        for copy in weights:
            copy.start()
        for copy in weights:
            copy.wait()

        def step(r, carry):
            slot = r % 2

            @pl.when(r + 1 < TEAM)
            def _():
                each_block(r + 1, lambda k: load(k, 1 - slot).start())

            load(0, slot).wait()

            @pl.when(r >= 2)
            def _():
                for j in range(5):
                    store(r - 2, slot, j).wait()

            def body(n):
                value = tok_v[slot, :n].astype(F32)
                normed = rms(value, gain_ref[...]).astype(BF16)
                normed_v[slot, :n] = normed
                qkv = product(normed, wa_v[...])
                qkv_v[slot, :n] = qkv
                logit = product_nt(normed, wh_v[...])
                logit_v[slot, :n] = logit
                cos, sin = cos_ref[:n], sin_ref[:n]
                key = qkv[:, q_cols : q_cols + size]
                key = turned(key * head_norm(key) * gains_ref[1:2], cos, sin).astype(BF16)
                values = qkv[:, q_cols + size :].astype(BF16)
                for h in range(mine):
                    query = qkv[:, h * size : (h + 1) * size]
                    query = turned(query * head_norm(query) * gains_ref[0:1], cos, sin).astype(BF16)
                    attention = weights_of(query, key, factor)
                    mixture = product(attention.astype(BF16), values)
                    gate = jax.nn.sigmoid(logit[:, h : h + 1])
                    gated_v[slot, :n, h * size : (h + 1) * size] = (mixture * gate).astype(BF16)
                part_v[slot, :n] = product(gated_v[slot, :n], wo_v[...]).astype(BF16)
                if n < rows:
                    part_v[slot, n:] = jnp.zeros((rows - n, width), BF16)
                    normed_v[slot, n:] = jnp.zeros((rows - n, width), BF16)
                    gated_v[slot, n:] = jnp.zeros((rows - n, q_cols), BF16)

            for_tiles(tiles_ref[r], rows // TILE, body)
            each_block(r, lambda k: store(r, slot, 0, k).start())
            for j in range(1, 5):
                store(r, slot, j).start()
            return carry

        lax.fori_loop(0, TEAM, step, 0)
        for r in (TEAM - 2, TEAM - 1):
            for j in range(5):
                store(r, r % 2, j).wait()

    whole = TEAM * rows
    result = pl.pallas_call(
        kernel,
        out_shape=[struct((rows, width), BF16)] * TEAM
        + [
            struct((whole, width), BF16),
            struct((whole, cols), F32),
            struct((whole, TILE), F32),
            struct((whole, q_cols), BF16),
            struct((8, 128), jnp.int32),
        ],
        in_specs=[SMEM] + [ANY] * (TEAM + 2) + [VMEM] * 4 + [ANY],
        out_specs=[ANY] * (TEAM + 4) + [VMEM],
        scratch_shapes=[
            pltpu.VMEM((2, rows, width), BF16),
            pltpu.VMEM((width, cols), BF16),
            pltpu.VMEM(weight_head.shape, BF16),
            pltpu.VMEM((q_cols, width), BF16),
            pltpu.VMEM((2, rows, width), BF16),
            pltpu.VMEM((2, rows, width), BF16),
            pltpu.VMEM((2, rows, cols), F32),
            pltpu.VMEM((2, rows, TILE), F32),
            pltpu.VMEM((2, rows, q_cols), BF16),
            pltpu.SemaphoreType.DMA((1 + gathered.shape[0] * (1 + width // cols),)),
            pltpu.SemaphoreType.DMA((2,)),
            pltpu.SemaphoreType.DMA((5, 2)),
        ],
        compiler_params=pltpu.CompilerParams(vmem_limit_bytes=48 << 20),
        cost_estimate=pl.CostEstimate(flops=30 << 30, bytes_accessed=60 << 20, transcendentals=1 << 20),
    )(tiles, *tokens, gathered, weight_head, gain, gains, cosine, sine, after)
    return result[:TEAM], result[TEAM : TEAM + 4], result[TEAM + 4]


def attend_back(tiles, hidden, consts, saved, mine, after):
    gathered, weight_head, gain, gains, cosine, sine = consts
    rows, width = hidden[0].shape
    size = gains.shape[1]
    q_cols = mine * size
    cols = gathered.shape[2]
    factor = size ** (-0.5)

    def kernel(*refs):
        tiles_ref, hids = refs[0], refs[1 : 1 + TEAM]
        wa, wh, normed_all, qkv_all, logit_all, gated_all = refs[1 + TEAM : 7 + TEAM]
        gains_ref, cos_ref, sin_ref, _ = refs[7 + TEAM : 11 + TEAM]
        parts = refs[11 + TEAM : 11 + 2 * TEAM]
        packed, head_sum, gain_sum, gains_sum = refs[11 + 2 * TEAM : 15 + 2 * TEAM]
        (
            hid_v, wa_v, wh_v, wo_v, normed_v, qkv_v, logit_v, gated_v, part_v, back_v, attn_sum, out_sum,
            w_sem, in_sem, out_sem,
        ) = refs[15 + 2 * TEAM :]

        def loads(r, slot, k):
            yield pltpu.make_async_copy(hids[k], hid_v.at[slot], in_sem.at[0, slot])
            here = rows_of(r, rows)
            for j, (src, dst) in enumerate(
                ((qkv_all, qkv_v), (logit_all, logit_v), (normed_all, normed_v), (gated_all, gated_v))
            ):
                yield pltpu.make_async_copy(src.at[here], dst.at[slot], in_sem.at[1 + j, slot])

        def start_loads(r, slot):
            def body(k):
                for copy in loads(r, slot, k):
                    copy.start()

            each_block(r, body)

        def store(slot, k=0):
            return pltpu.make_async_copy(part_v.at[slot], parts[k], out_sem.at[slot])

        for copy in loads(0, 0, 0):
            copy.start()
        weights = load_weights(wa, wh, wa_v, wo_v, wh_v, w_sem)
        for copy in weights:
            copy.start()
        for ref in (attn_sum, out_sum, gain_sum, gains_sum):
            ref[...] = jnp.zeros_like(ref)
        for copy in weights:
            copy.wait()

        def step(r, carry):
            slot = r % 2

            @pl.when(r + 1 < TEAM)
            def _():
                start_loads(r + 1, 1 - slot)

            for copy in loads(r, slot, 0):
                copy.wait()

            @pl.when(r >= 2)
            def _():
                store(slot).wait()

            def body(n):
                hidden_low = hid_v[slot, :n]
                normed = normed_v[slot, :n]
                out_sum[...] += product_tn(gated_v[slot, :n], hidden_low)
                gated_grad = product_nt(hidden_low, wo_v[...])
                cos, sin = cos_ref[:n], sin_ref[:n]
                key_raw = qkv_v[slot, :n, q_cols : q_cols + size]
                key = turned(key_raw * head_norm(key_raw) * gains_ref[1:2], cos, sin).astype(BF16)
                values = qkv_v[slot, :n, q_cols + size :].astype(BF16)
                lane = lax.broadcasted_iota(jnp.int32, (n, TILE), 1)
                logit_back = jnp.zeros((n, TILE), F32)
                values_back = jnp.zeros((n, size), F32)
                key_grad = jnp.zeros((n, size), F32)
                query_sum = jnp.zeros((1, size), F32)
                for h in range(mine):
                    span = slice(h * size, (h + 1) * size)
                    query_raw = qkv_v[slot, :n, span]
                    query = turned(query_raw * head_norm(query_raw) * gains_ref[0:1], cos, sin).astype(BF16)
                    attention = weights_of(query, key, factor)
                    attention_low = attention.astype(BF16)
                    mixture = product(attention_low, values)
                    gate = jax.nn.sigmoid(logit_v[slot, :n, h : h + 1])
                    head_grad = gated_grad[:, span]
                    mixture_back = (head_grad * gate).astype(BF16)
                    one = jnp.sum(head_grad * mixture, axis=-1, keepdims=True) * gate * (1.0 - gate)
                    logit_back = jnp.where(lane == h, one, logit_back)
                    values_back += product_tn(attention_low, mixture_back)
                    attention_grad = product_nt(mixture_back, values)
                    scores_back = (
                        attention
                        * (attention_grad - jnp.sum(attention_grad * attention, axis=-1, keepdims=True))
                    ).astype(BF16)
                    query_grad = product(scores_back, key) * factor
                    key_grad += product_tn(scores_back, query)
                    back, total = head_back(query_grad, query_raw, gains_ref[0:1], cos, sin)
                    back_v[:n, span] = back.astype(BF16)
                    query_sum += total
                back, key_sum = head_back(key_grad * factor, key_raw, gains_ref[1:2], cos, sin)
                back_v[:n, q_cols : q_cols + size] = back.astype(BF16)
                back_v[:n, q_cols + size : cols] = values_back.astype(BF16)
                logit_back = logit_back.astype(BF16)
                back_v[:n, cols:] = logit_back
                gains_sum[0:1] += query_sum
                gains_sum[1:2] += key_sum
                part = product_nt(back_v[:n, :cols], wa_v[...]) + product(logit_back, wh_v[...])
                part_v[slot, :n] = part.astype(BF16)
                gain_sum[0:1] += jnp.sum(part * normed.astype(F32), axis=0, keepdims=True)
                attn_sum[...] += product_tn(back_v[:n], normed)
                if n < rows:
                    part_v[slot, n:] = jnp.zeros((rows - n, width), BF16)

            for_tiles(tiles_ref[r], rows // TILE, body)
            each_block(r, lambda k: store(slot, k).start())
            return carry

        lax.fori_loop(0, TEAM, step, 0)
        head_sum[...] = attn_sum[cols : cols + 8]
        turned_sum = attn_sum[:cols].T.astype(BF16)
        groups, height, _ = packed.shape
        rho = width // (groups * TEAM)
        for g in range(groups):
            packed[g, : TEAM * rho] = turned_sum[g * TEAM * rho : (g + 1) * TEAM * rho]
            for k in range(width // cols):
                top = TEAM * rho + k * rho
                packed[g, top : top + rho] = out_sum[
                    g * rho : (g + 1) * rho, k * cols : (k + 1) * cols
                ].astype(BF16)
            packed[g, height - 16 :] = jnp.zeros((16, cols), BF16)
        store(0).wait()
        store(1).wait()

    result = pl.pallas_call(
        kernel,
        out_shape=[struct((rows, width), BF16)] * TEAM
        + [
            struct(gathered.shape, BF16),
            struct((8, width), F32),
            struct((8, width), F32),
            struct((8, size), F32),
        ],
        in_specs=[SMEM] + [ANY] * (TEAM + 6) + [VMEM] * 3 + [ANY],
        out_specs=[ANY] * TEAM + [VMEM] * 4,
        scratch_shapes=[
            pltpu.VMEM((2, rows, width), BF16),
            pltpu.VMEM((width, cols), BF16),
            pltpu.VMEM(weight_head.shape, BF16),
            pltpu.VMEM((q_cols, width), BF16),
            pltpu.VMEM((2, rows, width), BF16),
            pltpu.VMEM((2, rows, cols), F32),
            pltpu.VMEM((2, rows, TILE), F32),
            pltpu.VMEM((2, rows, q_cols), BF16),
            pltpu.VMEM((2, rows, width), BF16),
            pltpu.VMEM((rows, cols + TILE), BF16),
            pltpu.VMEM((cols + TILE, width), F32),
            pltpu.VMEM((q_cols, width), F32),
            pltpu.SemaphoreType.DMA((1 + gathered.shape[0] * (1 + width // cols),)),
            pltpu.SemaphoreType.DMA((5, 2)),
            pltpu.SemaphoreType.DMA((2,)),
        ],
        compiler_params=pltpu.CompilerParams(vmem_limit_bytes=56 << 20),
        cost_estimate=pl.CostEstimate(flops=45 << 30, bytes_accessed=70 << 20, transcendentals=1 << 20),
    )(tiles, *hidden, gathered, weight_head, *saved, gains, cosine, sine, after)
    return result[:TEAM], *result[TEAM : TEAM + 2], result[TEAM + 2][0], result[TEAM + 3][:2]


def tile_places(tiles_ref, rows):
    places, total = [], 0
    for r in range(TEAM):
        count = tiles_ref[r]
        for j in range(rows // TILE):
            places.append((r, j, j < count, total + j))
        total = total + count
    return places, total


def feed(tiles, twos, upstreams, weight_gate, weight_up, weight_down):
    rows, width = twos[0].shape
    ff_cols = weight_down.shape[0]
    whole = TEAM * rows
    chunk = 2 * TILE
    chunks = whole // chunk

    def kernel(*refs):
        tiles_ref, twos_ref, ups_ref = refs[0], refs[1 : 1 + TEAM], refs[1 + TEAM : 1 + 2 * TEAM]
        weights_ref = refs[1 + 2 * TEAM : 4 + 2 * TEAM]
        outs_ref = refs[4 + 2 * TEAM : 4 + 3 * TEAM]
        grads_ref = refs[4 + 3 * TEAM : 4 + 4 * TEAM]
        inner_all, back_all, two_all, ups_all = refs[4 + 4 * TEAM : 8 + 4 * TEAM]
        (
            two_v, ups_v, wg_v, wu_v, wd_v, inner_v, back_v, out_v, grad_v, zero_v,
            w_sem, load_sem, keep_sem, tile_sem, dead_sem,
        ) = refs[8 + 4 * TEAM :]
        places, total = tile_places(tiles_ref, rows)
        used = (total + 1) // 2

        def loads(sources, packed, which):
            for k, (r, j, live, place) in enumerate(places):
                yield live, pltpu.make_async_copy(
                    sources[r].at[rows_of(j)], packed.at[rows_of(place)], load_sem.at[which, k]
                )

        weights = [
            pltpu.make_async_copy(src, dst, w_sem.at[j])
            for j, (src, dst) in enumerate(zip(weights_ref, (wg_v, wu_v, wd_v)))
        ]
        for live, copy in loads(twos_ref, two_v, 0):
            pl.when(live)(copy.start)
        for copy in weights:
            copy.start()
        for live, copy in loads(ups_ref, ups_v, 1):
            pl.when(live)(copy.start)
        zero_v[...] = jnp.zeros_like(zero_v)

        def dead(k, r, j):
            zeros = zero_v.at[:TILE]
            yield pltpu.make_async_copy(zeros, grads_ref[r].at[rows_of(j)], dead_sem.at[0, k])
            yield pltpu.make_async_copy(zeros, outs_ref[r].at[rows_of(j)], dead_sem.at[1, k])

        for k, (r, j, live, place) in enumerate(places):

            @pl.when(jnp.logical_not(live))
            def _(k=k, r=r, j=j):
                for copy in dead(k, r, j):
                    copy.start()

        def keeps(c, sources):
            for j, (src, dst) in enumerate(zip(sources, (two_all, ups_all, inner_all, back_all))):
                yield pltpu.make_async_copy(src, dst.at[rows_of(c, chunk)], keep_sem.at[j, c])

        zeros = (zero_v, zero_v, zero_v.at[:, :ff_cols], zero_v.at[:, : 2 * ff_cols])
        for c in range(TEAM // 2, chunks):

            @pl.when(c >= used)
            def _(c=c):
                for copy in keeps(c, zeros):
                    copy.start()

        @pl.when(total % 2 == 1)
        def _():
            two_v[rows_of(total)] = jnp.zeros((TILE, width), BF16)
            ups_v[rows_of(total)] = jnp.zeros((TILE, width), BF16)

        for live, copy in loads(twos_ref, two_v, 0):
            pl.when(live)(copy.wait)
        for copy in weights:
            copy.wait()
        for live, copy in loads(ups_ref, ups_v, 1):
            pl.when(live)(copy.wait)

        def tile_stores(r, j, slot, side):
            here = pl.ds(side * TILE, TILE)
            yield pltpu.make_async_copy(
                grad_v.at[slot, here], grads_ref[r].at[rows_of(j)], tile_sem.at[0, slot, side]
            )
            yield pltpu.make_async_copy(
                out_v.at[slot, here], outs_ref[r].at[rows_of(j)], tile_sem.at[1, slot, side]
            )

        def wait_tiles(c, slot):
            for side in range(2):

                @pl.when(2 * c + side < total)
                def _(side=side):
                    for copy in tile_stores(0, 0, slot, side):
                        copy.wait()

        def body(c, carry):
            slot = c % 2
            span = rows_of(c, chunk)

            @pl.when(c >= 2)
            def _():
                wait_tiles(c - 2, slot)
                for j, copy in enumerate(keeps(c - 2, zeros)):
                    if j >= 2:
                        copy.wait()

            gate_part = product(two_v[span], wg_v[...])
            up_part = product(two_v[span], wu_v[...])
            sig = jax.nn.sigmoid(gate_part)
            silu = gate_part * sig
            inner_v[slot] = (silu * up_part).astype(BF16)
            inner_grad = product_nt(ups_v[span], wd_v[...])
            back_v[slot, :, :ff_cols] = (inner_grad * up_part * (sig + silu * (1.0 - sig))).astype(BF16)
            back_v[slot, :, ff_cols:] = (inner_grad * silu).astype(BF16)
            for copy in keeps(c, (two_v.at[span], ups_v.at[span], inner_v.at[slot], back_v.at[slot])):
                copy.start()
            grad = product_nt(back_v[slot, :, :ff_cols], wg_v[...]) + product_nt(
                back_v[slot, :, ff_cols:], wu_v[...]
            )
            grad_v[slot] = grad.astype(BF16)
            out_v[slot] = product(inner_v[slot], wd_v[...]).astype(BF16)
            for k, (r, j, live, place) in enumerate(places):
                for side in range(2):

                    @pl.when(jnp.logical_and(live, place == 2 * c + side))
                    def _(r=r, j=j, side=side):
                        for copy in tile_stores(r, j, slot, side):
                            copy.start()

            return carry

        lax.fori_loop(0, used, body, 0)
        wait_tiles(used - 2, used % 2)
        wait_tiles(used - 1, (used - 1) % 2)
        for k, (r, j, live, place) in enumerate(places):

            @pl.when(jnp.logical_not(live))
            def _(k=k, r=r, j=j):
                for copy in dead(k, r, j):
                    copy.wait()

        for c in range(chunks):
            for j, copy in enumerate(keeps(c, zeros)):
                if j < 2:
                    copy.wait()
                else:
                    pl.when(c >= used - 2)(copy.wait)

    count = whole // TILE
    result = pl.pallas_call(
        kernel,
        out_shape=[struct((rows, width), BF16)] * (2 * TEAM)
        + [
            struct((whole, ff_cols), BF16),
            struct((whole, 2 * ff_cols), BF16),
            struct((whole, width), BF16),
            struct((whole, width), BF16),
        ],
        in_specs=[SMEM] + [ANY] * (3 + 2 * TEAM),
        out_specs=[ANY] * (2 * TEAM + 4),
        scratch_shapes=[
            pltpu.VMEM((whole, width), BF16),
            pltpu.VMEM((whole, width), BF16),
            pltpu.VMEM(weight_gate.shape, BF16),
            pltpu.VMEM(weight_up.shape, BF16),
            pltpu.VMEM(weight_down.shape, BF16),
            pltpu.VMEM((2, chunk, ff_cols), BF16),
            pltpu.VMEM((2, chunk, 2 * ff_cols), BF16),
            pltpu.VMEM((2, chunk, width), BF16),
            pltpu.VMEM((2, chunk, width), BF16),
            pltpu.VMEM((chunk, width), BF16),
            pltpu.SemaphoreType.DMA((3,)),
            pltpu.SemaphoreType.DMA((2, count)),
            pltpu.SemaphoreType.DMA((4, chunks)),
            pltpu.SemaphoreType.DMA((2, 2, 2)),
            pltpu.SemaphoreType.DMA((2, count)),
        ],
        compiler_params=pltpu.CompilerParams(vmem_limit_bytes=60 << 20),
        cost_estimate=pl.CostEstimate(flops=58 << 30, bytes_accessed=100 << 20, transcendentals=1 << 20),
    )(tiles, *twos, *upstreams, weight_gate, weight_up, weight_down)
    return result[:TEAM], result[TEAM : 2 * TEAM], result[2 * TEAM :]


def local(
    groups,
    tokens,
    lengths,
    cotangent,
    attention_gain,
    query_weight,
    key_matrix,
    value_matrix,
    head_gate_weight,
    output_weight,
    query_key_gain,
    feedforward_gain,
    gate_weight,
    up_weight,
    down_weight,
):
    t = member()
    everyone = groups * TEAM
    rows, width = tokens.shape
    rho = query_weight.shape[0]
    ff = gate_weight.shape[1]
    pair_cols = query_key_gain.shape[1]
    size = pair_cols * everyone
    heads = query_weight.shape[1] // size
    mine = heads // TEAM
    q_cols = query_weight.shape[1] // TEAM
    k_cols = key_matrix.shape[1] // TEAM
    ff_cols = ff // TEAM

    def everyone_in_team(vector):
        return jnp.broadcast_to(vector.reshape(1, -1), (TEAM, vector.size))

    live_tiles = (lengths + (TILE - 1)) // TILE
    row = jnp.concatenate(
        [
            head_gate_weight.reshape(rho, TEAM, mine).transpose(1, 2, 0).reshape(TEAM, -1),
            everyone_in_team(attention_gain),
            everyone_in_team(feedforward_gain),
            everyone_in_team(query_key_gain),
            everyone_in_team(live_tiles.astype(BF16)),
        ],
        axis=1,
    )
    cols = q_cols + 2 * k_cols
    row = jnp.pad(row, ((0, 0), (0, cols - row.shape[1])))[:, None, :]
    attn = jnp.concatenate(
        [
            query_weight.reshape(rho, TEAM, q_cols),
            key_matrix.reshape(rho, TEAM, k_cols),
            value_matrix.reshape(rho, TEAM, k_cols),
        ],
        axis=2,
    ).transpose(1, 0, 2)
    attn = jnp.concatenate([attn, jnp.pad(row, ((0, 0), (0, 7), (0, 0)))], axis=1)
    attn = exchange(attn)
    head_lanes = mine * rho
    at_one, at_two, at_pair = head_lanes, head_lanes + rho, head_lanes + 2 * rho
    at_tiles = at_pair + 2 * pair_cols
    team_tiles = attn[:, rho, at_tiles].astype(jnp.int32)
    order = jnp.arange(TEAM, dtype=jnp.int32)
    tiles = jnp.sum(jnp.where((order[:, None] ^ t) == order[None, :], team_tiles[None, :], 0), axis=1)
    routed = lax.ppermute(output_weight, ALL, out_weight_routes(groups))
    team_rows = TEAM * rho
    small_at = team_rows + (width // cols) * rho
    stacked = jnp.concatenate(
        [attn[:, :rho].reshape(team_rows, cols)]
        + [routed[:, k : k + cols] for k in range(0, width, cols)]
        + [attn[:, rho], jnp.zeros((16 - TEAM, cols), BF16)],
        axis=0,
    )
    gathered = line_gather(stacked).reshape(groups, -1, cols)
    rows_small = gathered[:, small_at : small_at + TEAM].reshape(everyone, cols)
    weight_head = jnp.pad(
        rows_small[:, :head_lanes].reshape(everyone, mine, rho).transpose(1, 0, 2).reshape(mine, width),
        ((0, TILE - mine), (0, 0)),
    )
    gain_one = rows_small[:, at_one:at_two].reshape(1, width).astype(F32)
    gain_two = rows_small[:, at_two:at_pair].reshape(1, width).astype(F32)
    gain_pair = (
        rows_small[:, at_pair:at_tiles]
        .reshape(everyone, 2, pair_cols)
        .transpose(1, 0, 2)
        .reshape(2, size)
        .astype(F32)
    )
    def ff_split(w):
        return w.reshape(rho, TEAM, ff_cols).transpose(1, 0, 2)

    feed_shard = jnp.concatenate([ff_split(gate_weight), ff_split(up_weight)], axis=2)

    exponent = jnp.arange(size // 2, dtype=F32) * (-2.0 / size)
    frequency = jnp.power(ROPE_BASE, exponent)
    angles = jnp.arange(rows, dtype=F32)[:, None] * frequency[None, :]
    cosine = jnp.concatenate([jnp.cos(angles), jnp.cos(angles)], axis=1)
    sine = jnp.concatenate([-jnp.sin(angles), jnp.sin(angles)], axis=1)
    consts = (gathered, weight_head, gain_one, gain_pair, cosine, sine)
    team_tokens = team_gather(tokens)
    feed_shard = exchange(feed_shard).reshape(TEAM * rho, -1)
    weight_gate = line_gather(feed_shard[:, :ff_cols])
    live = lax.broadcasted_iota(jnp.int32, (rows, 1), 0) < lengths[0]
    live_rows = live.astype(F32)
    upstream = cotangent.astype(F32) * live_rows
    tick = mark([team_tokens[6]])
    later = lax.broadcasted_iota(jnp.int32, (rows, 1), 0) < lengths[0] + tick[0, 0]
    upstream_low = jnp.where(later, cotangent, jnp.zeros_like(cotangent))
    upstream_levels = TeamGather(upstream_low)
    parts, kept, tick = attend(tiles, team_tokens, consts, mine, mark([upstream_low]))
    normed, qkv, logit, gated = kept
    weight_up = line_gather(hold([feed_shard[:, ff_cols:]], tick)[0])
    routes = out_weight_routes(groups)
    returns = [(user, owner) for owner, user in routes]
    routed_down = lax.ppermute(hold([down_weight], upstream_low)[0], ALL, routes)
    parts = hold(parts, mark([upstream_levels.a1, upstream_levels.a2, upstream_levels.a4, tick, routed_down]))
    arrived = TeamSum(parts)
    arrived.first()
    weight_down = line_gather(hold([routed_down], arrived.sent[0])[0])
    inputs = tokens.astype(F32)
    hidden_state = inputs + arrived.total(weight_gate)

    normed_two = rms(hidden_state, gain_two).astype(BF16)
    team_upstream = upstream_levels.blocks(normed_two)
    team_two = TeamGather(normed_two).blocks(weight_up)
    outs, grads, saved = feed(tiles, team_two, team_upstream, weight_gate, weight_up, weight_down)
    inner, feed_back, two_all, ups_all = saved
    arrived = TeamSum(grads)
    arrived.first()
    two_grad = arrived.total()
    inner = hold([inner], mark(arrived.sent))[0]
    down_part = product_tn(inner, ups_all).astype(BF16)
    feed_back = hold([feed_back], mark([arrived.over_x, arrived.over_y]))[0]
    gate_part = product_tn(two_all, feed_back[:, :ff_cols]).astype(BF16)
    hidden_grad = upstream + rms_pull(hidden_state, gain_two, two_grad)
    hidden_low = hidden_grad.astype(BF16)
    feed_back = hold([feed_back], mark([gate_part, hidden_low]))[0]
    up_part = product_tn(two_all, feed_back[:, ff_cols:]).astype(BF16)
    parts_made = mark([gate_part, up_part])
    down_grad = line_sum(down_part)
    gate_grad = line_sum(hold([gate_part], down_grad)[0])
    up_grad = line_sum(hold([up_part], gate_grad)[0])
    feed_done = up_grad

    fed = TeamSum(hold(outs, arrived.over_x))
    team_hidden = TeamGather(hidden_low).blocks(mark(fed.ready + [gate_part, up_part]))
    two_scale = lax.rsqrt(jnp.mean(hidden_state * hidden_state, axis=-1, keepdims=True) + EPSILON)
    two_sum = jnp.sum(two_grad * hidden_state * two_scale, axis=0)
    first_hop = fed.first(mark(team_hidden + [parts_made]))
    parts, packed, head_sum, one_sum, pair_sum = attend_back(
        tiles, team_hidden, consts, (normed, qkv, logit, gated), mine, mark(fed.sent + [down_grad])
    )
    row = jnp.concatenate(
        [
            head_sum[:mine].reshape(mine, everyone, rho).transpose(1, 0, 2).reshape(everyone, -1),
            (one_sum / gain_one[0]).reshape(everyone, rho),
            two_sum.reshape(everyone, rho),
            pair_sum.reshape(2, everyone, pair_cols).transpose(1, 0, 2).reshape(everyone, -1),
        ],
        axis=1,
    ).astype(BF16)
    row = jnp.pad(row, ((0, 0), (0, cols - row.shape[1]))).reshape(groups, TEAM, cols)
    packed = lax.dynamic_update_slice(packed, row, (0, small_at, 0))
    down_owned = lax.ppermute(hold([down_grad], fed.sent[0])[0], ALL, returns)
    parts = hold(parts, mark(first_hop + [gate_grad, down_owned]))
    arrived = TeamSum(parts)
    arrived.first()
    packed = hold([packed.reshape(-1, cols)], mark([feed_done] + arrived.sent))[0]
    normed_grad = arrived.total(packed)
    packed = line_sum(packed)
    summed = packed
    layer_output = ((hidden_state + fed.total(mark([normed_grad, summed]))) * live_rows).astype(BF16)
    tokens_grad = (hidden_grad + rms_pull(inputs, gain_one, normed_grad)).astype(BF16)
    feed_grad = jnp.concatenate([gate_grad, hold([up_grad], mark(arrived.last_sent))[0]], axis=1)
    feed_grad = exchange(feed_grad.reshape(TEAM, rho, 2 * ff_cols))
    feed_grad = hold([feed_grad], mark(fed.last_sent))[0]

    def ff_join(w):
        return w.transpose(1, 0, 2).reshape(rho, ff)

    gate_grad, up_grad = hold(
        [ff_join(feed_grad[:, :, :ff_cols]), ff_join(feed_grad[:, :, ff_cols:])], summed
    )
    output_grad = packed[team_rows:small_at].reshape(-1, rho, cols).transpose(1, 0, 2).reshape(rho, width)
    output_grad = lax.ppermute(output_grad, ALL, returns)
    packed = jnp.concatenate(
        [
            packed[:team_rows].reshape(TEAM, rho, cols),
            jnp.pad(packed[small_at : small_at + TEAM][:, None], ((0, 0), (0, 7), (0, 0))),
        ],
        axis=1,
    )
    packed = exchange(packed)
    attn_grad = packed[:, :rho].transpose(1, 0, 2)
    rows_small = packed[:, rho].astype(F32)
    sums = jnp.sum(rows_small[:, head_lanes:], axis=0)
    head_gate_grad = rows_small[:, :head_lanes].reshape(heads, rho).T
    return (
        layer_output,
        tokens_grad,
        sums[:rho],
        attn_grad[:, :, :q_cols].reshape(rho, -1).astype(F32),
        attn_grad[:, :, q_cols : q_cols + k_cols].reshape(rho, -1).astype(F32),
        attn_grad[:, :, q_cols + k_cols :].reshape(rho, -1).astype(F32),
        head_gate_grad,
        output_grad.astype(F32),
        sums[2 * rho : 2 * rho + 2 * pair_cols].reshape(2, pair_cols),
        sums[rho : 2 * rho],
        gate_grad.astype(F32),
        up_grad.astype(F32),
        down_owned.astype(F32),
    )


def solution(mesh):
    groups = mesh.size // TEAM
    rows, vector, columns = P(ALL, None), P(ALL), P(None, ALL)

    def step(*args):
        return local(groups, *args)

    return jax.shard_map(
        step,
        mesh=mesh,
        in_specs=(
            rows, vector, rows, vector, rows, rows, rows, rows, rows, columns, vector, rows, rows, rows,
        ),
        out_specs=(
            rows, rows, vector, rows, rows, rows, rows, rows, columns, vector, rows, rows, rows,
        ),
        check_vma=False,
    )
```

```python
import jax
import jax.numpy as jnp
from jax import lax
from jax.experimental import pallas as pl
from jax.experimental.pallas import tpu as pltpu
from jax.sharding import PartitionSpec as P

EPSILON = 1e-06
ROPE_BASE = 1000000.0
TEAM = 8
ALL = ("dp", "fsdp")
F32 = jnp.float32
BF16 = jnp.bfloat16
TILE = 128
ANY = pl.BlockSpec(memory_space=pl.ANY)
VMEM = pl.BlockSpec(memory_space=pltpu.VMEM)
SMEM = pl.BlockSpec(memory_space=pltpu.SMEM)


def product(left, right):
    return jnp.dot(left, right, preferred_element_type=F32)


def product_nt(left, right):
    return lax.dot_general(left, right, (((1,), (1,)), ((), ())), preferred_element_type=F32)


def product_tn(left, right):
    return lax.dot_general(left, right, (((0,), (0,)), ((), ())), preferred_element_type=F32)


def world():
    return lax.axis_size(ALL)


def member():
    return lax.axis_index(ALL) % TEAM


def teams():
    return [[first + t for t in range(TEAM)] for first in range(0, world(), TEAM)]


def lines():
    return [list(range(t, world(), TEAM)) for t in range(TEAM)]


def permute(array, pairs):
    return lax.ppermute(
        array, ALL, [(team[a], team[b]) for team in teams() for a, b in pairs]
    )


def swap(array, bits):
    return permute(array, [(i, i ^ bits) for i in range(TEAM)])


def exchange(blocks):
    if lax.axis_size("fsdp") == TEAM:
        return lax.all_to_all(blocks, "fsdp", 0, 0, tiled=True)
    return lax.all_to_all(blocks, ALL, 0, 0, tiled=True, axis_index_groups=teams())


def line_gather(shard):
    if lax.axis_size("fsdp") == TEAM:
        return lax.all_gather(shard, "dp", axis=0, tiled=True)
    return lax.all_gather(shard, ALL, axis=0, tiled=True, axis_index_groups=lines())


def line_sum(array):
    if lax.axis_size("fsdp") == TEAM:
        return lax.psum_scatter(array, "dp", scatter_dimension=0, tiled=True)
    return lax.psum_scatter(array, ALL, scatter_dimension=0, tiled=True, axis_index_groups=lines())


class TeamGather:
    def __init__(self, own):
        self.own = own
        self.a1 = swap(own, 1)
        self.a2 = swap(own, 2)
        self.a4 = swap(own, 4)

    def blocks(self, tick=None):
        a2, a4 = self.a2, self.a4
        if tick is not None:
            a2, a4 = hold([a2, a4], tick)
        half = self.own.shape[0] // 2
        a6 = jnp.concatenate([swap(a4[:half], 2), swap(a2[half:], 4)], axis=0)
        return [self.own, self.a1, a2, swap(a2, 1), a4, swap(a4, 1), a6, swap(a6, 1)]


def team_gather(own):
    return TeamGather(own).blocks()


class TeamSum:
    def __init__(self, parts):
        half = parts[0].shape[0] // 2
        odd = {r: swap(parts[r + 1], 1) for r in (6, 2, 4, 0)}
        self.total6, self.total2, self.total4, self.total0 = (
            (parts[r].astype(F32) + odd[r].astype(F32)).astype(BF16) for r in (6, 2, 4, 0)
        )
        self.half = half
        self.ready = [
            jnp.concatenate([self.total6[:half], self.total2[:half]], axis=0),
            jnp.concatenate([self.total6[half:], self.total4[half:]], axis=0),
        ]

    def first(self, tick=None):
        self.sent = self.ready if tick is None else list(hold(self.ready, tick))
        self.over_x, self.over_y = swap(self.sent[0], 2), swap(self.sent[1], 4)
        return [self.over_x, self.over_y]

    def total(self, tick=None):
        half = self.half
        lasts = [
            (self.total2[half:].astype(F32) + self.over_y[:half].astype(F32)).astype(BF16),
            (self.total4[:half].astype(F32) + self.over_x[:half].astype(F32)).astype(BF16),
        ]
        x_low, y_top = lasts if tick is None else hold(lasts, tick)
        self.last_sent = [x_low, y_top]
        x_low = swap(x_low, 2).astype(F32)
        y_top = swap(y_top, 4).astype(F32)
        top = self.over_x[half:].astype(F32) + y_top
        low = x_low + self.over_y[half:].astype(F32)
        return self.total0.astype(F32) + jnp.concatenate([top, low], axis=0)


def out_weight_routes(groups):
    return [(i, TEAM * (i % groups) + i // groups) for i in range(groups * TEAM)]


def rms_pull(value, gain, grad):
    scale = lax.rsqrt(jnp.mean(value * value, axis=-1, keepdims=True) + EPSILON)
    weighted = grad * gain
    mean = jnp.mean(weighted * value, axis=-1, keepdims=True)
    return scale * weighted - scale * scale * scale * value * mean


def rms(value, gain):
    return value * lax.rsqrt(jnp.mean(value * value, axis=-1, keepdims=True) + EPSILON) * gain


def struct(shape, dtype):
    return jax.ShapeDtypeStruct(shape, dtype)


def hold(arrays, tick):
    def kernel(*refs):
        del refs

    count = len(arrays)
    return pl.pallas_call(
        kernel,
        out_shape=[struct(a.shape, a.dtype) for a in arrays],
        in_specs=[ANY] * count + [ANY],
        out_specs=[ANY] * count,
        input_output_aliases={i: i for i in range(count)},
    )(*arrays, tick)


def mark(arrays):
    def kernel(*refs):
        refs[-1][...] = jnp.zeros_like(refs[-1])

    return pl.pallas_call(
        kernel,
        out_shape=struct((8, 128), jnp.int32),
        in_specs=[ANY] * len(arrays),
        out_specs=VMEM,
    )(*arrays)


def for_tiles(tiles, most, body):
    for m in range(1, most + 1):

        @pl.when(tiles == m)
        def _(m=m):
            body(m * TILE)


def turned(u, cosine, sine):
    return u * cosine + pltpu.roll(u, u.shape[-1] // 2, 1) * sine


def head_norm(u):
    return lax.rsqrt(jnp.mean(u * u, axis=-1, keepdims=True) + EPSILON)


def head_back(grad, raw, gain, cosine, sine):
    e = turned(grad, cosine, -sine)
    scale = head_norm(raw)
    weighted = e * gain
    mean = jnp.mean(weighted * raw, axis=-1, keepdims=True)
    back = scale * weighted - scale * scale * scale * raw * mean
    return back, jnp.sum(e * raw * scale, axis=0, keepdims=True)


def weights_of(query, key, factor):
    scores = product_nt(query, key) * factor
    n = scores.shape[0]
    causal = lax.broadcasted_iota(jnp.int32, (n, n), 1) <= lax.broadcasted_iota(jnp.int32, (n, n), 0)
    scores = jnp.where(causal, scores, -jnp.inf)
    terms = jnp.exp(scores - jnp.max(scores, axis=-1, keepdims=True))
    return terms * (1.0 / jnp.sum(terms, axis=-1, keepdims=True))


def rows_of(tile, size=TILE):
    return pl.ds(pl.multiple_of(tile * size, size), size)


def each_block(r, body):
    for k in range(TEAM):
        pl.when(r == k)(lambda k=k: body(k))


def load_weights(gathered, weight_head, wa_v, wo_v, wh_v, sems):
    groups, _, cols = gathered.shape
    width = wo_v.shape[1]
    rho = width // (groups * TEAM)
    copies = [pltpu.make_async_copy(weight_head, wh_v, sems.at[0])]
    for g in range(groups):
        copies.append(
            pltpu.make_async_copy(
                gathered.at[g, pl.ds(0, TEAM * rho)],
                wa_v.at[pl.ds(g * TEAM * rho, TEAM * rho)],
                sems.at[len(copies)],
            )
        )
        for k in range(width // cols):
            copies.append(
                pltpu.make_async_copy(
                    gathered.at[g, pl.ds(TEAM * rho + k * rho, rho)],
                    wo_v.at[pl.ds(g * rho, rho), pl.ds(k * cols, cols)],
                    sems.at[len(copies)],
                )
            )
    return copies


def attend(tiles, tokens, consts, mine, after):
    gathered, weight_head, gain, gains, cosine, sine = consts
    rows, width = tokens[0].shape
    size = gains.shape[1]
    q_cols = mine * size
    cols = gathered.shape[2]
    factor = size ** (-0.5)

    def kernel(*refs):
        tiles_ref, toks = refs[0], refs[1 : 1 + TEAM]
        wa, wh, gain_ref, gains_ref, cos_ref, sin_ref, _ = refs[1 + TEAM : 8 + TEAM]
        parts = refs[8 + TEAM : 8 + 2 * TEAM]
        normed_all, qkv_all, logit_all, gated_all, tick = refs[8 + 2 * TEAM : 13 + 2 * TEAM]
        (
            tok_v, wa_v, wh_v, wo_v, part_v, normed_v, qkv_v, logit_v, gated_v, w_sem, in_sem, out_sem,
        ) = refs[13 + 2 * TEAM :]
        tick[...] = jnp.zeros_like(tick)

        def load(k, slot):
            return pltpu.make_async_copy(toks[k], tok_v.at[slot], in_sem.at[slot])

        def store(r, slot, j, k=0):
            src = (part_v, normed_v, qkv_v, logit_v, gated_v)[j].at[slot]
            dst = parts[k] if j == 0 else (normed_all, qkv_all, logit_all, gated_all)[j - 1].at[rows_of(r, rows)]
            return pltpu.make_async_copy(src, dst, out_sem.at[j, slot])

        load(0, 0).start()
        weights = load_weights(wa, wh, wa_v, wo_v, wh_v, w_sem)
        for copy in weights:
            copy.start()
        for copy in weights:
            copy.wait()

        def step(r, carry):
            slot = r % 2

            @pl.when(r + 1 < TEAM)
            def _():
                each_block(r + 1, lambda k: load(k, 1 - slot).start())

            load(0, slot).wait()

            @pl.when(r >= 2)
            def _():
                for j in range(5):
                    store(r - 2, slot, j).wait()

            def body(n):
                value = tok_v[slot, :n].astype(F32)
                normed = rms(value, gain_ref[...]).astype(BF16)
                normed_v[slot, :n] = normed
                qkv = product(normed, wa_v[...])
                qkv_v[slot, :n] = qkv
                logit = product_nt(normed, wh_v[...])
                logit_v[slot, :n] = logit
                cos, sin = cos_ref[:n], sin_ref[:n]
                key = qkv[:, q_cols : q_cols + size]
                key = turned(key * head_norm(key) * gains_ref[1:2], cos, sin).astype(BF16)
                values = qkv[:, q_cols + size :].astype(BF16)
                for h in range(mine):
                    query = qkv[:, h * size : (h + 1) * size]
                    query = turned(query * head_norm(query) * gains_ref[0:1], cos, sin).astype(BF16)
                    attention = weights_of(query, key, factor)
                    mixture = product(attention.astype(BF16), values)
                    gate = jax.nn.sigmoid(logit[:, h : h + 1])
                    gated_v[slot, :n, h * size : (h + 1) * size] = (mixture * gate).astype(BF16)
                part_v[slot, :n] = product(gated_v[slot, :n], wo_v[...]).astype(BF16)
                if n < rows:
                    part_v[slot, n:] = jnp.zeros((rows - n, width), BF16)
                    normed_v[slot, n:] = jnp.zeros((rows - n, width), BF16)
                    gated_v[slot, n:] = jnp.zeros((rows - n, q_cols), BF16)

            for_tiles(tiles_ref[r], rows // TILE, body)
            each_block(r, lambda k: store(r, slot, 0, k).start())
            for j in range(1, 5):
                store(r, slot, j).start()
            return carry

        lax.fori_loop(0, TEAM, step, 0)
        for r in (TEAM - 2, TEAM - 1):
            for j in range(5):
                store(r, r % 2, j).wait()

    whole = TEAM * rows
    result = pl.pallas_call(
        kernel,
        out_shape=[struct((rows, width), BF16)] * TEAM
        + [
            struct((whole, width), BF16),
            struct((whole, cols), F32),
            struct((whole, TILE), F32),
            struct((whole, q_cols), BF16),
            struct((8, 128), jnp.int32),
        ],
        in_specs=[SMEM] + [ANY] * (TEAM + 2) + [VMEM] * 4 + [ANY],
        out_specs=[ANY] * (TEAM + 4) + [VMEM],
        scratch_shapes=[
            pltpu.VMEM((2, rows, width), BF16),
            pltpu.VMEM((width, cols), BF16),
            pltpu.VMEM(weight_head.shape, BF16),
            pltpu.VMEM((q_cols, width), BF16),
            pltpu.VMEM((2, rows, width), BF16),
            pltpu.VMEM((2, rows, width), BF16),
            pltpu.VMEM((2, rows, cols), F32),
            pltpu.VMEM((2, rows, TILE), F32),
            pltpu.VMEM((2, rows, q_cols), BF16),
            pltpu.SemaphoreType.DMA((1 + gathered.shape[0] * (1 + width // cols),)),
            pltpu.SemaphoreType.DMA((2,)),
            pltpu.SemaphoreType.DMA((5, 2)),
        ],
        compiler_params=pltpu.CompilerParams(vmem_limit_bytes=48 << 20),
        cost_estimate=pl.CostEstimate(flops=30 << 30, bytes_accessed=60 << 20, transcendentals=1 << 20),
    )(tiles, *tokens, gathered, weight_head, gain, gains, cosine, sine, after)
    return result[:TEAM], result[TEAM : TEAM + 4], result[TEAM + 4]


def attend_back(tiles, hidden, consts, saved, mine, after):
    gathered, weight_head, gain, gains, cosine, sine = consts
    rows, width = hidden[0].shape
    size = gains.shape[1]
    q_cols = mine * size
    cols = gathered.shape[2]
    factor = size ** (-0.5)

    def kernel(*refs):
        tiles_ref, hids = refs[0], refs[1 : 1 + TEAM]
        wa, wh, normed_all, qkv_all, logit_all, gated_all = refs[1 + TEAM : 7 + TEAM]
        gains_ref, cos_ref, sin_ref, _ = refs[7 + TEAM : 11 + TEAM]
        parts = refs[11 + TEAM : 11 + 2 * TEAM]
        packed, head_sum, gain_sum, gains_sum = refs[11 + 2 * TEAM : 15 + 2 * TEAM]
        (
            hid_v, wa_v, wh_v, wo_v, normed_v, qkv_v, logit_v, gated_v, part_v, back_v, attn_sum, out_sum,
            w_sem, in_sem, out_sem,
        ) = refs[15 + 2 * TEAM :]

        def loads(r, slot, k):
            yield pltpu.make_async_copy(hids[k], hid_v.at[slot], in_sem.at[0, slot])
            here = rows_of(r, rows)
            for j, (src, dst) in enumerate(
                ((qkv_all, qkv_v), (logit_all, logit_v), (normed_all, normed_v), (gated_all, gated_v))
            ):
                yield pltpu.make_async_copy(src.at[here], dst.at[slot], in_sem.at[1 + j, slot])

        def start_loads(r, slot):
            def body(k):
                for copy in loads(r, slot, k):
                    copy.start()

            each_block(r, body)

        def store(slot, k=0):
            return pltpu.make_async_copy(part_v.at[slot], parts[k], out_sem.at[slot])

        for copy in loads(0, 0, 0):
            copy.start()
        weights = load_weights(wa, wh, wa_v, wo_v, wh_v, w_sem)
        for copy in weights:
            copy.start()
        for ref in (attn_sum, out_sum, gain_sum, gains_sum):
            ref[...] = jnp.zeros_like(ref)
        for copy in weights:
            copy.wait()

        def step(r, carry):
            slot = r % 2

            @pl.when(r + 1 < TEAM)
            def _():
                start_loads(r + 1, 1 - slot)

            for copy in loads(r, slot, 0):
                copy.wait()

            @pl.when(r >= 2)
            def _():
                store(slot).wait()

            def body(n):
                hidden_low = hid_v[slot, :n]
                normed = normed_v[slot, :n]
                out_sum[...] += product_tn(gated_v[slot, :n], hidden_low)
                gated_grad = product_nt(hidden_low, wo_v[...])
                cos, sin = cos_ref[:n], sin_ref[:n]
                key_raw = qkv_v[slot, :n, q_cols : q_cols + size]
                key = turned(key_raw * head_norm(key_raw) * gains_ref[1:2], cos, sin).astype(BF16)
                values = qkv_v[slot, :n, q_cols + size :].astype(BF16)
                lane = lax.broadcasted_iota(jnp.int32, (n, TILE), 1)
                logit_back = jnp.zeros((n, TILE), F32)
                values_back = jnp.zeros((n, size), F32)
                key_grad = jnp.zeros((n, size), F32)
                query_sum = jnp.zeros((1, size), F32)
                for h in range(mine):
                    span = slice(h * size, (h + 1) * size)
                    query_raw = qkv_v[slot, :n, span]
                    query = turned(query_raw * head_norm(query_raw) * gains_ref[0:1], cos, sin).astype(BF16)
                    attention = weights_of(query, key, factor)
                    attention_low = attention.astype(BF16)
                    mixture = product(attention_low, values)
                    gate = jax.nn.sigmoid(logit_v[slot, :n, h : h + 1])
                    head_grad = gated_grad[:, span]
                    mixture_back = (head_grad * gate).astype(BF16)
                    one = jnp.sum(head_grad * mixture, axis=-1, keepdims=True) * gate * (1.0 - gate)
                    logit_back = jnp.where(lane == h, one, logit_back)
                    values_back += product_tn(attention_low, mixture_back)
                    attention_grad = product_nt(mixture_back, values)
                    scores_back = (
                        attention
                        * (attention_grad - jnp.sum(attention_grad * attention, axis=-1, keepdims=True))
                    ).astype(BF16)
                    query_grad = product(scores_back, key) * factor
                    key_grad += product_tn(scores_back, query)
                    back, total = head_back(query_grad, query_raw, gains_ref[0:1], cos, sin)
                    back_v[:n, span] = back.astype(BF16)
                    query_sum += total
                back, key_sum = head_back(key_grad * factor, key_raw, gains_ref[1:2], cos, sin)
                back_v[:n, q_cols : q_cols + size] = back.astype(BF16)
                back_v[:n, q_cols + size : cols] = values_back.astype(BF16)
                logit_back = logit_back.astype(BF16)
                back_v[:n, cols:] = logit_back
                gains_sum[0:1] += query_sum
                gains_sum[1:2] += key_sum
                part = product_nt(back_v[:n, :cols], wa_v[...]) + product(logit_back, wh_v[...])
                part_v[slot, :n] = part.astype(BF16)
                gain_sum[0:1] += jnp.sum(part * normed.astype(F32), axis=0, keepdims=True)
                attn_sum[...] += product_tn(back_v[:n], normed)
                if n < rows:
                    part_v[slot, n:] = jnp.zeros((rows - n, width), BF16)

            for_tiles(tiles_ref[r], rows // TILE, body)
            each_block(r, lambda k: store(slot, k).start())
            return carry

        lax.fori_loop(0, TEAM, step, 0)
        head_sum[...] = attn_sum[cols : cols + 8]
        turned_sum = attn_sum[:cols].T.astype(BF16)
        groups, height, _ = packed.shape
        rho = width // (groups * TEAM)
        for g in range(groups):
            packed[g, : TEAM * rho] = turned_sum[g * TEAM * rho : (g + 1) * TEAM * rho]
            for k in range(width // cols):
                top = TEAM * rho + k * rho
                packed[g, top : top + rho] = out_sum[
                    g * rho : (g + 1) * rho, k * cols : (k + 1) * cols
                ].astype(BF16)
            packed[g, height - 16 :] = jnp.zeros((16, cols), BF16)
        store(0).wait()
        store(1).wait()

    result = pl.pallas_call(
        kernel,
        out_shape=[struct((rows, width), BF16)] * TEAM
        + [
            struct(gathered.shape, BF16),
            struct((8, width), F32),
            struct((8, width), F32),
            struct((8, size), F32),
        ],
        in_specs=[SMEM] + [ANY] * (TEAM + 6) + [VMEM] * 3 + [ANY],
        out_specs=[ANY] * TEAM + [VMEM] * 4,
        scratch_shapes=[
            pltpu.VMEM((2, rows, width), BF16),
            pltpu.VMEM((width, cols), BF16),
            pltpu.VMEM(weight_head.shape, BF16),
            pltpu.VMEM((q_cols, width), BF16),
            pltpu.VMEM((2, rows, width), BF16),
            pltpu.VMEM((2, rows, cols), F32),
            pltpu.VMEM((2, rows, TILE), F32),
            pltpu.VMEM((2, rows, q_cols), BF16),
            pltpu.VMEM((2, rows, width), BF16),
            pltpu.VMEM((rows, cols + TILE), BF16),
            pltpu.VMEM((cols + TILE, width), F32),
            pltpu.VMEM((q_cols, width), F32),
            pltpu.SemaphoreType.DMA((1 + gathered.shape[0] * (1 + width // cols),)),
            pltpu.SemaphoreType.DMA((5, 2)),
            pltpu.SemaphoreType.DMA((2,)),
        ],
        compiler_params=pltpu.CompilerParams(vmem_limit_bytes=56 << 20),
        cost_estimate=pl.CostEstimate(flops=45 << 30, bytes_accessed=70 << 20, transcendentals=1 << 20),
    )(tiles, *hidden, gathered, weight_head, *saved, gains, cosine, sine, after)
    return result[:TEAM], *result[TEAM : TEAM + 2], result[TEAM + 2][0], result[TEAM + 3][:2]


def tile_places(tiles_ref, rows):
    places, total = [], 0
    for r in range(TEAM):
        count = tiles_ref[r]
        for j in range(rows // TILE):
            places.append((r, j, j < count, total + j))
        total = total + count
    return places, total


def feed(tiles, twos, upstreams, weight_gate, weight_up, weight_down):
    rows, width = twos[0].shape
    ff_cols = weight_down.shape[0]
    whole = TEAM * rows
    chunk = 2 * TILE
    chunks = whole // chunk

    def kernel(*refs):
        tiles_ref, twos_ref, ups_ref = refs[0], refs[1 : 1 + TEAM], refs[1 + TEAM : 1 + 2 * TEAM]
        weights_ref = refs[1 + 2 * TEAM : 4 + 2 * TEAM]
        outs_ref = refs[4 + 2 * TEAM : 4 + 3 * TEAM]
        grads_ref = refs[4 + 3 * TEAM : 4 + 4 * TEAM]
        inner_all, back_all, two_all, ups_all = refs[4 + 4 * TEAM : 8 + 4 * TEAM]
        (
            two_v, ups_v, wg_v, wu_v, wd_v, inner_v, back_v, out_v, grad_v, zero_v,
            w_sem, load_sem, keep_sem, tile_sem, dead_sem,
        ) = refs[8 + 4 * TEAM :]
        places, total = tile_places(tiles_ref, rows)
        used = (total + 1) // 2

        def loads(sources, packed, which):
            for k, (r, j, live, place) in enumerate(places):
                yield live, pltpu.make_async_copy(
                    sources[r].at[rows_of(j)], packed.at[rows_of(place)], load_sem.at[which, k]
                )

        weights = [
            pltpu.make_async_copy(src, dst, w_sem.at[j])
            for j, (src, dst) in enumerate(zip(weights_ref, (wg_v, wu_v, wd_v)))
        ]
        for live, copy in loads(twos_ref, two_v, 0):
            pl.when(live)(copy.start)
        for copy in weights:
            copy.start()
        for live, copy in loads(ups_ref, ups_v, 1):
            pl.when(live)(copy.start)
        zero_v[...] = jnp.zeros_like(zero_v)

        def dead(k, r, j):
            zeros = zero_v.at[:TILE]
            yield pltpu.make_async_copy(zeros, grads_ref[r].at[rows_of(j)], dead_sem.at[0, k])
            yield pltpu.make_async_copy(zeros, outs_ref[r].at[rows_of(j)], dead_sem.at[1, k])

        for k, (r, j, live, place) in enumerate(places):

            @pl.when(jnp.logical_not(live))
            def _(k=k, r=r, j=j):
                for copy in dead(k, r, j):
                    copy.start()

        def keeps(c, sources):
            for j, (src, dst) in enumerate(zip(sources, (two_all, ups_all, inner_all, back_all))):
                yield pltpu.make_async_copy(src, dst.at[rows_of(c, chunk)], keep_sem.at[j, c])

        zeros = (zero_v, zero_v, zero_v.at[:, :ff_cols], zero_v.at[:, : 2 * ff_cols])
        for c in range(TEAM // 2, chunks):

            @pl.when(c >= used)
            def _(c=c):
                for copy in keeps(c, zeros):
                    copy.start()

        @pl.when(total % 2 == 1)
        def _():
            two_v[rows_of(total)] = jnp.zeros((TILE, width), BF16)
            ups_v[rows_of(total)] = jnp.zeros((TILE, width), BF16)

        for live, copy in loads(twos_ref, two_v, 0):
            pl.when(live)(copy.wait)
        for copy in weights:
            copy.wait()
        for live, copy in loads(ups_ref, ups_v, 1):
            pl.when(live)(copy.wait)

        def tile_stores(r, j, slot, side):
            here = pl.ds(side * TILE, TILE)
            yield pltpu.make_async_copy(
                grad_v.at[slot, here], grads_ref[r].at[rows_of(j)], tile_sem.at[0, slot, side]
            )
            yield pltpu.make_async_copy(
                out_v.at[slot, here], outs_ref[r].at[rows_of(j)], tile_sem.at[1, slot, side]
            )

        def wait_tiles(c, slot):
            for side in range(2):

                @pl.when(2 * c + side < total)
                def _(side=side):
                    for copy in tile_stores(0, 0, slot, side):
                        copy.wait()

        def body(c, carry):
            slot = c % 2
            span = rows_of(c, chunk)

            @pl.when(c >= 2)
            def _():
                wait_tiles(c - 2, slot)
                for j, copy in enumerate(keeps(c - 2, zeros)):
                    if j >= 2:
                        copy.wait()

            gate_part = product(two_v[span], wg_v[...])
            up_part = product(two_v[span], wu_v[...])
            sig = jax.nn.sigmoid(gate_part)
            silu = gate_part * sig
            inner_v[slot] = (silu * up_part).astype(BF16)
            inner_grad = product_nt(ups_v[span], wd_v[...])
            back_v[slot, :, :ff_cols] = (inner_grad * up_part * (sig + silu * (1.0 - sig))).astype(BF16)
            back_v[slot, :, ff_cols:] = (inner_grad * silu).astype(BF16)
            for copy in keeps(c, (two_v.at[span], ups_v.at[span], inner_v.at[slot], back_v.at[slot])):
                copy.start()
            grad = product_nt(back_v[slot, :, :ff_cols], wg_v[...]) + product_nt(
                back_v[slot, :, ff_cols:], wu_v[...]
            )
            grad_v[slot] = grad.astype(BF16)
            out_v[slot] = product(inner_v[slot], wd_v[...]).astype(BF16)
            for k, (r, j, live, place) in enumerate(places):
                for side in range(2):

                    @pl.when(jnp.logical_and(live, place == 2 * c + side))
                    def _(r=r, j=j, side=side):
                        for copy in tile_stores(r, j, slot, side):
                            copy.start()

            return carry

        lax.fori_loop(0, used, body, 0)
        wait_tiles(used - 2, used % 2)
        wait_tiles(used - 1, (used - 1) % 2)
        for k, (r, j, live, place) in enumerate(places):

            @pl.when(jnp.logical_not(live))
            def _(k=k, r=r, j=j):
                for copy in dead(k, r, j):
                    copy.wait()

        for c in range(chunks):
            for j, copy in enumerate(keeps(c, zeros)):
                if j < 2:
                    copy.wait()
                else:
                    pl.when(c >= used - 2)(copy.wait)

    count = whole // TILE
    result = pl.pallas_call(
        kernel,
        out_shape=[struct((rows, width), BF16)] * (2 * TEAM)
        + [
            struct((whole, ff_cols), BF16),
            struct((whole, 2 * ff_cols), BF16),
            struct((whole, width), BF16),
            struct((whole, width), BF16),
        ],
        in_specs=[SMEM] + [ANY] * (3 + 2 * TEAM),
        out_specs=[ANY] * (2 * TEAM + 4),
        scratch_shapes=[
            pltpu.VMEM((whole, width), BF16),
            pltpu.VMEM((whole, width), BF16),
            pltpu.VMEM(weight_gate.shape, BF16),
            pltpu.VMEM(weight_up.shape, BF16),
            pltpu.VMEM(weight_down.shape, BF16),
            pltpu.VMEM((2, chunk, ff_cols), BF16),
            pltpu.VMEM((2, chunk, 2 * ff_cols), BF16),
            pltpu.VMEM((2, chunk, width), BF16),
            pltpu.VMEM((2, chunk, width), BF16),
            pltpu.VMEM((chunk, width), BF16),
            pltpu.SemaphoreType.DMA((3,)),
            pltpu.SemaphoreType.DMA((2, count)),
            pltpu.SemaphoreType.DMA((4, chunks)),
            pltpu.SemaphoreType.DMA((2, 2, 2)),
            pltpu.SemaphoreType.DMA((2, count)),
        ],
        compiler_params=pltpu.CompilerParams(vmem_limit_bytes=60 << 20),
        cost_estimate=pl.CostEstimate(flops=58 << 30, bytes_accessed=100 << 20, transcendentals=1 << 20),
    )(tiles, *twos, *upstreams, weight_gate, weight_up, weight_down)
    return result[:TEAM], result[TEAM : 2 * TEAM], result[2 * TEAM :]


def local(
    groups,
    tokens,
    lengths,
    cotangent,
    attention_gain,
    query_weight,
    key_matrix,
    value_matrix,
    head_gate_weight,
    output_weight,
    query_key_gain,
    feedforward_gain,
    gate_weight,
    up_weight,
    down_weight,
):
    t = member()
    everyone = groups * TEAM
    rows, width = tokens.shape
    rho = query_weight.shape[0]
    phi = down_weight.shape[0]
    ff = gate_weight.shape[1]
    pair_cols = query_key_gain.shape[1]
    size = pair_cols * everyone
    heads = query_weight.shape[1] // size
    mine = heads // TEAM
    q_cols = query_weight.shape[1] // TEAM
    k_cols = key_matrix.shape[1] // TEAM
    ff_cols = ff // TEAM

    def everyone_in_team(vector):
        return jnp.broadcast_to(vector.reshape(1, -1), (TEAM, vector.size))

    live_tiles = (lengths + (TILE - 1)) // TILE
    row = jnp.concatenate(
        [
            head_gate_weight.reshape(rho, TEAM, mine).transpose(1, 2, 0).reshape(TEAM, -1),
            everyone_in_team(attention_gain),
            everyone_in_team(feedforward_gain),
            everyone_in_team(query_key_gain),
            everyone_in_team(live_tiles.astype(BF16)),
        ],
        axis=1,
    )
    cols = q_cols + 2 * k_cols
    row = jnp.pad(row, ((0, 0), (0, cols - row.shape[1])))[:, None, :]
    attn = jnp.concatenate(
        [
            query_weight.reshape(rho, TEAM, q_cols),
            key_matrix.reshape(rho, TEAM, k_cols),
            value_matrix.reshape(rho, TEAM, k_cols),
        ],
        axis=2,
    ).transpose(1, 0, 2)
    attn = jnp.concatenate([attn, jnp.pad(row, ((0, 0), (0, 7), (0, 0)))], axis=1)
    attn = exchange(attn)
    head_lanes = mine * rho
    at_one, at_two, at_pair = head_lanes, head_lanes + rho, head_lanes + 2 * rho
    at_tiles = at_pair + 2 * pair_cols
    team_tiles = attn[:, rho, at_tiles].astype(jnp.int32)
    order = jnp.arange(TEAM, dtype=jnp.int32)
    tiles = jnp.sum(jnp.where((order[:, None] ^ t) == order[None, :], team_tiles[None, :], 0), axis=1)
    routed = lax.ppermute(output_weight, ALL, out_weight_routes(groups))
    team_rows = TEAM * rho
    small_at = team_rows + (width // cols) * rho
    stacked = jnp.concatenate(
        [attn[:, :rho].reshape(team_rows, cols)]
        + [routed[:, k : k + cols] for k in range(0, width, cols)]
        + [attn[:, rho], jnp.zeros((16 - TEAM, cols), BF16)],
        axis=0,
    )
    gathered = line_gather(stacked).reshape(groups, -1, cols)
    rows_small = gathered[:, small_at : small_at + TEAM].reshape(everyone, cols)
    weight_head = jnp.pad(
        rows_small[:, :head_lanes].reshape(everyone, mine, rho).transpose(1, 0, 2).reshape(mine, width),
        ((0, TILE - mine), (0, 0)),
    )
    gain_one = rows_small[:, at_one:at_two].reshape(1, width).astype(F32)
    gain_two = rows_small[:, at_two:at_pair].reshape(1, width).astype(F32)
    gain_pair = (
        rows_small[:, at_pair:at_tiles]
        .reshape(everyone, 2, pair_cols)
        .transpose(1, 0, 2)
        .reshape(2, size)
        .astype(F32)
    )
    def ff_split(w):
        return w.reshape(rho, groups, TEAM, phi).transpose(2, 0, 1, 3).reshape(TEAM, rho, ff_cols)

    feed_shard = jnp.concatenate([ff_split(gate_weight), ff_split(up_weight)], axis=2)

    exponent = jnp.arange(size // 2, dtype=F32) * (-2.0 / size)
    frequency = jnp.power(ROPE_BASE, exponent)
    angles = jnp.arange(rows, dtype=F32)[:, None] * frequency[None, :]
    cosine = jnp.concatenate([jnp.cos(angles), jnp.cos(angles)], axis=1)
    sine = jnp.concatenate([-jnp.sin(angles), jnp.sin(angles)], axis=1)
    consts = (gathered, weight_head, gain_one, gain_pair, cosine, sine)
    team_tokens = team_gather(tokens)
    feed_shard = exchange(feed_shard).reshape(TEAM * rho, -1)
    weight_gate = line_gather(feed_shard[:, :ff_cols])
    live = lax.broadcasted_iota(jnp.int32, (rows, 1), 0) < lengths[0]
    live_rows = live.astype(F32)
    upstream = cotangent.astype(F32) * live_rows
    tick = mark([team_tokens[6]])
    later = lax.broadcasted_iota(jnp.int32, (rows, 1), 0) < lengths[0] + tick[0, 0]
    upstream_low = jnp.where(later, cotangent, jnp.zeros_like(cotangent))
    upstream_levels = TeamGather(upstream_low)
    parts, kept, tick = attend(tiles, team_tokens, consts, mine, mark([upstream_low]))
    normed, qkv, logit, gated = kept
    weight_up = line_gather(hold([feed_shard[:, ff_cols:]], tick)[0])
    parts = hold(parts, mark([upstream_levels.a1, upstream_levels.a2, upstream_levels.a4, tick]))
    arrived = TeamSum(parts)
    arrived.first()
    weight_down = line_gather(hold([down_weight], arrived.sent[0])[0])
    inputs = tokens.astype(F32)
    hidden_state = inputs + arrived.total(weight_gate)

    normed_two = rms(hidden_state, gain_two).astype(BF16)
    team_upstream = upstream_levels.blocks(normed_two)
    team_two = TeamGather(normed_two).blocks(weight_up)
    outs, grads, saved = feed(tiles, team_two, team_upstream, weight_gate, weight_up, weight_down)
    inner, feed_back, two_all, ups_all = saved
    arrived = TeamSum(grads)
    arrived.first()
    two_grad = arrived.total()
    inner = hold([inner], mark(arrived.sent))[0]
    down_part = product_tn(inner, ups_all).astype(BF16)
    feed_back = hold([feed_back], mark([arrived.over_x, arrived.over_y]))[0]
    gate_part = product_tn(two_all, feed_back[:, :ff_cols]).astype(BF16)
    hidden_grad = upstream + rms_pull(hidden_state, gain_two, two_grad)
    hidden_low = hidden_grad.astype(BF16)
    feed_back = hold([feed_back], mark([gate_part, hidden_low]))[0]
    up_part = product_tn(two_all, feed_back[:, ff_cols:]).astype(BF16)
    parts_made = mark([gate_part, up_part])
    down_grad = line_sum(down_part)
    gate_grad = line_sum(hold([gate_part], down_grad)[0])
    up_grad = line_sum(hold([up_part], gate_grad)[0])
    feed_done = up_grad

    fed = TeamSum(hold(outs, arrived.over_x))
    team_hidden = TeamGather(hidden_low).blocks(mark(fed.ready + [gate_part, up_part]))
    two_scale = lax.rsqrt(jnp.mean(hidden_state * hidden_state, axis=-1, keepdims=True) + EPSILON)
    two_sum = jnp.sum(two_grad * hidden_state * two_scale, axis=0)
    first_hop = fed.first(mark(team_hidden + [parts_made]))
    parts, packed, head_sum, one_sum, pair_sum = attend_back(
        tiles, team_hidden, consts, (normed, qkv, logit, gated), mine, mark(fed.sent + [down_grad])
    )
    row = jnp.concatenate(
        [
            head_sum[:mine].reshape(mine, everyone, rho).transpose(1, 0, 2).reshape(everyone, -1),
            (one_sum / gain_one[0]).reshape(everyone, rho),
            two_sum.reshape(everyone, rho),
            pair_sum.reshape(2, everyone, pair_cols).transpose(1, 0, 2).reshape(everyone, -1),
        ],
        axis=1,
    ).astype(BF16)
    row = jnp.pad(row, ((0, 0), (0, cols - row.shape[1]))).reshape(groups, TEAM, cols)
    packed = lax.dynamic_update_slice(packed, row, (0, small_at, 0))
    parts = hold(parts, mark(first_hop + [gate_grad]))
    arrived = TeamSum(parts)
    arrived.first()
    packed = hold([packed.reshape(-1, cols)], mark([feed_done] + arrived.sent))[0]
    normed_grad = arrived.total(packed)
    packed = line_sum(packed)
    summed = packed
    layer_output = ((hidden_state + fed.total(normed_grad)) * live_rows).astype(BF16)
    tokens_grad = (hidden_grad + rms_pull(inputs, gain_one, normed_grad)).astype(BF16)
    feed_grad = jnp.concatenate([gate_grad, hold([up_grad], mark(arrived.last_sent))[0]], axis=1)
    feed_grad = exchange(feed_grad.reshape(TEAM, rho, 2 * ff_cols))
    feed_grad = hold([feed_grad], mark(fed.last_sent + [summed]))[0]

    def ff_join(w):
        return w.reshape(TEAM, rho, groups, phi).transpose(1, 2, 0, 3).reshape(rho, ff)

    gate_grad, up_grad = hold(
        [ff_join(feed_grad[:, :, :ff_cols]), ff_join(feed_grad[:, :, ff_cols:])], summed
    )
    routes = [(user, owner) for owner, user in out_weight_routes(groups)]
    output_grad = packed[team_rows:small_at].reshape(-1, rho, cols).transpose(1, 0, 2).reshape(rho, width)
    output_grad = lax.ppermute(output_grad, ALL, routes)
    packed = jnp.concatenate(
        [
            packed[:team_rows].reshape(TEAM, rho, cols),
            jnp.pad(packed[small_at : small_at + TEAM][:, None], ((0, 0), (0, 7), (0, 0))),
        ],
        axis=1,
    )
    packed = exchange(packed)
    attn_grad = packed[:, :rho].transpose(1, 0, 2)
    rows_small = packed[:, rho].astype(F32)
    sums = jnp.sum(rows_small[:, head_lanes:], axis=0)
    head_gate_grad = rows_small[:, :head_lanes].reshape(heads, rho).T
    return (
        layer_output,
        tokens_grad,
        sums[:rho],
        attn_grad[:, :, :q_cols].reshape(rho, -1).astype(F32),
        attn_grad[:, :, q_cols : q_cols + k_cols].reshape(rho, -1).astype(F32),
        attn_grad[:, :, q_cols + k_cols :].reshape(rho, -1).astype(F32),
        head_gate_grad,
        output_grad.astype(F32),
        sums[2 * rho : 2 * rho + 2 * pair_cols].reshape(2, pair_cols),
        sums[rho : 2 * rho],
        gate_grad.astype(F32),
        up_grad.astype(F32),
        down_grad.astype(F32),
    )


def solution(mesh):
    groups = mesh.size // TEAM
    rows, vector, columns = P(ALL, None), P(ALL), P(None, ALL)

    def step(*args):
        return local(groups, *args)

    return jax.shard_map(
        step,
        mesh=mesh,
        in_specs=(
            rows, vector, rows, vector, rows, rows, rows, rows, rows, columns, vector, rows, rows, rows,
        ),
        out_specs=(
            rows, rows, vector, rows, rows, rows, rows, rows, columns, vector, rows, rows, rows,
        ),
        check_vma=False,
    )
```
